32 devices in a mesh: seq: 16 (over z, x, core), batch: 2 (over y).
Axes of the slice: x: 2, y: 2, z: 4, core: 2. Of those that a mesh axis runs over, the one named last changes fastest.
Arguments:
- inputs: bfloat16 [2, 2048, 768], P('batch', 'seq'), may hold values from -6 to 6
- attend_gain: bfloat16 [768], P(('seq', 'batch')), may hold values from 0.5 to 1.5
- attend_shift: bfloat16 [768], P(('seq', 'batch')), may hold values from -0.59765625 to 0.59765625
- mixing_weight: bfloat16 [768, 2304], P(('seq', 'batch')), may hold values from -0.21875 to 0.21875
- mixing_bias: bfloat16 [1536], P(('seq', 'batch')), may hold values from -0.119628906 to 0.119628906
- output_weight: bfloat16 [768, 768], P(('seq', 'batch')), may hold values from -0.875 to 0.875
- output_bias: bfloat16 [768], P(('seq', 'batch')), may hold values from -1.796875 to 1.796875
- feed_gain: bfloat16 [768], P(('seq', 'batch')), may hold values from 0.5 to 1.5
- feed_shift: bfloat16 [768], P(('seq', 'batch')), may hold values from -0.59765625 to 0.59765625
- up_weight: bfloat16 [768, 3072], P(('seq', 'batch')), may hold values from -0.21875 to 0.21875
- up_bias: bfloat16 [3072], P(('seq', 'batch')), may hold values from -0.59765625 to 0.59765625
- down_weight: bfloat16 [3072, 768], P(('seq', 'batch')), may hold values from -0.4375 to 0.4375
- down_bias: bfloat16 [768], P(('seq', 'batch')), may hold values from -2.390625 to 2.390625
- cotangent: bfloat16 [2, 2, 2048, 768], P(None, 'batch', 'seq'), may hold values from -6 to 6
Outputs:
- activations: bfloat16 [2, 2, 2048, 768], P(None, 'batch', 'seq')
- input_gradient: float32 [2, 2, 2048, 768], P(None, 'batch', 'seq')
- attend_gain_gradient: float32 [2, 768], P(None, ('seq', 'batch'))
- attend_shift_gradient: float32 [2, 768], P(None, ('seq', 'batch'))
- mixing_weight_gradient: float32 [2, 768, 2304], P(None, ('seq', 'batch'))
- mixing_bias_gradient: float32 [2, 1536], P(None, ('seq', 'batch'))
- output_weight_gradient: float32 [2, 768, 768], P(None, ('seq', 'batch'))
- output_bias_gradient: float32 [2, 768], P(None, ('seq', 'batch'))
- feed_gain_gradient: float32 [2, 768], P(None, ('seq', 'batch'))
- feed_shift_gradient: float32 [2, 768], P(None, ('seq', 'batch'))
- up_weight_gradient: float32 [2, 768, 3072], P(None, ('seq', 'batch'))
- up_bias_gradient: float32 [2, 3072], P(None, ('seq', 'batch'))
- down_weight_gradient: float32 [2, 3072, 768], P(None, ('seq', 'batch'))
- down_bias_gradient: float32 [2, 768], P(None, ('seq', 'batch'))
The draws below stay inside these ranges and needn't reach their ends.
All inputs are finite; a program needn't handle non-finite values.
Results may differ from the reference program's by a relative error of at most 0.014.
Values may be sent and summed in bfloat16 or wider, within the bound.
A program may use at most 320 MiB of HBM per device.

```python
from functools import partial
import jax
import jax.numpy as jnp
from jax import lax

D = 768
HEADS = 12
HEAD = 64
FF = 3072
SEQUENCES = 2
LENGTH = 2048


def block_levels(stream_key, shape, pieces, least, high):
    def one(dim, shards_of):
        draws = jax.random.uniform(jax.random.fold_in(jax.random.fold_in(stream_key, 6), dim), (shards_of,), jnp.float32, least / len(pieces), high / len(pieces))
        return jnp.repeat(jnp.exp(draws), shape[dim] // shards_of).reshape((-1,) + (1,) * (len(shape) - dim - 1))

    level = one(*pieces[0])
    for cut in pieces[1:]:
        level = level * one(*cut)
    return level


def centred(stream_key, dims, deviation, limit, split=(), held_as=jnp.bfloat16):
    factor_of = block_levels(stream_key, dims, split, -0.22, 0.18) if split else 1.0
    values = jax.random.normal(stream_key, dims, jnp.float32) * deviation * factor_of
    return jnp.minimum(jnp.maximum(values, -limit), limit).astype(held_as)


def setup_inputs(seed: int = 0) -> dict:
    key_of = jax.random.split(jax.random.key(seed), 15)
    inputs = centred(key_of[0], (SEQUENCES, LENGTH, D), 1.0, 6.0, ((0, 2), (1, 16)))
    attend_gain = jnp.clip(1.0 + 0.1 * jax.random.normal(key_of[1], (D,), jnp.float32), 0.5, 1.5).astype(jnp.bfloat16)
    attend_shift = centred(key_of[2], (D,), 0.1, 0.59765625, ((0, 32),))
    mixing_weight = centred(key_of[3], (D, 3 * D), D ** -0.5, 0.21875, ((0, 32),))
    mixing_bias = centred(key_of[4], (2 * D,), 0.02, 0.119628906, ((0, 32),))
    output_weight = centred(key_of[5], (D, D), (D // 16) ** -0.5, 0.875, ((0, 32),))
    output_bias = centred(key_of[6], (D,), 0.3, 1.796875, ((0, 32),))
    feed_gain = jnp.clip(1.0 + 0.1 * jax.random.normal(key_of[7], (D,), jnp.float32), 0.5, 1.5).astype(jnp.bfloat16)
    feed_shift = centred(key_of[8], (D,), 0.1, 0.59765625, ((0, 32),))
    up_weight = centred(key_of[9], (D, FF), D ** -0.5, 0.21875, ((0, 32),))
    up_bias = centred(key_of[10], (FF,), 0.1, 0.59765625, ((0, 32),))
    down_weight = centred(key_of[11], (FF, D), (FF // 16) ** -0.5, 0.4375, ((0, 32),))
    down_bias = centred(key_of[12], (D,), 0.4, 2.390625, ((0, 32),))
    cotangent = centred(key_of[13], (2, SEQUENCES, LENGTH, D), 1.0, 6.0, ((1, 2), (2, 16)))
    return {"inputs": inputs, "attend_gain": attend_gain, "attend_shift": attend_shift, "mixing_weight": mixing_weight, "mixing_bias": mixing_bias, "output_weight": output_weight, "output_bias": output_bias, "feed_gain": feed_gain, "feed_shift": feed_shift, "up_weight": up_weight, "up_bias": up_bias, "down_weight": down_weight, "down_bias": down_bias, "cotangent": cotangent}


EPS = 1e-05
SCALES = (12.0 ** (-0.5), 48.0 ** (-0.5))
PRECISE = lax.Precision.HIGHEST

@jax.custom_vjp
def low(v):
    return lax.optimization_barrier(v.astype(jnp.bfloat16)).astype(jnp.float32)

@jax.custom_vjp
def low_back(v):
    return v

def low_keep(v):
    return (low(v), None)

def low_pass(kept, grad):
    return (grad,)

def back_keep(v):
    return (v, None)

def back_low(kept, grad):
    return (low(grad),)
low.defvjp(low_keep, low_pass)
low_back.defvjp(back_keep, back_low)

def normalize(values, gain, shift):
    average = lax.optimization_barrier(jnp.mean(values, axis=-1, keepdims=True))
    centered = values - average
    variance = lax.optimization_barrier(jnp.mean(centered * centered, axis=-1, keepdims=True))
    return centered * lax.rsqrt(variance + EPS) * gain + shift

def attend_sequence(queries, key_rows, value_rows):
    length = queries.shape[0]
    block_rows = min(length, 512)
    key_pos = jnp.arange(length, dtype=jnp.int32)

    def block(start_row):
        query_block = lax.dynamic_slice_in_dim(queries, start_row, block_rows, 0)
        scores = jnp.einsum('qhe,khe->hqk', query_block, key_rows, precision=PRECISE) * HEAD ** (-0.5)
        query_pos = start_row + jnp.arange(block_rows, dtype=jnp.int32)
        scores = jnp.where(key_pos[None, None, :] <= query_pos[None, :, None], scores, -1e+30)
        scores = low_back(scores)
        probs = low(jax.nn.softmax(scores, axis=-1))
        return jnp.einsum('hqk,khe->qhe', probs, value_rows, precision=PRECISE)
    starts = jnp.arange(length // block_rows, dtype=jnp.int32) * block_rows
    blocks = lax.map(jax.checkpoint(block), starts)
    return blocks.reshape(length, HEADS * HEAD)

def layer(values, params, scale):
    attend_gain, attend_shift, mixing_weight, mixing_bias, output_weight, output_bias, feed_gain, feed_shift, up_weight, up_bias, down_weight, down_bias = params
    flat_rows = values.reshape(-1, D)
    first = low(normalize(flat_rows, attend_gain, attend_shift))
    bias_full = jnp.concatenate([mixing_bias[:D], jnp.zeros((D,), mixing_bias.dtype), mixing_bias[D:]])
    mixed = low_back(low(jnp.dot(first, mixing_weight, precision=PRECISE) + bias_full))
    mixed = mixed.reshape(SEQUENCES, LENGTH, 3, HEADS, HEAD)

    def per_sequence(carry, element):
        return (carry, attend_sequence(element[:, 0], element[:, 1], element[:, 2]))
    _, attended = lax.scan(per_sequence, None, mixed)
    attended = low_back(low(attended.reshape(-1, D)))
    branch = low_back(jnp.dot(attended, output_weight, precision=PRECISE) + output_bias)
    middle = flat_rows + scale * branch
    second = low(normalize(middle, feed_gain, feed_shift))
    hidden = low_back(jnp.dot(second, up_weight, precision=PRECISE) + up_bias)
    activated = low(jax.nn.gelu(hidden, approximate=True))
    feed = low_back(jnp.dot(activated, down_weight, precision=PRECISE) + down_bias)
    return (middle + scale * feed).reshape(values.shape)

def reference(inputs, attend_gain, attend_shift, mixing_weight, mixing_bias, output_weight, output_bias, feed_gain, feed_shift, up_weight, up_bias, down_weight, down_bias, cotangent):
    params = tuple((item.astype(jnp.float32) for item in (attend_gain, attend_shift, mixing_weight, mixing_bias, output_weight, output_bias, feed_gain, feed_shift, up_weight, up_bias, down_weight, down_bias)))
    values = inputs.astype(jnp.float32)
    outputs = []
    input_grads = []
    param_grads = []
    for depth in range(2):
        result, backward = jax.vjp(partial(layer, scale=SCALES[depth]), values, params)
        value_grad, weight_grads = backward(cotangent[depth].astype(jnp.float32))
        outputs.append(result.astype(jnp.bfloat16))
        input_grads.append(value_grad)
        param_grads.append(weight_grads)
    stacked = [jnp.stack([param_grads[0][index], param_grads[1][index]]) for index in range(12)]
    return (jnp.stack(outputs), jnp.stack(input_grads), stacked[0], stacked[1], stacked[2], stacked[3], stacked[4], stacked[5], stacked[6], stacked[7], stacked[8], stacked[9], stacked[10], stacked[11])
```

```python
from functools import partial

import jax
import jax.numpy as jnp
from jax import lax
from jax.experimental import pallas as pl
from jax.experimental.pallas import tpu as pltpu
from jax.sharding import PartitionSpec as P

HEADS = 12
EPS = 1e-05
SCALES = (12.0 ** (-0.5), 48.0 ** (-0.5))
NEGATIVE = -1e30
LOW = jnp.bfloat16
FULL = jnp.float32
TILE = 256


def normalize(values):
    average = jnp.mean(values, axis=-1, keepdims=True)
    centered = values - average
    inv_std = lax.rsqrt(jnp.mean(centered * centered, axis=-1, keepdims=True) + EPS)
    return centered * inv_std, inv_std


def norm_back(gradient, normed, inv_std, gain):
    scaled = gradient * gain
    inner = (
        scaled
        - jnp.mean(scaled, axis=-1, keepdims=True)
        - normed * jnp.mean(scaled * normed, axis=-1, keepdims=True)
    )
    return inv_std * inner


def dot(a, b, dims):
    return lax.dot_general(a, b, ((dims[:1], dims[1:]), ((), ())), preferred_element_type=FULL)


class Place:
    def __init__(self):
        self.s = lax.axis_size("seq")
        self.ny = lax.axis_size("batch")
        self.nz = self.s // 4
        seq = lax.axis_index("seq")
        self.y = lax.axis_index("batch")
        self.core = lax.rem(seq, 2)
        self.chip = seq // 2
        self.x = lax.rem(self.chip, 2)
        self.z = self.chip // 2
        self.sizes = {"z": self.nz, "x": 2, "y": self.ny, "core": 2}
        self.at = {"z": self.z, "x": self.x, "y": self.y, "core": self.core}

    def send(self, values, axis, d=1):
        pairs = []
        for s in range(self.s):
            for y in range(self.ny):
                c, x, z, t = s % 2, (s // 2) % 2, s // 4, y
                if axis == "z":
                    z = (z + d) % self.nz
                elif axis == "x":
                    x = 1 - x
                elif axis == "core":
                    c = 1 - c
                else:
                    t = (y + d) % self.ny
                pairs.append((s * self.ny + y, ((z * 2 + x) * 2 + c) * self.ny + t))
        return lax.ppermute(values, ("seq", "batch"), pairs)

    def gather(self, values, axis, dim):
        size, at = self.sizes[axis], self.at[axis]
        shape = values.shape[:dim] + (size,) + values.shape[dim:]
        whole = lax.dynamic_update_slice_in_dim(
            jnp.zeros(shape, values.dtype), jnp.expand_dims(values, dim), at, dim
        )
        for d in range(1, size):
            piece = jnp.expand_dims(self.send(values, axis, d), dim)
            whole = lax.dynamic_update_slice_in_dim(whole, piece, lax.rem(at + size - d, size), dim)
        return whole

    def scatter(self, values, axis, dim):
        size, at = self.sizes[axis], self.at[axis]

        def pick(i):
            return lax.dynamic_index_in_dim(values, lax.rem(i, size), dim, keepdims=False)

        total = pick(at).astype(FULL)
        for d in range(1, size):
            total = total + self.send(pick(at + d), axis, d).astype(FULL)
        return total

    def both(self, mine, theirs):
        got = self.send(theirs, "core")
        first = self.core == 0
        return jnp.stack([jnp.where(first, mine, got), jnp.where(first, got, mine)])


def attend_kernel(x_ref, gain_ref, shift_ref, w_ref, b_ref, h_ref, q_ref, k_ref, v_ref, o_ref, ot_ref, top_ref, vt_ref):
    length = x_ref.shape[0]
    head = q_ref.shape[1]
    tiles = length // TILE

    def project(i, _):
        rows = pl.ds(pl.multiple_of(i * TILE, TILE), TILE)
        normed, _ = normalize(x_ref[rows, :].astype(FULL))
        low = (normed * gain_ref[...] + shift_ref[...]).astype(LOW)
        h_ref[rows, :] = low
        mixed = dot(low, w_ref[...], (1, 0)) + b_ref[...]
        q_ref[rows, :] = (mixed[:, :head].astype(LOW) * (head ** (-0.5))).astype(LOW)
        k_ref[rows, :] = mixed[:, head : 2 * head].astype(LOW)
        value = mixed[:, 2 * head :].astype(LOW)
        v_ref[rows, :] = value
        vt_ref[:, rows] = value.T
        return 0

    lax.fori_loop(0, tiles, project, 0)

    def query_tile(i, _):
        rows = pl.ds(pl.multiple_of(i * TILE, TILE), TILE)
        query = q_ref[rows, :]

        def absorb(j, carry, masked):
            top, total, acc = carry
            keys = pl.ds(pl.multiple_of(j * TILE, TILE), TILE)
            scores = dot(k_ref[keys, :], query, (1, 1))
            if masked:
                key_pos = lax.broadcasted_iota(jnp.int32, scores.shape, 0)
                query_pos = lax.broadcasted_iota(jnp.int32, scores.shape, 1)
                scores = jnp.where(key_pos <= query_pos, scores, NEGATIVE)
            new_top = jnp.maximum(top, jnp.max(scores, axis=0, keepdims=True))
            weights = jnp.exp(scores - new_top)
            keep = jnp.exp(top - new_top)
            total = total * keep + jnp.sum(weights, axis=0, keepdims=True)
            acc = acc * keep + dot(vt_ref[:, keys], weights.astype(LOW), (1, 0))
            return new_top, total, acc

        start = (
            jnp.full((1, TILE), NEGATIVE, FULL),
            jnp.zeros((1, TILE), FULL),
            jnp.zeros((head, TILE), FULL),
        )
        carry = lax.fori_loop(0, i, lambda j, c: absorb(j, c, False), start)
        top, total, acc = absorb(i, carry, True)
        out = acc / total
        ot_ref[:, rows] = out
        o_ref[rows, :] = out.T.astype(LOW)
        top_ref[:, rows] = top + jnp.log(total)
        return 0

    lax.fori_loop(0, tiles, query_tile, 0)


def attend(x_all, gain, shift, weight, bias):
    length, head = x_all.shape[0], weight.shape[1] // 3
    low = jax.ShapeDtypeStruct((length, head), LOW)
    return pl.pallas_call(
        attend_kernel,
        out_shape=(
            jax.ShapeDtypeStruct(x_all.shape, LOW),
            low,
            low,
            low,
            low,
            jax.ShapeDtypeStruct((head, length), FULL),
            jax.ShapeDtypeStruct((1, length), FULL),
        ),
        scratch_shapes=[pltpu.VMEM((head, length), LOW)],
        compiler_params=pltpu.CompilerParams(vmem_limit_bytes=48 << 20),
        cost_estimate=pl.CostEstimate(
            flops=6 * length * length * head, bytes_accessed=8 * length * 768, transcendentals=length * length
        ),
        name="attend",
    )(x_all, gain, shift, weight, bias)


def attend_back_kernel(
    q_ref, k_ref, v_ref, ot_ref, top_ref, go_ref, gq_ref, gk_ref, gv_ref, kt_ref, got_ref, delta_ref, gqt_ref
):
    length, head = q_ref.shape
    tiles = length // TILE
    factor = head ** (-0.5)

    def prepare(i, _):
        rows = pl.ds(pl.multiple_of(i * TILE, TILE), TILE)
        kt_ref[:, rows] = k_ref[rows, :].T
        up = go_ref[rows, :].T
        for d in range(2):
            mine = up[d * head : (d + 1) * head, :]
            got_ref[d, :, rows] = mine
            delta_ref[d, :, rows] = jnp.sum(mine.astype(FULL) * ot_ref[:, rows], axis=0, keepdims=True)
            gqt_ref[d, :, rows] = jnp.zeros((head, TILE), FULL)
        return 0

    lax.fori_loop(0, tiles, prepare, 0)

    def key_tile(j, _):
        keys = pl.ds(pl.multiple_of(j * TILE, TILE), TILE)
        key = k_ref[keys, :]
        value = v_ref[keys, :]
        key_t = kt_ref[:, keys]

        def step(i, carry, masked):
            gv, gk0, gk1 = carry
            rows = pl.ds(pl.multiple_of(i * TILE, TILE), TILE)
            query = q_ref[rows, :]
            scores = dot(key, query, (1, 1))
            if masked:
                key_pos = lax.broadcasted_iota(jnp.int32, scores.shape, 0)
                query_pos = lax.broadcasted_iota(jnp.int32, scores.shape, 1)
                scores = jnp.where(key_pos <= query_pos, scores, NEGATIVE)
            probs = jnp.exp(scores - top_ref[:, rows])
            gv = gv + dot(probs.astype(LOW), go_ref[rows, :], (1, 0))
            gks = [gk0, gk1]
            for d in range(2):
                prob_grad = dot(value, got_ref[d, :, rows], (1, 0))
                score_low = (probs * (prob_grad - delta_ref[d, :, rows])).astype(LOW)
                gks[d] = gks[d] + dot(score_low, query, (1, 0))
                gqt_ref[d, :, rows] += dot(key_t, score_low, (1, 0))
            return gv, gks[0], gks[1]

        zero = jnp.zeros((TILE, head), FULL)
        carry = step(j, (jnp.zeros((TILE, 2 * head), FULL), zero, zero), True)
        gv, gk0, gk1 = lax.fori_loop(j + 1, tiles, lambda i, c: step(i, c, False), carry)
        gv_ref[keys, :] = gv.astype(LOW)
        gk_ref[keys, :] = jnp.concatenate([gk0, gk1], axis=1).astype(LOW)
        return 0

    lax.fori_loop(0, tiles, key_tile, 0)

    def finish(i, _):
        rows = pl.ds(pl.multiple_of(i * TILE, TILE), TILE)
        both = jnp.concatenate([gqt_ref[0, :, rows], gqt_ref[1, :, rows]], axis=0) * factor
        gq_ref[rows, :] = both.T.astype(LOW)
        return 0

    lax.fori_loop(0, tiles, finish, 0)


def attend_back(q, k, v, out_t, top, go):
    length, head = q.shape
    pair = jax.ShapeDtypeStruct((length, 2 * head), LOW)
    return pl.pallas_call(
        attend_back_kernel,
        out_shape=(pair, pair, pair),
        scratch_shapes=[
            pltpu.VMEM((head, length), LOW),
            pltpu.VMEM((2, head, length), LOW),
            pltpu.VMEM((2, 1, length), FULL),
            pltpu.VMEM((2, head, length), FULL),
        ],
        compiler_params=pltpu.CompilerParams(vmem_limit_bytes=48 << 20),
        cost_estimate=pl.CostEstimate(
            flops=20 * length * length * head, bytes_accessed=16 * length * head, transcendentals=length * length
        ),
        name="attend_back",
    )(q, k, v, out_t, top, go)


def on_device(
    inputs,
    attend_gain,
    attend_shift,
    mixing_weight,
    mixing_bias,
    output_weight,
    output_bias,
    feed_gain,
    feed_shift,
    up_weight,
    up_bias,
    down_weight,
    down_bias,
    cotangent,
):
    place = Place()
    _, span, width = inputs.shape
    nz, ny, core, chip = place.nz, place.ny, place.core, place.chip
    chips = nz * 2
    parts = chips * 2 * ny
    head = width // HEADS
    per_core = HEADS // 2
    slots = [int((j + 0.5) * chips / per_core) for j in range(per_core)]
    half = width // 2
    hidden = up_weight.shape[1]
    rows_in = width // parts
    rows_hid = hidden // parts
    groups = [[2 * i + c for i in range(chips)] for c in range(2)]

    def exchange(values):
        return lax.all_to_all(values, "seq", 0, 0, axis_index_groups=groups, tiled=True)

    def spread(blocks):
        filled = [jnp.zeros_like(blocks[0])] * chips
        for j, slot in enumerate(slots):
            filled[slot] = blocks[j]
        return jnp.stack(filled)

    def collect(blocks):
        return jnp.stack([blocks[slot] for slot in slots])

    owned = [-1] * chips
    for j, slot in enumerate(slots):
        owned[slot] = j
    my_head = jnp.array(owned, jnp.int32)[chip]
    busy = (my_head >= 0).astype(FULL)
    my_head = jnp.maximum(my_head, 0)

    def by_core(values, dim):
        mine = lax.dynamic_index_in_dim(values, core, dim, keepdims=False)
        theirs = lax.dynamic_index_in_dim(values, 1 - core, dim, keepdims=False)
        return mine, theirs

    vectors = jnp.concatenate(
        [attend_gain, attend_shift, feed_gain, feed_shift, output_bias, down_bias, mixing_bias, up_bias]
    )
    vectors = place.both(vectors, vectors)
    vectors = place.gather(vectors, "z", 0)
    vectors = place.gather(vectors, "x", 1)
    vectors = place.gather(vectors, "y", 3)
    vectors = vectors.reshape(parts, -1).astype(FULL)
    cuts = [vectors[:, i * rows_in : (i + 1) * rows_in].reshape(-1) for i in range(6)]
    first_gain, first_shift, second_gain, second_shift, out_bias, down_bias_all = cuts
    mix_bias = vectors[:, 6 * rows_in : 8 * rows_in].reshape(2, HEADS, head)
    up_bias_all = vectors[:, 8 * rows_in :].reshape(chips, 2, ny * rows_hid)
    up_bias_mine = lax.dynamic_index_in_dim(up_bias_all, core, 1, keepdims=False).reshape(-1)

    own = inputs.reshape(span, width)
    column = [own] + [place.send(own, "z", d) for d in range(1, nz)]
    beside = [place.send(piece, "x") for piece in column]
    x_all = jnp.zeros((nz, 2, span, width), LOW)
    for d in range(nz):
        at = lax.rem(place.z + nz - d, nz)
        x_all = lax.dynamic_update_slice(x_all, column[d][None, None], (at, place.x, 0, 0))
        x_all = lax.dynamic_update_slice(x_all, beside[d][None, None], (at, 1 - place.x, 0, 0))
    x_all = place.both(x_all, x_all).transpose(1, 2, 0, 3, 4)
    x_all = x_all.reshape(chips * 2 * span, width)

    def gather_rows(mine, theirs):
        block = place.both(mine, theirs)
        block = place.gather(block, "z", 0)
        block = place.gather(block, "x", 1)
        block = place.gather(block, "y", 3)
        return block.reshape(parts * block.shape[-2], block.shape[-1])

    mixing = mixing_weight.reshape(rows_in, 3, 2, half)
    mine, theirs = by_core(mixing, 2)
    mixing = gather_rows(mine.reshape(rows_in, -1), theirs.reshape(rows_in, -1))
    mine, theirs = by_core(output_weight.reshape(rows_in, 2, half), 1)
    out_half = gather_rows(mine, theirs)
    out_all = place.both(out_half, out_half).transpose(1, 0, 2).reshape(width, width)
    mine, theirs = by_core(up_weight.reshape(rows_in, chips, 2, ny * rows_hid), 2)
    up = gather_rows(mine.reshape(rows_in, -1), theirs.reshape(rows_in, -1))
    down = place.gather(down_weight, "z", 0)
    down = place.gather(down, "x", 1)
    down = place.gather(down, "y", 2).reshape(chips * ny * rows_hid, width)

    mixing = mixing.reshape(width, 3, per_core, head)
    head_weight = lax.dynamic_index_in_dim(mixing, my_head, 2, keepdims=False).reshape(width, 3 * head)
    whole_head = core * per_core + my_head
    head_bias = lax.dynamic_index_in_dim(mix_bias, whole_head, 1, keepdims=False)
    head_bias = jnp.concatenate([head_bias[0], jnp.zeros((head,), FULL), head_bias[1]])
    first_low, q, k, v, out, out_t, top = attend(
        x_all, first_gain[None], first_shift[None], head_weight, head_bias[None]
    )
    attended = collect(exchange(out.reshape(chips, 2 * span, head)))
    attended = attended.transpose(1, 0, 2).reshape(2 * span, half)
    attended = place.both(attended, attended).transpose(1, 0, 2).reshape(2 * span, width)

    residual = lax.dynamic_slice_in_dim(x_all, chip * 2 * span, 2 * span, 0).astype(FULL)
    branch = dot(attended, out_all, (1, 0)) + out_bias
    scale = jnp.array(SCALES, FULL)[:, None, None]
    middle = residual + scale * branch
    second_normed, second_inv = normalize(middle)
    second_low = (second_normed * second_gain + second_shift).astype(LOW)
    rows = second_low.reshape(4 * span, width)
    hidden_pre = dot(rows, up, (1, 0)) + up_bias_mine
    activated, gelu_back = jax.vjp(partial(jax.nn.gelu, approximate=True), hidden_pre)
    activated_low = activated.astype(LOW)
    feed_part = dot(activated_low, down, (1, 0)).reshape(2, 2, span, width)
    mine, theirs = by_core(feed_part, 1)
    feed_own = mine + place.send(theirs, "core") + down_bias_all

    def own_rows(values):
        return lax.dynamic_index_in_dim(
            values.reshape((2, 2, span) + values.shape[2:]), core, 1, keepdims=False
        )

    activations = (own_rows(middle) + scale * feed_own).astype(LOW)
    upstream_own = cotangent.reshape(2, span, width)
    upstream = place.both(upstream_own, upstream_own).transpose(1, 0, 2, 3)
    down_in = (scale[..., None] * upstream.astype(FULL)).astype(LOW).reshape(4 * span, width)
    hidden_low = gelu_back(dot(down_in, down, (1, 1)))[0].astype(LOW)
    second_part = dot(hidden_low, up, (1, 1)).reshape(2, 2, span, width)
    mine, theirs = by_core(second_part, 1)
    second_grad = mine + place.send(theirs, "core")
    normed_own, inv_own = own_rows(second_normed), own_rows(second_inv)
    middle_grad = upstream_own.astype(FULL) + norm_back(second_grad, normed_own, inv_own, second_gain)
    branch_own = (scale * middle_grad).astype(LOW)
    branch_low = place.both(branch_own, branch_own).transpose(1, 0, 2, 3).reshape(2, 2 * span, width)
    out_rows = lax.dynamic_slice_in_dim(out_all, core * half, half, 0)
    go = dot(branch_low.reshape(4 * span, width), out_rows, (1, 1)).astype(LOW)
    go = go.reshape(2, 2 * span, per_core, head).transpose(2, 1, 0, 3).reshape(per_core, 2 * span, 2 * head)
    go = exchange(spread(go)).reshape(chips * 2 * span, 2 * head)

    gq, gk, gv = attend_back(q, k, v, out_t, top, go)
    head_grads = jnp.concatenate([gq, gk, gv], axis=1)

    depth_rows = second_low.reshape(2, 2 * span, width)
    hidden_rows = hidden_low.reshape(2, 2 * span, -1)
    active_rows = activated_low.reshape(2, 2 * span, -1)
    in_rows = down_in.reshape(2, 2 * span, width)
    branch_cols = lax.dynamic_slice_in_dim(branch_low, core * half, half, 2)
    orders = (("y", "x"), ("x", "y"))

    def scatter_chips(values, order):
        dims = {"x": 1, "y": 2}
        values = place.scatter(values, order[0], dims[order[0]]).astype(LOW)
        values = place.scatter(values, order[1], 1).astype(LOW)
        return place.scatter(values, "z", 0)

    def scatter_rows(values, order):
        shaped = values.reshape(nz, 2, 2, ny, rows_in, -1).transpose(0, 1, 3, 2, 4, 5)
        summed = scatter_chips(shaped, order)
        mine, theirs = by_core(summed, 0)
        return place.both(mine, theirs)

    down_grads, up_grads, out_grads = [], [], []
    for depth in range(2):
        grad = dot(active_rows[depth], in_rows[depth], (0, 0)).astype(LOW)
        down_grads.append(scatter_chips(grad.reshape(nz, 2, ny, rows_hid, width), orders[depth]))
    for depth in range(2):
        grad = dot(depth_rows[depth], hidden_rows[depth], (0, 0)).astype(LOW)
        grad = scatter_rows(grad, orders[depth]).reshape(2, rows_in, chips, -1)
        up_grads.append(grad.transpose(1, 2, 0, 3).reshape(rows_in, hidden))
    for depth in range(2):
        grad = dot(attended, branch_cols[depth], (0, 0)).astype(LOW)
        out_grads.append(scatter_rows(grad, orders[depth]).transpose(1, 0, 2).reshape(rows_in, width))

    head_sum = dot(first_low, head_grads, (0, 0)).astype(LOW).reshape(nz, 2, 2, ny, rows_in, 6 * head)
    head_sum = place.scatter(head_sum, "y", 3).astype(LOW).reshape(chips, 2, rows_in, 6 * head)
    head_sum = collect(exchange(head_sum))
    mine, theirs = by_core(head_sum, 1)
    mixing_grad = place.both(mine, theirs).reshape(HEADS, rows_in, 3, 2, head)
    mixing_grad = mixing_grad.transpose(3, 1, 2, 0, 4).reshape(2, rows_in, 3 * width).astype(FULL)

    mixed_grads = collect(exchange(head_grads.reshape(chips, 2 * span, 6 * head)))
    mixed_grads = mixed_grads.reshape(per_core, 2 * span, 3, 2, head).transpose(3, 1, 2, 0, 4)
    mixed_grads = mixed_grads.reshape(4 * span, 3 * half)
    first_part = dot(mixed_grads, mixing.reshape(width, 3 * half), (1, 1)).reshape(2, 2, span, width)
    mine, theirs = by_core(first_part, 1)
    first_grad = mine + place.send(theirs, "core")
    first_normed, first_inv = normalize(own.astype(FULL))
    input_grad = middle_grad + norm_back(first_grad, first_normed, first_inv, first_gain)

    bias_sum = jnp.sum(head_grads.astype(FULL), axis=0).reshape(3, 2, head) * busy
    spot = (jnp.arange(HEADS) == whole_head).astype(FULL)[None, None, :, None]
    bias_sum = (jnp.stack([bias_sum[0], bias_sum[2]], axis=1)[:, :, None, :] * spot).reshape(2, parts, -1)
    hidden_sum = jnp.sum(hidden_rows.astype(FULL), axis=1).reshape(2, chips, 1, ny * rows_hid)
    hidden_spot = (jnp.arange(2) == core).astype(FULL)[None, None, :, None]
    hidden_sum = (hidden_sum * hidden_spot).reshape(2, parts, rows_hid)
    in_own = (scale * upstream_own.astype(FULL)).astype(LOW)
    sums = [
        jnp.sum(first_grad * first_normed, axis=1),
        jnp.sum(first_grad, axis=1),
        jnp.sum(second_grad * normed_own, axis=1),
        jnp.sum(second_grad, axis=1),
        jnp.sum(branch_own.astype(FULL), axis=1),
        jnp.sum(in_own.astype(FULL), axis=1),
    ]
    sums = [item.reshape(2, parts, rows_in) for item in sums] + [bias_sum, hidden_sum]
    sums = jnp.concatenate(sums, axis=2).reshape(2, nz, 2, 2, ny, -1)
    sums = place.scatter(sums, "y", 4)
    sums = place.scatter(sums, "x", 2)
    sums = place.scatter(sums, "core", 2)
    sums = place.scatter(sums, "z", 1)
    small = [sums[:, i * rows_in : (i + 1) * rows_in] for i in range(6)]
    return (
        activations[:, None],
        input_grad[:, None],
        small[0],
        small[1],
        mixing_grad,
        sums[:, 6 * rows_in : 8 * rows_in],
        jnp.stack(out_grads),
        small[4],
        small[2],
        small[3],
        jnp.stack(up_grads),
        sums[:, 8 * rows_in :],
        jnp.stack(down_grads),
        small[5],
    )


def solution(mesh):
    shard = P(("seq", "batch"))
    grad = P(None, ("seq", "batch"))
    row = P(None, "batch", "seq", None)
    return jax.shard_map(
        on_device,
        mesh=mesh,
        in_specs=(P("batch", "seq", None),) + (shard,) * 12 + (row,),
        out_specs=(row, row) + (grad,) * 12,
        check_vma=False,
    )
```

```python
from functools import partial

import jax
import jax.numpy as jnp
from jax import lax
from jax.experimental import pallas as pl
from jax.experimental.pallas import tpu as pltpu
from jax.sharding import PartitionSpec as P

HEADS = 12
EPS = 1e-05
SCALES = (12.0 ** (-0.5), 48.0 ** (-0.5))
NEGATIVE = -1e30
LOW = jnp.bfloat16
FULL = jnp.float32
TILE = 256


def normalize(values):
    average = jnp.mean(values, axis=-1, keepdims=True)
    centered = values - average
    inv_std = lax.rsqrt(jnp.mean(centered * centered, axis=-1, keepdims=True) + EPS)
    return centered * inv_std, inv_std


def norm_back(gradient, normed, inv_std, gain):
    scaled = gradient * gain
    inner = (
        scaled
        - jnp.mean(scaled, axis=-1, keepdims=True)
        - normed * jnp.mean(scaled * normed, axis=-1, keepdims=True)
    )
    return inv_std * inner


def dot(a, b, dims):
    return lax.dot_general(a, b, ((dims[:1], dims[1:]), ((), ())), preferred_element_type=FULL)


class Place:
    def __init__(self):
        self.s = lax.axis_size("seq")
        self.ny = lax.axis_size("batch")
        self.nz = self.s // 4
        seq = lax.axis_index("seq")
        self.y = lax.axis_index("batch")
        self.core = lax.rem(seq, 2)
        self.chip = seq // 2
        self.x = lax.rem(self.chip, 2)
        self.z = self.chip // 2
        self.sizes = {"z": self.nz, "x": 2, "y": self.ny, "core": 2}
        self.at = {"z": self.z, "x": self.x, "y": self.y, "core": self.core}

    def send(self, values, axis, d=1):
        pairs = []
        for s in range(self.s):
            for y in range(self.ny):
                c, x, z, t = s % 2, (s // 2) % 2, s // 4, y
                if axis == "z":
                    z = (z + d) % self.nz
                elif axis == "x":
                    x = 1 - x
                elif axis == "core":
                    c = 1 - c
                else:
                    t = (y + d) % self.ny
                pairs.append((s * self.ny + y, ((z * 2 + x) * 2 + c) * self.ny + t))
        return lax.ppermute(values, ("seq", "batch"), pairs)

    def gather(self, values, axis, dim):
        size, at = self.sizes[axis], self.at[axis]
        shape = values.shape[:dim] + (size,) + values.shape[dim:]
        whole = lax.dynamic_update_slice_in_dim(
            jnp.zeros(shape, values.dtype), jnp.expand_dims(values, dim), at, dim
        )
        for d in range(1, size):
            piece = jnp.expand_dims(self.send(values, axis, d), dim)
            whole = lax.dynamic_update_slice_in_dim(whole, piece, lax.rem(at + size - d, size), dim)
        return whole

    def scatter(self, values, axis, dim):
        size, at = self.sizes[axis], self.at[axis]

        def pick(i):
            return lax.dynamic_index_in_dim(values, lax.rem(i, size), dim, keepdims=False)

        total = pick(at).astype(FULL)
        for d in range(1, size):
            total = total + self.send(pick(at + d), axis, d).astype(FULL)
        return total

    def both(self, mine, theirs):
        got = self.send(theirs, "core")
        first = self.core == 0
        return jnp.stack([jnp.where(first, mine, got), jnp.where(first, got, mine)])


def attend_plain_kernel(x_ref, gain_ref, shift_ref, w_ref, b_ref, h_ref, q_ref, k_ref, v_ref, o_ref, ot_ref, top_ref, vt_ref):
    length = x_ref.shape[0]
    head = q_ref.shape[1]
    tiles = length // TILE

    def project(i, _):
        rows = pl.ds(pl.multiple_of(i * TILE, TILE), TILE)
        normed, _ = normalize(x_ref[rows, :].astype(FULL))
        low = (normed * gain_ref[...] + shift_ref[...]).astype(LOW)
        h_ref[rows, :] = low
        mixed = dot(low, w_ref[...], (1, 0)) + b_ref[...]
        q_ref[rows, :] = (mixed[:, :head].astype(LOW) * (head ** (-0.5))).astype(LOW)
        k_ref[rows, :] = mixed[:, head : 2 * head].astype(LOW)
        value = mixed[:, 2 * head :].astype(LOW)
        v_ref[rows, :] = value
        vt_ref[:, rows] = value.T
        return 0

    lax.fori_loop(0, tiles, project, 0)

    def query_tile(i, _):
        rows = pl.ds(pl.multiple_of(i * TILE, TILE), TILE)
        query = q_ref[rows, :]

        def absorb(j, carry, masked):
            top, total, acc = carry
            keys = pl.ds(pl.multiple_of(j * TILE, TILE), TILE)
            scores = dot(k_ref[keys, :], query, (1, 1))
            if masked:
                key_pos = lax.broadcasted_iota(jnp.int32, scores.shape, 0)
                query_pos = lax.broadcasted_iota(jnp.int32, scores.shape, 1)
                scores = jnp.where(key_pos <= query_pos, scores, NEGATIVE)
            new_top = jnp.maximum(top, jnp.max(scores, axis=0, keepdims=True))
            weights = jnp.exp(scores - new_top)
            keep = jnp.exp(top - new_top)
            total = total * keep + jnp.sum(weights, axis=0, keepdims=True)
            acc = acc * keep + dot(vt_ref[:, keys], weights.astype(LOW), (1, 0))
            return new_top, total, acc

        start = (
            jnp.full((1, TILE), NEGATIVE, FULL),
            jnp.zeros((1, TILE), FULL),
            jnp.zeros((head, TILE), FULL),
        )
        carry = lax.fori_loop(0, i, lambda j, c: absorb(j, c, False), start)
        top, total, acc = absorb(i, carry, True)
        out = acc / total
        ot_ref[:, rows] = out
        o_ref[rows, :] = out.T.astype(LOW)
        top_ref[:, rows] = top + jnp.log(total)
        return 0

    lax.fori_loop(0, tiles, query_tile, 0)


def attend_plain(x_all, gain, shift, weight, bias):
    length, head = x_all.shape[0], weight.shape[1] // 3
    low = jax.ShapeDtypeStruct((length, head), LOW)
    return pl.pallas_call(
        attend_plain_kernel,
        out_shape=(
            jax.ShapeDtypeStruct(x_all.shape, LOW),
            low,
            low,
            low,
            low,
            jax.ShapeDtypeStruct((head, length), FULL),
            jax.ShapeDtypeStruct((1, length), FULL),
        ),
        scratch_shapes=[pltpu.VMEM((head, length), LOW)],
        compiler_params=pltpu.CompilerParams(vmem_limit_bytes=48 << 20),
        cost_estimate=pl.CostEstimate(
            flops=6 * length * length * head, bytes_accessed=8 * length * 768, transcendentals=length * length
        ),
        name="attend_plain",
    )(x_all, gain, shift, weight, bias)


def attend_back_kernel(
    q_ref, k_ref, v_ref, ot_ref, top_ref, go_ref, gq_ref, gk_ref, gv_ref, kt_ref, got_ref, delta_ref, gqt_ref
):
    length, head = q_ref.shape
    tiles = length // TILE
    factor = head ** (-0.5)

    def prepare(i, _):
        rows = pl.ds(pl.multiple_of(i * TILE, TILE), TILE)
        kt_ref[:, rows] = k_ref[rows, :].T
        up = go_ref[rows, :].T
        for d in range(2):
            mine = up[d * head : (d + 1) * head, :]
            got_ref[d, :, rows] = mine
            delta_ref[d, :, rows] = jnp.sum(mine.astype(FULL) * ot_ref[:, rows], axis=0, keepdims=True)
            gqt_ref[d, :, rows] = jnp.zeros((head, TILE), FULL)
        return 0

    lax.fori_loop(0, tiles, prepare, 0)

    def key_tile(j, _):
        keys = pl.ds(pl.multiple_of(j * TILE, TILE), TILE)
        key = k_ref[keys, :]
        value = v_ref[keys, :]
        key_t = kt_ref[:, keys]

        def step(i, carry, masked):
            gv, gk0, gk1 = carry
            rows = pl.ds(pl.multiple_of(i * TILE, TILE), TILE)
            query = q_ref[rows, :]
            scores = dot(key, query, (1, 1))
            if masked:
                key_pos = lax.broadcasted_iota(jnp.int32, scores.shape, 0)
                query_pos = lax.broadcasted_iota(jnp.int32, scores.shape, 1)
                scores = jnp.where(key_pos <= query_pos, scores, NEGATIVE)
            probs = jnp.exp(scores - top_ref[:, rows])
            gv = gv + dot(probs.astype(LOW), go_ref[rows, :], (1, 0))
            gks = [gk0, gk1]
            for d in range(2):
                prob_grad = dot(value, got_ref[d, :, rows], (1, 0))
                score_low = (probs * (prob_grad - delta_ref[d, :, rows])).astype(LOW)
                gks[d] = gks[d] + dot(score_low, query, (1, 0))
                gqt_ref[d, :, rows] += dot(key_t, score_low, (1, 0))
            return gv, gks[0], gks[1]

        zero = jnp.zeros((TILE, head), FULL)
        carry = step(j, (jnp.zeros((TILE, 2 * head), FULL), zero, zero), True)
        gv, gk0, gk1 = lax.fori_loop(j + 1, tiles, lambda i, c: step(i, c, False), carry)
        gv_ref[keys, :] = gv.astype(LOW)
        gk_ref[keys, :] = jnp.concatenate([gk0, gk1], axis=1).astype(LOW)
        return 0

    lax.fori_loop(0, tiles, key_tile, 0)

    def finish(i, _):
        rows = pl.ds(pl.multiple_of(i * TILE, TILE), TILE)
        both = jnp.concatenate([gqt_ref[0, :, rows], gqt_ref[1, :, rows]], axis=0) * factor
        gq_ref[rows, :] = both.T.astype(LOW)
        return 0

    lax.fori_loop(0, tiles, finish, 0)


def attend_back(q, k, v, out_t, top, go):
    length, head = q.shape
    pair = jax.ShapeDtypeStruct((length, 2 * head), LOW)
    return pl.pallas_call(
        attend_back_kernel,
        out_shape=(pair, pair, pair),
        scratch_shapes=[
            pltpu.VMEM((head, length), LOW),
            pltpu.VMEM((2, head, length), LOW),
            pltpu.VMEM((2, 1, length), FULL),
            pltpu.VMEM((2, head, length), FULL),
        ],
        compiler_params=pltpu.CompilerParams(vmem_limit_bytes=48 << 20),
        cost_estimate=pl.CostEstimate(
            flops=20 * length * length * head, bytes_accessed=16 * length * head, transcendentals=length * length
        ),
        name="attend_back",
    )(q, k, v, out_t, top, go)


MESH = pl.DeviceIdType.MESH
DMA = pltpu.SemaphoreType.DMA


class Here:
    def __init__(self, nz, ny):
        self.nz, self.ny = nz, ny
        seq = lax.axis_index("seq")
        self.y = lax.axis_index("batch")
        self.core = lax.rem(seq, 2)
        self.chip = lax.div(seq, 2)
        self.x = lax.rem(self.chip, 2)
        self.z = lax.div(self.chip, 2)

    def device(self, z=None, x=None, core=None, y=None):
        z = self.z if z is None else z
        x = self.x if x is None else x
        core = self.core if core is None else core
        y = self.y if y is None else y
        return ((z * 2 + x) * 2 + core, y)

    def before(self, d):
        return lax.rem(self.z + self.nz - d, self.nz)

    def after(self, d):
        return lax.rem(self.z + d, self.nz)


def remote(src, dst, send, recv, device):
    return pltpu.make_async_remote_copy(
        src_ref=src, dst_ref=dst, send_sem=send, recv_sem=recv, device_id=device, device_id_type=MESH
    )


class Gather:
    def __init__(self, here, own, whole, x_first, sems):
        self.here, self.own, self.whole, self.x_first = here, own, whole, x_first
        self.zs, self.zr, self.as_, self.ar, self.bs, self.br, self.local = sems
        self.sent = []

    @staticmethod
    def scratch(nz, ny, x_first):
        first = nz if x_first else nz * ny
        second = nz * 2 * ny if x_first else nz * ny
        return [DMA((nz,)), DMA((nz,)), DMA((first,)), DMA((first,)), DMA((second,)), DMA((second,)), DMA]

    def _go(self, copy):
        copy.start()
        self.sent.append(copy)

    def _z(self, d, target):
        h = self.here
        z = h.z if target else h.before(d)
        return remote(self.own, self.whole.at[z, h.x, h.y], self.zs.at[d], self.zr.at[d], h.device(z=h.after(d)))

    def _source(self, d, x, y):
        h = self.here
        if d == 0 and x is h.x and y is h.y:
            return self.own
        return self.whole.at[h.before(d), x, y]

    def start(self):
        h = self.here
        self.kept = pltpu.make_async_copy(self.own, self.whole.at[h.z, h.x, h.y], self.local)
        self.kept.start()
        for d in range(1, h.nz):
            self._go(self._z(d, True))

    def finish_own(self):
        self.kept.wait()

    def _to_x(self, d, y, e, sems):
        h = self.here
        i = d * h.ny + e
        s, r = (sems[0].at[i], sems[1].at[i])
        return remote(self._source(d, h.x, y), self.whole.at[h.before(d), h.x, y], s, r, h.device(x=1 - h.x))

    def _from_x(self, d, y, e, sems):
        h = self.here
        i = d * h.ny + e
        spot = self.whole.at[h.before(d), 1 - h.x, y]
        return remote(spot, spot, sems[0].at[i], sems[1].at[i], h.device(x=1 - h.x))

    def _to_y(self, d, x, k, e, sems):
        h = self.here
        i = (d * 2 + k) * h.ny + e if self.x_first else d * h.ny + e
        spot = self.whole.at[h.before(d), x, h.y]
        return remote(
            self._source(d, x, h.y), spot, sems[0].at[i], sems[1].at[i], h.device(y=lax.rem(h.y + e, h.ny))
        )

    def _from_y(self, d, x, k, e, sems):
        h = self.here
        i = (d * 2 + k) * h.ny + e if self.x_first else d * h.ny + e
        spot = self.whole.at[h.before(d), x, lax.rem(h.y + h.ny - e, h.ny)]
        return remote(spot, spot, sems[0].at[i], sems[1].at[i], h.device(y=lax.rem(h.y + e, h.ny)))

    def arrived_z(self, d):
        h = self.here
        if d:
            self._z(d, False).wait_recv()
        if self.x_first:
            i = d
            s, r = self.as_.at[i], self.ar.at[i]
            self._go(remote(self._source(d, h.x, h.y), self.whole.at[h.before(d), h.x, h.y], s, r, h.device(x=1 - h.x)))
            for e in range(1, h.ny):
                self._go(self._to_y(d, h.x, 0, e, (self.bs, self.br)))
        else:
            for e in range(1, h.ny):
                self._go(self._to_y(d, h.x, 0, e, (self.as_, self.ar)))
            self._go(self._to_x(d, h.y, 0, (self.bs, self.br)))

    def arrived_second(self, d):
        h = self.here
        if self.x_first:
            spot = self.whole.at[h.before(d), 1 - h.x, h.y]
            remote(spot, spot, self.as_.at[d], self.ar.at[d], h.device(x=1 - h.x)).wait_recv()
            for e in range(1, h.ny):
                self._go(self._to_y(d, 1 - h.x, 1, e, (self.bs, self.br)))
        else:
            for e in range(1, h.ny):
                self._from_y(d, h.x, 0, e, (self.as_, self.ar)).wait_recv()
                self._go(self._to_x(d, lax.rem(h.y + h.ny - e, h.ny), e, (self.bs, self.br)))

    def arrived_third(self, d):
        h = self.here
        if self.x_first:
            for e in range(1, h.ny):
                self._from_y(d, h.x, 0, e, (self.bs, self.br)).wait_recv()
                self._from_y(d, 1 - h.x, 1, e, (self.bs, self.br)).wait_recv()
        else:
            for e in range(h.ny):
                self._from_x(d, lax.rem(h.y + h.ny - e, h.ny), e, (self.bs, self.br)).wait_recv()

    def finish(self):
        for copy in self.sent:
            copy.wait_send()


class GatherRows:
    def __init__(self, here, own, whole, sems):
        self.here, self.own, self.whole = here, own, whole
        self.zs, self.zr, self.xs, self.xr, self.cs, self.cr, self.local = sems
        self.sent = []

    @staticmethod
    def scratch(nz):
        return [DMA((nz,)), DMA((nz,)), DMA((nz,)), DMA((nz,)), DMA((2 * nz,)), DMA((2 * nz,)), DMA]

    def _go(self, copy):
        copy.start()
        self.sent.append(copy)

    def start(self):
        h = self.here
        self.kept = pltpu.make_async_copy(self.own, self.whole.at[h.z, h.x, h.core], self.local)
        self.kept.start()
        for d in range(1, h.nz):
            spot = self.whole.at[h.z, h.x, h.core]
            self._go(remote(self.own, spot, self.zs.at[d], self.zr.at[d], h.device(z=h.after(d))))

    def arrived_z(self, d):
        h = self.here
        spot = self.whole.at[h.before(d), h.x, h.core]
        if d:
            remote(spot, spot, self.zs.at[d], self.zr.at[d], h.device(z=h.after(d))).wait_recv()
        src = spot if d else self.own
        self._go(remote(src, spot, self.xs.at[d], self.xr.at[d], h.device(x=1 - h.x)))
        self._go(remote(src, spot, self.cs.at[2 * d], self.cr.at[2 * d], h.device(core=1 - h.core)))

    def arrived_x(self, d):
        h = self.here
        spot = self.whole.at[h.before(d), 1 - h.x, h.core]
        remote(spot, spot, self.xs.at[d], self.xr.at[d], h.device(x=1 - h.x)).wait_recv()
        self._go(remote(spot, spot, self.cs.at[2 * d + 1], self.cr.at[2 * d + 1], h.device(core=1 - h.core)))

    def arrived_core(self, d):
        h = self.here
        for k, x in ((0, h.x), (1, 1 - h.x)):
            spot = self.whole.at[h.before(d), x, 1 - h.core]
            i = 2 * d + k
            remote(spot, spot, self.cs.at[i], self.cr.at[i], h.device(core=1 - h.core)).wait_recv()

    def finish(self):
        self.kept.wait()
        for copy in self.sent:
            copy.wait_send()


def greet(devices):
    barrier = pltpu.get_barrier_semaphore()
    for device in devices:
        pl.semaphore_signal(barrier, inc=1, device_id=device, device_id_type=MESH)
    pl.semaphore_wait(barrier, len(devices))


def owner_of(chips):
    per_core = HEADS // 2
    return [int((j + 0.5) * chips / per_core) for j in range(per_core)]


def head_here(chip, slots):
    mine, has = jnp.int32(0), jnp.int32(0)
    for j, slot in enumerate(slots):
        same = (chip == slot).astype(jnp.int32)
        mine = mine + j * same
        has = has + same
    return mine, has


def attend_kernel(
    nz, ny, x_ref, mw_ref, up_ref, dn_ref, table_ref,
    mw_all, up_all, dn_all, h_ref, q_ref, k_ref, v_ref, ot_ref, top_ref, att_ref, x2_ref,
    xs, wt, vc, vt_ref, o_ref, load, att_s, att_r, pass_s, pass_r, *sems,
):
    here = Here(nz, ny)
    chips = 2 * nz
    slots = owner_of(chips)
    head = q_ref.shape[1]
    width = x_ref.shape[1]
    tile = 2 * x_ref.shape[0]
    mine, has = head_here(here.chip, slots)
    odd = lax.rem(mine, 2) == 1
    rows_sems, mw_sems, up_sems, dn_sems = sems[:7], sems[7:14], sems[14:21], sems[21:28]

    peers = [here.device(z=here.after(d)) for d in range(1, nz)]
    peers += [here.device(x=1 - here.x), here.device(core=1 - here.core)]
    peers += [here.device(z=here.after(d), x=1 - here.x) for d in range(1, nz)]
    peers += [here.device(y=lax.rem(here.y + e, ny)) for e in range(1, ny)]
    greet(peers)

    rows = GatherRows(here, x_ref, xs, rows_sems)
    mw = Gather(here, mw_ref, mw_all, True, mw_sems)
    up = Gather(here, up_ref, up_all, True, up_sems)
    dn = Gather(here, dn_ref, dn_all, False, dn_sems)
    rows.start()
    mw.start()
    for d in range(nz):
        rows.arrived_z(d)
        mw.arrived_z(d)
    for d in range(nz):
        rows.arrived_x(d)
        mw.arrived_second(d)
    up.start()
    dn.start()
    up.arrived_z(0)
    dn.arrived_z(0)
    for d in range(nz):
        mw.arrived_third(d)
    mw.finish_own()
    pair = pltpu.make_async_copy(mw_all.at[:, :, :, lax.div(mine, 2)], wt, load.at[0])
    pair.start()
    vectors = pltpu.make_async_copy(mw_all.at[:, :, :, 4], vc, load.at[1])
    vectors.start()
    for d in range(nz):
        rows.arrived_core(d)
    rows.kept.wait()
    pair.wait()
    vectors.wait()
    keep_rows = pltpu.make_async_copy(xs.at[here.z, here.x], x2_ref, load.at[2])
    keep_rows.start()

    steps = []
    for d in range(1, nz):
        steps += [partial(up.arrived_z, d), partial(dn.arrived_z, d)]
    for d in range(nz):
        steps += [partial(up.arrived_second, d), partial(dn.arrived_second, d)]
    for d in range(nz):
        steps += [partial(up.arrived_third, d), partial(dn.arrived_third, d)]

    @pl.when(has == 1)
    def _():
        pieces = vc[...].reshape(-1, vc.shape[-1])
        count = 2 * chips * ny
        unit = pieces.shape[0] // count
        pick_row = lax.broadcasted_iota(jnp.int32, (count, pieces.shape[0]), 0) * unit
        pick = (pick_row == lax.broadcasted_iota(jnp.int32, pick_row.shape, 1)).astype(LOW)
        pieces = dot(pick, pieces, (1, 0)).astype(LOW)
        cols, owners = table_ref[0:1, :], table_ref[1:2, :]
        spot = lax.broadcasted_iota(jnp.int32, (pieces.shape[1], cols.shape[1]), 0)
        moved = dot(pieces, (spot == cols).astype(LOW), (1, 0))
        from_row = lax.broadcasted_iota(jnp.int32, moved.shape, 0)
        flat = jnp.sum(jnp.where(from_row == owners, moved, 0.0), axis=0, keepdims=True)
        gain, shift, bias = flat[:, :width], flat[:, width : 2 * width], flat[:, 2 * width :]
        weight = wt[...].reshape(width, -1)

        def choose(values):
            return jnp.where(odd, values[:, head:], values[:, :head])

        for i in range(chips):
            span = slice(i * tile, (i + 1) * tile)
            values = xs[i // 2, i % 2].reshape(tile, width).astype(FULL)
            normed, _ = normalize(values)
            low = (normed * gain + shift).astype(LOW)
            h_ref[span, :] = low
            mixed = (dot(low, weight, (1, 0)) + bias).astype(LOW)
            q_ref[span, :] = (choose(mixed[:, : 2 * head]) * (head ** (-0.5))).astype(LOW)
            k_ref[span, :] = choose(mixed[:, 2 * head : 4 * head])
            value = choose(mixed[:, 4 * head :])
            v_ref[span, :] = value
            vt_ref[:, span] = value.T

    def query_tile(i):
        span = slice(i * tile, (i + 1) * tile)
        query = q_ref[span, :]

        def absorb(j, carry, masked):
            top, total, acc = carry
            keys = slice(j * tile, (j + 1) * tile)
            scores = dot(k_ref[keys, :], query, (1, 1))
            if masked:
                key_pos = lax.broadcasted_iota(jnp.int32, scores.shape, 0)
                query_pos = lax.broadcasted_iota(jnp.int32, scores.shape, 1)
                scores = jnp.where(key_pos <= query_pos, scores, NEGATIVE)
            new_top = jnp.maximum(top, jnp.max(scores, axis=0, keepdims=True))
            weights = jnp.exp(scores - new_top)
            keep = jnp.exp(top - new_top)
            total = total * keep + jnp.sum(weights, axis=0, keepdims=True)
            acc = acc * keep + dot(vt_ref[:, keys], weights.astype(LOW), (1, 0))
            return new_top, total, acc

        carry = (jnp.full((1, tile), NEGATIVE, FULL), jnp.zeros((1, tile), FULL), jnp.zeros((head, tile), FULL))
        for j in range(i + 1):
            carry = absorb(j, carry, j == i)
        top, total, acc = carry
        out = acc / total
        ot_ref[:, span] = out
        o_ref[i] = out.T.astype(LOW)
        top_ref[:, span] = top + jnp.log(total)

    def hand(i):
        spot = att_ref.at[here.core, mine]
        return (
            pltpu.make_async_copy(o_ref.at[i], spot, att_s.at[i]),
            remote(o_ref.at[i], spot, att_s.at[i], att_r.at[mine], here.device(z=i // 2, x=i % 2)),
        )

    for i in range(chips):
        @pl.when(has == 1)
        def _(i=i):
            query_tile(i)
            stay, leave = hand(i)
            pl.when(here.chip == i)(stay.start)
            pl.when(here.chip != i)(leave.start)

        for step in steps[3 * i : 3 * i + 3]:
            step()
    for step in steps[3 * chips :]:
        step()

    for i in range(chips):
        @pl.when(has == 1)
        def _(i=i):
            stay, leave = hand(i)
            pl.when(here.chip == i)(stay.wait)
            pl.when(here.chip != i)(leave.wait_send)

    for j, slot in enumerate(slots):
        @pl.when(here.chip != slot)
        def _(j=j, slot=slot):
            spot = att_ref.at[here.core, j]
            remote(spot, spot, att_s.at[0], att_r.at[j], here.device(z=slot // 2, x=slot % 2)).wait_recv()

    spot = att_ref.at[here.core]
    give = remote(spot, spot, pass_s, pass_r, here.device(core=1 - here.core))
    give.start()
    spot = att_ref.at[1 - here.core]
    remote(spot, spot, pass_s, pass_r, here.device(core=1 - here.core)).wait_recv()
    give.wait_send()
    keep_rows.wait()
    for item in (up, dn):
        item.finish_own()
    for item in (mw, up, dn):
        item.finish()
    for copy in rows.sent:
        copy.wait_send()


def attend(nz, ny, own, mw, up, dn, table):
    span, width = own.shape
    length = 4 * nz * span
    head = width // HEADS
    units = (nz, 2, ny)
    low = jax.ShapeDtypeStruct((length, head), LOW)
    anywhere = pl.BlockSpec(memory_space=pl.ANY)
    vmem = pl.BlockSpec(memory_space=pltpu.VMEM)
    return pl.pallas_call(
        partial(attend_kernel, nz, ny),
        out_shape=(
            jax.ShapeDtypeStruct(units + mw.shape, LOW),
            jax.ShapeDtypeStruct(units + up.shape, LOW),
            jax.ShapeDtypeStruct(units + dn.shape, LOW),
            jax.ShapeDtypeStruct((length, width), LOW),
            low,
            low,
            low,
            jax.ShapeDtypeStruct((head, length), FULL),
            jax.ShapeDtypeStruct((1, length), FULL),
            jax.ShapeDtypeStruct((2, HEADS // 2, 2 * span, head), LOW),
            jax.ShapeDtypeStruct((2, span, width), LOW),
        ),
        in_specs=[anywhere] * 4 + [vmem],
        out_specs=[anywhere] * 3 + [vmem] * 6 + [anywhere] * 2,
        scratch_shapes=[
            pltpu.VMEM((nz, 2, 2, span, width), LOW),
            pltpu.VMEM(units + mw.shape[1:], LOW),
            pltpu.VMEM(units + mw.shape[1:], LOW),
            pltpu.VMEM((head, length), LOW),
            pltpu.VMEM((2 * nz, 2 * span, head), LOW),
            DMA((3,)),
            DMA((2 * nz,)),
            DMA((HEADS // 2,)),
            DMA,
            DMA,
        ]
        + GatherRows.scratch(nz)
        + Gather.scratch(nz, ny, True)
        + Gather.scratch(nz, ny, True)
        + Gather.scratch(nz, ny, False),
        compiler_params=pltpu.CompilerParams(vmem_limit_bytes=56 << 20, collective_id=0, has_side_effects=True),
        cost_estimate=pl.CostEstimate(
            flops=6 * length * length * head, bytes_accessed=8 * length * width, transcendentals=length * length
        ),
        name="attend",
    )(own, mw, up, dn, table)


def plain_on_device(
    inputs,
    attend_gain,
    attend_shift,
    mixing_weight,
    mixing_bias,
    output_weight,
    output_bias,
    feed_gain,
    feed_shift,
    up_weight,
    up_bias,
    down_weight,
    down_bias,
    cotangent,
):
    place = Place()
    _, span, width = inputs.shape
    nz, ny, core, chip = place.nz, place.ny, place.core, place.chip
    chips = nz * 2
    parts = chips * 2 * ny
    head = width // HEADS
    per_core = HEADS // 2
    slots = [int((j + 0.5) * chips / per_core) for j in range(per_core)]
    half = width // 2
    hidden = up_weight.shape[1]
    rows_in = width // parts
    rows_hid = hidden // parts
    groups = [[2 * i + c for i in range(chips)] for c in range(2)]

    def exchange(values):
        return lax.all_to_all(values, "seq", 0, 0, axis_index_groups=groups, tiled=True)

    def spread(blocks):
        filled = [jnp.zeros_like(blocks[0])] * chips
        for j, slot in enumerate(slots):
            filled[slot] = blocks[j]
        return jnp.stack(filled)

    def collect(blocks):
        return jnp.stack([blocks[slot] for slot in slots])

    owned = [-1] * chips
    for j, slot in enumerate(slots):
        owned[slot] = j
    my_head = jnp.array(owned, jnp.int32)[chip]
    busy = (my_head >= 0).astype(FULL)
    my_head = jnp.maximum(my_head, 0)

    def by_core(values, dim):
        mine = lax.dynamic_index_in_dim(values, core, dim, keepdims=False)
        theirs = lax.dynamic_index_in_dim(values, 1 - core, dim, keepdims=False)
        return mine, theirs

    vectors = jnp.concatenate(
        [attend_gain, attend_shift, feed_gain, feed_shift, output_bias, down_bias, mixing_bias, up_bias]
    )
    vectors = place.both(vectors, vectors)
    vectors = place.gather(vectors, "z", 0)
    vectors = place.gather(vectors, "x", 1)
    vectors = place.gather(vectors, "y", 3)
    vectors = vectors.reshape(parts, -1).astype(FULL)
    cuts = [vectors[:, i * rows_in : (i + 1) * rows_in].reshape(-1) for i in range(6)]
    first_gain, first_shift, second_gain, second_shift, out_bias, down_bias_all = cuts
    mix_bias = vectors[:, 6 * rows_in : 8 * rows_in].reshape(2, HEADS, head)
    up_bias_all = vectors[:, 8 * rows_in :].reshape(chips, 2, ny * rows_hid)
    up_bias_mine = lax.dynamic_index_in_dim(up_bias_all, core, 1, keepdims=False).reshape(-1)

    own = inputs.reshape(span, width)
    column = [own] + [place.send(own, "z", d) for d in range(1, nz)]
    beside = [place.send(piece, "x") for piece in column]
    x_all = jnp.zeros((nz, 2, span, width), LOW)
    for d in range(nz):
        at = lax.rem(place.z + nz - d, nz)
        x_all = lax.dynamic_update_slice(x_all, column[d][None, None], (at, place.x, 0, 0))
        x_all = lax.dynamic_update_slice(x_all, beside[d][None, None], (at, 1 - place.x, 0, 0))
    x_all = place.both(x_all, x_all).transpose(1, 2, 0, 3, 4)
    x_all = x_all.reshape(chips * 2 * span, width)

    def gather_rows(mine, theirs):
        block = place.both(mine, theirs)
        block = place.gather(block, "z", 0)
        block = place.gather(block, "x", 1)
        block = place.gather(block, "y", 3)
        return block.reshape(parts * block.shape[-2], block.shape[-1])

    mixing = mixing_weight.reshape(rows_in, 3, 2, half)
    mine, theirs = by_core(mixing, 2)
    mixing = gather_rows(mine.reshape(rows_in, -1), theirs.reshape(rows_in, -1))
    mine, theirs = by_core(output_weight.reshape(rows_in, 2, half), 1)
    out_half = gather_rows(mine, theirs)
    out_all = place.both(out_half, out_half).transpose(1, 0, 2).reshape(width, width)
    mine, theirs = by_core(up_weight.reshape(rows_in, chips, 2, ny * rows_hid), 2)
    up = gather_rows(mine.reshape(rows_in, -1), theirs.reshape(rows_in, -1))
    down = place.gather(down_weight, "z", 0)
    down = place.gather(down, "x", 1)
    down = place.gather(down, "y", 2).reshape(chips * ny * rows_hid, width)

    mixing = mixing.reshape(width, 3, per_core, head)
    head_weight = lax.dynamic_index_in_dim(mixing, my_head, 2, keepdims=False).reshape(width, 3 * head)
    whole_head = core * per_core + my_head
    head_bias = lax.dynamic_index_in_dim(mix_bias, whole_head, 1, keepdims=False)
    head_bias = jnp.concatenate([head_bias[0], jnp.zeros((head,), FULL), head_bias[1]])
    first_low, q, k, v, out, out_t, top = attend_plain(
        x_all, first_gain[None], first_shift[None], head_weight, head_bias[None]
    )
    attended = collect(exchange(out.reshape(chips, 2 * span, head)))
    attended = attended.transpose(1, 0, 2).reshape(2 * span, half)
    attended = place.both(attended, attended).transpose(1, 0, 2).reshape(2 * span, width)

    residual = lax.dynamic_slice_in_dim(x_all, chip * 2 * span, 2 * span, 0).astype(FULL)
    branch = dot(attended, out_all, (1, 0)) + out_bias
    scale = jnp.array(SCALES, FULL)[:, None, None]
    middle = residual + scale * branch
    second_normed, second_inv = normalize(middle)
    second_low = (second_normed * second_gain + second_shift).astype(LOW)
    rows = second_low.reshape(4 * span, width)
    hidden_pre = dot(rows, up, (1, 0)) + up_bias_mine
    activated, gelu_back = jax.vjp(partial(jax.nn.gelu, approximate=True), hidden_pre)
    activated_low = activated.astype(LOW)
    feed_part = dot(activated_low, down, (1, 0)).reshape(2, 2, span, width)
    mine, theirs = by_core(feed_part, 1)
    feed_own = mine + place.send(theirs, "core") + down_bias_all

    def own_rows(values):
        return lax.dynamic_index_in_dim(
            values.reshape((2, 2, span) + values.shape[2:]), core, 1, keepdims=False
        )

    activations = (own_rows(middle) + scale * feed_own).astype(LOW)
    upstream_own = cotangent.reshape(2, span, width)
    upstream = place.both(upstream_own, upstream_own).transpose(1, 0, 2, 3)
    down_in = (scale[..., None] * upstream.astype(FULL)).astype(LOW).reshape(4 * span, width)
    hidden_low = gelu_back(dot(down_in, down, (1, 1)))[0].astype(LOW)
    second_part = dot(hidden_low, up, (1, 1)).reshape(2, 2, span, width)
    mine, theirs = by_core(second_part, 1)
    second_grad = mine + place.send(theirs, "core")
    normed_own, inv_own = own_rows(second_normed), own_rows(second_inv)
    middle_grad = upstream_own.astype(FULL) + norm_back(second_grad, normed_own, inv_own, second_gain)
    branch_own = (scale * middle_grad).astype(LOW)
    branch_low = place.both(branch_own, branch_own).transpose(1, 0, 2, 3).reshape(2, 2 * span, width)
    out_rows = lax.dynamic_slice_in_dim(out_all, core * half, half, 0)
    go = dot(branch_low.reshape(4 * span, width), out_rows, (1, 1)).astype(LOW)
    go = go.reshape(2, 2 * span, per_core, head).transpose(2, 1, 0, 3).reshape(per_core, 2 * span, 2 * head)
    go = exchange(spread(go)).reshape(chips * 2 * span, 2 * head)

    gq, gk, gv = attend_back(q, k, v, out_t, top, go)
    head_grads = jnp.concatenate([gq, gk, gv], axis=1)

    depth_rows = second_low.reshape(2, 2 * span, width)
    hidden_rows = hidden_low.reshape(2, 2 * span, -1)
    active_rows = activated_low.reshape(2, 2 * span, -1)
    in_rows = down_in.reshape(2, 2 * span, width)
    branch_cols = lax.dynamic_slice_in_dim(branch_low, core * half, half, 2)
    orders = (("y", "x"), ("x", "y"))

    def scatter_chips(values, order):
        dims = {"x": 1, "y": 2}
        values = place.scatter(values, order[0], dims[order[0]]).astype(LOW)
        values = place.scatter(values, order[1], 1).astype(LOW)
        return place.scatter(values, "z", 0)

    def scatter_rows(values, order):
        shaped = values.reshape(nz, 2, 2, ny, rows_in, -1).transpose(0, 1, 3, 2, 4, 5)
        summed = scatter_chips(shaped, order)
        mine, theirs = by_core(summed, 0)
        return place.both(mine, theirs)

    down_grads, up_grads, out_grads = [], [], []
    for depth in range(2):
        grad = dot(active_rows[depth], in_rows[depth], (0, 0)).astype(LOW)
        down_grads.append(scatter_chips(grad.reshape(nz, 2, ny, rows_hid, width), orders[depth]))
    for depth in range(2):
        grad = dot(depth_rows[depth], hidden_rows[depth], (0, 0)).astype(LOW)
        grad = scatter_rows(grad, orders[depth]).reshape(2, rows_in, chips, -1)
        up_grads.append(grad.transpose(1, 2, 0, 3).reshape(rows_in, hidden))
    for depth in range(2):
        grad = dot(attended, branch_cols[depth], (0, 0)).astype(LOW)
        out_grads.append(scatter_rows(grad, orders[depth]).transpose(1, 0, 2).reshape(rows_in, width))

    head_sum = dot(first_low, head_grads, (0, 0)).astype(LOW).reshape(nz, 2, 2, ny, rows_in, 6 * head)
    head_sum = place.scatter(head_sum, "y", 3).astype(LOW).reshape(chips, 2, rows_in, 6 * head)
    head_sum = collect(exchange(head_sum))
    mine, theirs = by_core(head_sum, 1)
    mixing_grad = place.both(mine, theirs).reshape(HEADS, rows_in, 3, 2, head)
    mixing_grad = mixing_grad.transpose(3, 1, 2, 0, 4).reshape(2, rows_in, 3 * width).astype(FULL)

    mixed_grads = collect(exchange(head_grads.reshape(chips, 2 * span, 6 * head)))
    mixed_grads = mixed_grads.reshape(per_core, 2 * span, 3, 2, head).transpose(3, 1, 2, 0, 4)
    mixed_grads = mixed_grads.reshape(4 * span, 3 * half)
    first_part = dot(mixed_grads, mixing.reshape(width, 3 * half), (1, 1)).reshape(2, 2, span, width)
    mine, theirs = by_core(first_part, 1)
    first_grad = mine + place.send(theirs, "core")
    first_normed, first_inv = normalize(own.astype(FULL))
    input_grad = middle_grad + norm_back(first_grad, first_normed, first_inv, first_gain)

    bias_sum = jnp.sum(head_grads.astype(FULL), axis=0).reshape(3, 2, head) * busy
    spot = (jnp.arange(HEADS) == whole_head).astype(FULL)[None, None, :, None]
    bias_sum = (jnp.stack([bias_sum[0], bias_sum[2]], axis=1)[:, :, None, :] * spot).reshape(2, parts, -1)
    hidden_sum = jnp.sum(hidden_rows.astype(FULL), axis=1).reshape(2, chips, 1, ny * rows_hid)
    hidden_spot = (jnp.arange(2) == core).astype(FULL)[None, None, :, None]
    hidden_sum = (hidden_sum * hidden_spot).reshape(2, parts, rows_hid)
    in_own = (scale * upstream_own.astype(FULL)).astype(LOW)
    sums = [
        jnp.sum(first_grad * first_normed, axis=1),
        jnp.sum(first_grad, axis=1),
        jnp.sum(second_grad * normed_own, axis=1),
        jnp.sum(second_grad, axis=1),
        jnp.sum(branch_own.astype(FULL), axis=1),
        jnp.sum(in_own.astype(FULL), axis=1),
    ]
    sums = [item.reshape(2, parts, rows_in) for item in sums] + [bias_sum, hidden_sum]
    sums = jnp.concatenate(sums, axis=2).reshape(2, nz, 2, 2, ny, -1)
    sums = place.scatter(sums, "y", 4)
    sums = place.scatter(sums, "x", 2)
    sums = place.scatter(sums, "core", 2)
    sums = place.scatter(sums, "z", 1)
    small = [sums[:, i * rows_in : (i + 1) * rows_in] for i in range(6)]
    return (
        activations[:, None],
        input_grad[:, None],
        small[0],
        small[1],
        mixing_grad,
        sums[:, 6 * rows_in : 8 * rows_in],
        jnp.stack(out_grads),
        small[4],
        small[2],
        small[3],
        jnp.stack(up_grads),
        sums[:, 8 * rows_in :],
        jnp.stack(down_grads),
        small[5],
    )


def on_device(
    inputs,
    attend_gain,
    attend_shift,
    mixing_weight,
    mixing_bias,
    output_weight,
    output_bias,
    feed_gain,
    feed_shift,
    up_weight,
    up_bias,
    down_weight,
    down_bias,
    cotangent,
):
    place = Place()
    _, span, width = inputs.shape
    nz, ny, core, chip = place.nz, place.ny, place.core, place.chip
    chips = nz * 2
    parts = chips * 2 * ny
    head = width // HEADS
    per_core = HEADS // 2
    slots = [int((j + 0.5) * chips / per_core) for j in range(per_core)]
    half = width // 2
    hidden = up_weight.shape[1]
    rows_in = width // parts
    rows_hid = hidden // parts
    groups = [[2 * i + c for i in range(chips)] for c in range(2)]

    def exchange(values):
        return lax.all_to_all(values, "seq", 0, 0, axis_index_groups=groups, tiled=True)

    def spread(blocks):
        filled = [jnp.zeros_like(blocks[0])] * chips
        for j, slot in enumerate(slots):
            filled[slot] = blocks[j]
        return jnp.stack(filled)

    def collect(blocks):
        return jnp.stack([blocks[slot] for slot in slots])

    owned = [-1] * chips
    for j, slot in enumerate(slots):
        owned[slot] = j
    my_head = jnp.array(owned, jnp.int32)[chip]
    busy = (my_head >= 0).astype(FULL)
    my_head = jnp.maximum(my_head, 0)

    def by_core(values, dim):
        mine = lax.dynamic_index_in_dim(values, core, dim, keepdims=False)
        theirs = lax.dynamic_index_in_dim(values, 1 - core, dim, keepdims=False)
        return mine, theirs

    own = inputs.reshape(span, width)
    pairs = per_core // 2
    mix = mixing_weight.reshape(rows_in, 3, 2, pairs, 2, head).transpose(2, 3, 0, 1, 4, 5)
    mix = mix.reshape(2, pairs, rows_in, half)
    out_cols = output_weight.reshape(rows_in, 2, half).transpose(1, 0, 2)[:, None]
    vectors = jnp.concatenate(
        [attend_gain, attend_shift, feed_gain, feed_shift, output_bias, down_bias, mixing_bias, up_bias]
    )
    pieces = vectors.shape[0]
    vectors = jnp.pad(vectors[None], ((0, rows_in - 1), (0, half - pieces)))
    vectors = jnp.broadcast_to(vectors, (2, 1) + vectors.shape)
    packed = jnp.concatenate([mix, out_cols, vectors], axis=1)
    up_cols = up_weight.reshape(rows_in, chips, 2, ny * rows_hid).transpose(2, 0, 1, 3).reshape(2, rows_in, -1)
    mine, theirs = by_core(packed, 0)
    packed = place.both(mine, theirs).transpose(1, 0, 2, 3).reshape(pairs + 2, 2 * rows_in, half)
    mine, theirs = by_core(up_cols, 0)
    up_unit = place.both(mine, theirs).reshape(2 * rows_in, -1)

    def order(values, axis):
        shape = values.shape
        split = shape[:axis] + (chips, 2, ny, rows_in) + shape[axis + 1 :]
        return jnp.swapaxes(values.reshape(split), axis + 1, axis + 2).reshape(shape)

    def unorder(values, axis):
        shape = values.shape
        split = shape[:axis] + (chips, ny, 2, rows_in) + shape[axis + 1 :]
        return jnp.swapaxes(values.reshape(split), axis + 1, axis + 2).reshape(shape)

    lane = jnp.arange(width, dtype=jnp.int32)
    in_rows_of = lane // rows_in
    pair_lane = jnp.arange(2 * head, dtype=jnp.int32) + (core * pairs + my_head // 2) * 2 * head
    bias_cols, bias_rows = [], []
    for start in (0, width):
        spot = start + pair_lane
        device = spot // (2 * rows_in)
        bias_cols.append(6 * rows_in + spot % (2 * rows_in))
        bias_rows.append((device // (2 * ny)) * 2 * ny + (device % ny) * 2 + (device // ny) % 2)
    none = jnp.full((2 * head,), -1, jnp.int32)
    table = jnp.stack([
        jnp.concatenate([lane % rows_in, rows_in + lane % rows_in, bias_cols[0], none, bias_cols[1]]),
        jnp.concatenate([in_rows_of, in_rows_of, bias_rows[0], none, bias_rows[1]]),
    ])
    mw_all, up_all, dn_all, first_low, q, k, v, out_t, top, attended, x2 = attend(
        nz, ny, order(own, 1), packed, up_unit, down_weight, table
    )

    vectors = mw_all[:, :, :, pairs + 1].reshape(nz, 2, ny, 2, rows_in, half)[..., 0, :pieces]
    vectors = jnp.swapaxes(vectors, 2, 3).reshape(parts, -1).astype(FULL)
    cuts = [vectors[:, i * rows_in : (i + 1) * rows_in].reshape(-1) for i in range(6)]
    first_gain, first_shift, second_gain, second_shift, out_bias, down_bias_all = cuts
    up_bias_all = vectors[:, 8 * rows_in :].reshape(chips, 2, ny * rows_hid)
    up_bias_mine = lax.dynamic_index_in_dim(up_bias_all, core, 1, keepdims=False).reshape(-1)
    whole_head = core * per_core + my_head

    out_half = unorder(mw_all[:, :, :, pairs].reshape(width, half), 0)
    out_all = place.both(out_half, out_half).transpose(1, 0, 2).reshape(width, width)
    up = unorder(up_all.reshape(width, -1), 0)
    down = dn_all.reshape(chips * ny * rows_hid, width)
    attended = attended.transpose(2, 0, 1, 3).reshape(2 * span, width)

    residual = unorder(x2.reshape(2 * span, width), 1).astype(FULL)
    branch = dot(attended, out_all, (1, 0)) + out_bias
    scale = jnp.array(SCALES, FULL)[:, None, None]
    middle = residual + scale * branch
    second_normed, second_inv = normalize(middle)
    second_low = (second_normed * second_gain + second_shift).astype(LOW)
    rows = second_low.reshape(4 * span, width)
    hidden_pre = dot(rows, up, (1, 0)) + up_bias_mine
    activated, gelu_back = jax.vjp(partial(jax.nn.gelu, approximate=True), hidden_pre)
    activated_low = activated.astype(LOW)
    feed_part = dot(activated_low, down, (1, 0)).reshape(2, 2, span, width)
    mine, theirs = by_core(feed_part, 1)
    feed_own = mine + place.send(theirs, "core") + down_bias_all

    def own_rows(values):
        return lax.dynamic_index_in_dim(
            values.reshape((2, 2, span) + values.shape[2:]), core, 1, keepdims=False
        )

    activations = (own_rows(middle) + scale * feed_own).astype(LOW)
    upstream_own = cotangent.reshape(2, span, width)
    upstream = place.both(upstream_own, upstream_own).transpose(1, 0, 2, 3)
    down_in = (scale[..., None] * upstream.astype(FULL)).astype(LOW).reshape(4 * span, width)
    hidden_low = gelu_back(dot(down_in, down, (1, 1)))[0].astype(LOW)
    second_part = dot(hidden_low, up, (1, 1)).reshape(2, 2, span, width)
    mine, theirs = by_core(second_part, 1)
    second_grad = mine + place.send(theirs, "core")
    normed_own, inv_own = own_rows(second_normed), own_rows(second_inv)
    middle_grad = upstream_own.astype(FULL) + norm_back(second_grad, normed_own, inv_own, second_gain)
    branch_own = (scale * middle_grad).astype(LOW)
    branch_low = place.both(branch_own, branch_own).transpose(1, 0, 2, 3).reshape(2, 2 * span, width)
    out_rows = lax.dynamic_slice_in_dim(out_all, core * half, half, 0)
    go = dot(branch_low.reshape(4 * span, width), out_rows, (1, 1)).astype(LOW)
    go = go.reshape(2, 2 * span, per_core, head).transpose(2, 1, 0, 3).reshape(per_core, 2 * span, 2 * head)
    go = exchange(spread(go)).reshape(chips * 2 * span, 2 * head)

    gq, gk, gv = attend_back(q, k, v, out_t, top, go)
    head_grads = jnp.concatenate([gq, gk, gv], axis=1)

    depth_rows = second_low.reshape(2, 2 * span, width)
    hidden_rows = hidden_low.reshape(2, 2 * span, -1)
    active_rows = activated_low.reshape(2, 2 * span, -1)
    in_rows = down_in.reshape(2, 2 * span, width)
    branch_cols = lax.dynamic_slice_in_dim(branch_low, core * half, half, 2)
    orders = (("y", "x"), ("x", "y"))

    def scatter_chips(values, order):
        dims = {"x": 1, "y": 2}
        values = place.scatter(values, order[0], dims[order[0]]).astype(LOW)
        values = place.scatter(values, order[1], 1).astype(LOW)
        return place.scatter(values, "z", 0)

    def scatter_rows(values, order):
        shaped = values.reshape(nz, 2, 2, ny, rows_in, -1).transpose(0, 1, 3, 2, 4, 5)
        summed = scatter_chips(shaped, order)
        mine, theirs = by_core(summed, 0)
        return place.both(mine, theirs)

    down_grads, up_grads, out_grads = [], [], []
    for depth in range(2):
        grad = dot(active_rows[depth], in_rows[depth], (0, 0)).astype(LOW)
        down_grads.append(scatter_chips(grad.reshape(nz, 2, ny, rows_hid, width), orders[depth]))
    for depth in range(2):
        grad = dot(depth_rows[depth], hidden_rows[depth], (0, 0)).astype(LOW)
        grad = scatter_rows(grad, orders[depth]).reshape(2, rows_in, chips, -1)
        up_grads.append(grad.transpose(1, 2, 0, 3).reshape(rows_in, hidden))
    for depth in range(2):
        grad = dot(attended, branch_cols[depth], (0, 0)).astype(LOW)
        out_grads.append(scatter_rows(grad, orders[depth]).transpose(1, 0, 2).reshape(rows_in, width))

    head_sum = unorder(dot(first_low, head_grads, (0, 0)).astype(LOW), 0).reshape(nz, 2, 2, ny, rows_in, 6 * head)
    head_sum = place.scatter(head_sum, "y", 3).astype(LOW).reshape(chips, 2, rows_in, 6 * head)
    head_sum = collect(exchange(head_sum))
    mine, theirs = by_core(head_sum, 1)
    mixing_grad = place.both(mine, theirs).reshape(HEADS, rows_in, 3, 2, head)
    mixing_grad = mixing_grad.transpose(3, 1, 2, 0, 4).reshape(2, rows_in, 3 * width).astype(FULL)

    mixed_grads = collect(exchange(head_grads.reshape(chips, 2 * span, 6 * head)))
    mixed_grads = mixed_grads.reshape(per_core, 2 * span, 3, 2, head).transpose(3, 1, 2, 0, 4)
    mixed_grads = mixed_grads.reshape(4 * span, 3 * half)
    mixing = mw_all[:, :, :, :pairs].transpose(3, 0, 1, 2, 4, 5).reshape(pairs, width, 3, 2, head)
    mixing = unorder(mixing.transpose(1, 2, 0, 3, 4).reshape(width, 3 * half), 0)
    first_part = dot(mixed_grads, mixing, (1, 1)).reshape(2, 2, span, width)
    mine, theirs = by_core(first_part, 1)
    first_grad = mine + place.send(theirs, "core")
    first_normed, first_inv = normalize(own.astype(FULL))
    input_grad = middle_grad + norm_back(first_grad, first_normed, first_inv, first_gain)

    bias_sum = jnp.sum(head_grads.astype(FULL), axis=0).reshape(3, 2, head) * busy
    spot = (jnp.arange(HEADS) == whole_head).astype(FULL)[None, None, :, None]
    bias_sum = (jnp.stack([bias_sum[0], bias_sum[2]], axis=1)[:, :, None, :] * spot).reshape(2, parts, -1)
    hidden_sum = jnp.sum(hidden_rows.astype(FULL), axis=1).reshape(2, chips, 1, ny * rows_hid)
    hidden_spot = (jnp.arange(2) == core).astype(FULL)[None, None, :, None]
    hidden_sum = (hidden_sum * hidden_spot).reshape(2, parts, rows_hid)
    in_own = (scale * upstream_own.astype(FULL)).astype(LOW)
    sums = [
        jnp.sum(first_grad * first_normed, axis=1),
        jnp.sum(first_grad, axis=1),
        jnp.sum(second_grad * normed_own, axis=1),
        jnp.sum(second_grad, axis=1),
        jnp.sum(branch_own.astype(FULL), axis=1),
        jnp.sum(in_own.astype(FULL), axis=1),
    ]
    sums = [item.reshape(2, parts, rows_in) for item in sums] + [bias_sum, hidden_sum]
    sums = jnp.concatenate(sums, axis=2).reshape(2, nz, 2, 2, ny, -1)
    sums = place.scatter(sums, "y", 4)
    sums = place.scatter(sums, "x", 2)
    sums = place.scatter(sums, "core", 2)
    sums = place.scatter(sums, "z", 1)
    small = [sums[:, i * rows_in : (i + 1) * rows_in] for i in range(6)]
    return (
        activations[:, None],
        input_grad[:, None],
        small[0],
        small[1],
        mixing_grad,
        sums[:, 6 * rows_in : 8 * rows_in],
        jnp.stack(out_grads),
        small[4],
        small[2],
        small[3],
        jnp.stack(up_grads),
        sums[:, 8 * rows_in :],
        jnp.stack(down_grads),
        small[5],
    )


def solution(mesh):
    shard = P(("seq", "batch"))
    grad = P(None, ("seq", "batch"))
    row = P(None, "batch", "seq", None)
    return jax.shard_map(
        on_device,
        mesh=mesh,
        in_specs=(P("batch", "seq", None),) + (shard,) * 12 + (row,),
        out_specs=(row, row) + (grad,) * 12,
        check_vma=False,
    )
```

```python
from functools import partial

import jax
import jax.numpy as jnp
from jax import lax
from jax.experimental import pallas as pl
from jax.experimental.pallas import tpu as pltpu
from jax.sharding import PartitionSpec as P

HEADS = 12
EPS = 1e-05
SCALES = (12.0 ** (-0.5), 48.0 ** (-0.5))
NEGATIVE = -1e30
LOW = jnp.bfloat16
FULL = jnp.float32
TILE = 256


def normalize(values):
    average = jnp.mean(values, axis=-1, keepdims=True)
    centered = values - average
    inv_std = lax.rsqrt(jnp.mean(centered * centered, axis=-1, keepdims=True) + EPS)
    return centered * inv_std, inv_std


def norm_back(gradient, normed, inv_std, gain):
    scaled = gradient * gain
    inner = (
        scaled
        - jnp.mean(scaled, axis=-1, keepdims=True)
        - normed * jnp.mean(scaled * normed, axis=-1, keepdims=True)
    )
    return inv_std * inner


def dot(a, b, dims):
    return lax.dot_general(a, b, ((dims[:1], dims[1:]), ((), ())), preferred_element_type=FULL)


class Place:
    def __init__(self):
        self.s = lax.axis_size("seq")
        self.ny = lax.axis_size("batch")
        self.nz = self.s // 4
        seq = lax.axis_index("seq")
        self.y = lax.axis_index("batch")
        self.core = lax.rem(seq, 2)
        self.chip = seq // 2
        self.x = lax.rem(self.chip, 2)
        self.z = self.chip // 2
        self.sizes = {"z": self.nz, "x": 2, "y": self.ny, "core": 2}
        self.at = {"z": self.z, "x": self.x, "y": self.y, "core": self.core}

    def send(self, values, axis, d=1):
        pairs = []
        for s in range(self.s):
            for y in range(self.ny):
                c, x, z, t = s % 2, (s // 2) % 2, s // 4, y
                if axis == "z":
                    z = (z + d) % self.nz
                elif axis == "x":
                    x = 1 - x
                elif axis == "core":
                    c = 1 - c
                else:
                    t = (y + d) % self.ny
                pairs.append((s * self.ny + y, ((z * 2 + x) * 2 + c) * self.ny + t))
        return lax.ppermute(values, ("seq", "batch"), pairs)

    def gather(self, values, axis, dim):
        size, at = self.sizes[axis], self.at[axis]
        shape = values.shape[:dim] + (size,) + values.shape[dim:]
        whole = lax.dynamic_update_slice_in_dim(
            jnp.zeros(shape, values.dtype), jnp.expand_dims(values, dim), at, dim
        )
        for d in range(1, size):
            piece = jnp.expand_dims(self.send(values, axis, d), dim)
            whole = lax.dynamic_update_slice_in_dim(whole, piece, lax.rem(at + size - d, size), dim)
        return whole

    def scatter(self, values, axis, dim):
        size, at = self.sizes[axis], self.at[axis]

        def pick(i):
            return lax.dynamic_index_in_dim(values, lax.rem(i, size), dim, keepdims=False)

        total = pick(at).astype(FULL)
        for d in range(1, size):
            total = total + self.send(pick(at + d), axis, d).astype(FULL)
        return total

    def both(self, mine, theirs):
        got = self.send(theirs, "core")
        first = self.core == 0
        return jnp.stack([jnp.where(first, mine, got), jnp.where(first, got, mine)])


def attend_plain_kernel(x_ref, gain_ref, shift_ref, w_ref, b_ref, h_ref, q_ref, k_ref, v_ref, o_ref, ot_ref, top_ref, vt_ref):
    length = x_ref.shape[0]
    head = q_ref.shape[1]
    tiles = length // TILE

    def project(i, _):
        rows = pl.ds(pl.multiple_of(i * TILE, TILE), TILE)
        normed, _ = normalize(x_ref[rows, :].astype(FULL))
        low = (normed * gain_ref[...] + shift_ref[...]).astype(LOW)
        h_ref[rows, :] = low
        mixed = dot(low, w_ref[...], (1, 0)) + b_ref[...]
        q_ref[rows, :] = (mixed[:, :head].astype(LOW) * (head ** (-0.5))).astype(LOW)
        k_ref[rows, :] = mixed[:, head : 2 * head].astype(LOW)
        value = mixed[:, 2 * head :].astype(LOW)
        v_ref[rows, :] = value
        vt_ref[:, rows] = value.T
        return 0

    lax.fori_loop(0, tiles, project, 0)

    def query_tile(i, _):
        rows = pl.ds(pl.multiple_of(i * TILE, TILE), TILE)
        query = q_ref[rows, :]

        def absorb(j, carry, masked):
            top, total, acc = carry
            keys = pl.ds(pl.multiple_of(j * TILE, TILE), TILE)
            scores = dot(k_ref[keys, :], query, (1, 1))
            if masked:
                key_pos = lax.broadcasted_iota(jnp.int32, scores.shape, 0)
                query_pos = lax.broadcasted_iota(jnp.int32, scores.shape, 1)
                scores = jnp.where(key_pos <= query_pos, scores, NEGATIVE)
            new_top = jnp.maximum(top, jnp.max(scores, axis=0, keepdims=True))
            weights = jnp.exp(scores - new_top)
            keep = jnp.exp(top - new_top)
            total = total * keep + jnp.sum(weights, axis=0, keepdims=True)
            acc = acc * keep + dot(vt_ref[:, keys], weights.astype(LOW), (1, 0))
            return new_top, total, acc

        start = (
            jnp.full((1, TILE), NEGATIVE, FULL),
            jnp.zeros((1, TILE), FULL),
            jnp.zeros((head, TILE), FULL),
        )
        carry = lax.fori_loop(0, i, lambda j, c: absorb(j, c, False), start)
        top, total, acc = absorb(i, carry, True)
        out = acc / total
        ot_ref[:, rows] = out
        o_ref[rows, :] = out.T.astype(LOW)
        top_ref[:, rows] = top + jnp.log(total)
        return 0

    lax.fori_loop(0, tiles, query_tile, 0)


def attend_plain(x_all, gain, shift, weight, bias):
    length, head = x_all.shape[0], weight.shape[1] // 3
    low = jax.ShapeDtypeStruct((length, head), LOW)
    return pl.pallas_call(
        attend_plain_kernel,
        out_shape=(
            jax.ShapeDtypeStruct(x_all.shape, LOW),
            low,
            low,
            low,
            low,
            jax.ShapeDtypeStruct((head, length), FULL),
            jax.ShapeDtypeStruct((1, length), FULL),
        ),
        scratch_shapes=[pltpu.VMEM((head, length), LOW)],
        compiler_params=pltpu.CompilerParams(vmem_limit_bytes=48 << 20),
        cost_estimate=pl.CostEstimate(
            flops=6 * length * length * head, bytes_accessed=8 * length * 768, transcendentals=length * length
        ),
        name="attend_plain",
    )(x_all, gain, shift, weight, bias)


def attend_back_kernel(
    q_ref, k_ref, v_ref, ot_ref, top_ref, go_ref, gq_ref, gk_ref, gv_ref, kt_ref, got_ref, delta_ref, gqt_ref
):
    length, head = q_ref.shape
    tiles = length // TILE
    factor = head ** (-0.5)

    def prepare(i, _):
        rows = pl.ds(pl.multiple_of(i * TILE, TILE), TILE)
        kt_ref[:, rows] = k_ref[rows, :].T
        up = go_ref[rows, :].T
        for d in range(2):
            mine = up[d * head : (d + 1) * head, :]
            got_ref[d, :, rows] = mine
            delta_ref[d, :, rows] = jnp.sum(mine.astype(FULL) * ot_ref[:, rows], axis=0, keepdims=True)
            gqt_ref[d, :, rows] = jnp.zeros((head, TILE), FULL)
        return 0

    lax.fori_loop(0, tiles, prepare, 0)

    def key_tile(j, _):
        keys = pl.ds(pl.multiple_of(j * TILE, TILE), TILE)
        key = k_ref[keys, :]
        value = v_ref[keys, :]
        key_t = kt_ref[:, keys]

        def step(i, carry, masked):
            gv, gk0, gk1 = carry
            rows = pl.ds(pl.multiple_of(i * TILE, TILE), TILE)
            query = q_ref[rows, :]
            scores = dot(key, query, (1, 1))
            if masked:
                key_pos = lax.broadcasted_iota(jnp.int32, scores.shape, 0)
                query_pos = lax.broadcasted_iota(jnp.int32, scores.shape, 1)
                scores = jnp.where(key_pos <= query_pos, scores, NEGATIVE)
            probs = jnp.exp(scores - top_ref[:, rows])
            gv = gv + dot(probs.astype(LOW), go_ref[rows, :], (1, 0))
            gks = [gk0, gk1]
            for d in range(2):
                prob_grad = dot(value, got_ref[d, :, rows], (1, 0))
                score_low = (probs * (prob_grad - delta_ref[d, :, rows])).astype(LOW)
                gks[d] = gks[d] + dot(score_low, query, (1, 0))
                gqt_ref[d, :, rows] += dot(key_t, score_low, (1, 0))
            return gv, gks[0], gks[1]

        zero = jnp.zeros((TILE, head), FULL)
        carry = step(j, (jnp.zeros((TILE, 2 * head), FULL), zero, zero), True)
        gv, gk0, gk1 = lax.fori_loop(j + 1, tiles, lambda i, c: step(i, c, False), carry)
        gv_ref[keys, :] = gv.astype(LOW)
        gk_ref[keys, :] = jnp.concatenate([gk0, gk1], axis=1).astype(LOW)
        return 0

    lax.fori_loop(0, tiles, key_tile, 0)

    def finish(i, _):
        rows = pl.ds(pl.multiple_of(i * TILE, TILE), TILE)
        both = jnp.concatenate([gqt_ref[0, :, rows], gqt_ref[1, :, rows]], axis=0) * factor
        gq_ref[rows, :] = both.T.astype(LOW)
        return 0

    lax.fori_loop(0, tiles, finish, 0)


def attend_back(q, k, v, out_t, top, go):
    length, head = q.shape
    pair = jax.ShapeDtypeStruct((length, 2 * head), LOW)
    return pl.pallas_call(
        attend_back_kernel,
        out_shape=(pair, pair, pair),
        scratch_shapes=[
            pltpu.VMEM((head, length), LOW),
            pltpu.VMEM((2, head, length), LOW),
            pltpu.VMEM((2, 1, length), FULL),
            pltpu.VMEM((2, head, length), FULL),
        ],
        compiler_params=pltpu.CompilerParams(vmem_limit_bytes=48 << 20),
        cost_estimate=pl.CostEstimate(
            flops=20 * length * length * head, bytes_accessed=16 * length * head, transcendentals=length * length
        ),
        name="attend_back",
    )(q, k, v, out_t, top, go)


MESH = pl.DeviceIdType.MESH
DMA = pltpu.SemaphoreType.DMA


class Here:
    def __init__(self, nz, ny):
        self.nz, self.ny = nz, ny
        seq = lax.axis_index("seq")
        self.y = lax.axis_index("batch")
        self.core = lax.rem(seq, 2)
        self.chip = lax.div(seq, 2)
        self.x = lax.rem(self.chip, 2)
        self.z = lax.div(self.chip, 2)

    def device(self, z=None, x=None, core=None, y=None):
        z = self.z if z is None else z
        x = self.x if x is None else x
        core = self.core if core is None else core
        y = self.y if y is None else y
        return ((z * 2 + x) * 2 + core, y)

    def before(self, d):
        return lax.rem(self.z + self.nz - d, self.nz)

    def after(self, d):
        return lax.rem(self.z + d, self.nz)


def remote(src, dst, send, recv, device):
    return pltpu.make_async_remote_copy(
        src_ref=src, dst_ref=dst, send_sem=send, recv_sem=recv, device_id=device, device_id_type=MESH
    )


class Gather:
    def __init__(self, here, own, whole, x_first, sems):
        self.here, self.own, self.whole, self.x_first = here, own, whole, x_first
        self.zs, self.zr, self.as_, self.ar, self.bs, self.br, self.local = sems
        self.sent = []

    @staticmethod
    def scratch(nz, ny, x_first):
        first = nz if x_first else nz * ny
        second = nz * 2 * ny if x_first else nz * ny
        return [DMA((nz,)), DMA((nz,)), DMA((first,)), DMA((first,)), DMA((second,)), DMA((second,)), DMA]

    def _go(self, copy):
        copy.start()
        self.sent.append(copy)

    def _z(self, d, target):
        h = self.here
        z = h.z if target else h.before(d)
        return remote(self.own, self.whole.at[z, h.x, h.y], self.zs.at[d], self.zr.at[d], h.device(z=h.after(d)))

    def _source(self, d, x, y):
        h = self.here
        if d == 0 and x is h.x and y is h.y:
            return self.own
        return self.whole.at[h.before(d), x, y]

    def start(self):
        h = self.here
        self.kept = pltpu.make_async_copy(self.own, self.whole.at[h.z, h.x, h.y], self.local)
        self.kept.start()
        for d in range(1, h.nz):
            self._go(self._z(d, True))

    def finish_own(self):
        self.kept.wait()

    def _to_x(self, d, y, e, sems):
        h = self.here
        i = d * h.ny + e
        s, r = (sems[0].at[i], sems[1].at[i])
        return remote(self._source(d, h.x, y), self.whole.at[h.before(d), h.x, y], s, r, h.device(x=1 - h.x))

    def _from_x(self, d, y, e, sems):
        h = self.here
        i = d * h.ny + e
        spot = self.whole.at[h.before(d), 1 - h.x, y]
        return remote(spot, spot, sems[0].at[i], sems[1].at[i], h.device(x=1 - h.x))

    def _to_y(self, d, x, k, e, sems):
        h = self.here
        i = (d * 2 + k) * h.ny + e if self.x_first else d * h.ny + e
        spot = self.whole.at[h.before(d), x, h.y]
        return remote(
            self._source(d, x, h.y), spot, sems[0].at[i], sems[1].at[i], h.device(y=lax.rem(h.y + e, h.ny))
        )

    def _from_y(self, d, x, k, e, sems):
        h = self.here
        i = (d * 2 + k) * h.ny + e if self.x_first else d * h.ny + e
        spot = self.whole.at[h.before(d), x, lax.rem(h.y + h.ny - e, h.ny)]
        return remote(spot, spot, sems[0].at[i], sems[1].at[i], h.device(y=lax.rem(h.y + e, h.ny)))

    def arrived_z(self, d):
        h = self.here
        if d:
            self._z(d, False).wait_recv()
        if self.x_first:
            i = d
            s, r = self.as_.at[i], self.ar.at[i]
            self._go(remote(self._source(d, h.x, h.y), self.whole.at[h.before(d), h.x, h.y], s, r, h.device(x=1 - h.x)))
            for e in range(1, h.ny):
                self._go(self._to_y(d, h.x, 0, e, (self.bs, self.br)))
        else:
            for e in range(1, h.ny):
                self._go(self._to_y(d, h.x, 0, e, (self.as_, self.ar)))
            self._go(self._to_x(d, h.y, 0, (self.bs, self.br)))

    def arrived_second(self, d):
        h = self.here
        if self.x_first:
            spot = self.whole.at[h.before(d), 1 - h.x, h.y]
            remote(spot, spot, self.as_.at[d], self.ar.at[d], h.device(x=1 - h.x)).wait_recv()
            for e in range(1, h.ny):
                self._go(self._to_y(d, 1 - h.x, 1, e, (self.bs, self.br)))
        else:
            for e in range(1, h.ny):
                self._from_y(d, h.x, 0, e, (self.as_, self.ar)).wait_recv()
                self._go(self._to_x(d, lax.rem(h.y + h.ny - e, h.ny), e, (self.bs, self.br)))

    def arrived_third(self, d):
        h = self.here
        if self.x_first:
            for e in range(1, h.ny):
                self._from_y(d, h.x, 0, e, (self.bs, self.br)).wait_recv()
                self._from_y(d, 1 - h.x, 1, e, (self.bs, self.br)).wait_recv()
        else:
            for e in range(h.ny):
                self._from_x(d, lax.rem(h.y + h.ny - e, h.ny), e, (self.bs, self.br)).wait_recv()

    def finish(self):
        for copy in self.sent:
            copy.wait_send()


class GatherRows:
    def __init__(self, here, own, whole, sems):
        self.here, self.own, self.whole = here, own, whole
        self.zs, self.zr, self.xs, self.xr, self.cs, self.cr, self.local = sems
        self.sent = []

    @staticmethod
    def scratch(nz):
        return [DMA((nz,)), DMA((nz,)), DMA((nz,)), DMA((nz,)), DMA((2 * nz,)), DMA((2 * nz,)), DMA]

    def _go(self, copy):
        copy.start()
        self.sent.append(copy)

    def start(self):
        h = self.here
        self.kept = pltpu.make_async_copy(self.own, self.whole.at[h.z, h.x, h.core], self.local)
        self.kept.start()
        for d in range(1, h.nz):
            spot = self.whole.at[h.z, h.x, h.core]
            self._go(remote(self.own, spot, self.zs.at[d], self.zr.at[d], h.device(z=h.after(d))))

    def arrived_z(self, d):
        h = self.here
        spot = self.whole.at[h.before(d), h.x, h.core]
        if d:
            remote(spot, spot, self.zs.at[d], self.zr.at[d], h.device(z=h.after(d))).wait_recv()
        src = spot if d else self.own
        self._go(remote(src, spot, self.xs.at[d], self.xr.at[d], h.device(x=1 - h.x)))
        self._go(remote(src, spot, self.cs.at[2 * d], self.cr.at[2 * d], h.device(core=1 - h.core)))

    def arrived_x(self, d):
        h = self.here
        spot = self.whole.at[h.before(d), 1 - h.x, h.core]
        remote(spot, spot, self.xs.at[d], self.xr.at[d], h.device(x=1 - h.x)).wait_recv()
        self._go(remote(spot, spot, self.cs.at[2 * d + 1], self.cr.at[2 * d + 1], h.device(core=1 - h.core)))

    def arrived_core(self, d):
        h = self.here
        for k, x in ((0, h.x), (1, 1 - h.x)):
            spot = self.whole.at[h.before(d), x, 1 - h.core]
            i = 2 * d + k
            remote(spot, spot, self.cs.at[i], self.cr.at[i], h.device(core=1 - h.core)).wait_recv()

    def finish(self):
        self.kept.wait()
        for copy in self.sent:
            copy.wait_send()


def greet(devices):
    barrier = pltpu.get_barrier_semaphore()
    for device in devices:
        pl.semaphore_signal(barrier, inc=1, device_id=device, device_id_type=MESH)
    pl.semaphore_wait(barrier, len(devices))


def owner_of(chips):
    per_core = HEADS // 2
    return [int((j + 0.5) * chips / per_core) for j in range(per_core)]


def head_here(chip, slots):
    mine, has = jnp.int32(0), jnp.int32(0)
    for j, slot in enumerate(slots):
        same = (chip == slot).astype(jnp.int32)
        mine = mine + j * same
        has = has + same
    return mine, has


def attend_kernel(
    nz, ny, x_ref, mw_ref, up_ref, dn_ref, table_ref,
    mw_all, up_all, dn_all, h_ref, q_ref, k_ref, v_ref, ot_ref, top_ref, att_ref, x2_ref,
    xs, wt, vc, vt_ref, o_ref, load, att_s, att_r, pass_s, pass_r, *sems,
):
    here = Here(nz, ny)
    chips = 2 * nz
    slots = owner_of(chips)
    head = q_ref.shape[1]
    width = x_ref.shape[1]
    tile = 2 * x_ref.shape[0]
    mine, has = head_here(here.chip, slots)
    odd = lax.rem(mine, 2) == 1
    rows_sems, mw_sems, up_sems, dn_sems = sems[:7], sems[7:14], sems[14:21], sems[21:28]

    peers = [here.device(z=here.after(d)) for d in range(1, nz)]
    peers += [here.device(x=1 - here.x), here.device(core=1 - here.core)]
    peers += [here.device(z=here.after(d), x=1 - here.x) for d in range(1, nz)]
    peers += [here.device(y=lax.rem(here.y + e, ny)) for e in range(1, ny)]
    greet(peers)

    rows = GatherRows(here, x_ref, xs, rows_sems)
    mw = Gather(here, mw_ref, mw_all, True, mw_sems)
    up = Gather(here, up_ref, up_all, True, up_sems)
    dn = Gather(here, dn_ref, dn_all, False, dn_sems)
    rows.start()
    mw.start()
    for d in range(nz):
        rows.arrived_z(d)
        mw.arrived_z(d)
    for d in range(nz):
        rows.arrived_x(d)
        mw.arrived_second(d)
    up.start()
    dn.start()
    up.arrived_z(0)
    dn.arrived_z(0)
    for d in range(nz):
        mw.arrived_third(d)
    mw.finish_own()
    pair = pltpu.make_async_copy(mw_all.at[:, :, :, lax.div(mine, 2)], wt, load.at[0])
    pair.start()
    vectors = pltpu.make_async_copy(mw_all.at[:, :, :, 4], vc, load.at[1])
    vectors.start()
    for d in range(nz):
        rows.arrived_core(d)
    rows.kept.wait()
    pair.wait()
    vectors.wait()
    keep_rows = pltpu.make_async_copy(xs.at[here.z, here.x], x2_ref, load.at[2])
    keep_rows.start()

    steps = []
    for d in range(1, nz):
        steps += [partial(up.arrived_z, d), partial(dn.arrived_z, d)]
    for d in range(nz):
        steps += [partial(up.arrived_second, d), partial(dn.arrived_second, d)]
    for d in range(nz):
        steps += [partial(up.arrived_third, d), partial(dn.arrived_third, d)]

    @pl.when(has == 1)
    def _():
        pieces = vc[...].reshape(-1, vc.shape[-1])
        count = 2 * chips * ny
        unit = pieces.shape[0] // count
        pick_row = lax.broadcasted_iota(jnp.int32, (count, pieces.shape[0]), 0) * unit
        pick = (pick_row == lax.broadcasted_iota(jnp.int32, pick_row.shape, 1)).astype(LOW)
        pieces = dot(pick, pieces, (1, 0)).astype(LOW)
        cols, owners = table_ref[0:1, :], table_ref[1:2, :]
        spot = lax.broadcasted_iota(jnp.int32, (pieces.shape[1], cols.shape[1]), 0)
        moved = dot(pieces, (spot == cols).astype(LOW), (1, 0))
        from_row = lax.broadcasted_iota(jnp.int32, moved.shape, 0)
        flat = jnp.sum(jnp.where(from_row == owners, moved, 0.0), axis=0, keepdims=True)
        gain, shift, bias = flat[:, :width], flat[:, width : 2 * width], flat[:, 2 * width :]
        weight = wt[...].reshape(width, -1)

        def choose(values):
            return jnp.where(odd, values[:, head:], values[:, :head])

        for i in range(chips):
            span = slice(i * tile, (i + 1) * tile)
            values = xs[i // 2, i % 2].reshape(tile, width).astype(FULL)
            normed, _ = normalize(values)
            low = (normed * gain + shift).astype(LOW)
            h_ref[span, :] = low
            mixed = (dot(low, weight, (1, 0)) + bias).astype(LOW)
            q_ref[span, :] = (choose(mixed[:, : 2 * head]) * (head ** (-0.5))).astype(LOW)
            k_ref[span, :] = choose(mixed[:, 2 * head : 4 * head])
            value = choose(mixed[:, 4 * head :])
            v_ref[span, :] = value
            vt_ref[:, span] = value.T

    def query_tile(i):
        span = slice(i * tile, (i + 1) * tile)
        query = q_ref[span, :]

        def absorb(j, carry, masked):
            top, total, acc = carry
            keys = slice(j * tile, (j + 1) * tile)
            scores = dot(k_ref[keys, :], query, (1, 1))
            if masked:
                key_pos = lax.broadcasted_iota(jnp.int32, scores.shape, 0)
                query_pos = lax.broadcasted_iota(jnp.int32, scores.shape, 1)
                scores = jnp.where(key_pos <= query_pos, scores, NEGATIVE)
            new_top = jnp.maximum(top, jnp.max(scores, axis=0, keepdims=True))
            weights = jnp.exp(scores - new_top)
            keep = jnp.exp(top - new_top)
            total = total * keep + jnp.sum(weights, axis=0, keepdims=True)
            acc = acc * keep + dot(vt_ref[:, keys], weights.astype(LOW), (1, 0))
            return new_top, total, acc

        carry = (jnp.full((1, tile), NEGATIVE, FULL), jnp.zeros((1, tile), FULL), jnp.zeros((head, tile), FULL))
        for j in range(i + 1):
            carry = absorb(j, carry, j == i)
        top, total, acc = carry
        out = acc / total
        ot_ref[:, span] = out
        o_ref[i] = out.T.astype(LOW)
        top_ref[:, span] = top + jnp.log(total)

    def hand(i):
        spot = att_ref.at[here.core, mine]
        return (
            pltpu.make_async_copy(o_ref.at[i], spot, att_s.at[i]),
            remote(o_ref.at[i], spot, att_s.at[i], att_r.at[mine], here.device(z=i // 2, x=i % 2)),
        )

    for i in range(chips):
        @pl.when(has == 1)
        def _(i=i):
            query_tile(i)
            stay, leave = hand(i)
            pl.when(here.chip == i)(stay.start)
            pl.when(here.chip != i)(leave.start)

        for step in steps[3 * i : 3 * i + 3]:
            step()
    for step in steps[3 * chips :]:
        step()

    for i in range(chips):
        @pl.when(has == 1)
        def _(i=i):
            stay, leave = hand(i)
            pl.when(here.chip == i)(stay.wait)
            pl.when(here.chip != i)(leave.wait_send)

    for j, slot in enumerate(slots):
        @pl.when(here.chip != slot)
        def _(j=j, slot=slot):
            spot = att_ref.at[here.core, j]
            remote(spot, spot, att_s.at[0], att_r.at[j], here.device(z=slot // 2, x=slot % 2)).wait_recv()

    spot = att_ref.at[here.core]
    give = remote(spot, spot, pass_s, pass_r, here.device(core=1 - here.core))
    give.start()
    spot = att_ref.at[1 - here.core]
    remote(spot, spot, pass_s, pass_r, here.device(core=1 - here.core)).wait_recv()
    give.wait_send()
    keep_rows.wait()
    for item in (up, dn):
        item.finish_own()
    for item in (mw, up, dn):
        item.finish()
    for copy in rows.sent:
        copy.wait_send()


def attend(nz, ny, own, mw, up, dn, table):
    span, width = own.shape
    length = 4 * nz * span
    head = width // HEADS
    units = (nz, 2, ny)
    low = jax.ShapeDtypeStruct((length, head), LOW)
    anywhere = pl.BlockSpec(memory_space=pl.ANY)
    vmem = pl.BlockSpec(memory_space=pltpu.VMEM)
    return pl.pallas_call(
        partial(attend_kernel, nz, ny),
        out_shape=(
            jax.ShapeDtypeStruct(units + mw.shape, LOW),
            jax.ShapeDtypeStruct(units + up.shape, LOW),
            jax.ShapeDtypeStruct(units + dn.shape, LOW),
            jax.ShapeDtypeStruct((length, width), LOW),
            low,
            low,
            low,
            jax.ShapeDtypeStruct((head, length), FULL),
            jax.ShapeDtypeStruct((1, length), FULL),
            jax.ShapeDtypeStruct((2, HEADS // 2, 2 * span, head), LOW),
            jax.ShapeDtypeStruct((2, span, width), LOW),
        ),
        in_specs=[anywhere] * 4 + [vmem],
        out_specs=[anywhere] * 3 + [vmem] * 6 + [anywhere] * 2,
        scratch_shapes=[
            pltpu.VMEM((nz, 2, 2, span, width), LOW),
            pltpu.VMEM(units + mw.shape[1:], LOW),
            pltpu.VMEM(units + mw.shape[1:], LOW),
            pltpu.VMEM((head, length), LOW),
            pltpu.VMEM((2 * nz, 2 * span, head), LOW),
            DMA((3,)),
            DMA((2 * nz,)),
            DMA((HEADS // 2,)),
            DMA,
            DMA,
        ]
        + GatherRows.scratch(nz)
        + Gather.scratch(nz, ny, True)
        + Gather.scratch(nz, ny, True)
        + Gather.scratch(nz, ny, False),
        compiler_params=pltpu.CompilerParams(vmem_limit_bytes=56 << 20, collective_id=0, has_side_effects=True),
        cost_estimate=pl.CostEstimate(
            flops=6 * length * length * head, bytes_accessed=8 * length * width, transcendentals=length * length
        ),
        name="attend",
    )(own, mw, up, dn, table)


GELU_K = 0.7978845608028654
GELU_C = 0.044715


def gelu_pair(u):
    square = u * u
    tanh = jnp.tanh(GELU_K * u * (1.0 + GELU_C * square))
    half = 0.5 * (1.0 + tanh)
    slope = half + (0.5 * GELU_K) * u * (1.0 - tanh * tanh) * (1.0 + 3.0 * GELU_C * square)
    return u * half, slope


def feed_kernel(
    nz, ny, hidden_tile, x2_ref, att_ref, cot_ref, mw_all, up_ref, dn_ref, table_ref,
    act_ref, gmid_ref, go_ref, sum_ref, upsum_ref, gain_ref, grads_ref,
    up, dn, ow, own, pm, vc, att, cot, h2, act_low, gu, normed, inv, mid, feed, feed_in, gh2, gh2_in,
    eb, grads, load, out_s, send, recv,
):
    here = Here(nz, ny)
    core = here.core
    width = cot_ref.shape[-1]
    span = cot_ref.shape[1]
    rows = 2 * span
    half = width // 2
    hidden = up_ref.shape[1]
    per_core = att_ref.shape[1]
    head = att_ref.shape[3]
    partner = here.device(core=1 - core)
    my_rows = pl.ds(pl.multiple_of(core * span, span), span)
    their_rows = pl.ds(pl.multiple_of((1 - core) * span, span), span)

    loads = [
        pltpu.make_async_copy(mw_all.at[:, :, :, 3], ow.at[core], load.at[0]),
        pltpu.make_async_copy(mw_all.at[:, :, :, 4], vc, load.at[1]),
        pltpu.make_async_copy(up_ref, up, load.at[2]),
        pltpu.make_async_copy(dn_ref, dn, load.at[3]),
        pltpu.make_async_copy(cot_ref, cot.at[:, my_rows], load.at[4]),
    ]
    for copy in loads:
        copy.start()
    greet([partner])

    def pass_on(i, src, dst):
        return remote(src, dst, send.at[i], recv.at[i], partner)

    give_cot = pass_on(0, cot_ref, cot.at[:, my_rows])
    give_cot.start()
    loads[0].wait()
    give_ow = pass_on(1, ow.at[core], ow.at[core])
    give_ow.start()

    cols, owners, natural = table_ref[0:1, :], table_ref[1:2, :], table_ref[2:3, :width]
    from_row = lax.broadcasted_iota(jnp.int32, (width, width), 0)
    pm[...] = (from_row == natural).astype(LOW)
    loads[1].wait()
    pieces = vc[...].reshape(-1, vc.shape[-1])
    count = 4 * nz * ny
    unit = pieces.shape[0] // count
    pick_row = lax.broadcasted_iota(jnp.int32, (count, pieces.shape[0]), 0) * unit
    pick = (pick_row == lax.broadcasted_iota(jnp.int32, pick_row.shape, 1)).astype(LOW)
    pieces = dot(pick, pieces, (1, 0)).astype(LOW)
    spot = lax.broadcasted_iota(jnp.int32, (pieces.shape[1], cols.shape[1]), 0)
    moved = dot(pieces, (spot == cols).astype(LOW), (1, 0))
    piece_row = lax.broadcasted_iota(jnp.int32, moved.shape, 0)
    flat = jnp.sum(jnp.where(piece_row == owners, moved, 0.0), axis=0, keepdims=True)
    gain, shift, out_bias, down_bias = (flat[:, i * width : (i + 1) * width] for i in range(4))
    gain_ref[...] = flat[:, 4 * width : 5 * width]
    up_bias = flat[:, 5 * width :]

    natural_att = jnp.concatenate([att_ref[c, j] for c in range(2) for j in range(per_core)], axis=1)
    att[...] = dot(natural_att, pm[...], (1, 0)).astype(LOW)
    remote(ow.at[1 - core], ow.at[1 - core], send.at[1], recv.at[1], partner).wait_recv()
    for c in range(2):
        cols_c = slice(c * half, (c + 1) * half)
        own[:, cols_c] = dot(pm[...], ow[c].reshape(width, half), (1, 0)).astype(LOW)
    branch = dot(natural_att, own[...], (1, 0)) + out_bias
    x2 = x2_ref[...].reshape(rows, width).astype(FULL)
    for d in range(2):
        middle = x2 + SCALES[d] * branch
        n, r = normalize(middle)
        h2[d] = (n * gain + shift).astype(LOW)
        mid[d] = middle
        normed[d] = n
        inv[d] = r
    loads[4].wait()
    theirs_cot = cot.at[:, their_rows]
    remote(theirs_cot, theirs_cot, send.at[0], recv.at[0], partner).wait_recv()
    loads[2].wait()
    loads[3].wait()

    def upstream(d):
        return (SCALES[d] * cot[d].astype(FULL)).astype(LOW)

    exchanges = []
    for d in range(2):
        low_in = upstream(d)
        for t in range(hidden // hidden_tile):
            cut = slice(t * hidden_tile, (t + 1) * hidden_tile)
            u = dot(h2[d], up[:, cut], (1, 0)) + up_bias[:, cut]
            active, slope = gelu_pair(u)
            active = active.astype(LOW)
            act_low[d, :, cut] = active
            back = (dot(low_in, dn[cut, :], (1, 1)) * slope).astype(LOW)
            gu[d, :, cut] = back
            upsum_ref[d : d + 1, cut] = jnp.sum(back.astype(FULL), axis=0, keepdims=True)
            part = dot(back, up[:, cut], (1, 1))
            feed_part = dot(active, dn[cut, :], (1, 0))
            if t == 0:
                gh2[d] = part
                feed[d] = feed_part
            else:
                gh2[d] += part
                feed[d] += feed_part
        for i, (src, dst) in ((2, (gh2, gh2_in)), (4, (feed, feed_in))):
            copy = pass_on(i + d, src.at[d, their_rows], dst.at[d])
            copy.start()
            exchanges.append(copy)

    outs = []

    def write(src, dst, i):
        copy = pltpu.make_async_copy(src, dst, out_s.at[i])
        copy.start()
        outs.append(copy)

    slab_rows = 2 * unit

    def keep(d, values, first_row, first_col, base, rows_of):
        for i in range(0, values.shape[0], slab_rows):
            row = first_row + i
            u, within = row // rows_of, (row % rows_of) // slab_rows
            place = (u // (2 * ny), (u // ny) % 2, u % ny)
            for c in range(0, values.shape[1], half):
                slab = base + within * 2 + (first_col + c) // half
                grads[(d,) + place + (slab,)] = values[i : i + slab_rows, c : c + half]

    def hidden_grads(d):
        low_in = upstream(d)
        for t in range(0, hidden, half):
            keep(d, dot(act_low[d, :, t : t + half], low_in, (0, 0)).astype(LOW), t, 0, 0, 2 * slab_rows)
        for t in range(0, hidden, 2 * half):
            for m in range(0, width, half):
                part = dot(h2[d, :, m : m + half], gu[d, :, t : t + 2 * half], (0, 0)).astype(LOW)
                keep(d, part, m, t, 4, slab_rows)

    def row_sum(i, values):
        sum_ref[i : i + 1, :] = jnp.sum(values, axis=0, keepdims=True)

    hidden_grads(0)
    for d in range(2):
        remote(gh2_in.at[d], gh2_in.at[d], send.at[2 + d], recv.at[2 + d], partner).wait_recv()
        grad = gh2[d, my_rows, :] + gh2_in[d]
        n = normed[d, my_rows, :]
        row_sum(2 * 0 + d, grad * n)
        row_sum(2 * 1 + d, grad)
        own_cot = cot[d, my_rows, :].astype(FULL)
        middle_grad = own_cot + norm_back(grad, n, inv[d, my_rows, :], gain)
        gmid_ref[d] = middle_grad
        branch_low = (SCALES[d] * middle_grad).astype(LOW)
        row_sum(2 * 2 + d, branch_low.astype(FULL))
        row_sum(2 * 3 + d, (SCALES[d] * own_cot).astype(LOW).astype(FULL))
        eb[d, my_rows, :] = branch_low
        copy = pass_on(6 + d, eb.at[d, my_rows], eb.at[d, my_rows])
        copy.start()
        exchanges.append(copy)
    hidden_grads(1)
    own_half = own.at[pl.ds(pl.multiple_of(core * half, half), half), :]
    for d in range(2):
        spot = eb.at[d, their_rows]
        remote(spot, spot, send.at[6 + d], recv.at[6 + d], partner).wait_recv()
        go = dot(eb[d], own_half[...], (1, 1)).astype(LOW)
        for j in range(per_core):
            go_ref[j, :, d * head : (d + 1) * head] = go[:, j * head : (j + 1) * head]
        mine = eb[d, :, pl.ds(pl.multiple_of(core * half, half), half)]
        for m in range(0, width, half):
            keep(d, dot(att[:, m : m + half], mine, (0, 0)).astype(LOW), m, 0, 8, slab_rows)
        write(grads.at[d], grads_ref.at[d], d)
    for d in range(2):
        remote(feed_in.at[d], feed_in.at[d], send.at[4 + d], recv.at[4 + d], partner).wait_recv()
        out = mid[d, my_rows, :] + SCALES[d] * (feed[d, my_rows, :] + feed_in[d] + down_bias)
        act_ref[d] = dot(out.astype(LOW), pm[...], (1, 1)).astype(LOW)
    give_cot.wait_send()
    give_ow.wait_send()
    for copy in exchanges:
        copy.wait_send()
    for copy in outs:
        copy.wait()


def feed_forward(nz, ny, x2, attended, cot, mw_all, up, dn, table):
    _, span, width = cot.shape
    hidden = up.shape[1]
    half = width // 2
    per_core, head = attended.shape[1], attended.shape[3]
    rows = 2 * span
    anywhere = pl.BlockSpec(memory_space=pl.ANY)
    vmem = pl.BlockSpec(memory_space=pltpu.VMEM)
    units = mw_all.shape[:3]
    return pl.pallas_call(
        partial(feed_kernel, nz, ny, 512),
        out_shape=(
            jax.ShapeDtypeStruct((2, span, width), LOW),
            jax.ShapeDtypeStruct((2, span, width), FULL),
            jax.ShapeDtypeStruct((per_core, rows, 2 * head), LOW),
            jax.ShapeDtypeStruct((8, width), FULL),
            jax.ShapeDtypeStruct((2, hidden), FULL),
            jax.ShapeDtypeStruct((1, width), FULL),
            jax.ShapeDtypeStruct((2,) + units + (9, mw_all.shape[4], half), LOW),
        ),
        in_specs=[vmem, vmem, anywhere, anywhere, anywhere, anywhere, vmem],
        out_specs=[vmem] * 6 + [anywhere],
        scratch_shapes=[
            pltpu.VMEM((width, hidden), LOW),
            pltpu.VMEM((hidden, width), LOW),
            pltpu.VMEM((2,) + units + mw_all.shape[4:], LOW),
            pltpu.VMEM((width, width), LOW),
            pltpu.VMEM((width, width), LOW),
            pltpu.VMEM(units + mw_all.shape[4:], LOW),
            pltpu.VMEM((rows, width), LOW),
            pltpu.VMEM((2, rows, width), LOW),
            pltpu.VMEM((2, rows, width), LOW),
            pltpu.VMEM((2, rows, hidden), LOW),
            pltpu.VMEM((2, rows, hidden), LOW),
            pltpu.VMEM((2, rows, width), FULL),
            pltpu.VMEM((2, rows, 1), FULL),
            pltpu.VMEM((2, rows, width), FULL),
            pltpu.VMEM((2, rows, width), FULL),
            pltpu.VMEM((2, span, width), FULL),
            pltpu.VMEM((2, rows, width), FULL),
            pltpu.VMEM((2, span, width), FULL),
            pltpu.VMEM((2, rows, width), LOW),
            pltpu.VMEM((2,) + units + (9, mw_all.shape[4], half), LOW),
            DMA((5,)),
            DMA((2,)),
            DMA((8,)),
            DMA((8,)),
        ],
        compiler_params=pltpu.CompilerParams(vmem_limit_bytes=60 << 20, collective_id=1, has_side_effects=True),
        cost_estimate=pl.CostEstimate(
            flops=28 * rows * width * hidden, bytes_accessed=20 * width * hidden, transcendentals=2 * rows * hidden
        ),
        name="feed_forward",
    )(x2, attended, cot, mw_all, up, dn, table)


def split_dot(values, turn, dims):
    high = values.astype(LOW)
    rest = values - high.astype(FULL)
    middle = rest.astype(LOW)
    low = (rest - middle.astype(FULL)).astype(LOW)
    return dot(high, turn, dims) + dot(middle, turn, dims) + dot(low, turn, dims)


def back_kernel(
    nz, q_ref, k_ref, v_ref, ot_ref, top_ref, h_ref, go_ref, grads, gmid_ref, x_ref, gain_ref, sum_ref, upsum_ref,
    mw_all, table_ref, bias_ref,
    ing_ref, dn_ref, up_ref, out_ref, mix_ref, vec_ref,
    go_all, kt_ref, got_ref, delta_ref, gqt_ref, gsend, gat, mw, pm, head_sum, hs_in, mix_in, mixf, mix_swap,
    mine, r1, r2, r3, fin, swap, first, first_in, pack, vec_in,
    load, go_s, go_r, kv_s, kv_r, q_s, q_r, s1, t1, s2, t2, s3, t3, ex_s, ex_r, vec_s, vec_r, mix_s, mix_r,
):
    ny = 2
    here = Here(nz, ny)
    core, chip, x, y, z = here.core, here.chip, here.x, here.y, here.z
    chips = 2 * nz
    slots = owner_of(chips)
    per_core = len(slots)
    length, head = q_ref.shape
    tile = length // chips
    span = tile // 2
    width = x_ref.shape[1]
    half = width // 2
    factor = head ** (-0.5)
    job, has = head_here(chip, slots)
    partner = here.device(core=1 - core)
    unit_rows = fin.shape[2]
    rows_in = unit_rows // 2
    parts = 4 * nz * ny
    slabs = fin.shape[1]

    def flat(zz, xx, yy, cc):
        return ((zz * 2 + xx) * ny + yy) * 2 + cc

    others = []
    for dz in range(nz):
        for dx in range(2):
            for dy in range(ny):
                for dc in range(2):
                    if dz or dx or dy or dc:
                        zz = lax.rem(z + dz, nz)
                        xx = 1 - x if dx else x
                        yy = 1 - y if dy else y
                        cc = 1 - core if dc else core
                        back = (lax.rem(z + nz - dz, nz), xx, yy, cc)
                        others.append((here.device(zz, xx, cc, yy), flat(zz, xx, yy, cc), flat(*back)))

    def a1(d):
        return here.device(y=1 - y) if d == 0 else here.device(x=1 - x)

    def a2(d):
        return here.device(x=1 - x) if d == 0 else here.device(y=1 - y)

    def at2(d):
        return x if d == 0 else y

    zis = []
    for i in range((nz + 1) // 2):
        zis += [nz - 1 - i] + ([i] if i != nz - 1 - i else [])
    loads = {}
    for zi in zis:
        loads[0, zi] = pltpu.make_async_copy(grads.at[0, zi, :, y], mine.at[0, zi], load.at[0, zi])
        loads[1, zi] = pltpu.make_async_copy(grads.at[1, zi, x], mine.at[1, zi], load.at[1, zi])
        loads[0, zi].start()
        loads[1, zi].start()
    weights = pltpu.make_async_copy(mw_all.at[:, :, :, 0:3], mw, load.at[2, 0])
    weights.start()
    greet([device for device, _, _ in others])

    def go_copies(j):
        slot = slots[j]
        return (
            pltpu.make_async_copy(go_ref.at[j], go_all.at[chip], go_s.at[j]),
            remote(go_ref.at[j], go_all.at[chip], go_s.at[j], go_r.at[chip], here.device(z=slot // 2, x=slot % 2)),
        )

    for j, slot in enumerate(slots):
        stay, leave = go_copies(j)
        pl.when(chip == slot)(stay.start)
        pl.when(chip != slot)(leave.start)

    def stage1(d, zi):
        src = grads.at[0, zi, :, 1 - y] if d == 0 else grads.at[1, zi, 1 - x]
        return remote(src, r1.at[d, zi], s1.at[d, zi], t1.at[d, zi], a1(d))

    def stage2(d, zi):
        return remote(mine.at[d, zi, 1 - at2(d)], r2.at[d, zi], s2.at[d, zi], t2.at[d, zi], a2(d))

    def stage3(d, zi, up):
        to = here.device(z=lax.min(z + 1, nz - 1)) if up else here.device(z=lax.max(z - 1, 0))
        way = 0 if up else 1
        return remote(r2.at[d, zi], r3.at[d, way, zi], s3.at[d, zi], t3.at[d, way, zi], to)

    for zi in zis:
        for d in range(2):
            stage1(d, zi).start()

    def add_into(target, other, lead):
        def one(i, _):
            a, b = target(i), other(i)
            a[...] = (a[...].astype(FULL) + b[...].astype(FULL)).astype(LOW)
            return 0

        lax.fori_loop(0, lead, one, 0)

    def after1(d, zi):
        loads[d, zi].wait()
        stage1(d, zi).wait_recv()
        add_into(
            lambda i: mine.at[d, zi, lax.div(i, slabs), lax.rem(i, slabs)],
            lambda i: r1.at[d, zi, lax.div(i, slabs), lax.rem(i, slabs)],
            2 * slabs,
        )
        stage2(d, zi).start()

    def after2(d, zi):
        stage2(d, zi).wait_recv()
        add_into(lambda i: r2.at[d, zi, i], lambda i: mine.at[d, zi, at2(d), i], slabs)

        @pl.when(jnp.logical_and(z == 0, zi > 0))
        def _():
            stage3(d, zi, True).start()

        @pl.when(jnp.logical_and(z == nz - 1, zi < nz - 1))
        def _():
            stage3(d, zi, False).start()

    def after3(d, zi):
        @pl.when(jnp.logical_and(z < zi, z > 0))
        def _():
            stage3(d, zi, True).wait_recv()
            add_into(lambda i: r2.at[d, zi, i], lambda i: r3.at[d, 0, zi, i], slabs)
            stage3(d, zi, True).start()

        @pl.when(jnp.logical_and(z > zi, z < nz - 1))
        def _():
            stage3(d, zi, False).wait_recv()
            add_into(lambda i: r2.at[d, zi, i], lambda i: r3.at[d, 1, zi, i], slabs)
            stage3(d, zi, False).start()

    def last3(d, zi):
        @pl.when(z == zi)
        def _():
            if zi > 0:
                stage3(d, zi, True).wait_recv()
            if zi < nz - 1:
                stage3(d, zi, False).wait_recv()

            def one(i, _):
                total = r2[d, zi, i].astype(FULL)
                if zi > 0:
                    total = total + r3[d, 0, zi, i].astype(FULL)
                if zi < nz - 1:
                    total = total + r3[d, 1, zi, i].astype(FULL)
                fin[d, i] = total
                return 0

            lax.fori_loop(0, slabs, one, 0)

    def finish_sends():
        for zi in zis:
            for d in range(2):
                stage1(d, zi).wait_send()
                stage2(d, zi).wait_send()
                pl.when(z != zi)(stage3(d, zi, True).wait_send)

    @pl.when(has == 1)
    def _():
        for t in range(chips):
            stay = pltpu.make_async_copy(go_ref.at[0], go_all.at[t], go_s.at[job])
            come = remote(go_ref.at[0], go_all.at[t], go_s.at[0], go_r.at[t], here.device(z=t // 2, x=t % 2))
            pl.when(chip == t)(stay.wait)
            pl.when(chip != t)(come.wait_recv)
        for i in range(chips):
            rows = slice(i * tile, (i + 1) * tile)
            kt_ref[:, rows] = k_ref[rows, :].T
            up_t = go_all[i].T
            for d in range(2):
                part = up_t[d * head : (d + 1) * head, :]
                got_ref[d, :, rows] = part
                delta_ref[d, :, rows] = jnp.sum(part.astype(FULL) * ot_ref[:, rows], axis=0, keepdims=True)
                gqt_ref[d, :, rows] = jnp.zeros((head, tile), FULL)

    def key_tile(j):
        keys = slice(j * tile, (j + 1) * tile)
        key = k_ref[keys, :]
        value = v_ref[keys, :]
        key_t = kt_ref[:, keys]

        def step(i, carry, masked):
            gv, gk0, gk1 = carry
            rows = pl.ds(i * tile if masked else pl.multiple_of(i * tile, tile), tile)
            query = q_ref[rows, :]
            scores = dot(key, query, (1, 1))
            if masked:
                key_pos = lax.broadcasted_iota(jnp.int32, scores.shape, 0)
                query_pos = lax.broadcasted_iota(jnp.int32, scores.shape, 1)
                scores = jnp.where(key_pos <= query_pos, scores, NEGATIVE)
            probs = jnp.exp(scores - top_ref[:, rows])
            gv = gv + dot(probs.astype(LOW), go_all[i], (1, 0))
            gks = [gk0, gk1]
            for d in range(2):
                prob_grad = dot(value, got_ref[d, :, rows], (1, 0))
                score_low = (probs * (prob_grad - delta_ref[d, :, rows])).astype(LOW)
                gks[d] = gks[d] + dot(score_low, query, (1, 0))
                gqt_ref[d, :, rows] += dot(key_t, score_low, (1, 0))
            return gv, gks[0], gks[1]

        zero = jnp.zeros((tile, head), FULL)
        carry = step(j, (jnp.zeros((tile, 2 * head), FULL), zero, zero), True)
        gv, gk0, gk1 = lax.fori_loop(j + 1, chips, lambda i, c: step(i, c, False), carry)
        gsend[j, 1] = jnp.concatenate([gk0, gk1], axis=1).astype(LOW)
        gsend[j, 2] = gv.astype(LOW)

    def kv_copies(t):
        src, dst = gsend.at[t, pl.ds(1, 2)], gat.at[job, pl.ds(1, 2)]
        to = here.device(z=t // 2, x=t % 2)
        return pltpu.make_async_copy(src, dst, kv_s.at[t]), remote(src, dst, kv_s.at[t], kv_r.at[job], to)

    def q_copies(t):
        src, dst = gsend.at[t, 0], gat.at[job, 0]
        to = here.device(z=t // 2, x=t % 2)
        return pltpu.make_async_copy(src, dst, q_s.at[t]), remote(src, dst, q_s.at[t], q_r.at[job], to)

    def launch(copies, t):
        stay, leave = copies(t)
        pl.when(chip == t)(stay.start)
        pl.when(chip != t)(leave.start)

    between = {chips // 2 - 1: [(0, 0), (1, 0)], chips - 1: [(0, 1), (1, 1)]}
    for j in range(chips):
        @pl.when(has == 1)
        def _(j=j):
            key_tile(j)
            launch(kv_copies, j)

        for d, n in between.get(j, []):
            if n < nz:
                after1(d, zis[n])

    @pl.when(has == 1)
    def _():
        for i in range(chips):
            rows = slice(i * tile, (i + 1) * tile)
            both = jnp.concatenate([gqt_ref[0, :, rows], gqt_ref[1, :, rows]], axis=0) * factor
            gsend[i, 0] = both.T.astype(LOW)
            launch(q_copies, i)

    def mix_y():
        return remote(head_sum.at[:, :, 1 - y], hs_in, ex_s.at[0], ex_r.at[0], here.device(y=1 - y))

    def mix_copies(t):
        src, dst = head_sum.at[t // 2, t % 2, y], mix_in.at[job]
        to = here.device(z=t // 2, x=t % 2)
        return pltpu.make_async_copy(src, dst, mix_s.at[t]), remote(src, dst, mix_s.at[t], mix_r.at[job], to)

    @pl.when(has == 1)
    def _():
        for t in range(3):
            acc = None
            for i in range(chips):
                rows = slice(i * tile, (i + 1) * tile)
                part = dot(h_ref[rows, :], gsend[i, t], (0, 0))
                acc = part if acc is None else acc + part
            low = acc.astype(LOW)
            for u in range(parts // 2):
                zz, xx, yy = u // (2 * ny), (u // ny) % 2, u % ny
                head_sum[zz, xx, yy, :, t * 2 * head : (t + 1) * 2 * head] = low[u * unit_rows : (u + 1) * unit_rows]
        mix_y().start()

    for zi in zis[2:3]:
        for d in range(2):
            after1(d, zi)

    @pl.when(has == 1)
    def _():
        mix_y().wait_recv()
        mix_y().wait_send()
        add_into(
            lambda i: head_sum.at[lax.div(i, 2), lax.rem(i, 2), y],
            lambda i: hs_in.at[lax.div(i, 2), lax.rem(i, 2)],
            chips,
        )
        for t in range(chips):
            launch(mix_copies, t)

    for d in range(2):
        after2(d, zis[0])
    for zi in zis[3:]:
        for d in range(2):
            after1(d, zi)
    for d in range(2):
        after2(d, zis[1])
        after3(d, zis[0])

    weights.wait()
    for j, slot in enumerate(slots):
        @pl.when(chip != slot)
        def _(j=j, slot=slot):
            to = here.device(z=slot // 2, x=slot % 2)
            remote(gat.at[j, pl.ds(1, 2)], gat.at[j, pl.ds(1, 2)], kv_s.at[0], kv_r.at[j], to).wait_recv()
            remote(gat.at[j, 0], gat.at[j, 0], q_s.at[0], q_r.at[j], to).wait_recv()

        @pl.when(chip == slot)
        def _(j=j, slot=slot):
            kv_copies(slot)[0].wait()
            q_copies(slot)[0].wait()

    for d in range(2):
        lanes = slice(d * head, (d + 1) * head)
        total = None
        for p in range(per_core // 2):
            left = jnp.concatenate(
                [gat[2 * p + o, t][:, lanes] for t in range(3) for o in range(2)], axis=1
            )
            weight = mw[:, :, :, p].reshape(width, half)
            part = dot(left, weight, (1, 1))
            total = part if total is None else total + part
        first[d] = total
    my_rows = pl.ds(pl.multiple_of(core * span, span), span)
    their_rows = pl.ds(pl.multiple_of((1 - core) * span, span), span)

    def first_swap(d):
        return remote(first.at[d, their_rows], first_in.at[d], ex_s.at[1 + d], ex_r.at[1 + d], partner)

    for d in range(2):
        first_swap(d).start()

    from_row = lax.broadcasted_iota(jnp.int32, (width, width), 0)
    pm[...] = (from_row == table_ref[0:1, :width]).astype(LOW)
    normed, inv = normalize(x_ref[...].astype(FULL))
    gain = gain_ref[...]

    def place(total, vector, owners, columns):
        rows = lax.broadcasted_iota(jnp.int32, (parts, vector.shape[1]), 0)
        spread = jnp.where(rows == owners, vector, 0.0)
        turn = (lax.broadcasted_iota(jnp.int32, (vector.shape[1], total.shape[1]), 1) == columns).astype(LOW)
        high = spread.astype(LOW)
        low = (spread - high.astype(FULL)).astype(LOW)
        return total + dot(high, turn, (1, 0)) + dot(low, turn, (1, 0))

    stride = pack.shape[1] * pack.shape[2] // 2
    lane = lax.broadcasted_iota(jnp.int32, (width, 1), 0)
    in_piece = lax.rem(lane, rows_in)
    wide_owner = table_ref[1:2, :width]
    total = jnp.zeros((parts, 2 * stride), FULL)
    for v in range(4):
        for d in range(2):
            row = sum_ref[2 * v + d : 2 * v + d + 1, :]
            total = place(total, row, wide_owner, in_piece + ((v + 2) * rows_in + d * stride))
    hidden = upsum_ref.shape[1]
    rows_hid = 2 * hidden // parts
    hid_lane = lax.broadcasted_iota(jnp.int32, (hidden, 1), 0)
    for d in range(2):
        columns = lax.rem(hid_lane, rows_hid) + (8 * rows_in + d * stride)
        total = place(total, upsum_ref[d : d + 1, :], table_ref[2:3, :hidden], columns)

    biases = []
    for t in (0, 2):
        acc = jnp.zeros((1, 2 * head), FULL)
        for i in range(chips):
            acc = acc + jnp.sum(gsend[i, t].astype(FULL), axis=0, keepdims=True)
        biases.append(jnp.where(has == 1, acc, 0.0))
    for b in range(2):
        total = place(total, biases[b], table_ref[3 + b : 4 + b, : 2 * head], bias_ref[:, b : b + 1])

    for d in range(2):
        first_swap(d).wait_recv()
        grad = first[d, my_rows, :] + first_in[d]
        for v, row in ((0, jnp.sum(grad * normed, axis=0, keepdims=True)), (1, jnp.sum(grad, axis=0, keepdims=True))):
            total = place(total, row, wide_owner, in_piece + (v * rows_in + d * stride))
        whole = gmid_ref[d] + norm_back(grad, normed, inv, gain)
        ing_ref[d] = split_dot(whole, pm[...], (1, 1))
    for c in range(pack.shape[1]):
        pack[:, c, :] = total[:, c * 128 : (c + 1) * 128]
    me = flat(z, x, y, core)

    def vec_copy(n):
        device, index, _ = others[n]
        return remote(pack.at[index], vec_in.at[me], vec_s.at[n], vec_r.at[n], device)

    def vec_come(n):
        device, _, index = others[n]
        return remote(pack.at[index], vec_in.at[index], vec_s.at[n], vec_r.at[n], device)

    for n in range(len(others)):
        vec_copy(n).start()

    for zi in zis[2:]:
        for d in range(2):
            after2(d, zi)
    for zi in zis[1:]:
        for d in range(2):
            after3(d, zi)
    for zi in zis:
        for d in range(2):
            last3(d, zi)
    mine_in = pl.ds(pl.multiple_of(core * rows_in, 8), rows_in)
    their_in = pl.ds(pl.multiple_of((1 - core) * rows_in, 8), rows_in)

    def last_swap(d):
        return remote(fin.at[d, pl.ds(4, slabs - 4), their_in], swap.at[d], ex_s.at[3 + d], ex_r.at[3 + d], partner)

    for d in range(2):
        last_swap(d).start()
    for j, slot in enumerate(slots):
        @pl.when(chip != slot)
        def _(j=j, slot=slot):
            to = here.device(z=slot // 2, x=slot % 2)
            remote(mix_in.at[j], mix_in.at[j], mix_s.at[0], mix_r.at[j], to).wait_recv()

        @pl.when(chip == slot)
        def _(j=j, slot=slot):
            mix_copies(slot)[0].wait()

        mixf[j] = mix_in[j].astype(FULL)
    mix_pass = remote(mixf.at[:, their_in], mix_swap, ex_s.at[5], ex_r.at[5], partner)
    mix_pass.start()

    for d in range(2):
        top_half = jnp.concatenate([fin[d, 0], fin[d, 1]], axis=1)
        low_half = jnp.concatenate([fin[d, 2], fin[d, 3]], axis=1)
        dn_ref[d] = split_dot(jnp.concatenate([top_half, low_half], axis=0), pm[...], (1, 1))
    is_first = core == 0

    def by_core(a, b):
        return jnp.where(is_first, a, b), jnp.where(is_first, b, a)

    block = 2 * hidden // parts * ny
    for d in range(2):
        last_swap(d).wait_recv()
        ours = jnp.concatenate([fin[d, s, mine_in, :] for s in range(4, slabs - 1)], axis=1)
        came = jnp.concatenate([swap[d, s] for s in range(slabs - 5)], axis=1)
        one, two = by_core(ours, came)
        pieces = []
        for i in range(hidden // block):
            pieces += [one[:, i * block : (i + 1) * block], two[:, i * block : (i + 1) * block]]
        up_ref[d] = jnp.concatenate(pieces, axis=1)
        one, two = by_core(fin[d, slabs - 1, mine_in, :], swap[d, slabs - 5])
        out_ref[d] = split_dot(jnp.concatenate([one, two], axis=1), pm[...], (1, 1))
    mix_pass.wait_recv()
    sides = [by_core(mixf[j, mine_in, :], mix_swap[j]) for j in range(per_core)]
    for d in range(2):
        pieces = []
        for t in range(3):
            for c in range(2):
                for j in range(per_core):
                    start = t * 2 * head + d * head
                    pieces.append(sides[j][c][:, start : start + head])
        mix_ref[d] = jnp.concatenate(pieces, axis=1)
    for n in range(len(others)):
        vec_come(n).wait_recv()
    vec_in[me] = pack[me]
    vec_ref[...] = jnp.sum(vec_in[...], axis=0)

    finish_sends()
    for j, slot in enumerate(slots):
        pl.when(chip != slot)(go_copies(j)[1].wait_send)
        pl.when(jnp.logical_and(chip == slot, has == 0))(go_copies(j)[0].wait)

    @pl.when(has == 1)
    def _():
        for t in range(chips):
            @pl.when(chip != t)
            def _(t=t):
                kv_copies(t)[1].wait_send()
                q_copies(t)[1].wait_send()
                mix_copies(t)[1].wait_send()

    for d in range(2):
        first_swap(d).wait_send()
        last_swap(d).wait_send()
    mix_pass.wait_send()
    for n in range(len(others)):
        vec_copy(n).wait_send()


def back(nz, q, k, v, out_t, top, first_low, go, grads, gmid, x, gain, sums, up_sums, mw_all, table, bias_cols):
    length, head = q.shape
    span, width = x.shape
    chips = 2 * nz
    tile = 2 * span
    per_core = HEADS // 2
    slabs, unit, half = grads.shape[-3:]
    rows_in = unit // 2
    hidden = up_sums.shape[1]
    parts = 8 * nz
    anywhere = pl.BlockSpec(memory_space=pl.ANY)
    vmem = pl.BlockSpec(memory_space=pltpu.VMEM)
    return pl.pallas_call(
        partial(back_kernel, nz),
        out_shape=(
            jax.ShapeDtypeStruct((2, span, width), FULL),
            jax.ShapeDtypeStruct((2, 2 * unit, width), FULL),
            jax.ShapeDtypeStruct((2, rows_in, 2 * hidden), FULL),
            jax.ShapeDtypeStruct((2, rows_in, width), FULL),
            jax.ShapeDtypeStruct((2, rows_in, 3 * width), FULL),
            jax.ShapeDtypeStruct((5, 128), FULL),
        ),
        in_specs=[vmem] * 7 + [anywhere] + [vmem] * 5 + [anywhere] + [vmem] * 2,
        out_specs=[vmem] * 6,
        scratch_shapes=[
            pltpu.VMEM((chips, tile, 2 * head), LOW),
            pltpu.VMEM((head, length), LOW),
            pltpu.VMEM((2, head, length), LOW),
            pltpu.VMEM((2, 1, length), FULL),
            pltpu.VMEM((2, head, length), FULL),
            pltpu.VMEM((chips, 3, tile, 2 * head), LOW),
            pltpu.VMEM((per_core, 3, tile, 2 * head), LOW),
            pltpu.VMEM((nz, 2, 2, 3, unit, half), LOW),
            pltpu.VMEM((width, width), LOW),
            pltpu.VMEM((nz, 2, 2, unit, half), LOW),
            pltpu.VMEM((nz, 2, unit, half), LOW),
            pltpu.VMEM((per_core, unit, half), LOW),
            pltpu.VMEM((per_core, unit, half), FULL),
            pltpu.VMEM((per_core, rows_in, half), FULL),
            pltpu.VMEM((2, nz, 2, slabs, unit, half), LOW),
            pltpu.VMEM((2, nz, 2, slabs, unit, half), LOW),
            pltpu.VMEM((2, nz, slabs, unit, half), LOW),
            pltpu.VMEM((2, 2, nz, slabs, unit, half), LOW),
            pltpu.VMEM((2, slabs, unit, half), FULL),
            pltpu.VMEM((2, slabs - 4, rows_in, half), FULL),
            pltpu.VMEM((2, tile, width), FULL),
            pltpu.VMEM((2, span, width), FULL),
            pltpu.VMEM((parts, 5, 128), FULL),
            pltpu.VMEM((parts, 5, 128), FULL),
            DMA((3, nz)),
            DMA((per_core,)),
            DMA((chips,)),
            DMA((chips,)),
            DMA((per_core,)),
            DMA((chips,)),
            DMA((per_core,)),
            DMA((2, nz)),
            DMA((2, nz)),
            DMA((2, nz)),
            DMA((2, nz)),
            DMA((2, nz)),
            DMA((2, 2, nz)),
            DMA((6,)),
            DMA((6,)),
            DMA((parts - 1,)),
            DMA((parts - 1,)),
            DMA((chips,)),
            DMA((per_core,)),
        ],
        compiler_params=pltpu.CompilerParams(vmem_limit_bytes=60 << 20, collective_id=2, has_side_effects=True),
        cost_estimate=pl.CostEstimate(
            flops=20 * length * length * head, bytes_accessed=16 * length * head, transcendentals=length * length
        ),
        name="back",
    )(q, k, v, out_t, top, first_low, go, grads, gmid, x, gain, sums, up_sums, mw_all, table, bias_cols)


def plain_on_device(
    inputs,
    attend_gain,
    attend_shift,
    mixing_weight,
    mixing_bias,
    output_weight,
    output_bias,
    feed_gain,
    feed_shift,
    up_weight,
    up_bias,
    down_weight,
    down_bias,
    cotangent,
):
    place = Place()
    _, span, width = inputs.shape
    nz, ny, core, chip = place.nz, place.ny, place.core, place.chip
    chips = nz * 2
    parts = chips * 2 * ny
    head = width // HEADS
    per_core = HEADS // 2
    slots = [int((j + 0.5) * chips / per_core) for j in range(per_core)]
    half = width // 2
    hidden = up_weight.shape[1]
    rows_in = width // parts
    rows_hid = hidden // parts
    groups = [[2 * i + c for i in range(chips)] for c in range(2)]

    def exchange(values):
        return lax.all_to_all(values, "seq", 0, 0, axis_index_groups=groups, tiled=True)

    def spread(blocks):
        filled = [jnp.zeros_like(blocks[0])] * chips
        for j, slot in enumerate(slots):
            filled[slot] = blocks[j]
        return jnp.stack(filled)

    def collect(blocks):
        return jnp.stack([blocks[slot] for slot in slots])

    owned = [-1] * chips
    for j, slot in enumerate(slots):
        owned[slot] = j
    my_head = jnp.array(owned, jnp.int32)[chip]
    busy = (my_head >= 0).astype(FULL)
    my_head = jnp.maximum(my_head, 0)

    def by_core(values, dim):
        mine = lax.dynamic_index_in_dim(values, core, dim, keepdims=False)
        theirs = lax.dynamic_index_in_dim(values, 1 - core, dim, keepdims=False)
        return mine, theirs

    vectors = jnp.concatenate(
        [attend_gain, attend_shift, feed_gain, feed_shift, output_bias, down_bias, mixing_bias, up_bias]
    )
    vectors = place.both(vectors, vectors)
    vectors = place.gather(vectors, "z", 0)
    vectors = place.gather(vectors, "x", 1)
    vectors = place.gather(vectors, "y", 3)
    vectors = vectors.reshape(parts, -1).astype(FULL)
    cuts = [vectors[:, i * rows_in : (i + 1) * rows_in].reshape(-1) for i in range(6)]
    first_gain, first_shift, second_gain, second_shift, out_bias, down_bias_all = cuts
    mix_bias = vectors[:, 6 * rows_in : 8 * rows_in].reshape(2, HEADS, head)
    up_bias_all = vectors[:, 8 * rows_in :].reshape(chips, 2, ny * rows_hid)
    up_bias_mine = lax.dynamic_index_in_dim(up_bias_all, core, 1, keepdims=False).reshape(-1)

    own = inputs.reshape(span, width)
    column = [own] + [place.send(own, "z", d) for d in range(1, nz)]
    beside = [place.send(piece, "x") for piece in column]
    x_all = jnp.zeros((nz, 2, span, width), LOW)
    for d in range(nz):
        at = lax.rem(place.z + nz - d, nz)
        x_all = lax.dynamic_update_slice(x_all, column[d][None, None], (at, place.x, 0, 0))
        x_all = lax.dynamic_update_slice(x_all, beside[d][None, None], (at, 1 - place.x, 0, 0))
    x_all = place.both(x_all, x_all).transpose(1, 2, 0, 3, 4)
    x_all = x_all.reshape(chips * 2 * span, width)

    def gather_rows(mine, theirs):
        block = place.both(mine, theirs)
        block = place.gather(block, "z", 0)
        block = place.gather(block, "x", 1)
        block = place.gather(block, "y", 3)
        return block.reshape(parts * block.shape[-2], block.shape[-1])

    mixing = mixing_weight.reshape(rows_in, 3, 2, half)
    mine, theirs = by_core(mixing, 2)
    mixing = gather_rows(mine.reshape(rows_in, -1), theirs.reshape(rows_in, -1))
    mine, theirs = by_core(output_weight.reshape(rows_in, 2, half), 1)
    out_half = gather_rows(mine, theirs)
    out_all = place.both(out_half, out_half).transpose(1, 0, 2).reshape(width, width)
    mine, theirs = by_core(up_weight.reshape(rows_in, chips, 2, ny * rows_hid), 2)
    up = gather_rows(mine.reshape(rows_in, -1), theirs.reshape(rows_in, -1))
    down = place.gather(down_weight, "z", 0)
    down = place.gather(down, "x", 1)
    down = place.gather(down, "y", 2).reshape(chips * ny * rows_hid, width)

    mixing = mixing.reshape(width, 3, per_core, head)
    head_weight = lax.dynamic_index_in_dim(mixing, my_head, 2, keepdims=False).reshape(width, 3 * head)
    whole_head = core * per_core + my_head
    head_bias = lax.dynamic_index_in_dim(mix_bias, whole_head, 1, keepdims=False)
    head_bias = jnp.concatenate([head_bias[0], jnp.zeros((head,), FULL), head_bias[1]])
    first_low, q, k, v, out, out_t, top = attend_plain(
        x_all, first_gain[None], first_shift[None], head_weight, head_bias[None]
    )
    attended = collect(exchange(out.reshape(chips, 2 * span, head)))
    attended = attended.transpose(1, 0, 2).reshape(2 * span, half)
    attended = place.both(attended, attended).transpose(1, 0, 2).reshape(2 * span, width)

    residual = lax.dynamic_slice_in_dim(x_all, chip * 2 * span, 2 * span, 0).astype(FULL)
    branch = dot(attended, out_all, (1, 0)) + out_bias
    scale = jnp.array(SCALES, FULL)[:, None, None]
    middle = residual + scale * branch
    second_normed, second_inv = normalize(middle)
    second_low = (second_normed * second_gain + second_shift).astype(LOW)
    rows = second_low.reshape(4 * span, width)
    hidden_pre = dot(rows, up, (1, 0)) + up_bias_mine
    activated, gelu_back = jax.vjp(partial(jax.nn.gelu, approximate=True), hidden_pre)
    activated_low = activated.astype(LOW)
    feed_part = dot(activated_low, down, (1, 0)).reshape(2, 2, span, width)
    mine, theirs = by_core(feed_part, 1)
    feed_own = mine + place.send(theirs, "core") + down_bias_all

    def own_rows(values):
        return lax.dynamic_index_in_dim(
            values.reshape((2, 2, span) + values.shape[2:]), core, 1, keepdims=False
        )

    activations = (own_rows(middle) + scale * feed_own).astype(LOW)
    upstream_own = cotangent.reshape(2, span, width)
    upstream = place.both(upstream_own, upstream_own).transpose(1, 0, 2, 3)
    down_in = (scale[..., None] * upstream.astype(FULL)).astype(LOW).reshape(4 * span, width)
    hidden_low = gelu_back(dot(down_in, down, (1, 1)))[0].astype(LOW)
    second_part = dot(hidden_low, up, (1, 1)).reshape(2, 2, span, width)
    mine, theirs = by_core(second_part, 1)
    second_grad = mine + place.send(theirs, "core")
    normed_own, inv_own = own_rows(second_normed), own_rows(second_inv)
    middle_grad = upstream_own.astype(FULL) + norm_back(second_grad, normed_own, inv_own, second_gain)
    branch_own = (scale * middle_grad).astype(LOW)
    branch_low = place.both(branch_own, branch_own).transpose(1, 0, 2, 3).reshape(2, 2 * span, width)
    out_rows = lax.dynamic_slice_in_dim(out_all, core * half, half, 0)
    go = dot(branch_low.reshape(4 * span, width), out_rows, (1, 1)).astype(LOW)
    go = go.reshape(2, 2 * span, per_core, head).transpose(2, 1, 0, 3).reshape(per_core, 2 * span, 2 * head)
    go = exchange(spread(go)).reshape(chips * 2 * span, 2 * head)

    gq, gk, gv = attend_back(q, k, v, out_t, top, go)
    head_grads = jnp.concatenate([gq, gk, gv], axis=1)

    depth_rows = second_low.reshape(2, 2 * span, width)
    hidden_rows = hidden_low.reshape(2, 2 * span, -1)
    active_rows = activated_low.reshape(2, 2 * span, -1)
    in_rows = down_in.reshape(2, 2 * span, width)
    branch_cols = lax.dynamic_slice_in_dim(branch_low, core * half, half, 2)
    orders = (("y", "x"), ("x", "y"))

    def scatter_chips(values, order):
        dims = {"x": 1, "y": 2}
        values = place.scatter(values, order[0], dims[order[0]]).astype(LOW)
        values = place.scatter(values, order[1], 1).astype(LOW)
        return place.scatter(values, "z", 0)

    def scatter_rows(values, order):
        shaped = values.reshape(nz, 2, 2, ny, rows_in, -1).transpose(0, 1, 3, 2, 4, 5)
        summed = scatter_chips(shaped, order)
        mine, theirs = by_core(summed, 0)
        return place.both(mine, theirs)

    down_grads, up_grads, out_grads = [], [], []
    for depth in range(2):
        grad = dot(active_rows[depth], in_rows[depth], (0, 0)).astype(LOW)
        down_grads.append(scatter_chips(grad.reshape(nz, 2, ny, rows_hid, width), orders[depth]))
    for depth in range(2):
        grad = dot(depth_rows[depth], hidden_rows[depth], (0, 0)).astype(LOW)
        grad = scatter_rows(grad, orders[depth]).reshape(2, rows_in, chips, -1)
        up_grads.append(grad.transpose(1, 2, 0, 3).reshape(rows_in, hidden))
    for depth in range(2):
        grad = dot(attended, branch_cols[depth], (0, 0)).astype(LOW)
        out_grads.append(scatter_rows(grad, orders[depth]).transpose(1, 0, 2).reshape(rows_in, width))

    head_sum = dot(first_low, head_grads, (0, 0)).astype(LOW).reshape(nz, 2, 2, ny, rows_in, 6 * head)
    head_sum = place.scatter(head_sum, "y", 3).astype(LOW).reshape(chips, 2, rows_in, 6 * head)
    head_sum = collect(exchange(head_sum))
    mine, theirs = by_core(head_sum, 1)
    mixing_grad = place.both(mine, theirs).reshape(HEADS, rows_in, 3, 2, head)
    mixing_grad = mixing_grad.transpose(3, 1, 2, 0, 4).reshape(2, rows_in, 3 * width).astype(FULL)

    mixed_grads = collect(exchange(head_grads.reshape(chips, 2 * span, 6 * head)))
    mixed_grads = mixed_grads.reshape(per_core, 2 * span, 3, 2, head).transpose(3, 1, 2, 0, 4)
    mixed_grads = mixed_grads.reshape(4 * span, 3 * half)
    first_part = dot(mixed_grads, mixing.reshape(width, 3 * half), (1, 1)).reshape(2, 2, span, width)
    mine, theirs = by_core(first_part, 1)
    first_grad = mine + place.send(theirs, "core")
    first_normed, first_inv = normalize(own.astype(FULL))
    input_grad = middle_grad + norm_back(first_grad, first_normed, first_inv, first_gain)

    bias_sum = jnp.sum(head_grads.astype(FULL), axis=0).reshape(3, 2, head) * busy
    spot = (jnp.arange(HEADS) == whole_head).astype(FULL)[None, None, :, None]
    bias_sum = (jnp.stack([bias_sum[0], bias_sum[2]], axis=1)[:, :, None, :] * spot).reshape(2, parts, -1)
    hidden_sum = jnp.sum(hidden_rows.astype(FULL), axis=1).reshape(2, chips, 1, ny * rows_hid)
    hidden_spot = (jnp.arange(2) == core).astype(FULL)[None, None, :, None]
    hidden_sum = (hidden_sum * hidden_spot).reshape(2, parts, rows_hid)
    in_own = (scale * upstream_own.astype(FULL)).astype(LOW)
    sums = [
        jnp.sum(first_grad * first_normed, axis=1),
        jnp.sum(first_grad, axis=1),
        jnp.sum(second_grad * normed_own, axis=1),
        jnp.sum(second_grad, axis=1),
        jnp.sum(branch_own.astype(FULL), axis=1),
        jnp.sum(in_own.astype(FULL), axis=1),
    ]
    sums = [item.reshape(2, parts, rows_in) for item in sums] + [bias_sum, hidden_sum]
    sums = jnp.concatenate(sums, axis=2).reshape(2, nz, 2, 2, ny, -1)
    sums = place.scatter(sums, "y", 4)
    sums = place.scatter(sums, "x", 2)
    sums = place.scatter(sums, "core", 2)
    sums = place.scatter(sums, "z", 1)
    small = [sums[:, i * rows_in : (i + 1) * rows_in] for i in range(6)]
    return (
        activations[:, None],
        input_grad[:, None],
        small[0],
        small[1],
        mixing_grad,
        sums[:, 6 * rows_in : 8 * rows_in],
        jnp.stack(out_grads),
        small[4],
        small[2],
        small[3],
        jnp.stack(up_grads),
        sums[:, 8 * rows_in :],
        jnp.stack(down_grads),
        small[5],
    )


def on_device(
    inputs,
    attend_gain,
    attend_shift,
    mixing_weight,
    mixing_bias,
    output_weight,
    output_bias,
    feed_gain,
    feed_shift,
    up_weight,
    up_bias,
    down_weight,
    down_bias,
    cotangent,
):
    place = Place()
    _, span, width = inputs.shape
    nz, ny, core, chip = place.nz, place.ny, place.core, place.chip
    chips = nz * 2
    parts = chips * 2 * ny
    head = width // HEADS
    per_core = HEADS // 2
    half = width // 2
    hidden = up_weight.shape[1]
    rows_in = width // parts
    rows_hid = hidden // parts
    groups = [[2 * i + c for i in range(chips)] for c in range(2)]

    slots = owner_of(chips)
    owned = [-1] * chips
    for j, slot in enumerate(slots):
        owned[slot] = j
    my_head = jnp.array(owned, jnp.int32)[chip]
    my_head = jnp.maximum(my_head, 0)

    def by_core(values, dim):
        mine = lax.dynamic_index_in_dim(values, core, dim, keepdims=False)
        theirs = lax.dynamic_index_in_dim(values, 1 - core, dim, keepdims=False)
        return mine, theirs

    own = inputs.reshape(span, width)
    pairs = per_core // 2
    mix = mixing_weight.reshape(rows_in, 3, 2, pairs, 2, head).transpose(2, 3, 0, 1, 4, 5)
    mix = mix.reshape(2, pairs, rows_in, half)
    lane = jnp.arange(width, dtype=jnp.int32)
    rest = lane % (2 * ny * rows_in)
    natural = lane - rest + ((rest // rows_in) % 2) * ny * rows_in + (rest // (2 * rows_in)) * rows_in + lane % rows_in
    turn = (lane[:, None] == natural[None, :]).astype(LOW)
    turned = jnp.concatenate([own, cotangent.reshape(2 * span, width), output_weight, down_weight])
    turned = dot(turned, turn, (1, 0)).astype(LOW)
    own, cot = turned[:span], turned[span : 3 * span].reshape(2, span, width)
    out_weight, down_weight = turned[3 * span : 3 * span + rows_in], turned[3 * span + rows_in :]
    out_cols = out_weight.reshape(rows_in, 2, half).transpose(1, 0, 2)[:, None]
    vectors = jnp.concatenate(
        [attend_gain, attend_shift, feed_gain, feed_shift, output_bias, down_bias, mixing_bias, up_bias]
    )
    pieces = vectors.shape[0]
    vectors = jnp.pad(vectors[None], ((0, rows_in - 1), (0, half - pieces)))
    vectors = jnp.broadcast_to(vectors, (2, 1) + vectors.shape)
    packed = jnp.concatenate([mix, out_cols, vectors], axis=1)
    up_cols = up_weight.reshape(rows_in, chips, 2, ny * rows_hid).transpose(2, 0, 1, 3).reshape(2, rows_in, -1)
    mine, theirs = by_core(packed, 0)
    packed = place.both(mine, theirs).transpose(1, 0, 2, 3).reshape(pairs + 2, 2 * rows_in, half)
    mine, theirs = by_core(up_cols, 0)
    up_unit = place.both(mine, theirs).reshape(2 * rows_in, -1)

    in_rows_of = lane // rows_in
    pair_lane = jnp.arange(2 * head, dtype=jnp.int32) + (core * pairs + my_head // 2) * 2 * head
    bias_cols, bias_rows = [], []
    for start in (0, width):
        spot = start + pair_lane
        device = spot // (2 * rows_in)
        bias_cols.append(6 * rows_in + spot % (2 * rows_in))
        bias_rows.append((device // (2 * ny)) * 2 * ny + (device % ny) * 2 + (device // ny) % 2)
    none = jnp.full((2 * head,), -1, jnp.int32)
    table = jnp.stack([
        jnp.concatenate([lane % rows_in, rows_in + lane % rows_in, bias_cols[0], none, bias_cols[1]]),
        jnp.concatenate([in_rows_of, in_rows_of, bias_rows[0], none, bias_rows[1]]),
    ])
    mw_all, up_all, dn_all, first_low, q, k, v, out_t, top, attended, x2 = attend(
        nz, ny, own, packed, up_unit, down_weight, table
    )

    hid = jnp.arange(chips * ny * rows_hid, dtype=jnp.int32)
    feed_cols = [i * rows_in + lane % rows_in for i in (2, 3, 4, 5, 0)] + [8 * rows_in + hid % rows_hid]
    hid_rows = (hid // rows_hid) * 2 + core
    feed_table = jnp.stack([
        jnp.concatenate(feed_cols),
        jnp.concatenate([in_rows_of] * 5 + [hid_rows]),
        jnp.concatenate([natural, jnp.zeros((4 * width + hid.shape[0],), jnp.int32)]),
    ])
    activations, middle_grad, go, small, up_sums, gain, grads = feed_forward(
        nz, ny, x2, attended, cot, mw_all, up_all.reshape(width, -1), dn_all.reshape(-1, width), feed_table
    )

    stride = 320
    head_lane = jnp.arange(2 * head, dtype=jnp.int32)
    columns, owners = [], []
    for start in (0, width):
        spot = start + (core * per_core + my_head) * head + head_lane % head
        device = spot // (2 * rows_in)
        columns.append(6 * rows_in + spot % (2 * rows_in) + (head_lane // head) * stride)
        owners.append((device // (2 * ny)) * 2 * ny + (device % ny) * 2 + (device // ny) % 2)

    def wide(values):
        return jnp.pad(values, (0, hid.shape[0] - values.shape[0]))

    table = jnp.stack([wide(natural), wide(in_rows_of), hid_rows, wide(owners[0]), wide(owners[1])])
    input_grad, down_grad, up_grad, out_grad, mixing_grad, sums = back(
        nz, q, k, v, out_t, top, first_low, go, grads, middle_grad, own, gain, small, up_sums, mw_all, table,
        jnp.stack(columns, axis=1),
    )
    sums = sums.reshape(2, stride)
    small = [sums[:, i * rows_in : (i + 1) * rows_in] for i in range(6)]
    return (
        activations[:, None],
        input_grad[:, None],
        small[0],
        small[1],
        mixing_grad,
        sums[:, 6 * rows_in : 8 * rows_in],
        out_grad,
        small[4],
        small[2],
        small[3],
        up_grad,
        sums[:, 8 * rows_in : 8 * rows_in + rows_hid],
        down_grad,
        small[5],
    )


def tiles_well(mesh):
    ny, seq = mesh.shape["batch"], mesh.shape["seq"]
    rows_in = 768 // (seq * ny)
    return ny == 2 and seq // 2 >= HEADS // 2 and 2 * rows_in % 16 == 0 and 2 * rows_in * seq * ny == 2 * 768


def solution(mesh):
    shard = P(("seq", "batch"))
    grad = P(None, ("seq", "batch"))
    row = P(None, "batch", "seq", None)
    return jax.shard_map(
        on_device if tiles_well(mesh) else plain_on_device,
        mesh=mesh,
        in_specs=(P("batch", "seq", None),) + (shard,) * 12 + (row,),
        out_specs=(row, row) + (grad,) * 12,
        check_vma=False,
    )
```

```python
from functools import partial

import jax
import jax.numpy as jnp
from jax import lax
from jax.experimental import pallas as pl
from jax.experimental.pallas import tpu as pltpu
from jax.sharding import PartitionSpec as P

HEADS = 12
EPS = 1e-05
SCALES = (12.0 ** (-0.5), 48.0 ** (-0.5))
NEGATIVE = -1e30
LOW = jnp.bfloat16
FULL = jnp.float32
TILE = 256


def normalize(values):
    average = jnp.mean(values, axis=-1, keepdims=True)
    centered = values - average
    inv_std = lax.rsqrt(jnp.mean(centered * centered, axis=-1, keepdims=True) + EPS)
    return centered * inv_std, inv_std


def norm_back(gradient, normed, inv_std, gain):
    scaled = gradient * gain
    inner = (
        scaled
        - jnp.mean(scaled, axis=-1, keepdims=True)
        - normed * jnp.mean(scaled * normed, axis=-1, keepdims=True)
    )
    return inv_std * inner


def dot(a, b, dims):
    return lax.dot_general(a, b, ((dims[:1], dims[1:]), ((), ())), preferred_element_type=FULL)


class Place:
    def __init__(self):
        self.s = lax.axis_size("seq")
        self.ny = lax.axis_size("batch")
        self.nz = self.s // 4
        seq = lax.axis_index("seq")
        self.y = lax.axis_index("batch")
        self.core = lax.rem(seq, 2)
        self.chip = seq // 2
        self.x = lax.rem(self.chip, 2)
        self.z = self.chip // 2
        self.sizes = {"z": self.nz, "x": 2, "y": self.ny, "core": 2}
        self.at = {"z": self.z, "x": self.x, "y": self.y, "core": self.core}

    def send(self, values, axis, d=1):
        pairs = []
        for s in range(self.s):
            for y in range(self.ny):
                c, x, z, t = s % 2, (s // 2) % 2, s // 4, y
                if axis == "z":
                    z = (z + d) % self.nz
                elif axis == "x":
                    x = 1 - x
                elif axis == "core":
                    c = 1 - c
                else:
                    t = (y + d) % self.ny
                pairs.append((s * self.ny + y, ((z * 2 + x) * 2 + c) * self.ny + t))
        return lax.ppermute(values, ("seq", "batch"), pairs)

    def gather(self, values, axis, dim):
        size, at = self.sizes[axis], self.at[axis]
        shape = values.shape[:dim] + (size,) + values.shape[dim:]
        whole = lax.dynamic_update_slice_in_dim(
            jnp.zeros(shape, values.dtype), jnp.expand_dims(values, dim), at, dim
        )
        for d in range(1, size):
            piece = jnp.expand_dims(self.send(values, axis, d), dim)
            whole = lax.dynamic_update_slice_in_dim(whole, piece, lax.rem(at + size - d, size), dim)
        return whole

    def scatter(self, values, axis, dim):
        size, at = self.sizes[axis], self.at[axis]

        def pick(i):
            return lax.dynamic_index_in_dim(values, lax.rem(i, size), dim, keepdims=False)

        total = pick(at).astype(FULL)
        for d in range(1, size):
            total = total + self.send(pick(at + d), axis, d).astype(FULL)
        return total

    def both(self, mine, theirs):
        got = self.send(theirs, "core")
        first = self.core == 0
        return jnp.stack([jnp.where(first, mine, got), jnp.where(first, got, mine)])


def attend_plain_kernel(x_ref, gain_ref, shift_ref, w_ref, b_ref, h_ref, q_ref, k_ref, v_ref, o_ref, ot_ref, top_ref, vt_ref):
    length = x_ref.shape[0]
    head = q_ref.shape[1]
    tiles = length // TILE

    def project(i, _):
        rows = pl.ds(pl.multiple_of(i * TILE, TILE), TILE)
        normed, _ = normalize(x_ref[rows, :].astype(FULL))
        low = (normed * gain_ref[...] + shift_ref[...]).astype(LOW)
        h_ref[rows, :] = low
        mixed = dot(low, w_ref[...], (1, 0)) + b_ref[...]
        q_ref[rows, :] = (mixed[:, :head].astype(LOW) * (head ** (-0.5))).astype(LOW)
        k_ref[rows, :] = mixed[:, head : 2 * head].astype(LOW)
        value = mixed[:, 2 * head :].astype(LOW)
        v_ref[rows, :] = value
        vt_ref[:, rows] = value.T
        return 0

    lax.fori_loop(0, tiles, project, 0)

    def query_tile(i, _):
        rows = pl.ds(pl.multiple_of(i * TILE, TILE), TILE)
        query = q_ref[rows, :]

        def absorb(j, carry, masked):
            top, total, acc = carry
            keys = pl.ds(pl.multiple_of(j * TILE, TILE), TILE)
            scores = dot(k_ref[keys, :], query, (1, 1))
            if masked:
                key_pos = lax.broadcasted_iota(jnp.int32, scores.shape, 0)
                query_pos = lax.broadcasted_iota(jnp.int32, scores.shape, 1)
                scores = jnp.where(key_pos <= query_pos, scores, NEGATIVE)
            new_top = jnp.maximum(top, jnp.max(scores, axis=0, keepdims=True))
            weights = jnp.exp(scores - new_top)
            keep = jnp.exp(top - new_top)
            total = total * keep + jnp.sum(weights, axis=0, keepdims=True)
            acc = acc * keep + dot(vt_ref[:, keys], weights.astype(LOW), (1, 0))
            return new_top, total, acc

        start = (
            jnp.full((1, TILE), NEGATIVE, FULL),
            jnp.zeros((1, TILE), FULL),
            jnp.zeros((head, TILE), FULL),
        )
        carry = lax.fori_loop(0, i, lambda j, c: absorb(j, c, False), start)
        top, total, acc = absorb(i, carry, True)
        out = acc / total
        ot_ref[:, rows] = out
        o_ref[rows, :] = out.T.astype(LOW)
        top_ref[:, rows] = top + jnp.log(total)
        return 0

    lax.fori_loop(0, tiles, query_tile, 0)


def attend_plain(x_all, gain, shift, weight, bias):
    length, head = x_all.shape[0], weight.shape[1] // 3
    low = jax.ShapeDtypeStruct((length, head), LOW)
    return pl.pallas_call(
        attend_plain_kernel,
        out_shape=(
            jax.ShapeDtypeStruct(x_all.shape, LOW),
            low,
            low,
            low,
            low,
            jax.ShapeDtypeStruct((head, length), FULL),
            jax.ShapeDtypeStruct((1, length), FULL),
        ),
        scratch_shapes=[pltpu.VMEM((head, length), LOW)],
        compiler_params=pltpu.CompilerParams(vmem_limit_bytes=48 << 20),
        cost_estimate=pl.CostEstimate(
            flops=6 * length * length * head, bytes_accessed=8 * length * 768, transcendentals=length * length
        ),
        name="attend_plain",
    )(x_all, gain, shift, weight, bias)


def attend_back_kernel(
    q_ref, k_ref, v_ref, ot_ref, top_ref, go_ref, gq_ref, gk_ref, gv_ref, kt_ref, got_ref, delta_ref, gqt_ref
):
    length, head = q_ref.shape
    tiles = length // TILE
    factor = head ** (-0.5)

    def prepare(i, _):
        rows = pl.ds(pl.multiple_of(i * TILE, TILE), TILE)
        kt_ref[:, rows] = k_ref[rows, :].T
        up = go_ref[rows, :].T
        for d in range(2):
            mine = up[d * head : (d + 1) * head, :]
            got_ref[d, :, rows] = mine
            delta_ref[d, :, rows] = jnp.sum(mine.astype(FULL) * ot_ref[:, rows], axis=0, keepdims=True)
            gqt_ref[d, :, rows] = jnp.zeros((head, TILE), FULL)
        return 0

    lax.fori_loop(0, tiles, prepare, 0)

    def key_tile(j, _):
        keys = pl.ds(pl.multiple_of(j * TILE, TILE), TILE)
        key = k_ref[keys, :]
        value = v_ref[keys, :]
        key_t = kt_ref[:, keys]

        def step(i, carry, masked):
            gv, gk0, gk1 = carry
            rows = pl.ds(pl.multiple_of(i * TILE, TILE), TILE)
            query = q_ref[rows, :]
            scores = dot(key, query, (1, 1))
            if masked:
                key_pos = lax.broadcasted_iota(jnp.int32, scores.shape, 0)
                query_pos = lax.broadcasted_iota(jnp.int32, scores.shape, 1)
                scores = jnp.where(key_pos <= query_pos, scores, NEGATIVE)
            probs = jnp.exp(scores - top_ref[:, rows])
            gv = gv + dot(probs.astype(LOW), go_ref[rows, :], (1, 0))
            gks = [gk0, gk1]
            for d in range(2):
                prob_grad = dot(value, got_ref[d, :, rows], (1, 0))
                score_low = (probs * (prob_grad - delta_ref[d, :, rows])).astype(LOW)
                gks[d] = gks[d] + dot(score_low, query, (1, 0))
                gqt_ref[d, :, rows] += dot(key_t, score_low, (1, 0))
            return gv, gks[0], gks[1]

        zero = jnp.zeros((TILE, head), FULL)
        carry = step(j, (jnp.zeros((TILE, 2 * head), FULL), zero, zero), True)
        gv, gk0, gk1 = lax.fori_loop(j + 1, tiles, lambda i, c: step(i, c, False), carry)
        gv_ref[keys, :] = gv.astype(LOW)
        gk_ref[keys, :] = jnp.concatenate([gk0, gk1], axis=1).astype(LOW)
        return 0

    lax.fori_loop(0, tiles, key_tile, 0)

    def finish(i, _):
        rows = pl.ds(pl.multiple_of(i * TILE, TILE), TILE)
        both = jnp.concatenate([gqt_ref[0, :, rows], gqt_ref[1, :, rows]], axis=0) * factor
        gq_ref[rows, :] = both.T.astype(LOW)
        return 0

    lax.fori_loop(0, tiles, finish, 0)


def attend_back(q, k, v, out_t, top, go):
    length, head = q.shape
    pair = jax.ShapeDtypeStruct((length, 2 * head), LOW)
    return pl.pallas_call(
        attend_back_kernel,
        out_shape=(pair, pair, pair),
        scratch_shapes=[
            pltpu.VMEM((head, length), LOW),
            pltpu.VMEM((2, head, length), LOW),
            pltpu.VMEM((2, 1, length), FULL),
            pltpu.VMEM((2, head, length), FULL),
        ],
        compiler_params=pltpu.CompilerParams(vmem_limit_bytes=48 << 20),
        cost_estimate=pl.CostEstimate(
            flops=20 * length * length * head, bytes_accessed=16 * length * head, transcendentals=length * length
        ),
        name="attend_back",
    )(q, k, v, out_t, top, go)


MESH = pl.DeviceIdType.MESH
DMA = pltpu.SemaphoreType.DMA


class Here:
    def __init__(self, nz, ny):
        self.nz, self.ny = nz, ny
        seq = lax.axis_index("seq")
        self.y = lax.axis_index("batch")
        self.core = lax.rem(seq, 2)
        self.chip = lax.div(seq, 2)
        self.x = lax.rem(self.chip, 2)
        self.z = lax.div(self.chip, 2)

    def device(self, z=None, x=None, core=None, y=None):
        z = self.z if z is None else z
        x = self.x if x is None else x
        core = self.core if core is None else core
        y = self.y if y is None else y
        return ((z * 2 + x) * 2 + core, y)

    def before(self, d):
        return lax.rem(self.z + self.nz - d, self.nz)

    def after(self, d):
        return lax.rem(self.z + d, self.nz)


def remote(src, dst, send, recv, device):
    return pltpu.make_async_remote_copy(
        src_ref=src, dst_ref=dst, send_sem=send, recv_sem=recv, device_id=device, device_id_type=MESH
    )


class Gather:
    def __init__(self, here, own, whole, x_first, sems):
        self.here, self.own, self.whole, self.x_first = here, own, whole, x_first
        self.zs, self.zr, self.as_, self.ar, self.bs, self.br, self.local = sems
        self.kept = pltpu.make_async_copy(own, whole.at[here.z, here.x, here.y], self.local)

    @staticmethod
    def scratch(nz, ny):
        return [DMA((2, nz)), DMA((nz,)), DMA((nz, ny)), DMA((nz, ny)), DMA((nz, 2, ny)), DMA((nz, 2, ny)), DMA]

    def _along(self, source, up, own=False):
        h = self.here
        spot = self.whole.at[source, h.x, h.y]
        to = h.device(z=lax.min(h.z + 1, h.nz - 1)) if up else h.device(z=lax.max(h.z - 1, 0))
        src = self.own if own else spot
        return remote(src, spot, self.zs.at[0 if up else 1, source], self.zr.at[source], to)

    def _to_x(self, source, y, out, own=False):
        h = self.here
        spot = self.whole.at[source, h.x if out else 1 - h.x, y]
        s, r = (self.as_, self.ar) if self.x_first else (self.bs, self.br)
        i = (source, 0) if self.x_first else (source, 0, y)
        return remote(self.own if own else spot, spot, s.at[i], r.at[i], h.device(x=1 - h.x))

    def _to_y(self, source, x, e, out, own=False):
        h = self.here
        spot = self.whole.at[source, x, h.y if out else lax.rem(h.y + h.ny - e, h.ny)]
        s, r = (self.bs, self.br) if self.x_first else (self.as_, self.ar)
        i = (source, x, e) if self.x_first else (source, e)
        return remote(self.own if own else spot, spot, s.at[i], r.at[i], h.device(y=lax.rem(h.y + e, h.ny)))

    def start_z(self):
        h = self.here
        pl.when(h.z < h.nz - 1)(self._along(h.z, True, True).start)
        pl.when(h.z > 0)(self._along(h.z, False, True).start)

    def take_z(self, source, up):
        h = self.here
        self._along(source, up).wait_recv()
        pl.when(h.z < h.nz - 1 if up else h.z > 0)(self._along(source, up).start)

    def spread(self, source, own):
        h = self.here
        if self.x_first:
            self._to_x(source, h.y, True, own).start()
            for e in range(1, h.ny):
                self._to_y(source, h.x, e, True, own).start()
        else:
            for e in range(1, h.ny):
                self._to_y(source, h.x, e, True, own).start()
            self._to_x(source, h.y, True, own).start()

    def second(self, source):
        h = self.here
        if self.x_first:
            self._to_x(source, h.y, False).wait_recv()
            for e in range(1, h.ny):
                self._to_y(source, 1 - h.x, e, True).start()
        else:
            for e in range(1, h.ny):
                self._to_y(source, h.x, e, False).wait_recv()
                self._to_x(source, lax.rem(h.y + h.ny - e, h.ny), True).start()

    def third(self, source):
        h = self.here
        if self.x_first:
            for e in range(1, h.ny):
                self._to_y(source, h.x, e, False).wait_recv()
                self._to_y(source, 1 - h.x, e, False).wait_recv()
        else:
            for y in range(h.ny):
                self._to_x(source, y, False).wait_recv()

    def finish(self):
        h = self.here
        for source in range(h.nz):
            pl.when(jnp.logical_and(source <= h.z, h.z < h.nz - 1))(self._along(source, True).wait_send)
            pl.when(jnp.logical_and(source >= h.z, h.z > 0))(self._along(source, False).wait_send)
            if self.x_first:
                self._to_x(source, h.y, True).wait_send()
                for e in range(1, h.ny):
                    for x in range(2):
                        self._to_y(source, x, e, True).wait_send()
            else:
                for e in range(1, h.ny):
                    self._to_y(source, h.x, e, True).wait_send()
                for y in range(h.ny):
                    self._to_x(source, y, True).wait_send()


class GatherRows:
    def __init__(self, here, own, whole, sems):
        self.here, self.own, self.whole = here, own, whole
        self.zs, self.zr, self.xs, self.xr, self.cs, self.cr, self.local = sems
        self.kept = pltpu.make_async_copy(own, whole.at[here.z, here.x, here.core], self.local)

    @staticmethod
    def scratch(nz):
        return [DMA((2, nz)), DMA((nz,)), DMA((nz,)), DMA((nz,)), DMA((nz, 2)), DMA((nz, 2)), DMA]

    def _along(self, source, up, own=False):
        h = self.here
        spot = self.whole.at[source, h.x, h.core]
        to = h.device(z=lax.min(h.z + 1, h.nz - 1)) if up else h.device(z=lax.max(h.z - 1, 0))
        src = self.own if own else spot
        return remote(src, spot, self.zs.at[0 if up else 1, source], self.zr.at[source], to)

    def _to_x(self, source, out, own=False):
        h = self.here
        spot = self.whole.at[source, h.x if out else 1 - h.x, h.core]
        return remote(self.own if own else spot, spot, self.xs.at[source], self.xr.at[source], h.device(x=1 - h.x))

    def _to_core(self, source, x, out, own=False):
        h = self.here
        spot = self.whole.at[source, x, h.core if out else 1 - h.core]
        return remote(self.own if own else spot, spot, self.cs.at[source, x], self.cr.at[source, x], h.device(core=1 - h.core))

    start_z = Gather.start_z
    take_z = Gather.take_z

    def spread(self, source, own):
        self._to_x(source, True, own).start()
        self._to_core(source, self.here.x, True, own).start()

    def second(self, source):
        self._to_x(source, False).wait_recv()
        self._to_core(source, 1 - self.here.x, True).start()

    def third(self, source):
        for x in range(2):
            self._to_core(source, x, False).wait_recv()

    def finish(self):
        h = self.here
        for source in range(h.nz):
            pl.when(jnp.logical_and(source <= h.z, h.z < h.nz - 1))(self._along(source, True).wait_send)
            pl.when(jnp.logical_and(source >= h.z, h.z > 0))(self._along(source, False).wait_send)
            self._to_x(source, True).wait_send()
            for x in range(2):
                self._to_core(source, x, True).wait_send()


def at_distance(here, k, act):
    if k == 0:
        act(here.z, None)
    else:
        pl.when(here.z >= k)(lambda: act(here.z - k, True))
        pl.when(here.z + k < here.nz)(lambda: act(here.z + k, False))


def greet(devices):
    barrier = pltpu.get_barrier_semaphore()
    for device in devices:
        pl.semaphore_signal(barrier, inc=1, device_id=device, device_id_type=MESH)
    pl.semaphore_wait(barrier, len(devices))


def owner_of(chips):
    per_core = HEADS // 2
    return [int((j + 0.5) * chips / per_core) for j in range(per_core)]


def head_here(chip, slots):
    mine, has = jnp.int32(0), jnp.int32(0)
    for j, slot in enumerate(slots):
        same = (chip == slot).astype(jnp.int32)
        mine = mine + j * same
        has = has + same
    return mine, has


def attend_kernel(
    nz, ny, x_ref, mw_ref, up_ref, dn_ref, table_ref,
    mw_all, up_all, dn_all, h_ref, q_ref, k_ref, v_ref, ot_ref, top_ref, att_ref, x2_ref,
    xs, wt, vc, vt_ref, o_ref, load, att_s, att_r, pass_s, pass_r, *sems,
):
    here = Here(nz, ny)
    chips = 2 * nz
    slots = owner_of(chips)
    head = q_ref.shape[1]
    width = x_ref.shape[1]
    tile = 2 * x_ref.shape[0]
    mine, has = head_here(here.chip, slots)
    odd = lax.rem(mine, 2) == 1
    rows_sems, mw_sems, up_sems, dn_sems = sems[:7], sems[7:14], sems[14:21], sems[21:28]

    peers = [here.device(z=here.after(d)) for d in range(1, nz)]
    peers += [here.device(x=1 - here.x), here.device(core=1 - here.core)]
    peers += [here.device(z=here.after(d), x=1 - here.x) for d in range(1, nz)]
    peers += [here.device(y=lax.rem(here.y + e, ny)) for e in range(1, ny)]
    rows = GatherRows(here, x_ref, xs, rows_sems)
    mw = Gather(here, mw_ref, mw_all, True, mw_sems)
    up = Gather(here, up_ref, up_all, True, up_sems)
    dn = Gather(here, dn_ref, dn_all, False, dn_sems)
    first, later = (rows, mw), (up, dn)
    for item in first + later:
        item.kept.start()
    greet(peers)

    def take(items, k):
        def act(source, way):
            for item in items:
                if k:
                    item.take_z(source, way)
            for item in items:
                item.spread(source, k == 0)

        at_distance(here, k, act)

    def then(items, k, stage):
        def act(source, _):
            for item in items:
                getattr(item, stage)(source)

        at_distance(here, k, act)

    for item in first:
        item.start_z()
    take(first, 0)
    for k in range(1, nz):
        take(first, k)
        then(first, k - 1, "second")
    for item in later:
        item.start_z()
    then(first, nz - 1, "second")
    take(later, 0)
    for k in range(nz):
        then((mw,), k, "third")
    mw.kept.wait()
    pair = pltpu.make_async_copy(mw_all.at[:, :, :, lax.div(mine, 2)], wt, load.at[0])
    pair.start()
    vectors = pltpu.make_async_copy(mw_all.at[:, :, :, 4], vc, load.at[1])
    vectors.start()
    for k in range(nz):
        then((rows,), k, "third")
    rows.kept.wait()
    pair.wait()
    vectors.wait()
    keep_rows = pltpu.make_async_copy(xs.at[here.z, here.x], x2_ref, load.at[2])
    keep_rows.start()

    steps = []
    for k in range(1, nz):
        steps += [partial(take, later, k), partial(then, later, k - 1, "second")]
    steps += [partial(then, later, nz - 1, "second")] + [partial(then, later, k, "third") for k in range(nz)]

    @pl.when(has == 1)
    def _():
        pieces = vc[...].reshape(-1, vc.shape[-1])
        count = 2 * chips * ny
        unit = pieces.shape[0] // count
        pick_row = lax.broadcasted_iota(jnp.int32, (count, pieces.shape[0]), 0) * unit
        pick = (pick_row == lax.broadcasted_iota(jnp.int32, pick_row.shape, 1)).astype(LOW)
        pieces = dot(pick, pieces, (1, 0)).astype(LOW)
        cols, owners = table_ref[0:1, :], table_ref[1:2, :]
        spot = lax.broadcasted_iota(jnp.int32, (pieces.shape[1], cols.shape[1]), 0)
        moved = dot(pieces, (spot == cols).astype(LOW), (1, 0))
        from_row = lax.broadcasted_iota(jnp.int32, moved.shape, 0)
        flat = jnp.sum(jnp.where(from_row == owners, moved, 0.0), axis=0, keepdims=True)
        gain, shift, bias = flat[:, :width], flat[:, width : 2 * width], flat[:, 2 * width :]
        weight = wt[...].reshape(width, -1)

        def choose(values):
            return jnp.where(odd, values[:, head:], values[:, :head])

        for i in range(chips):
            span = slice(i * tile, (i + 1) * tile)
            values = xs[i // 2, i % 2].reshape(tile, width).astype(FULL)
            normed, _ = normalize(values)
            low = (normed * gain + shift).astype(LOW)
            h_ref[span, :] = low
            mixed = (dot(low, weight, (1, 0)) + bias).astype(LOW)
            q_ref[span, :] = (choose(mixed[:, : 2 * head]) * (head ** (-0.5))).astype(LOW)
            k_ref[span, :] = choose(mixed[:, 2 * head : 4 * head])
            value = choose(mixed[:, 4 * head :])
            v_ref[span, :] = value
            vt_ref[:, span] = value.T

    def query_tile(i):
        span = slice(i * tile, (i + 1) * tile)
        query = q_ref[span, :]

        def absorb(j, carry, masked):
            top, total, acc = carry
            keys = slice(j * tile, (j + 1) * tile)
            scores = dot(k_ref[keys, :], query, (1, 1))
            if masked:
                key_pos = lax.broadcasted_iota(jnp.int32, scores.shape, 0)
                query_pos = lax.broadcasted_iota(jnp.int32, scores.shape, 1)
                scores = jnp.where(key_pos <= query_pos, scores, NEGATIVE)
            new_top = jnp.maximum(top, jnp.max(scores, axis=0, keepdims=True))
            weights = jnp.exp(scores - new_top)
            keep = jnp.exp(top - new_top)
            total = total * keep + jnp.sum(weights, axis=0, keepdims=True)
            acc = acc * keep + dot(vt_ref[:, keys], weights.astype(LOW), (1, 0))
            return new_top, total, acc

        carry = (jnp.full((1, tile), NEGATIVE, FULL), jnp.zeros((1, tile), FULL), jnp.zeros((head, tile), FULL))
        for j in range(i + 1):
            carry = absorb(j, carry, j == i)
        top, total, acc = carry
        out = acc / total
        ot_ref[:, span] = out
        o_ref[i] = out.T.astype(LOW)
        top_ref[:, span] = top + jnp.log(total)

    def hand(i):
        spot = att_ref.at[here.core, mine]
        return (
            pltpu.make_async_copy(o_ref.at[i], spot, att_s.at[i]),
            remote(o_ref.at[i], spot, att_s.at[i], att_r.at[mine], here.device(z=i // 2, x=i % 2)),
        )

    for i in range(chips):
        @pl.when(has == 1)
        def _(i=i):
            query_tile(i)
            stay, leave = hand(i)
            pl.when(here.chip == i)(stay.start)
            pl.when(here.chip != i)(leave.start)

        if i < len(steps):
            steps[i]()
    for step in steps[chips:]:
        step()

    for i in range(chips):
        @pl.when(has == 1)
        def _(i=i):
            stay, leave = hand(i)
            pl.when(here.chip == i)(stay.wait)
            pl.when(here.chip != i)(leave.wait_send)

    for j, slot in enumerate(slots):
        @pl.when(here.chip != slot)
        def _(j=j, slot=slot):
            spot = att_ref.at[here.core, j]
            remote(spot, spot, att_s.at[0], att_r.at[j], here.device(z=slot // 2, x=slot % 2)).wait_recv()

    spot = att_ref.at[here.core]
    give = remote(spot, spot, pass_s, pass_r, here.device(core=1 - here.core))
    give.start()
    spot = att_ref.at[1 - here.core]
    remote(spot, spot, pass_s, pass_r, here.device(core=1 - here.core)).wait_recv()
    give.wait_send()
    keep_rows.wait()
    for item in later:
        item.kept.wait()
    for item in first + later:
        item.finish()


def attend(nz, ny, own, mw, up, dn, table):
    span, width = own.shape
    length = 4 * nz * span
    head = width // HEADS
    units = (nz, 2, ny)
    low = jax.ShapeDtypeStruct((length, head), LOW)
    anywhere = pl.BlockSpec(memory_space=pl.ANY)
    vmem = pl.BlockSpec(memory_space=pltpu.VMEM)
    return pl.pallas_call(
        partial(attend_kernel, nz, ny),
        out_shape=(
            jax.ShapeDtypeStruct(units + mw.shape, LOW),
            jax.ShapeDtypeStruct(units + up.shape, LOW),
            jax.ShapeDtypeStruct(units + dn.shape, LOW),
            jax.ShapeDtypeStruct((length, width), LOW),
            low,
            low,
            low,
            jax.ShapeDtypeStruct((head, length), FULL),
            jax.ShapeDtypeStruct((1, length), FULL),
            jax.ShapeDtypeStruct((2, HEADS // 2, 2 * span, head), LOW),
            jax.ShapeDtypeStruct((2, span, width), LOW),
        ),
        in_specs=[anywhere] * 4 + [vmem],
        out_specs=[anywhere] * 3 + [vmem] * 6 + [anywhere] * 2,
        scratch_shapes=[
            pltpu.VMEM((nz, 2, 2, span, width), LOW),
            pltpu.VMEM(units + mw.shape[1:], LOW),
            pltpu.VMEM(units + mw.shape[1:], LOW),
            pltpu.VMEM((head, length), LOW),
            pltpu.VMEM((2 * nz, 2 * span, head), LOW),
            DMA((3,)),
            DMA((2 * nz,)),
            DMA((HEADS // 2,)),
            DMA,
            DMA,
        ]
        + GatherRows.scratch(nz)
        + Gather.scratch(nz, ny) * 3,
        compiler_params=pltpu.CompilerParams(vmem_limit_bytes=56 << 20, collective_id=0, has_side_effects=True),
        cost_estimate=pl.CostEstimate(
            flops=6 * length * length * head, bytes_accessed=8 * length * width, transcendentals=length * length
        ),
        name="attend",
    )(own, mw, up, dn, table)


GELU_K = 0.7978845608028654
GELU_C = 0.044715


def gelu_pair(u):
    square = u * u
    tanh = jnp.tanh(GELU_K * u * (1.0 + GELU_C * square))
    half = 0.5 * (1.0 + tanh)
    slope = half + (0.5 * GELU_K) * u * (1.0 - tanh * tanh) * (1.0 + 3.0 * GELU_C * square)
    return u * half, slope


def split_dot(values, turn, dims):
    high = values.astype(LOW)
    rest = values - high.astype(FULL)
    middle = rest.astype(LOW)
    low = (rest - middle.astype(FULL)).astype(LOW)
    return dot(high, turn, dims) + dot(middle, turn, dims) + dot(low, turn, dims)


def rest_kernel(
    nz, hidden_tile,
    x2_ref, att_ref, cot_ref, mw_all, up_ref, dn_ref, table_ref,
    q_ref, k_ref, v_ref, ot_ref, top_ref, h_all, x_ref, spot_ref, bias_ref,
    act_ref, ing_ref, gdn_ref, gup_ref, gout_ref, mix_ref, vec_ref,
    up, dn, ow, own, pm, vc, att, cot, h2, act_low, gu, branch, feed, feed_in, gh2, gh2_in, gmid, eb, grads, go_send,
    go_all, kt_ref, got_ref, delta_ref, gqt_ref, gsend, gat, mw, hbuf, head_acc, head_sum, hs_in, mix_in, mixf, mix_swap,
    r1, r2, r3, fin, swap, pack, vec_in,
    load, near_s, near_r, h_s, go_s, go_r, kv_s, kv_r, q_s, q_r, s1, t1, s2, t2, s3, t3, ex_s, ex_r,
    vec_s, vec_r, mix_s, mix_r,
):
    ny = 2
    here = Here(nz, ny)
    core, chip, x, y, z = here.core, here.chip, here.x, here.y, here.z
    chips = 2 * nz
    parts = 4 * nz * ny
    slots = owner_of(chips)
    per_core = len(slots)
    length, head = q_ref.shape
    tile = length // chips
    span, width = x_ref.shape
    half = width // 2
    hidden = up_ref.shape[1]
    rows_hid = 2 * hidden // parts
    factor = head ** (-0.5)
    job, has = head_here(chip, slots)
    partner = here.device(core=1 - core)
    slabs, unit = grads.shape[4], grads.shape[5]
    rows_in = unit // 2
    my_rows = pl.ds(pl.multiple_of(core * span, span), span)
    their_rows = pl.ds(pl.multiple_of((1 - core) * span, span), span)

    def flat(zz, xx, yy, cc):
        return ((zz * 2 + xx) * ny + yy) * 2 + cc

    others = []
    for dz in range(nz):
        for dx in range(2):
            for dy in range(ny):
                for dc in range(2):
                    if dz or dx or dy or dc:
                        zz = lax.rem(z + dz, nz)
                        xx = 1 - x if dx else x
                        yy = 1 - y if dy else y
                        cc = 1 - core if dc else core
                        behind = (lax.rem(z + nz - dz, nz), xx, yy, cc)
                        others.append((here.device(zz, xx, cc, yy), flat(zz, xx, yy, cc), flat(*behind)))

    loads = [
        pltpu.make_async_copy(mw_all.at[:, :, :, 3], ow.at[core], load.at[0]),
        pltpu.make_async_copy(mw_all.at[:, :, :, 4], vc, load.at[1]),
        pltpu.make_async_copy(up_ref, up, load.at[2]),
        pltpu.make_async_copy(dn_ref, dn, load.at[3]),
        pltpu.make_async_copy(cot_ref, cot.at[:, my_rows], load.at[4]),
        pltpu.make_async_copy(mw_all.at[:, :, :, 0:3], mw, load.at[5]),
    ]
    for copy in loads:
        copy.start()
    greet([device for device, _, _ in others])

    def pass_on(i, src, dst):
        return remote(src, dst, near_s.at[i], near_r.at[i], partner)

    give_cot = pass_on(0, cot_ref, cot.at[:, my_rows])
    give_cot.start()
    loads[0].wait()
    give_ow = pass_on(1, ow.at[core], ow.at[core])
    give_ow.start()

    cols, owners, natural = table_ref[0:1, :], table_ref[1:2, :], table_ref[2:3, :width]
    from_row = lax.broadcasted_iota(jnp.int32, (width, width), 0)
    pm[...] = (from_row == natural).astype(LOW)
    loads[1].wait()
    pieces = vc[...].reshape(-1, vc.shape[-1])
    pick_row = lax.broadcasted_iota(jnp.int32, (parts, pieces.shape[0]), 0) * rows_in
    pick = (pick_row == lax.broadcasted_iota(jnp.int32, pick_row.shape, 1)).astype(LOW)
    pieces = dot(pick, pieces, (1, 0)).astype(LOW)
    spot = lax.broadcasted_iota(jnp.int32, (pieces.shape[1], cols.shape[1]), 0)
    moved = dot(pieces, (spot == cols).astype(LOW), (1, 0))
    piece_row = lax.broadcasted_iota(jnp.int32, moved.shape, 0)
    vectors = jnp.sum(jnp.where(piece_row == owners, moved, 0.0), axis=0, keepdims=True)
    gain, shift, out_bias, down_bias, first_gain = (vectors[:, i * width : (i + 1) * width] for i in range(5))
    up_bias = vectors[:, 5 * width :]

    natural_att = jnp.concatenate([att_ref[c, j] for c in range(2) for j in range(per_core)], axis=1)
    att[...] = dot(natural_att, pm[...], (1, 0)).astype(LOW)
    remote(ow.at[1 - core], ow.at[1 - core], near_s.at[1], near_r.at[1], partner).wait_recv()
    for c in range(2):
        own[:, c * half : (c + 1) * half] = dot(pm[...], ow[c].reshape(width, half), (1, 0)).astype(LOW)
    branch[...] = dot(natural_att, own[...], (1, 0)) + out_bias

    def middle_of(d, rows):
        return x2_ref[rows, :].astype(FULL) + SCALES[d] * branch[rows, :]

    for d in range(2):
        n, _ = normalize(middle_of(d, slice(None)))
        h2[d] = (n * gain + shift).astype(LOW)
    loads[4].wait()
    theirs_cot = cot.at[:, their_rows]
    remote(theirs_cot, theirs_cot, near_s.at[0], near_r.at[0], partner).wait_recv()
    loads[2].wait()
    loads[3].wait()

    def upstream(d):
        return (SCALES[d] * cot[d].astype(FULL)).astype(LOW)

    stride = pack.shape[1] * pack.shape[2] // 2
    lane = lax.broadcasted_iota(jnp.int32, (width, 128), 0)
    in_piece = (lax.rem(lane, rows_in) == lax.broadcasted_iota(jnp.int32, lane.shape, 1)).astype(LOW)
    wide_owner = spot_ref[1:2, :width]

    def placed(vector, owner, turn, start):
        rows = lax.broadcasted_iota(jnp.int32, (parts, vector.shape[1]), 0)
        spread = jnp.where(rows == owner, vector, 0.0)
        high = spread.astype(LOW)
        low = (spread - high.astype(FULL)).astype(LOW)
        values = dot(high, turn, (1, 0)) + dot(low, turn, (1, 0))
        return jnp.pad(values, ((0, 0), (start, 2 * stride)))[:, : 2 * stride]

    sums = {}

    def row_sum(v, d, values):
        sums[v, d] = jnp.sum(values, axis=0, keepdims=True)

    exchanges = []

    def forth_and_back(d):
        low_in = upstream(d)
        ups = []
        for t in range(0, hidden, hidden_tile):
            cut = slice(t, t + hidden_tile)
            u = dot(h2[d], up[:, cut], (1, 0)) + up_bias[:, cut]
            active, slope = gelu_pair(u)
            active = active.astype(LOW)
            act_low[d, :, cut] = active
            grad = (dot(low_in, dn[cut, :], (1, 1)) * slope).astype(LOW)
            gu[d, :, cut] = grad
            ups.append(jnp.sum(grad.astype(FULL), axis=0, keepdims=True))
            part = dot(grad, up[:, cut], (1, 1))
            feed_part = dot(active, dn[cut, :], (1, 0))
            if t == 0:
                gh2[d] = part
                feed[d] = feed_part
            else:
                gh2[d] += part
                feed[d] += feed_part
        sums["up", d] = jnp.concatenate(ups, axis=1)
        for i, (src, dst) in ((2, (gh2, gh2_in)), (4, (feed, feed_in))):
            copy = pass_on(i + d, src.at[d, their_rows], dst.at[d])
            copy.start()
            exchanges.append(copy)

    def keep(d, values, first_row, first_col, base, rows_of):
        for i in range(0, values.shape[0], unit):
            row = first_row + i
            u, within = row // rows_of, (row % rows_of) // unit
            place = (u // (2 * ny), (u // ny) % 2, u % ny)
            for c in range(0, values.shape[1], half):
                slab = base + within * 2 + (first_col + c) // half
                grads[(d,) + place + (slab,)] = values[i : i + unit, c : c + half]

    def hidden_grads(d):
        low_in = upstream(d)
        for t in range(0, hidden, half):
            keep(d, dot(act_low[d, :, t : t + half], low_in, (0, 0)).astype(LOW), t, 0, 0, 2 * unit)
        for t in range(0, hidden, 2 * half):
            for m in range(0, width, half):
                part = dot(h2[d, :, m : m + half], gu[d, :, t : t + 2 * half], (0, 0)).astype(LOW)
                keep(d, part, m, t, 4, unit)

    def norm_feed_back(d):
        remote(gh2_in.at[d], gh2_in.at[d], near_s.at[2 + d], near_r.at[2 + d], partner).wait_recv()
        grad = gh2[d, my_rows, :] + gh2_in[d]
        n, r = normalize(middle_of(d, my_rows))
        row_sum(2, d, grad * n)
        row_sum(3, d, grad)
        own_cot = cot[d, my_rows, :].astype(FULL)
        middle_grad = own_cot + norm_back(grad, n, r, gain)
        gmid[d] = middle_grad
        branch_low = (SCALES[d] * middle_grad).astype(LOW)
        row_sum(4, d, branch_low.astype(FULL))
        row_sum(5, d, (SCALES[d] * own_cot).astype(LOW).astype(FULL))
        eb[d, my_rows, :] = branch_low
        copy = pass_on(6 + d, eb.at[d, my_rows], eb.at[d, my_rows])
        copy.start()
        exchanges.append(copy)

    zis = []
    for i in range((nz + 1) // 2):
        zis += [nz - 1 - i] + ([i] if i != nz - 1 - i else [])
    cuts = [(0, slabs // 2), (slabs // 2, slabs)]
    chunks = [(zi, part) for part in range(len(cuts)) for zi in zis]

    def a1(d):
        return here.device(y=1 - y) if d == 0 else here.device(x=1 - x)

    def a2(d):
        return here.device(x=1 - x) if d == 0 else here.device(y=1 - y)

    def at2(d):
        return x if d == 0 else y

    def mine(d, zi, i, slab):
        return grads.at[0, zi, i, y, slab] if d == 0 else grads.at[1, zi, x, i, slab]

    def some(part):
        return pl.ds(cuts[part][0], cuts[part][1] - cuts[part][0])

    def stage1(d, zi, part):
        slab = some(part)
        src = grads.at[0, zi, :, 1 - y, slab] if d == 0 else grads.at[1, zi, 1 - x, :, slab]
        return remote(src, r1.at[d, zi, :, slab], s1.at[d, zi, part], t1.at[d, zi, part], a1(d))

    def stage2(d, zi, part):
        slab = some(part)
        src = mine(d, zi, 1 - at2(d), slab)
        return remote(src, r2.at[d, zi, slab], s2.at[d, zi, part], t2.at[d, zi, part], a2(d))

    def spare(zi, up):
        return zi if up else jnp.where(z - 1 == zi, nz, zi)

    def stage3(d, zi, part, up):
        to = here.device(z=lax.min(z + 1, nz - 1)) if up else here.device(z=lax.max(z - 1, 0))
        way = 0 if up else 1
        slab = some(part)
        src, dst = r2.at[d, zi, slab], r3.at[d, spare(zi, up), slab]
        return remote(src, dst, s3.at[d, zi, part], t3.at[d, way, zi, part], to)

    def arrive3(d, zi, part, up):
        way = 0 if up else 1
        spot = r3.at[d, zi, some(part)]
        return remote(spot, spot, s3.at[d, zi, part], t3.at[d, way, zi, part], partner)

    def begin(d, n):
        if n < len(chunks):
            stage1(d, *chunks[n]).start()

    def add_into(target, other, lead):
        def one(i, _):
            a, b = target(i), other(i)
            a[...] = (a[...].astype(FULL) + b[...].astype(FULL)).astype(LOW)
            return 0

        lax.fori_loop(0, lead, one, 0)

    def after1(d, zi, part):
        stage1(d, zi, part).wait_recv()
        low, high = cuts[part]
        size = high - low
        add_into(
            lambda i: mine(d, zi, lax.div(i, size), low + lax.rem(i, size)),
            lambda i: r1.at[d, zi, lax.div(i, size), low + lax.rem(i, size)],
            2 * size,
        )
        stage2(d, zi, part).start()

    def after2(d, zi, part):
        low, high = cuts[part]
        stage2(d, zi, part).wait_recv()
        add_into(lambda i: r2.at[d, zi, low + i], lambda i: mine(d, zi, at2(d), low + i), high - low)
        if zi > 0:
            pl.when(z == 0)(stage3(d, zi, part, True).start)
        if zi < nz - 1:
            pl.when(z == nz - 1)(stage3(d, zi, part, False).start)

    def after3(d, zi, part, far):
        low, high = cuts[part]
        if far < zi:
            @pl.when(z == far)
            def _():
                arrive3(d, zi, part, True).wait_recv()
                add_into(lambda i: r2.at[d, zi, low + i], lambda i: r3.at[d, zi, low + i], high - low)
                stage3(d, zi, part, True).start()

        if nz - 1 - far > zi:
            @pl.when(z == nz - 1 - far)
            def _():
                arrive3(d, zi, part, False).wait_recv()
                add_into(lambda i: r2.at[d, zi, low + i], lambda i: r3.at[d, zi, low + i], high - low)
                stage3(d, zi, part, False).start()

    def last3(d, zi, part):
        low, high = cuts[part]

        @pl.when(z == zi)
        def _():
            if zi > 0:
                arrive3(d, zi, part, True).wait_recv()
            if zi < nz - 1:
                arrive3(d, zi, part, False).wait_recv()

            def one(i, _):
                total = r2[d, zi, i].astype(FULL)
                if zi > 0:
                    total = total + r3[d, zi, i].astype(FULL)
                if zi < nz - 1:
                    total = total + r3[d, nz, i].astype(FULL)
                fin[d, i] = total
                return 0

            lax.fori_loop(low, high, one, 0)

    def advance(n):
        for d in range(2):
            begin(d, n + 2)
        stages = [after1, after2] + [partial(after3, far=far) for far in range(1, nz - 1)] + [last3]
        for behind, stage in enumerate(stages):
            if 0 <= n - behind < len(chunks):
                for d in range(2):
                    stage(d, *chunks[n - behind])

    steps = len(chunks) + nz

    def finish_sends():
        for zi, part in chunks:
            for d in range(2):
                stage1(d, zi, part).wait_send()
                stage2(d, zi, part).wait_send()
                pl.when(z != zi)(stage3(d, zi, part, True).wait_send)

    forth_and_back(0)
    hidden_grads(0)
    begin(0, 0)
    begin(0, 1)
    forth_and_back(1)
    norm_feed_back(0)
    hidden_grads(1)
    begin(1, 0)
    begin(1, 1)
    norm_feed_back(1)

    def go_copies(j):
        slot = slots[j]
        return (
            pltpu.make_async_copy(go_send.at[j], go_all.at[chip], go_s.at[j]),
            remote(go_send.at[j], go_all.at[chip], go_s.at[j], go_r.at[chip], here.device(z=slot // 2, x=slot % 2)),
        )

    own_half = own.at[pl.ds(pl.multiple_of(core * half, half), half), :]
    for d in range(2):
        spot = eb.at[d, their_rows]
        remote(spot, spot, near_s.at[6 + d], near_r.at[6 + d], partner).wait_recv()
        go = dot(eb[d], own_half[...], (1, 1)).astype(LOW)
        for j in range(per_core):
            go_send[j, :, d * head : (d + 1) * head] = go[:, j * head : (j + 1) * head]
    for j, slot in enumerate(slots):
        stay, leave = go_copies(j)
        pl.when(chip == slot)(stay.start)
        pl.when(chip != slot)(leave.start)
    for d in range(2):
        ours = eb[d, :, pl.ds(pl.multiple_of(core * half, half), half)]
        for m in range(0, width, half):
            keep(d, dot(att[:, m : m + half], ours, (0, 0)).astype(LOW), m, 0, 8, unit)

    for d in range(2):
        remote(feed_in.at[d], feed_in.at[d], near_s.at[4 + d], near_r.at[4 + d], partner).wait_recv()
        out = middle_of(d, my_rows) + SCALES[d] * (feed[d, my_rows, :] + feed_in[d] + down_bias)
        act_ref[d] = dot(out.astype(LOW), pm[...], (1, 1)).astype(LOW)
    total = jnp.zeros((parts, 2 * stride), FULL)
    for v in range(2, 6):
        for d in range(2):
            total = total + placed(sums[v, d], wide_owner, in_piece, v * rows_in + d * stride)
    hid_lane = lax.broadcasted_iota(jnp.int32, (hidden, 128), 0)
    in_hidden = (lax.rem(hid_lane, rows_hid) == lax.broadcasted_iota(jnp.int32, hid_lane.shape, 1)).astype(LOW)
    for d in range(2):
        total = total + placed(sums["up", d], spot_ref[2:3, :hidden], in_hidden, 8 * rows_in + d * stride)
    for c in range(pack.shape[1]):
        pack[:, c, :] = total[:, c * 128 : (c + 1) * 128]
    advance(0)

    def h_copy(i):
        rows = slice(i * tile, (i + 1) * tile)
        return pltpu.make_async_copy(h_all.at[rows], hbuf.at[i % 2], h_s.at[i % 2])

    @pl.when(has == 1)
    def _():
        h_copy(0).start()
        h_copy(1).start()
        for t in range(chips):
            stay = pltpu.make_async_copy(go_send.at[0], go_all.at[t], go_s.at[job])
            come = remote(go_send.at[0], go_all.at[t], go_s.at[0], go_r.at[t], here.device(z=t // 2, x=t % 2))
            pl.when(chip == t)(stay.wait)
            pl.when(chip != t)(come.wait_recv)
        for i in range(chips):
            rows = slice(i * tile, (i + 1) * tile)
            kt_ref[:, rows] = k_ref[rows, :].T
            up_t = go_all[i].T
            for d in range(2):
                part = up_t[d * head : (d + 1) * head, :]
                got_ref[d, :, rows] = part
                delta_ref[d, :, rows] = jnp.sum(part.astype(FULL) * ot_ref[:, rows], axis=0, keepdims=True)
                gqt_ref[d, :, rows] = jnp.zeros((head, tile), FULL)

    def key_tile(j):
        keys = slice(j * tile, (j + 1) * tile)
        key = k_ref[keys, :]
        value = v_ref[keys, :]
        key_t = kt_ref[:, keys]

        def step(i, carry, masked):
            gv, gk0, gk1 = carry
            rows = pl.ds(i * tile if masked else pl.multiple_of(i * tile, tile), tile)
            query = q_ref[rows, :]
            scores = dot(key, query, (1, 1))
            if masked:
                key_pos = lax.broadcasted_iota(jnp.int32, scores.shape, 0)
                query_pos = lax.broadcasted_iota(jnp.int32, scores.shape, 1)
                scores = jnp.where(key_pos <= query_pos, scores, NEGATIVE)
            probs = jnp.exp(scores - top_ref[:, rows])
            gv = gv + dot(probs.astype(LOW), go_all[i], (1, 0))
            gks = [gk0, gk1]
            for d in range(2):
                prob_grad = dot(value, got_ref[d, :, rows], (1, 0))
                score_low = (probs * (prob_grad - delta_ref[d, :, rows])).astype(LOW)
                gks[d] = gks[d] + dot(score_low, query, (1, 0))
                gqt_ref[d, :, rows] += dot(key_t, score_low, (1, 0))
            return gv, gks[0], gks[1]

        zero = jnp.zeros((tile, head), FULL)
        carry = step(j, (jnp.zeros((tile, 2 * head), FULL), zero, zero), True)
        gv, gk0, gk1 = lax.fori_loop(j + 1, chips, lambda i, c: step(i, c, False), carry)
        gsend[j, 1] = jnp.concatenate([gk0, gk1], axis=1).astype(LOW)
        gsend[j, 2] = gv.astype(LOW)

    def kv_copies(t):
        src, dst = gsend.at[t, pl.ds(1, 2)], gat.at[job, pl.ds(1, 2)]
        to = here.device(z=t // 2, x=t % 2)
        return pltpu.make_async_copy(src, dst, kv_s.at[t]), remote(src, dst, kv_s.at[t], kv_r.at[job], to)

    def q_copies(t):
        src, dst = gsend.at[t, 0], gat.at[job, 0]
        to = here.device(z=t // 2, x=t % 2)
        return pltpu.make_async_copy(src, dst, q_s.at[t]), remote(src, dst, q_s.at[t], q_r.at[job], to)

    def launch(copies, t):
        stay, leave = copies(t)
        pl.when(chip == t)(stay.start)
        pl.when(chip != t)(leave.start)

    between = {1: 1, 3: 2, 7: 3}
    for j in range(chips):
        @pl.when(has == 1)
        def _(j=j):
            key_tile(j)
            launch(kv_copies, j)

        if j in between:
            advance(between[j])

    @pl.when(has == 1)
    def _():
        for i in range(chips):
            rows = slice(i * tile, (i + 1) * tile)
            both = jnp.concatenate([gqt_ref[0, :, rows], gqt_ref[1, :, rows]], axis=0) * factor
            gsend[i, 0] = both.T.astype(LOW)
            launch(q_copies, i)

    def mix_y():
        return remote(head_sum.at[:, :, 1 - y], hs_in, ex_s.at[0], ex_r.at[0], here.device(y=1 - y))

    def mix_copies(t):
        src, dst = head_sum.at[t // 2, t % 2, y], mix_in.at[job]
        to = here.device(z=t // 2, x=t % 2)
        return pltpu.make_async_copy(src, dst, mix_s.at[t]), remote(src, dst, mix_s.at[t], mix_r.at[job], to)

    @pl.when(has == 1)
    def _():
        for i in range(chips):
            h_copy(i).wait()
            right = jnp.concatenate([gsend[i, t] for t in range(3)], axis=1)
            part = dot(hbuf[i % 2], right, (0, 0))
            if i == 0:
                head_acc[...] = part
            else:
                head_acc[...] += part
            if i + 2 < chips:
                h_copy(i + 2).start()
        for u in range(parts // 2):
            zz, xx, yy = u // (2 * ny), (u // ny) % 2, u % ny
            head_sum[zz, xx, yy] = head_acc[u * unit : (u + 1) * unit, :].astype(LOW)
        mix_y().start()

    advance(4)

    @pl.when(has == 1)
    def _():
        mix_y().wait_recv()
        mix_y().wait_send()
        add_into(
            lambda i: head_sum.at[lax.div(i, 2), lax.rem(i, 2), y],
            lambda i: hs_in.at[lax.div(i, 2), lax.rem(i, 2)],
            chips,
        )
        for t in range(chips):
            launch(mix_copies, t)

    biases = []
    for t in (0, 2):
        acc = jnp.zeros((1, 2 * head), FULL)
        for i in range(chips):
            acc = acc + jnp.sum(gsend[i, t].astype(FULL), axis=0, keepdims=True)
        biases.append(jnp.where(has == 1, acc, 0.0))
    total = jnp.concatenate([pack[:, c, :] for c in range(pack.shape[1])], axis=1)
    for b in range(2):
        rows = lax.broadcasted_iota(jnp.int32, (parts, 2 * head), 0)
        spread = jnp.where(rows == spot_ref[3 + b : 4 + b, : 2 * head], biases[b], 0.0)
        turn = lax.broadcasted_iota(jnp.int32, (2 * head, 2 * stride), 1) == bias_ref[:, b : b + 1]
        high = spread.astype(LOW)
        low = (spread - high.astype(FULL)).astype(LOW)
        total = total + dot(high, turn.astype(LOW), (1, 0)) + dot(low, turn.astype(LOW), (1, 0))
    advance(5)

    for copy in exchanges:
        copy.wait_send()
    loads[5].wait()
    for j, slot in enumerate(slots):
        @pl.when(chip != slot)
        def _(j=j, slot=slot):
            to = here.device(z=slot // 2, x=slot % 2)
            remote(gat.at[j, pl.ds(1, 2)], gat.at[j, pl.ds(1, 2)], kv_s.at[0], kv_r.at[j], to).wait_recv()
            remote(gat.at[j, 0], gat.at[j, 0], q_s.at[0], q_r.at[j], to).wait_recv()

        @pl.when(chip == slot)
        def _(j=j, slot=slot):
            kv_copies(slot)[0].wait()
            q_copies(slot)[0].wait()

    def first_swap(d):
        return remote(gh2.at[d, their_rows], gh2_in.at[d], ex_s.at[1 + d], ex_r.at[1 + d], partner)

    for d in range(2):
        lanes = slice(d * head, (d + 1) * head)
        first = None
        for p in range(per_core // 2):
            left = jnp.concatenate(
                [gat[2 * p + o, t][:, lanes] for t in range(3) for o in range(2)], axis=1
            )
            part = dot(left, mw[:, :, :, p].reshape(width, half), (1, 1))
            first = part if first is None else first + part
        gh2[d] = first
        first_swap(d).start()
    normed, inv = normalize(x_ref[...].astype(FULL))
    for d in range(2):
        first_swap(d).wait_recv()
        grad = gh2[d, my_rows, :] + gh2_in[d]
        for v, row in ((0, jnp.sum(grad * normed, axis=0, keepdims=True)), (1, jnp.sum(grad, axis=0, keepdims=True))):
            total = total + placed(row, wide_owner, in_piece, v * rows_in + d * stride)
        whole = gmid[d] + norm_back(grad, normed, inv, first_gain)
        ing_ref[d] = split_dot(whole, pm[...], (1, 1))
    for c in range(pack.shape[1]):
        pack[:, c, :] = total[:, c * 128 : (c + 1) * 128]
    me = flat(z, x, y, core)

    def vec_copy(n):
        device, index, _ = others[n]
        return remote(pack.at[index], vec_in.at[me], vec_s.at[n], vec_r.at[n], device)

    def vec_come(n):
        device, _, index = others[n]
        return remote(pack.at[index], vec_in.at[index], vec_s.at[n], vec_r.at[n], device)

    for n in range(len(others)):
        vec_copy(n).start()

    for n in range(6, steps):
        advance(n)
    mine_in = pl.ds(pl.multiple_of(core * rows_in, 8), rows_in)
    their_in = pl.ds(pl.multiple_of((1 - core) * rows_in, 8), rows_in)

    def last_swap(d):
        return remote(fin.at[d, pl.ds(4, slabs - 4), their_in], swap.at[d], ex_s.at[3 + d], ex_r.at[3 + d], partner)

    for d in range(2):
        last_swap(d).start()
    for j, slot in enumerate(slots):
        @pl.when(chip != slot)
        def _(j=j, slot=slot):
            to = here.device(z=slot // 2, x=slot % 2)
            remote(mix_in.at[j], mix_in.at[j], mix_s.at[0], mix_r.at[j], to).wait_recv()

        @pl.when(chip == slot)
        def _(j=j, slot=slot):
            mix_copies(slot)[0].wait()

        mixf[j] = mix_in[j].astype(FULL)
    mix_pass = remote(mixf.at[:, their_in], mix_swap, ex_s.at[5], ex_r.at[5], partner)
    mix_pass.start()

    for d in range(2):
        top_half = jnp.concatenate([fin[d, 0], fin[d, 1]], axis=1)
        low_half = jnp.concatenate([fin[d, 2], fin[d, 3]], axis=1)
        gdn_ref[d] = split_dot(jnp.concatenate([top_half, low_half], axis=0), pm[...], (1, 1))
    is_first = core == 0

    def by_core(a, b):
        return jnp.where(is_first, a, b), jnp.where(is_first, b, a)

    block = ny * rows_hid
    for d in range(2):
        last_swap(d).wait_recv()
        ours = jnp.concatenate([fin[d, s, mine_in, :] for s in range(4, slabs - 1)], axis=1)
        came = jnp.concatenate([swap[d, s] for s in range(slabs - 5)], axis=1)
        one, two = by_core(ours, came)
        blocks = []
        for i in range(hidden // block):
            blocks += [one[:, i * block : (i + 1) * block], two[:, i * block : (i + 1) * block]]
        gup_ref[d] = jnp.concatenate(blocks, axis=1)
        one, two = by_core(fin[d, slabs - 1, mine_in, :], swap[d, slabs - 5])
        gout_ref[d] = split_dot(jnp.concatenate([one, two], axis=1), pm[...], (1, 1))
    mix_pass.wait_recv()
    sides = [by_core(mixf[j, mine_in, :], mix_swap[j]) for j in range(per_core)]
    for d in range(2):
        blocks = []
        for t in range(3):
            for c in range(2):
                for j in range(per_core):
                    start = t * 2 * head + d * head
                    blocks.append(sides[j][c][:, start : start + head])
        mix_ref[d] = jnp.concatenate(blocks, axis=1)
    for n in range(len(others)):
        vec_come(n).wait_recv()
    vec_in[me] = pack[me]
    vec_ref[...] = jnp.sum(vec_in[...], axis=0)

    give_cot.wait_send()
    give_ow.wait_send()
    finish_sends()
    for j, slot in enumerate(slots):
        pl.when(chip != slot)(go_copies(j)[1].wait_send)

    @pl.when(has == 1)
    def _():
        for t in range(chips):
            @pl.when(chip != t)
            def _(t=t):
                kv_copies(t)[1].wait_send()
                q_copies(t)[1].wait_send()
                mix_copies(t)[1].wait_send()

    for d in range(2):
        first_swap(d).wait_send()
        last_swap(d).wait_send()
    mix_pass.wait_send()
    for n in range(len(others)):
        vec_copy(n).wait_send()


def rest(nz, x2, attended, cot, mw_all, up, dn, table, q, k, v, out_t, top, first_low, x, spots, bias_cols):
    length, head = q.shape
    span, width = x.shape
    hidden = up.shape[1]
    half = width // 2
    chips = 2 * nz
    parts = 8 * nz
    rows = 2 * span
    per_core = HEADS // 2
    unit = mw_all.shape[4]
    units = mw_all.shape[:3]
    rows_in = unit // 2
    slabs = 9
    anywhere = pl.BlockSpec(memory_space=pl.ANY)
    vmem = pl.BlockSpec(memory_space=pltpu.VMEM)
    low, full = partial(pltpu.VMEM, dtype=LOW), partial(pltpu.VMEM, dtype=FULL)
    return pl.pallas_call(
        partial(rest_kernel, nz, 512),
        out_shape=(
            jax.ShapeDtypeStruct((2, span, width), LOW),
            jax.ShapeDtypeStruct((2, span, width), FULL),
            jax.ShapeDtypeStruct((2, 2 * unit, width), FULL),
            jax.ShapeDtypeStruct((2, rows_in, 2 * hidden), FULL),
            jax.ShapeDtypeStruct((2, rows_in, width), FULL),
            jax.ShapeDtypeStruct((2, rows_in, 3 * width), FULL),
            jax.ShapeDtypeStruct((5, 128), FULL),
        ),
        in_specs=[vmem, vmem] + [anywhere] * 4 + [vmem] * 6 + [anywhere] + [vmem] * 3,
        out_specs=[vmem] * 7,
        scratch_shapes=[
            low((width, hidden)),
            low((hidden, width)),
            low((2,) + units + (unit, half)),
            low((width, width)),
            low((width, width)),
            low(units + (unit, half)),
            low((rows, width)),
            low((2, rows, width)),
            low((2, rows, width)),
            low((2, rows, hidden)),
            low((2, rows, hidden)),
            full((rows, width)),
            full((2, rows, width)),
            full((2, span, width)),
            full((2, rows, width)),
            full((2, span, width)),
            full((2, span, width)),
            low((2, rows, width)),
            low((2,) + units + (slabs, unit, half)),
            low((per_core, rows, 2 * head)),
            low((chips, rows, 2 * head)),
            low((head, length)),
            low((2, head, length)),
            full((2, 1, length)),
            full((2, head, length)),
            low((chips, 3, rows, 2 * head)),
            low((per_core, 3, rows, 2 * head)),
            low(units + (3, unit, half)),
            low((2, rows, width)),
            full((width, half)),
            low(units + (unit, half)),
            low((nz, 2, unit, half)),
            low((per_core, unit, half)),
            full((per_core, unit, half)),
            full((per_core, rows_in, half)),
            low((2, nz, 2, slabs, unit, half)),
            low((2, nz, slabs, unit, half)),
            low((2, nz + 1, slabs, unit, half)),
            full((2, slabs, unit, half)),
            full((2, slabs - 4, rows_in, half)),
            full((parts, 5, 128)),
            full((parts, 5, 128)),
            DMA((6,)),
            DMA((8,)),
            DMA((8,)),
            DMA((2,)),
            DMA((per_core,)),
            DMA((chips,)),
            DMA((chips,)),
            DMA((per_core,)),
            DMA((chips,)),
            DMA((per_core,)),
            DMA((2, nz, 2)),
            DMA((2, nz, 2)),
            DMA((2, nz, 2)),
            DMA((2, nz, 2)),
            DMA((2, nz, 2)),
            DMA((2, 2, nz, 2)),
            DMA((6,)),
            DMA((6,)),
            DMA((parts - 1,)),
            DMA((parts - 1,)),
            DMA((chips,)),
            DMA((per_core,)),
        ],
        compiler_params=pltpu.CompilerParams(vmem_limit_bytes=62 << 20, collective_id=1, has_side_effects=True),
        cost_estimate=pl.CostEstimate(
            flops=60 * rows * width * hidden, bytes_accessed=60 * width * hidden, transcendentals=length * length
        ),
        name="rest",
    )(x2, attended, cot, mw_all, up, dn, table, q, k, v, out_t, top, first_low, x, spots, bias_cols)


def plain_on_device(
    inputs,
    attend_gain,
    attend_shift,
    mixing_weight,
    mixing_bias,
    output_weight,
    output_bias,
    feed_gain,
    feed_shift,
    up_weight,
    up_bias,
    down_weight,
    down_bias,
    cotangent,
):
    place = Place()
    _, span, width = inputs.shape
    nz, ny, core, chip = place.nz, place.ny, place.core, place.chip
    chips = nz * 2
    parts = chips * 2 * ny
    head = width // HEADS
    per_core = HEADS // 2
    slots = [int((j + 0.5) * chips / per_core) for j in range(per_core)]
    half = width // 2
    hidden = up_weight.shape[1]
    rows_in = width // parts
    rows_hid = hidden // parts
    groups = [[2 * i + c for i in range(chips)] for c in range(2)]

    def exchange(values):
        return lax.all_to_all(values, "seq", 0, 0, axis_index_groups=groups, tiled=True)

    def spread(blocks):
        filled = [jnp.zeros_like(blocks[0])] * chips
        for j, slot in enumerate(slots):
            filled[slot] = blocks[j]
        return jnp.stack(filled)

    def collect(blocks):
        return jnp.stack([blocks[slot] for slot in slots])

    owned = [-1] * chips
    for j, slot in enumerate(slots):
        owned[slot] = j
    my_head = jnp.array(owned, jnp.int32)[chip]
    busy = (my_head >= 0).astype(FULL)
    my_head = jnp.maximum(my_head, 0)

    def by_core(values, dim):
        mine = lax.dynamic_index_in_dim(values, core, dim, keepdims=False)
        theirs = lax.dynamic_index_in_dim(values, 1 - core, dim, keepdims=False)
        return mine, theirs

    vectors = jnp.concatenate(
        [attend_gain, attend_shift, feed_gain, feed_shift, output_bias, down_bias, mixing_bias, up_bias]
    )
    vectors = place.both(vectors, vectors)
    vectors = place.gather(vectors, "z", 0)
    vectors = place.gather(vectors, "x", 1)
    vectors = place.gather(vectors, "y", 3)
    vectors = vectors.reshape(parts, -1).astype(FULL)
    cuts = [vectors[:, i * rows_in : (i + 1) * rows_in].reshape(-1) for i in range(6)]
    first_gain, first_shift, second_gain, second_shift, out_bias, down_bias_all = cuts
    mix_bias = vectors[:, 6 * rows_in : 8 * rows_in].reshape(2, HEADS, head)
    up_bias_all = vectors[:, 8 * rows_in :].reshape(chips, 2, ny * rows_hid)
    up_bias_mine = lax.dynamic_index_in_dim(up_bias_all, core, 1, keepdims=False).reshape(-1)

    own = inputs.reshape(span, width)
    column = [own] + [place.send(own, "z", d) for d in range(1, nz)]
    beside = [place.send(piece, "x") for piece in column]
    x_all = jnp.zeros((nz, 2, span, width), LOW)
    for d in range(nz):
        at = lax.rem(place.z + nz - d, nz)
        x_all = lax.dynamic_update_slice(x_all, column[d][None, None], (at, place.x, 0, 0))
        x_all = lax.dynamic_update_slice(x_all, beside[d][None, None], (at, 1 - place.x, 0, 0))
    x_all = place.both(x_all, x_all).transpose(1, 2, 0, 3, 4)
    x_all = x_all.reshape(chips * 2 * span, width)

    def gather_rows(mine, theirs):
        block = place.both(mine, theirs)
        block = place.gather(block, "z", 0)
        block = place.gather(block, "x", 1)
        block = place.gather(block, "y", 3)
        return block.reshape(parts * block.shape[-2], block.shape[-1])

    mixing = mixing_weight.reshape(rows_in, 3, 2, half)
    mine, theirs = by_core(mixing, 2)
    mixing = gather_rows(mine.reshape(rows_in, -1), theirs.reshape(rows_in, -1))
    mine, theirs = by_core(output_weight.reshape(rows_in, 2, half), 1)
    out_half = gather_rows(mine, theirs)
    out_all = place.both(out_half, out_half).transpose(1, 0, 2).reshape(width, width)
    mine, theirs = by_core(up_weight.reshape(rows_in, chips, 2, ny * rows_hid), 2)
    up = gather_rows(mine.reshape(rows_in, -1), theirs.reshape(rows_in, -1))
    down = place.gather(down_weight, "z", 0)
    down = place.gather(down, "x", 1)
    down = place.gather(down, "y", 2).reshape(chips * ny * rows_hid, width)

    mixing = mixing.reshape(width, 3, per_core, head)
    head_weight = lax.dynamic_index_in_dim(mixing, my_head, 2, keepdims=False).reshape(width, 3 * head)
    whole_head = core * per_core + my_head
    head_bias = lax.dynamic_index_in_dim(mix_bias, whole_head, 1, keepdims=False)
    head_bias = jnp.concatenate([head_bias[0], jnp.zeros((head,), FULL), head_bias[1]])
    first_low, q, k, v, out, out_t, top = attend_plain(
        x_all, first_gain[None], first_shift[None], head_weight, head_bias[None]
    )
    attended = collect(exchange(out.reshape(chips, 2 * span, head)))
    attended = attended.transpose(1, 0, 2).reshape(2 * span, half)
    attended = place.both(attended, attended).transpose(1, 0, 2).reshape(2 * span, width)

    residual = lax.dynamic_slice_in_dim(x_all, chip * 2 * span, 2 * span, 0).astype(FULL)
    branch = dot(attended, out_all, (1, 0)) + out_bias
    scale = jnp.array(SCALES, FULL)[:, None, None]
    middle = residual + scale * branch
    second_normed, second_inv = normalize(middle)
    second_low = (second_normed * second_gain + second_shift).astype(LOW)
    rows = second_low.reshape(4 * span, width)
    hidden_pre = dot(rows, up, (1, 0)) + up_bias_mine
    activated, gelu_back = jax.vjp(partial(jax.nn.gelu, approximate=True), hidden_pre)
    activated_low = activated.astype(LOW)
    feed_part = dot(activated_low, down, (1, 0)).reshape(2, 2, span, width)
    mine, theirs = by_core(feed_part, 1)
    feed_own = mine + place.send(theirs, "core") + down_bias_all

    def own_rows(values):
        return lax.dynamic_index_in_dim(
            values.reshape((2, 2, span) + values.shape[2:]), core, 1, keepdims=False
        )

    activations = (own_rows(middle) + scale * feed_own).astype(LOW)
    upstream_own = cotangent.reshape(2, span, width)
    upstream = place.both(upstream_own, upstream_own).transpose(1, 0, 2, 3)
    down_in = (scale[..., None] * upstream.astype(FULL)).astype(LOW).reshape(4 * span, width)
    hidden_low = gelu_back(dot(down_in, down, (1, 1)))[0].astype(LOW)
    second_part = dot(hidden_low, up, (1, 1)).reshape(2, 2, span, width)
    mine, theirs = by_core(second_part, 1)
    second_grad = mine + place.send(theirs, "core")
    normed_own, inv_own = own_rows(second_normed), own_rows(second_inv)
    middle_grad = upstream_own.astype(FULL) + norm_back(second_grad, normed_own, inv_own, second_gain)
    branch_own = (scale * middle_grad).astype(LOW)
    branch_low = place.both(branch_own, branch_own).transpose(1, 0, 2, 3).reshape(2, 2 * span, width)
    out_rows = lax.dynamic_slice_in_dim(out_all, core * half, half, 0)
    go = dot(branch_low.reshape(4 * span, width), out_rows, (1, 1)).astype(LOW)
    go = go.reshape(2, 2 * span, per_core, head).transpose(2, 1, 0, 3).reshape(per_core, 2 * span, 2 * head)
    go = exchange(spread(go)).reshape(chips * 2 * span, 2 * head)

    gq, gk, gv = attend_back(q, k, v, out_t, top, go)
    head_grads = jnp.concatenate([gq, gk, gv], axis=1)

    depth_rows = second_low.reshape(2, 2 * span, width)
    hidden_rows = hidden_low.reshape(2, 2 * span, -1)
    active_rows = activated_low.reshape(2, 2 * span, -1)
    in_rows = down_in.reshape(2, 2 * span, width)
    branch_cols = lax.dynamic_slice_in_dim(branch_low, core * half, half, 2)
    orders = (("y", "x"), ("x", "y"))

    def scatter_chips(values, order):
        dims = {"x": 1, "y": 2}
        values = place.scatter(values, order[0], dims[order[0]]).astype(LOW)
        values = place.scatter(values, order[1], 1).astype(LOW)
        return place.scatter(values, "z", 0)

    def scatter_rows(values, order):
        shaped = values.reshape(nz, 2, 2, ny, rows_in, -1).transpose(0, 1, 3, 2, 4, 5)
        summed = scatter_chips(shaped, order)
        mine, theirs = by_core(summed, 0)
        return place.both(mine, theirs)

    down_grads, up_grads, out_grads = [], [], []
    for depth in range(2):
        grad = dot(active_rows[depth], in_rows[depth], (0, 0)).astype(LOW)
        down_grads.append(scatter_chips(grad.reshape(nz, 2, ny, rows_hid, width), orders[depth]))
    for depth in range(2):
        grad = dot(depth_rows[depth], hidden_rows[depth], (0, 0)).astype(LOW)
        grad = scatter_rows(grad, orders[depth]).reshape(2, rows_in, chips, -1)
        up_grads.append(grad.transpose(1, 2, 0, 3).reshape(rows_in, hidden))
    for depth in range(2):
        grad = dot(attended, branch_cols[depth], (0, 0)).astype(LOW)
        out_grads.append(scatter_rows(grad, orders[depth]).transpose(1, 0, 2).reshape(rows_in, width))

    head_sum = dot(first_low, head_grads, (0, 0)).astype(LOW).reshape(nz, 2, 2, ny, rows_in, 6 * head)
    head_sum = place.scatter(head_sum, "y", 3).astype(LOW).reshape(chips, 2, rows_in, 6 * head)
    head_sum = collect(exchange(head_sum))
    mine, theirs = by_core(head_sum, 1)
    mixing_grad = place.both(mine, theirs).reshape(HEADS, rows_in, 3, 2, head)
    mixing_grad = mixing_grad.transpose(3, 1, 2, 0, 4).reshape(2, rows_in, 3 * width).astype(FULL)

    mixed_grads = collect(exchange(head_grads.reshape(chips, 2 * span, 6 * head)))
    mixed_grads = mixed_grads.reshape(per_core, 2 * span, 3, 2, head).transpose(3, 1, 2, 0, 4)
    mixed_grads = mixed_grads.reshape(4 * span, 3 * half)
    first_part = dot(mixed_grads, mixing.reshape(width, 3 * half), (1, 1)).reshape(2, 2, span, width)
    mine, theirs = by_core(first_part, 1)
    first_grad = mine + place.send(theirs, "core")
    first_normed, first_inv = normalize(own.astype(FULL))
    input_grad = middle_grad + norm_back(first_grad, first_normed, first_inv, first_gain)

    bias_sum = jnp.sum(head_grads.astype(FULL), axis=0).reshape(3, 2, head) * busy
    spot = (jnp.arange(HEADS) == whole_head).astype(FULL)[None, None, :, None]
    bias_sum = (jnp.stack([bias_sum[0], bias_sum[2]], axis=1)[:, :, None, :] * spot).reshape(2, parts, -1)
    hidden_sum = jnp.sum(hidden_rows.astype(FULL), axis=1).reshape(2, chips, 1, ny * rows_hid)
    hidden_spot = (jnp.arange(2) == core).astype(FULL)[None, None, :, None]
    hidden_sum = (hidden_sum * hidden_spot).reshape(2, parts, rows_hid)
    in_own = (scale * upstream_own.astype(FULL)).astype(LOW)
    sums = [
        jnp.sum(first_grad * first_normed, axis=1),
        jnp.sum(first_grad, axis=1),
        jnp.sum(second_grad * normed_own, axis=1),
        jnp.sum(second_grad, axis=1),
        jnp.sum(branch_own.astype(FULL), axis=1),
        jnp.sum(in_own.astype(FULL), axis=1),
    ]
    sums = [item.reshape(2, parts, rows_in) for item in sums] + [bias_sum, hidden_sum]
    sums = jnp.concatenate(sums, axis=2).reshape(2, nz, 2, 2, ny, -1)
    sums = place.scatter(sums, "y", 4)
    sums = place.scatter(sums, "x", 2)
    sums = place.scatter(sums, "core", 2)
    sums = place.scatter(sums, "z", 1)
    small = [sums[:, i * rows_in : (i + 1) * rows_in] for i in range(6)]
    return (
        activations[:, None],
        input_grad[:, None],
        small[0],
        small[1],
        mixing_grad,
        sums[:, 6 * rows_in : 8 * rows_in],
        jnp.stack(out_grads),
        small[4],
        small[2],
        small[3],
        jnp.stack(up_grads),
        sums[:, 8 * rows_in :],
        jnp.stack(down_grads),
        small[5],
    )


def on_device(
    inputs,
    attend_gain,
    attend_shift,
    mixing_weight,
    mixing_bias,
    output_weight,
    output_bias,
    feed_gain,
    feed_shift,
    up_weight,
    up_bias,
    down_weight,
    down_bias,
    cotangent,
):
    place = Place()
    _, span, width = inputs.shape
    nz, ny, core, chip = place.nz, place.ny, place.core, place.chip
    chips = nz * 2
    parts = chips * 2 * ny
    head = width // HEADS
    per_core = HEADS // 2
    half = width // 2
    hidden = up_weight.shape[1]
    rows_in = width // parts
    rows_hid = hidden // parts
    groups = [[2 * i + c for i in range(chips)] for c in range(2)]

    slots = owner_of(chips)
    owned = [-1] * chips
    for j, slot in enumerate(slots):
        owned[slot] = j
    my_head = jnp.array(owned, jnp.int32)[chip]
    my_head = jnp.maximum(my_head, 0)

    def by_core(values, dim):
        mine = lax.dynamic_index_in_dim(values, core, dim, keepdims=False)
        theirs = lax.dynamic_index_in_dim(values, 1 - core, dim, keepdims=False)
        return mine, theirs

    own = inputs.reshape(span, width)
    pairs = per_core // 2
    mix = mixing_weight.reshape(rows_in, 3, 2, pairs, 2, head).transpose(2, 3, 0, 1, 4, 5)
    mix = mix.reshape(2, pairs, rows_in, half)
    lane = jnp.arange(width, dtype=jnp.int32)
    within = lane % (2 * ny * rows_in)
    natural = lane - within + ((within // rows_in) % 2) * ny * rows_in + (within // (2 * rows_in)) * rows_in + lane % rows_in
    turn = (lane[:, None] == natural[None, :]).astype(LOW)
    turned = jnp.concatenate([own, cotangent.reshape(2 * span, width), output_weight, down_weight])
    turned = dot(turned, turn, (1, 0)).astype(LOW)
    own, cot = turned[:span], turned[span : 3 * span].reshape(2, span, width)
    out_weight, down_weight = turned[3 * span : 3 * span + rows_in], turned[3 * span + rows_in :]
    out_cols = out_weight.reshape(rows_in, 2, half).transpose(1, 0, 2)[:, None]
    vectors = jnp.concatenate(
        [attend_gain, attend_shift, feed_gain, feed_shift, output_bias, down_bias, mixing_bias, up_bias]
    )
    pieces = vectors.shape[0]
    vectors = jnp.pad(vectors[None], ((0, rows_in - 1), (0, half - pieces)))
    vectors = jnp.broadcast_to(vectors, (2, 1) + vectors.shape)
    packed = jnp.concatenate([mix, out_cols, vectors], axis=1)
    up_cols = up_weight.reshape(rows_in, chips, 2, ny * rows_hid).transpose(2, 0, 1, 3).reshape(2, rows_in, -1)
    mine, theirs = by_core(packed, 0)
    packed = place.both(mine, theirs).transpose(1, 0, 2, 3).reshape(pairs + 2, 2 * rows_in, half)
    mine, theirs = by_core(up_cols, 0)
    up_unit = place.both(mine, theirs).reshape(2 * rows_in, -1)

    in_rows_of = lane // rows_in
    pair_lane = jnp.arange(2 * head, dtype=jnp.int32) + (core * pairs + my_head // 2) * 2 * head
    bias_cols, bias_rows = [], []
    for start in (0, width):
        spot = start + pair_lane
        device = spot // (2 * rows_in)
        bias_cols.append(6 * rows_in + spot % (2 * rows_in))
        bias_rows.append((device // (2 * ny)) * 2 * ny + (device % ny) * 2 + (device // ny) % 2)
    none = jnp.full((2 * head,), -1, jnp.int32)
    table = jnp.stack([
        jnp.concatenate([lane % rows_in, rows_in + lane % rows_in, bias_cols[0], none, bias_cols[1]]),
        jnp.concatenate([in_rows_of, in_rows_of, bias_rows[0], none, bias_rows[1]]),
    ])
    mw_all, up_all, dn_all, first_low, q, k, v, out_t, top, attended, x2 = attend(
        nz, ny, own, packed, up_unit, down_weight, table
    )

    hid = jnp.arange(chips * ny * rows_hid, dtype=jnp.int32)
    feed_cols = [i * rows_in + lane % rows_in for i in (2, 3, 4, 5, 0)] + [8 * rows_in + hid % rows_hid]
    hid_rows = (hid // rows_hid) * 2 + core
    feed_table = jnp.stack([
        jnp.concatenate(feed_cols),
        jnp.concatenate([in_rows_of] * 5 + [hid_rows]),
        jnp.concatenate([natural, jnp.zeros((4 * width + hid.shape[0],), jnp.int32)]),
    ])
    stride = 320
    head_lane = jnp.arange(2 * head, dtype=jnp.int32)
    columns, owners = [], []
    for start in (0, width):
        spot = start + (core * per_core + my_head) * head + head_lane % head
        device = spot // (2 * rows_in)
        columns.append(6 * rows_in + spot % (2 * rows_in) + (head_lane // head) * stride)
        owners.append((device // (2 * ny)) * 2 * ny + (device % ny) * 2 + (device // ny) % 2)

    def wide(values):
        return jnp.pad(values, (0, hid.shape[0] - values.shape[0]))

    table = jnp.stack([wide(natural), wide(in_rows_of), hid_rows, wide(owners[0]), wide(owners[1])])
    activations, input_grad, down_grad, up_grad, out_grad, mixing_grad, sums = rest(
        nz, x2.reshape(2 * span, width), attended, cot, mw_all, up_all.reshape(width, -1), dn_all.reshape(-1, width),
        feed_table, q, k, v, out_t, top, first_low, own, table, jnp.stack(columns, axis=1),
    )
    sums = sums.reshape(2, stride)
    small = [sums[:, i * rows_in : (i + 1) * rows_in] for i in range(6)]
    return (
        activations[:, None],
        input_grad[:, None],
        small[0],
        small[1],
        mixing_grad,
        sums[:, 6 * rows_in : 8 * rows_in],
        out_grad,
        small[4],
        small[2],
        small[3],
        up_grad,
        sums[:, 8 * rows_in : 8 * rows_in + rows_hid],
        down_grad,
        small[5],
    )


def tiles_well(mesh):
    ny, seq = mesh.shape["batch"], mesh.shape["seq"]
    rows_in = 768 // (seq * ny)
    return ny == 2 and seq // 2 >= HEADS // 2 and 2 * rows_in % 16 == 0 and 2 * rows_in * seq * ny == 2 * 768


def solution(mesh):
    shard = P(("seq", "batch"))
    grad = P(None, ("seq", "batch"))
    row = P(None, "batch", "seq", None)
    return jax.shard_map(
        on_device if tiles_well(mesh) else plain_on_device,
        mesh=mesh,
        in_specs=(P("batch", "seq", None),) + (shard,) * 12 + (row,),
        out_specs=(row, row) + (grad,) * 12,
        check_vma=False,
    )
```

```python
from functools import partial

import jax
import jax.numpy as jnp
from jax import lax
from jax.experimental import pallas as pl
from jax.experimental.pallas import tpu as pltpu
from jax.sharding import PartitionSpec as P

HEADS = 12
EPS = 1e-05
SCALES = (12.0 ** (-0.5), 48.0 ** (-0.5))
NEGATIVE = -1e30
LOW = jnp.bfloat16
FULL = jnp.float32
TILE = 256


def normalize(values):
    average = jnp.mean(values, axis=-1, keepdims=True)
    centered = values - average
    inv_std = lax.rsqrt(jnp.mean(centered * centered, axis=-1, keepdims=True) + EPS)
    return centered * inv_std, inv_std


def norm_back(gradient, normed, inv_std, gain):
    scaled = gradient * gain
    inner = (
        scaled
        - jnp.mean(scaled, axis=-1, keepdims=True)
        - normed * jnp.mean(scaled * normed, axis=-1, keepdims=True)
    )
    return inv_std * inner


def dot(a, b, dims):
    return lax.dot_general(a, b, ((dims[:1], dims[1:]), ((), ())), preferred_element_type=FULL)


class Place:
    def __init__(self):
        self.s = lax.axis_size("seq")
        self.ny = lax.axis_size("batch")
        self.nz = self.s // 4
        seq = lax.axis_index("seq")
        self.y = lax.axis_index("batch")
        self.core = lax.rem(seq, 2)
        self.chip = seq // 2
        self.x = lax.rem(self.chip, 2)
        self.z = self.chip // 2
        self.sizes = {"z": self.nz, "x": 2, "y": self.ny, "core": 2}
        self.at = {"z": self.z, "x": self.x, "y": self.y, "core": self.core}

    def send(self, values, axis, d=1):
        pairs = []
        for s in range(self.s):
            for y in range(self.ny):
                c, x, z, t = s % 2, (s // 2) % 2, s // 4, y
                if axis == "z":
                    z = (z + d) % self.nz
                elif axis == "x":
                    x = 1 - x
                elif axis == "core":
                    c = 1 - c
                else:
                    t = (y + d) % self.ny
                pairs.append((s * self.ny + y, ((z * 2 + x) * 2 + c) * self.ny + t))
        return lax.ppermute(values, ("seq", "batch"), pairs)

    def gather(self, values, axis, dim):
        size, at = self.sizes[axis], self.at[axis]
        shape = values.shape[:dim] + (size,) + values.shape[dim:]
        whole = lax.dynamic_update_slice_in_dim(
            jnp.zeros(shape, values.dtype), jnp.expand_dims(values, dim), at, dim
        )
        for d in range(1, size):
            piece = jnp.expand_dims(self.send(values, axis, d), dim)
            whole = lax.dynamic_update_slice_in_dim(whole, piece, lax.rem(at + size - d, size), dim)
        return whole

    def scatter(self, values, axis, dim):
        size, at = self.sizes[axis], self.at[axis]

        def pick(i):
            return lax.dynamic_index_in_dim(values, lax.rem(i, size), dim, keepdims=False)

        total = pick(at).astype(FULL)
        for d in range(1, size):
            total = total + self.send(pick(at + d), axis, d).astype(FULL)
        return total

    def both(self, mine, theirs):
        got = self.send(theirs, "core")
        first = self.core == 0
        return jnp.stack([jnp.where(first, mine, got), jnp.where(first, got, mine)])


def attend_plain_kernel(x_ref, gain_ref, shift_ref, w_ref, b_ref, h_ref, q_ref, k_ref, v_ref, o_ref, ot_ref, top_ref, vt_ref):
    length = x_ref.shape[0]
    head = q_ref.shape[1]
    tiles = length // TILE

    def project(i, _):
        rows = pl.ds(pl.multiple_of(i * TILE, TILE), TILE)
        normed, _ = normalize(x_ref[rows, :].astype(FULL))
        low = (normed * gain_ref[...] + shift_ref[...]).astype(LOW)
        h_ref[rows, :] = low
        mixed = dot(low, w_ref[...], (1, 0)) + b_ref[...]
        q_ref[rows, :] = (mixed[:, :head].astype(LOW) * (head ** (-0.5))).astype(LOW)
        k_ref[rows, :] = mixed[:, head : 2 * head].astype(LOW)
        value = mixed[:, 2 * head :].astype(LOW)
        v_ref[rows, :] = value
        vt_ref[:, rows] = value.T
        return 0

    lax.fori_loop(0, tiles, project, 0)

    def query_tile(i, _):
        rows = pl.ds(pl.multiple_of(i * TILE, TILE), TILE)
        query = q_ref[rows, :]

        def absorb(j, carry, masked):
            top, total, acc = carry
            keys = pl.ds(pl.multiple_of(j * TILE, TILE), TILE)
            scores = dot(k_ref[keys, :], query, (1, 1))
            if masked:
                key_pos = lax.broadcasted_iota(jnp.int32, scores.shape, 0)
                query_pos = lax.broadcasted_iota(jnp.int32, scores.shape, 1)
                scores = jnp.where(key_pos <= query_pos, scores, NEGATIVE)
            new_top = jnp.maximum(top, jnp.max(scores, axis=0, keepdims=True))
            weights = jnp.exp(scores - new_top)
            keep = jnp.exp(top - new_top)
            total = total * keep + jnp.sum(weights, axis=0, keepdims=True)
            acc = acc * keep + dot(vt_ref[:, keys], weights.astype(LOW), (1, 0))
            return new_top, total, acc

        start = (
            jnp.full((1, TILE), NEGATIVE, FULL),
            jnp.zeros((1, TILE), FULL),
            jnp.zeros((head, TILE), FULL),
        )
        carry = lax.fori_loop(0, i, lambda j, c: absorb(j, c, False), start)
        top, total, acc = absorb(i, carry, True)
        out = acc / total
        ot_ref[:, rows] = out
        o_ref[rows, :] = out.T.astype(LOW)
        top_ref[:, rows] = top + jnp.log(total)
        return 0

    lax.fori_loop(0, tiles, query_tile, 0)


def attend_plain(x_all, gain, shift, weight, bias):
    length, head = x_all.shape[0], weight.shape[1] // 3
    low = jax.ShapeDtypeStruct((length, head), LOW)
    return pl.pallas_call(
        attend_plain_kernel,
        out_shape=(
            jax.ShapeDtypeStruct(x_all.shape, LOW),
            low,
            low,
            low,
            low,
            jax.ShapeDtypeStruct((head, length), FULL),
            jax.ShapeDtypeStruct((1, length), FULL),
        ),
        scratch_shapes=[pltpu.VMEM((head, length), LOW)],
        compiler_params=pltpu.CompilerParams(vmem_limit_bytes=48 << 20),
        cost_estimate=pl.CostEstimate(
            flops=6 * length * length * head, bytes_accessed=8 * length * 768, transcendentals=length * length
        ),
        name="attend_plain",
    )(x_all, gain, shift, weight, bias)


def attend_back_kernel(
    q_ref, k_ref, v_ref, ot_ref, top_ref, go_ref, gq_ref, gk_ref, gv_ref, kt_ref, got_ref, delta_ref, gqt_ref
):
    length, head = q_ref.shape
    tiles = length // TILE
    factor = head ** (-0.5)

    def prepare(i, _):
        rows = pl.ds(pl.multiple_of(i * TILE, TILE), TILE)
        kt_ref[:, rows] = k_ref[rows, :].T
        up = go_ref[rows, :].T
        for d in range(2):
            mine = up[d * head : (d + 1) * head, :]
            got_ref[d, :, rows] = mine
            delta_ref[d, :, rows] = jnp.sum(mine.astype(FULL) * ot_ref[:, rows], axis=0, keepdims=True)
            gqt_ref[d, :, rows] = jnp.zeros((head, TILE), FULL)
        return 0

    lax.fori_loop(0, tiles, prepare, 0)

    def key_tile(j, _):
        keys = pl.ds(pl.multiple_of(j * TILE, TILE), TILE)
        key = k_ref[keys, :]
        value = v_ref[keys, :]
        key_t = kt_ref[:, keys]

        def step(i, carry, masked):
            gv, gk0, gk1 = carry
            rows = pl.ds(pl.multiple_of(i * TILE, TILE), TILE)
            query = q_ref[rows, :]
            scores = dot(key, query, (1, 1))
            if masked:
                key_pos = lax.broadcasted_iota(jnp.int32, scores.shape, 0)
                query_pos = lax.broadcasted_iota(jnp.int32, scores.shape, 1)
                scores = jnp.where(key_pos <= query_pos, scores, NEGATIVE)
            probs = jnp.exp(scores - top_ref[:, rows])
            gv = gv + dot(probs.astype(LOW), go_ref[rows, :], (1, 0))
            gks = [gk0, gk1]
            for d in range(2):
                prob_grad = dot(value, got_ref[d, :, rows], (1, 0))
                score_low = (probs * (prob_grad - delta_ref[d, :, rows])).astype(LOW)
                gks[d] = gks[d] + dot(score_low, query, (1, 0))
                gqt_ref[d, :, rows] += dot(key_t, score_low, (1, 0))
            return gv, gks[0], gks[1]

        zero = jnp.zeros((TILE, head), FULL)
        carry = step(j, (jnp.zeros((TILE, 2 * head), FULL), zero, zero), True)
        gv, gk0, gk1 = lax.fori_loop(j + 1, tiles, lambda i, c: step(i, c, False), carry)
        gv_ref[keys, :] = gv.astype(LOW)
        gk_ref[keys, :] = jnp.concatenate([gk0, gk1], axis=1).astype(LOW)
        return 0

    lax.fori_loop(0, tiles, key_tile, 0)

    def finish(i, _):
        rows = pl.ds(pl.multiple_of(i * TILE, TILE), TILE)
        both = jnp.concatenate([gqt_ref[0, :, rows], gqt_ref[1, :, rows]], axis=0) * factor
        gq_ref[rows, :] = both.T.astype(LOW)
        return 0

    lax.fori_loop(0, tiles, finish, 0)


def attend_back(q, k, v, out_t, top, go):
    length, head = q.shape
    pair = jax.ShapeDtypeStruct((length, 2 * head), LOW)
    return pl.pallas_call(
        attend_back_kernel,
        out_shape=(pair, pair, pair),
        scratch_shapes=[
            pltpu.VMEM((head, length), LOW),
            pltpu.VMEM((2, head, length), LOW),
            pltpu.VMEM((2, 1, length), FULL),
            pltpu.VMEM((2, head, length), FULL),
        ],
        compiler_params=pltpu.CompilerParams(vmem_limit_bytes=48 << 20),
        cost_estimate=pl.CostEstimate(
            flops=20 * length * length * head, bytes_accessed=16 * length * head, transcendentals=length * length
        ),
        name="attend_back",
    )(q, k, v, out_t, top, go)


MESH = pl.DeviceIdType.MESH
DMA = pltpu.SemaphoreType.DMA


class Here:
    def __init__(self, nz, ny):
        self.nz, self.ny = nz, ny
        seq = lax.axis_index("seq")
        self.y = lax.axis_index("batch")
        self.core = lax.rem(seq, 2)
        self.chip = lax.div(seq, 2)
        self.x = lax.rem(self.chip, 2)
        self.z = lax.div(self.chip, 2)

    def device(self, z=None, x=None, core=None, y=None):
        z = self.z if z is None else z
        x = self.x if x is None else x
        core = self.core if core is None else core
        y = self.y if y is None else y
        return ((z * 2 + x) * 2 + core, y)

    def before(self, d):
        return lax.rem(self.z + self.nz - d, self.nz)

    def after(self, d):
        return lax.rem(self.z + d, self.nz)


def remote(src, dst, send, recv, device):
    return pltpu.make_async_remote_copy(
        src_ref=src, dst_ref=dst, send_sem=send, recv_sem=recv, device_id=device, device_id_type=MESH
    )


class Gather:
    def __init__(self, here, own, whole, x_first, sems):
        self.here, self.own, self.whole, self.x_first = here, own, whole, x_first
        self.zs, self.zr, self.as_, self.ar, self.bs, self.br, self.local = sems
        self.kept = pltpu.make_async_copy(own, whole.at[here.z, here.x, here.y], self.local)

    @staticmethod
    def scratch(nz, ny):
        return [DMA((2, nz)), DMA((nz,)), DMA((nz, ny)), DMA((nz, ny)), DMA((nz, 2, ny)), DMA((nz, 2, ny)), DMA]

    def _along(self, source, up, own=False):
        h = self.here
        spot = self.whole.at[source, h.x, h.y]
        to = h.device(z=lax.min(h.z + 1, h.nz - 1)) if up else h.device(z=lax.max(h.z - 1, 0))
        src = self.own if own else spot
        return remote(src, spot, self.zs.at[0 if up else 1, source], self.zr.at[source], to)

    def _to_x(self, source, y, out, own=False):
        h = self.here
        spot = self.whole.at[source, h.x if out else 1 - h.x, y]
        s, r = (self.as_, self.ar) if self.x_first else (self.bs, self.br)
        i = (source, 0) if self.x_first else (source, 0, y)
        return remote(self.own if own else spot, spot, s.at[i], r.at[i], h.device(x=1 - h.x))

    def _to_y(self, source, x, e, out, own=False):
        h = self.here
        spot = self.whole.at[source, x, h.y if out else lax.rem(h.y + h.ny - e, h.ny)]
        s, r = (self.bs, self.br) if self.x_first else (self.as_, self.ar)
        i = (source, x, e) if self.x_first else (source, e)
        return remote(self.own if own else spot, spot, s.at[i], r.at[i], h.device(y=lax.rem(h.y + e, h.ny)))

    def start_z(self):
        h = self.here
        pl.when(h.z < h.nz - 1)(self._along(h.z, True, True).start)
        pl.when(h.z > 0)(self._along(h.z, False, True).start)

    def take_z(self, source, up):
        h = self.here
        self._along(source, up).wait_recv()
        pl.when(h.z < h.nz - 1 if up else h.z > 0)(self._along(source, up).start)

    def spread(self, source, own):
        h = self.here
        if self.x_first:
            self._to_x(source, h.y, True, own).start()
            for e in range(1, h.ny):
                self._to_y(source, h.x, e, True, own).start()
        else:
            for e in range(1, h.ny):
                self._to_y(source, h.x, e, True, own).start()
            self._to_x(source, h.y, True, own).start()

    def second(self, source):
        h = self.here
        if self.x_first:
            self._to_x(source, h.y, False).wait_recv()
            for e in range(1, h.ny):
                self._to_y(source, 1 - h.x, e, True).start()
        else:
            for e in range(1, h.ny):
                self._to_y(source, h.x, e, False).wait_recv()
                self._to_x(source, lax.rem(h.y + h.ny - e, h.ny), True).start()

    def third(self, source):
        h = self.here
        if self.x_first:
            for e in range(1, h.ny):
                self._to_y(source, h.x, e, False).wait_recv()
                self._to_y(source, 1 - h.x, e, False).wait_recv()
        else:
            for y in range(h.ny):
                self._to_x(source, y, False).wait_recv()

    def finish(self):
        h = self.here
        for source in range(h.nz):
            pl.when(jnp.logical_and(source <= h.z, h.z < h.nz - 1))(self._along(source, True).wait_send)
            pl.when(jnp.logical_and(source >= h.z, h.z > 0))(self._along(source, False).wait_send)
            if self.x_first:
                self._to_x(source, h.y, True).wait_send()
                for e in range(1, h.ny):
                    for x in range(2):
                        self._to_y(source, x, e, True).wait_send()
            else:
                for e in range(1, h.ny):
                    self._to_y(source, h.x, e, True).wait_send()
                for y in range(h.ny):
                    self._to_x(source, y, True).wait_send()


class GatherRows:
    def __init__(self, here, own, whole, sems):
        self.here, self.own, self.whole = here, own, whole
        self.zs, self.zr, self.xs, self.xr, self.cs, self.cr, self.local = sems
        self.kept = pltpu.make_async_copy(own, whole.at[here.z, here.x, here.core], self.local)

    @staticmethod
    def scratch(nz):
        return [DMA((2, nz)), DMA((nz,)), DMA((nz,)), DMA((nz,)), DMA((nz, 2)), DMA((nz, 2)), DMA]

    def _along(self, source, up, own=False):
        h = self.here
        spot = self.whole.at[source, h.x, h.core]
        to = h.device(z=lax.min(h.z + 1, h.nz - 1)) if up else h.device(z=lax.max(h.z - 1, 0))
        src = self.own if own else spot
        return remote(src, spot, self.zs.at[0 if up else 1, source], self.zr.at[source], to)

    def _to_x(self, source, out, own=False):
        h = self.here
        spot = self.whole.at[source, h.x if out else 1 - h.x, h.core]
        return remote(self.own if own else spot, spot, self.xs.at[source], self.xr.at[source], h.device(x=1 - h.x))

    def _to_core(self, source, x, out, own=False):
        h = self.here
        spot = self.whole.at[source, x, h.core if out else 1 - h.core]
        return remote(self.own if own else spot, spot, self.cs.at[source, x], self.cr.at[source, x], h.device(core=1 - h.core))

    start_z = Gather.start_z
    take_z = Gather.take_z

    def spread(self, source, own):
        self._to_x(source, True, own).start()
        self._to_core(source, self.here.x, True, own).start()

    def second(self, source):
        self._to_x(source, False).wait_recv()
        self._to_core(source, 1 - self.here.x, True).start()

    def third(self, source):
        for x in range(2):
            self._to_core(source, x, False).wait_recv()

    def finish(self):
        h = self.here
        for source in range(h.nz):
            pl.when(jnp.logical_and(source <= h.z, h.z < h.nz - 1))(self._along(source, True).wait_send)
            pl.when(jnp.logical_and(source >= h.z, h.z > 0))(self._along(source, False).wait_send)
            self._to_x(source, True).wait_send()
            for x in range(2):
                self._to_core(source, x, True).wait_send()


def at_distance(here, k, act):
    if k == 0:
        act(here.z, None)
    else:
        pl.when(here.z >= k)(lambda: act(here.z - k, True))
        pl.when(here.z + k < here.nz)(lambda: act(here.z + k, False))


def natural_of(shape, axis, rows_in, ny):
    lane = lax.broadcasted_iota(jnp.int32, shape, axis)
    within = lax.rem(lane, 2 * ny * rows_in)
    core = lax.rem(lax.div(within, rows_in), 2)
    y = lax.div(within, 2 * rows_in)
    return lane - within + (core * ny + y) * rows_in + lax.rem(lane, rows_in)


def bias_piece(entry, rows_in, ny):
    device = lax.div(entry, 2 * rows_in)
    chip = lax.div(device, 2 * ny)
    row = chip * 2 * ny + lax.rem(device, ny) * 2 + lax.rem(lax.div(device, ny), 2)
    return row, 6 * rows_in + lax.rem(entry, 2 * rows_in)


def greet(devices):
    barrier = pltpu.get_barrier_semaphore()
    for device in devices:
        pl.semaphore_signal(barrier, inc=1, device_id=device, device_id_type=MESH)
    return lambda: pl.semaphore_wait(barrier, len(devices))


def owner_of(chips):
    per_core = HEADS // 2
    return [int((j + 0.5) * chips / per_core) for j in range(per_core)]


def head_here(chip, slots):
    mine, has = jnp.int32(0), jnp.int32(0)
    for j, slot in enumerate(slots):
        same = (chip == slot).astype(jnp.int32)
        mine = mine + j * same
        has = has + same
    return mine, has


def attend_kernel(
    nz, ny, x_ref, mw_ref, up_ref, dn_ref,
    mw_all, up_all, dn_all, h_ref, q_ref, k_ref, v_ref, ot_ref, top_ref, att_ref, x2_ref,
    xs, wt, vc, vt_ref, o_ref, pm, x_own, up_own, dn_own, load, att_s, att_r, pass_s, pass_r, *sems,
):
    here = Here(nz, ny)
    chips = 2 * nz
    slots = owner_of(chips)
    head = q_ref.shape[1]
    width = x_ref.shape[1]
    tile = 2 * x_ref.shape[0]
    mine, has = head_here(here.chip, slots)
    odd = lax.rem(mine, 2) == 1
    rows_sems, mw_sems, up_sems, dn_sems = sems[:7], sems[7:14], sems[14:21], sems[21:28]

    peers = [here.device(z=here.after(d)) for d in range(1, nz)]
    peers += [here.device(x=1 - here.x), here.device(core=1 - here.core)]
    peers += [here.device(z=here.after(d), x=1 - here.x) for d in range(1, nz)]
    peers += [here.device(y=lax.rem(here.y + e, ny)) for e in range(1, ny)]
    met = greet(peers)
    half = width // 2
    unit = up_ref.shape[1]
    rows_in = unit // 2
    pair_rows = HEADS // 4 * unit
    from_row = lax.broadcasted_iota(jnp.int32, (width, width), 0)
    pm[...] = (from_row == natural_of((1, width), 1, rows_in, ny)).astype(LOW)
    x_own[...] = dot(x_ref[...], pm[...], (1, 0)).astype(LOW)
    dn_own[...] = dot(dn_ref[...], pm[...], (1, 0)).astype(LOW)
    up_own[...] = up_ref[...]
    up_own[4] = dot(up_ref[4], pm[:half, :half], (1, 0)).astype(LOW)
    rows = GatherRows(here, x_own, xs, rows_sems)
    mw = Gather(here, mw_ref, mw_all, True, mw_sems)
    up = Gather(here, up_own, up_all, True, up_sems)
    dn = Gather(here, dn_own, dn_all, False, dn_sems)
    first, later = (rows, mw), (up, dn)
    for item in first + later:
        item.kept.start()
    met()

    def take(items, k):
        def act(source, way):
            for item in items:
                if k:
                    item.take_z(source, way)
            for item in items:
                item.spread(source, k == 0)

        at_distance(here, k, act)

    def then(items, k, stage):
        def act(source, _):
            for item in items:
                getattr(item, stage)(source)

        at_distance(here, k, act)

    for item in first:
        item.start_z()
    take(first, 0)
    for k in range(1, nz):
        take(first, k)
        then(first, k - 1, "second")
    for item in later:
        item.start_z()
    then(first, nz - 1, "second")
    take(later, 0)
    for k in range(nz):
        then((mw,), k, "third")
    mw.kept.wait()
    my_pair = pl.ds(pl.multiple_of(lax.div(mine, 2) * unit, unit), unit)
    pair = pltpu.make_async_copy(mw_all.at[:, :, :, my_pair], wt, load.at[0])
    pair.start()
    vectors = pltpu.make_async_copy(mw_all.at[:, :, :, pl.ds(pair_rows, 16)], vc, load.at[1])
    vectors.start()
    for k in range(nz):
        then((rows,), k, "third")
    rows.kept.wait()
    pair.wait()
    vectors.wait()
    keep_rows = pltpu.make_async_copy(xs.at[here.z, here.x], x2_ref, load.at[2])
    keep_rows.start()

    steps = []
    for k in range(1, nz):
        steps += [partial(take, later, k), partial(then, later, k - 1, "second")]
    steps += [partial(then, later, nz - 1, "second")] + [partial(then, later, k, "third") for k in range(nz)]

    @pl.when(has == 1)
    def _():
        pieces = vc[...].reshape(-1, vc.shape[-1])
        count = 2 * chips * ny
        pick_row = lax.broadcasted_iota(jnp.int32, (count, pieces.shape[0]), 0) * 8
        pick = (pick_row == lax.broadcasted_iota(jnp.int32, pick_row.shape, 1)).astype(LOW)
        pieces = dot(pick, pieces, (1, 0)).astype(LOW)
        lane = lax.broadcasted_iota(jnp.int32, (1, width), 1)
        pair_lane = lax.broadcasted_iota(jnp.int32, (1, 2 * head), 1)
        pair_lane = pair_lane + (here.core * (HEADS // 4) + lax.div(mine, 2)) * 2 * head
        q_row, q_col = bias_piece(pair_lane, rows_in, ny)
        v_row, v_col = bias_piece(pair_lane + width, rows_in, ny)
        none = jnp.full((1, 2 * head), -1, jnp.int32)
        in_row, owner = lax.rem(lane, rows_in), lax.div(lane, rows_in)
        cols = jnp.concatenate([in_row, rows_in + in_row, q_col, none, v_col], axis=1)
        owners = jnp.concatenate([owner, owner, q_row, none, v_row], axis=1)
        spot = lax.broadcasted_iota(jnp.int32, (pieces.shape[1], cols.shape[1]), 0)
        moved = dot(pieces, (spot == cols).astype(LOW), (1, 0))
        from_row = lax.broadcasted_iota(jnp.int32, moved.shape, 0)
        flat = jnp.sum(jnp.where(from_row == owners, moved, 0.0), axis=0, keepdims=True)
        gain, shift, bias = flat[:, :width], flat[:, width : 2 * width], flat[:, 2 * width :]
        weight = wt[...].reshape(width, -1)

        def choose(values):
            return jnp.where(odd, values[:, head:], values[:, :head])

        for i in range(chips):
            span = slice(i * tile, (i + 1) * tile)
            values = xs[i // 2, i % 2].reshape(tile, width).astype(FULL)
            normed, _ = normalize(values)
            low = (normed * gain + shift).astype(LOW)
            h_ref[span, :] = low
            mixed = (dot(low, weight, (1, 0)) + bias).astype(LOW)
            q_ref[span, :] = (choose(mixed[:, : 2 * head]) * (head ** (-0.5))).astype(LOW)
            k_ref[span, :] = choose(mixed[:, 2 * head : 4 * head])
            value = choose(mixed[:, 4 * head :])
            v_ref[span, :] = value
            vt_ref[:, span] = value.T

    def query_tile(i):
        span = slice(i * tile, (i + 1) * tile)
        query = q_ref[span, :]

        def absorb(j, carry, masked):
            top, total, acc = carry
            keys = slice(j * tile, (j + 1) * tile)
            scores = dot(k_ref[keys, :], query, (1, 1))
            if masked:
                key_pos = lax.broadcasted_iota(jnp.int32, scores.shape, 0)
                query_pos = lax.broadcasted_iota(jnp.int32, scores.shape, 1)
                scores = jnp.where(key_pos <= query_pos, scores, NEGATIVE)
            new_top = jnp.maximum(top, jnp.max(scores, axis=0, keepdims=True))
            weights = jnp.exp(scores - new_top)
            keep = jnp.exp(top - new_top)
            total = total * keep + jnp.sum(weights, axis=0, keepdims=True)
            acc = acc * keep + dot(vt_ref[:, keys], weights.astype(LOW), (1, 0))
            return new_top, total, acc

        carry = (jnp.full((1, tile), NEGATIVE, FULL), jnp.zeros((1, tile), FULL), jnp.zeros((head, tile), FULL))
        for j in range(i + 1):
            carry = absorb(j, carry, j == i)
        top, total, acc = carry
        out = acc / total
        ot_ref[:, span] = out
        o_ref[i] = out.T.astype(LOW)
        top_ref[:, span] = top + jnp.log(total)

    def hand(i):
        spot = att_ref.at[here.core, mine]
        return (
            pltpu.make_async_copy(o_ref.at[i], spot, att_s.at[i]),
            remote(o_ref.at[i], spot, att_s.at[i], att_r.at[mine], here.device(z=i // 2, x=i % 2)),
        )

    for i in range(chips):
        @pl.when(has == 1)
        def _(i=i):
            query_tile(i)
            stay, leave = hand(i)
            pl.when(here.chip == i)(stay.start)
            pl.when(here.chip != i)(leave.start)

        if i < len(steps):
            steps[i]()
    for step in steps[chips:]:
        step()

    for i in range(chips):
        @pl.when(has == 1)
        def _(i=i):
            stay, leave = hand(i)
            pl.when(here.chip == i)(stay.wait)
            pl.when(here.chip != i)(leave.wait_send)

    for j, slot in enumerate(slots):
        @pl.when(here.chip != slot)
        def _(j=j, slot=slot):
            spot = att_ref.at[here.core, j]
            remote(spot, spot, att_s.at[0], att_r.at[j], here.device(z=slot // 2, x=slot % 2)).wait_recv()

    spot = att_ref.at[here.core]
    give = remote(spot, spot, pass_s, pass_r, here.device(core=1 - here.core))
    give.start()
    spot = att_ref.at[1 - here.core]
    remote(spot, spot, pass_s, pass_r, here.device(core=1 - here.core)).wait_recv()
    give.wait_send()
    keep_rows.wait()
    for item in later:
        item.kept.wait()
    for item in first + later:
        item.finish()


def attend(nz, ny, own, mw, up, dn):
    span, width = own.shape
    length = 4 * nz * span
    head = width // HEADS
    units = (nz, 2, ny)
    low = jax.ShapeDtypeStruct((length, head), LOW)
    anywhere = pl.BlockSpec(memory_space=pl.ANY)
    vmem = pl.BlockSpec(memory_space=pltpu.VMEM)
    return pl.pallas_call(
        partial(attend_kernel, nz, ny),
        out_shape=(
            jax.ShapeDtypeStruct(units + mw.shape, LOW),
            jax.ShapeDtypeStruct(units + up.shape, LOW),
            jax.ShapeDtypeStruct(units + dn.shape, LOW),
            jax.ShapeDtypeStruct((length, width), LOW),
            low,
            low,
            low,
            jax.ShapeDtypeStruct((head, length), FULL),
            jax.ShapeDtypeStruct((1, length), FULL),
            jax.ShapeDtypeStruct((2, HEADS // 2, 2 * span, head), LOW),
            jax.ShapeDtypeStruct((2, span, width), LOW),
        ),
        in_specs=[vmem] * 4,
        out_specs=[anywhere] * 3 + [vmem] * 6 + [anywhere] * 2,
        scratch_shapes=[
            pltpu.VMEM((nz, 2, 2, span, width), LOW),
            pltpu.VMEM(units + up.shape[1:], LOW),
            pltpu.VMEM(units + (16,) + mw.shape[1:], LOW),
            pltpu.VMEM((head, length), LOW),
            pltpu.VMEM((2 * nz, 2 * span, head), LOW),
            pltpu.VMEM((width, width), LOW),
            pltpu.VMEM(own.shape, LOW),
            pltpu.VMEM(up.shape, LOW),
            pltpu.VMEM(dn.shape, LOW),
            DMA((3,)),
            DMA((2 * nz,)),
            DMA((HEADS // 2,)),
            DMA,
            DMA,
        ]
        + GatherRows.scratch(nz)
        + Gather.scratch(nz, ny) * 3,
        compiler_params=pltpu.CompilerParams(vmem_limit_bytes=56 << 20, collective_id=0, has_side_effects=True),
        cost_estimate=pl.CostEstimate(
            flops=6 * length * length * head, bytes_accessed=8 * length * width, transcendentals=length * length
        ),
        name="attend",
    )(own, mw, up, dn)


GELU_K = 0.7978845608028654
GELU_C = 0.044715


def gelu_pair(u):
    square = u * u
    tanh = jnp.tanh(GELU_K * u * (1.0 + GELU_C * square))
    half = 0.5 * (1.0 + tanh)
    slope = half + (0.5 * GELU_K) * u * (1.0 - tanh * tanh) * (1.0 + 3.0 * GELU_C * square)
    return u * half, slope


def split_dot(values, turn, dims):
    high = values.astype(LOW)
    rest = values - high.astype(FULL)
    middle = rest.astype(LOW)
    low = (rest - middle.astype(FULL)).astype(LOW)
    return dot(high, turn, dims) + dot(middle, turn, dims) + dot(low, turn, dims)


def rest_kernel(
    nz, hidden_tile,
    x2_ref, att_ref, cot_ref, mw_all, up_ref, dn_ref,
    q_ref, k_ref, v_ref, ot_ref, top_ref, h_all,
    act_ref, ing_ref, fin, swap, mixf, mix_swap, vec_ref,
    up, dn, ow, own, pm, vc, att, cot, h2, act_low, gu, branch, feed, feed_in, gh2, gh2_in, gmid, eb, grads, go_send,
    go_all, kt_ref, got_ref, delta_ref, gqt_ref, gsend, gat, mw, hbuf, head_acc, head_sum, hs_in, mix_in,
    r1, r2, r3, pack, vec_in,
    load, near_s, near_r, h_s, go_s, go_r, kv_s, kv_r, q_s, q_r, s1, t1, s2, t2, s3, t3, ex_s, ex_r,
    vec_s, vec_r, mix_s, mix_r,
):
    ny = 2
    here = Here(nz, ny)
    core, chip, x, y, z = here.core, here.chip, here.x, here.y, here.z
    chips = 2 * nz
    parts = 4 * nz * ny
    slots = owner_of(chips)
    per_core = len(slots)
    length, head = q_ref.shape
    tile = length // chips
    _, span, width = cot_ref.shape
    half = width // 2
    hidden = dn_ref.shape[0]
    rows_hid = 2 * hidden // parts
    factor = head ** (-0.5)
    job, has = head_here(chip, slots)
    partner = here.device(core=1 - core)
    slabs, unit = grads.shape[4], grads.shape[5]
    pairs = per_core // 2
    rows_in = unit // 2
    my_rows = pl.ds(pl.multiple_of(core * span, span), span)
    their_rows = pl.ds(pl.multiple_of((1 - core) * span, span), span)

    def flat(zz, xx, yy, cc):
        return ((zz * 2 + xx) * ny + yy) * 2 + cc

    others = []
    for dz in range(nz):
        for dx in range(2):
            for dy in range(ny):
                for dc in range(2):
                    if dz or dx or dy or dc:
                        zz = lax.rem(z + dz, nz)
                        xx = 1 - x if dx else x
                        yy = 1 - y if dy else y
                        cc = 1 - core if dc else core
                        behind = (lax.rem(z + nz - dz, nz), xx, yy, cc)
                        others.append((here.device(zz, xx, cc, yy), flat(zz, xx, yy, cc), flat(*behind)))

    loads = [
        pltpu.make_async_copy(up_ref.at[:, :, :, 4], ow.at[core], load.at[0]),
        pltpu.make_async_copy(mw_all.at[:, :, :, pl.ds(pairs * unit, 16)], vc, load.at[1]),
        pltpu.make_async_copy(dn_ref, dn, load.at[2]),
        pltpu.make_async_copy(mw_all.at[:, :, :, pl.ds(0, pairs * unit)], mw, load.at[3]),
    ]
    for t in range(4):
        spot = up.at[:, :, :, :, pl.ds(t * half, half)]
        loads.append(pltpu.make_async_copy(up_ref.at[:, :, :, t], spot, load.at[4 + t]))
    for copy in loads:
        copy.start()
    met = greet([device for device, _, _ in others])

    def pass_on(i, src, dst):
        return remote(src, dst, near_s.at[i], near_r.at[i], partner)

    natural = natural_of((1, width), 1, rows_in, ny)
    from_row = lax.broadcasted_iota(jnp.int32, (width, width), 0)
    pm[...] = (from_row == natural).astype(LOW)
    for d in range(2):
        cot[d, my_rows, :] = dot(cot_ref[d], pm[...], (1, 0)).astype(LOW)
    met()
    give_cot = pass_on(0, cot.at[:, my_rows], cot.at[:, my_rows])
    give_cot.start()
    loads[0].wait()
    give_ow = pass_on(1, ow.at[core], ow.at[core])
    give_ow.start()

    wide = lax.broadcasted_iota(jnp.int32, (1, width), 1)
    wide_owner = lax.div(wide, rows_in)
    hid = lax.broadcasted_iota(jnp.int32, (1, hidden), 1)
    hid_owner = lax.div(hid, rows_hid) * 2 + core
    in_row = lax.rem(wide, rows_in)
    cols = [in_row + i * rows_in for i in (2, 3, 4, 5, 0)] + [lax.rem(hid, rows_hid) + 8 * rows_in]
    cols = jnp.concatenate(cols, axis=1)
    owners = jnp.concatenate([wide_owner] * 5 + [hid_owner], axis=1)
    loads[1].wait()
    pieces = vc[...].reshape(-1, vc.shape[-1])
    pick_row = lax.broadcasted_iota(jnp.int32, (parts, pieces.shape[0]), 0) * 8
    pick = (pick_row == lax.broadcasted_iota(jnp.int32, pick_row.shape, 1)).astype(LOW)
    pieces = dot(pick, pieces, (1, 0)).astype(LOW)
    spot = lax.broadcasted_iota(jnp.int32, (pieces.shape[1], cols.shape[1]), 0)
    moved = dot(pieces, (spot == cols).astype(LOW), (1, 0))
    piece_row = lax.broadcasted_iota(jnp.int32, moved.shape, 0)
    vectors = jnp.sum(jnp.where(piece_row == owners, moved, 0.0), axis=0, keepdims=True)
    gain, shift, out_bias, down_bias, first_gain = (vectors[:, i * width : (i + 1) * width] for i in range(5))
    up_bias = vectors[:, 5 * width :]

    natural_att = jnp.concatenate([att_ref[c, j] for c in range(2) for j in range(per_core)], axis=1)
    att[...] = dot(natural_att, pm[...], (1, 0)).astype(LOW)
    remote(ow.at[1 - core], ow.at[1 - core], near_s.at[1], near_r.at[1], partner).wait_recv()
    for c in range(2):
        own[:, c * half : (c + 1) * half] = dot(pm[...], ow[c].reshape(width, half), (1, 0)).astype(LOW)
    branch[...] = dot(natural_att, own[...], (1, 0)) + out_bias

    def middle_of(d, rows):
        return x2_ref[rows, :].astype(FULL) + SCALES[d] * branch[rows, :]

    for d in range(2):
        n, _ = normalize(middle_of(d, slice(None)))
        h2[d] = (n * gain + shift).astype(LOW)
    theirs_cot = cot.at[:, their_rows]
    remote(theirs_cot, theirs_cot, near_s.at[0], near_r.at[0], partner).wait_recv()
    loads[2].wait()
    for copy in loads[4:]:
        copy.wait()

    def up_cols(cut):
        return up[:, :, :, :, cut].reshape(width, -1)

    def upstream(d):
        return (SCALES[d] * cot[d].astype(FULL)).astype(LOW)

    stride = pack.shape[1] * pack.shape[2] // 2
    lane = lax.broadcasted_iota(jnp.int32, (width, 128), 0)
    in_piece = (lax.rem(lane, rows_in) == lax.broadcasted_iota(jnp.int32, lane.shape, 1)).astype(LOW)

    def placed(vector, owner, turn, start):
        rows = lax.broadcasted_iota(jnp.int32, (parts, vector.shape[1]), 0)
        spread = jnp.where(rows == owner, vector, 0.0)
        high = spread.astype(LOW)
        low = (spread - high.astype(FULL)).astype(LOW)
        values = dot(high, turn, (1, 0)) + dot(low, turn, (1, 0))
        return jnp.pad(values, ((0, 0), (start, 2 * stride)))[:, : 2 * stride]

    sums = {}

    def row_sum(v, d, values):
        sums[v, d] = jnp.sum(values, axis=0, keepdims=True)

    exchanges = []

    def forth(d):
        low_in = upstream(d)
        ups = []
        for t in range(0, hidden, hidden_tile):
            cut = slice(t, t + hidden_tile)
            u = dot(h2[d], up_cols(cut), (1, 0)) + up_bias[:, cut]
            active, slope = gelu_pair(u)
            active = active.astype(LOW)
            act_low[d, :, cut] = active
            grad = (dot(low_in, dn[cut, :], (1, 1)) * slope).astype(LOW)
            gu[d, :, cut] = grad
            ups.append(jnp.sum(grad.astype(FULL), axis=0, keepdims=True))
        sums["up", d] = jnp.concatenate(ups, axis=1)

    def back_to_width(d):
        gh2[d] = dot(gu[d], up_cols(slice(None)), (1, 1))
        feed[d] = dot(act_low[d], dn[...], (1, 0))
        for i, (src, dst) in ((2, (gh2, gh2_in)), (4, (feed, feed_in))):
            copy = pass_on(i + d, src.at[d, their_rows], dst.at[d])
            copy.start()
            exchanges.append(copy)

    def keep(d, values, first_row, first_col, base, rows_of):
        for i in range(0, values.shape[0], unit):
            row = first_row + i
            u, within = row // rows_of, (row % rows_of) // unit
            place = (u // (2 * ny), (u // ny) % 2, u % ny)
            for c in range(0, values.shape[1], half):
                slab = base + within * 2 + (first_col + c) // half
                grads[(d,) + place + (slab,)] = values[i : i + unit, c : c + half]

    def down_grads(d):
        low_in = upstream(d)
        for t in range(0, hidden, half):
            keep(d, dot(act_low[d, :, t : t + half], low_in, (0, 0)).astype(LOW), t, 0, 0, 2 * unit)

    def up_grads(d):
        for t in range(0, hidden, 2 * half):
            for m in range(0, width, half):
                part = dot(h2[d, :, m : m + half], gu[d, :, t : t + 2 * half], (0, 0)).astype(LOW)
                keep(d, part, m, t, 4, unit)

    def norm_feed_back(d):
        remote(gh2_in.at[d], gh2_in.at[d], near_s.at[2 + d], near_r.at[2 + d], partner).wait_recv()
        grad = gh2[d, my_rows, :] + gh2_in[d]
        n, r = normalize(middle_of(d, my_rows))
        row_sum(2, d, grad * n)
        row_sum(3, d, grad)
        own_cot = cot[d, my_rows, :].astype(FULL)
        middle_grad = own_cot + norm_back(grad, n, r, gain)
        gmid[d] = middle_grad
        branch_low = (SCALES[d] * middle_grad).astype(LOW)
        row_sum(4, d, branch_low.astype(FULL))
        row_sum(5, d, (SCALES[d] * own_cot).astype(LOW).astype(FULL))
        eb[d, my_rows, :] = branch_low
        copy = pass_on(6 + d, eb.at[d, my_rows], eb.at[d, my_rows])
        copy.start()
        exchanges.append(copy)

    zis = []
    for i in range((nz + 1) // 2):
        zis += [nz - 1 - i] + ([i] if i != nz - 1 - i else [])
    cuts = [(0, slabs // 2), (slabs // 2, slabs)]
    chunks = [(zi, part) for part in range(len(cuts)) for zi in zis]

    def y_first(d, zi, part):
        return d == 0 or chunks.index((zi, part)) % 2 == 1

    def mine(d, zi, part, i, slab):
        return grads.at[d, zi, i, y, slab] if y_first(d, zi, part) else grads.at[d, zi, x, i, slab]

    def some(part):
        return pl.ds(cuts[part][0], cuts[part][1] - cuts[part][0])

    def stage1(d, zi, part):
        slab = some(part)
        if y_first(d, zi, part):
            src, to = grads.at[d, zi, :, 1 - y, slab], here.device(y=1 - y)
        else:
            src, to = grads.at[d, zi, 1 - x, :, slab], here.device(x=1 - x)
        return remote(src, r1.at[d, zi, :, slab], s1.at[d, zi, part], t1.at[d, zi, part], to)

    def stage2(d, zi, part):
        slab = some(part)
        if y_first(d, zi, part):
            src, to = mine(d, zi, part, 1 - x, slab), here.device(x=1 - x)
        else:
            src, to = mine(d, zi, part, 1 - y, slab), here.device(y=1 - y)
        return remote(src, r2.at[d, zi, slab], s2.at[d, zi, part], t2.at[d, zi, part], to)

    def spare(zi, up):
        return zi if up else jnp.where(z - 1 == zi, nz, zi)

    def stage3(d, zi, part, up):
        to = here.device(z=lax.min(z + 1, nz - 1)) if up else here.device(z=lax.max(z - 1, 0))
        way = 0 if up else 1
        slab = some(part)
        src, dst = r2.at[d, zi, slab], r3.at[d, spare(zi, up), slab]
        return remote(src, dst, s3.at[d, zi, part], t3.at[d, way, zi, part], to)

    def arrive3(d, zi, part, up):
        way = 0 if up else 1
        spot = r3.at[d, zi, some(part)]
        return remote(spot, spot, s3.at[d, zi, part], t3.at[d, way, zi, part], partner)

    def begin(d, n):
        if n < len(chunks):
            stage1(d, *chunks[n]).start()

    def add_into(target, other, lead):
        def one(i, _):
            a, b = target(i), other(i)
            a[...] = (a[...].astype(FULL) + b[...].astype(FULL)).astype(LOW)
            return 0

        lax.fori_loop(0, lead, one, 0)

    def after1(d, zi, part):
        stage1(d, zi, part).wait_recv()
        low, high = cuts[part]
        size = high - low
        add_into(
            lambda i: mine(d, zi, part, lax.div(i, size), low + lax.rem(i, size)),
            lambda i: r1.at[d, zi, lax.div(i, size), low + lax.rem(i, size)],
            2 * size,
        )
        stage2(d, zi, part).start()

    def after2(d, zi, part):
        low, high = cuts[part]
        stage2(d, zi, part).wait_recv()
        own_place = x if y_first(d, zi, part) else y
        add_into(lambda i: r2.at[d, zi, low + i], lambda i: mine(d, zi, part, own_place, low + i), high - low)
        if zi > 0:
            pl.when(z == 0)(stage3(d, zi, part, True).start)
        if zi < nz - 1:
            pl.when(z == nz - 1)(stage3(d, zi, part, False).start)

    def after3(d, zi, part, far):
        low, high = cuts[part]
        if far < zi:
            @pl.when(z == far)
            def _():
                arrive3(d, zi, part, True).wait_recv()
                add_into(lambda i: r2.at[d, zi, low + i], lambda i: r3.at[d, zi, low + i], high - low)
                stage3(d, zi, part, True).start()

        if nz - 1 - far > zi:
            @pl.when(z == nz - 1 - far)
            def _():
                arrive3(d, zi, part, False).wait_recv()
                add_into(lambda i: r2.at[d, zi, low + i], lambda i: r3.at[d, zi, low + i], high - low)
                stage3(d, zi, part, False).start()

    def last3(d, zi, part):
        low, high = cuts[part]

        @pl.when(z == zi)
        def _():
            if zi > 0:
                arrive3(d, zi, part, True).wait_recv()
            if zi < nz - 1:
                arrive3(d, zi, part, False).wait_recv()

            def one(i, _):
                total = r2[d, zi, i].astype(FULL)
                if zi > 0:
                    total = total + r3[d, zi, i].astype(FULL)
                if zi < nz - 1:
                    total = total + r3[d, nz, i].astype(FULL)
                fin[d, i] = total
                return 0

            lax.fori_loop(low, high, one, 0)

    def advance(n):
        stages = [after1, after2] + [partial(after3, far=far) for far in range(1, nz - 1)] + [last3]
        for behind, stage in enumerate(stages):
            for d in range(2):
                if 0 <= n - behind < len(chunks):
                    stage(d, *chunks[n - behind])
                if not behind:
                    begin(d, n + 2)

    steps = len(chunks) + nz

    def finish_sends():
        for zi, part in chunks:
            for d in range(2):
                stage1(d, zi, part).wait_send()
                stage2(d, zi, part).wait_send()
                pl.when(z != zi)(stage3(d, zi, part, True).wait_send)

    for d in range(2):
        forth(d)
        down_grads(d)
        begin(d, 0)
        begin(d, 1)
    for d in range(2):
        back_to_width(d)
    up_grads(0)
    norm_feed_back(0)
    up_grads(1)
    norm_feed_back(1)

    def go_copies(j):
        slot = slots[j]
        return (
            pltpu.make_async_copy(go_send.at[j], go_all.at[chip], go_s.at[j]),
            remote(go_send.at[j], go_all.at[chip], go_s.at[j], go_r.at[chip], here.device(z=slot // 2, x=slot % 2)),
        )

    own_half = own.at[pl.ds(pl.multiple_of(core * half, half), half), :]
    for d in range(2):
        spot = eb.at[d, their_rows]
        remote(spot, spot, near_s.at[6 + d], near_r.at[6 + d], partner).wait_recv()
        go = dot(eb[d], own_half[...], (1, 1)).astype(LOW)
        for j in range(per_core):
            go_send[j, :, d * head : (d + 1) * head] = go[:, j * head : (j + 1) * head]
    for j, slot in enumerate(slots):
        stay, leave = go_copies(j)
        pl.when(chip == slot)(stay.start)
        pl.when(chip != slot)(leave.start)
    for d in range(2):
        ours = eb[d, :, pl.ds(pl.multiple_of(core * half, half), half)]
        for m in range(0, width, half):
            keep(d, dot(att[:, m : m + half], ours, (0, 0)).astype(LOW), m, 0, 8, unit)

    for d in range(2):
        remote(feed_in.at[d], feed_in.at[d], near_s.at[4 + d], near_r.at[4 + d], partner).wait_recv()
        out = middle_of(d, my_rows) + SCALES[d] * (feed[d, my_rows, :] + feed_in[d] + down_bias)
        act_ref[d] = out.astype(LOW)
    total = jnp.zeros((parts, 2 * stride), FULL)
    for v in range(2, 6):
        for d in range(2):
            total = total + placed(sums[v, d], wide_owner, in_piece, v * rows_in + d * stride)
    hid_lane = lax.broadcasted_iota(jnp.int32, (hidden, 128), 0)
    in_hidden = (lax.rem(hid_lane, rows_hid) == lax.broadcasted_iota(jnp.int32, hid_lane.shape, 1)).astype(LOW)
    for d in range(2):
        total = total + placed(sums["up", d], hid_owner, in_hidden, 8 * rows_in + d * stride)
    for c in range(pack.shape[1]):
        pack[:, c, :] = total[:, c * 128 : (c + 1) * 128]
    advance(0)

    def h_copy(i):
        rows = slice(i * tile, (i + 1) * tile)
        return pltpu.make_async_copy(h_all.at[rows], hbuf.at[i % 2], h_s.at[i % 2])

    @pl.when(has == 1)
    def _():
        h_copy(0).start()
        h_copy(1).start()
        for t in range(chips):
            stay = pltpu.make_async_copy(go_send.at[0], go_all.at[t], go_s.at[job])
            come = remote(go_send.at[0], go_all.at[t], go_s.at[0], go_r.at[t], here.device(z=t // 2, x=t % 2))
            pl.when(chip == t)(stay.wait)
            pl.when(chip != t)(come.wait_recv)
        for i in range(chips):
            rows = slice(i * tile, (i + 1) * tile)
            kt_ref[:, rows] = k_ref[rows, :].T
            up_t = go_all[i].T
            for d in range(2):
                part = up_t[d * head : (d + 1) * head, :]
                got_ref[d, :, rows] = part
                delta_ref[d, :, rows] = jnp.sum(part.astype(FULL) * ot_ref[:, rows], axis=0, keepdims=True)
                gqt_ref[d, :, rows] = jnp.zeros((head, tile), FULL)

    def key_tile(j):
        keys = slice(j * tile, (j + 1) * tile)
        key = k_ref[keys, :]
        value = v_ref[keys, :]
        key_t = kt_ref[:, keys]

        def step(i, carry, masked):
            gv, gk0, gk1 = carry
            rows = pl.ds(i * tile if masked else pl.multiple_of(i * tile, tile), tile)
            query = q_ref[rows, :]
            scores = dot(key, query, (1, 1))
            if masked:
                key_pos = lax.broadcasted_iota(jnp.int32, scores.shape, 0)
                query_pos = lax.broadcasted_iota(jnp.int32, scores.shape, 1)
                scores = jnp.where(key_pos <= query_pos, scores, NEGATIVE)
            probs = jnp.exp(scores - top_ref[:, rows])
            gv = gv + dot(probs.astype(LOW), go_all[i], (1, 0))
            gks = [gk0, gk1]
            for d in range(2):
                prob_grad = dot(value, got_ref[d, :, rows], (1, 0))
                score_low = (probs * (prob_grad - delta_ref[d, :, rows])).astype(LOW)
                gks[d] = gks[d] + dot(score_low, query, (1, 0))
                gqt_ref[d, :, rows] += dot(key_t, score_low, (1, 0))
            return gv, gks[0], gks[1]

        zero = jnp.zeros((tile, head), FULL)
        carry = step(j, (jnp.zeros((tile, 2 * head), FULL), zero, zero), True)
        gv, gk0, gk1 = lax.fori_loop(j + 1, chips, lambda i, c: step(i, c, False), carry)
        gsend[j, 1] = jnp.concatenate([gk0, gk1], axis=1).astype(LOW)
        gsend[j, 2] = gv.astype(LOW)

    def kv_copies(t):
        src, dst = gsend.at[t, pl.ds(1, 2)], gat.at[job, pl.ds(1, 2)]
        to = here.device(z=t // 2, x=t % 2)
        return pltpu.make_async_copy(src, dst, kv_s.at[t]), remote(src, dst, kv_s.at[t], kv_r.at[job], to)

    def q_copies(t):
        src, dst = gsend.at[t, 0], gat.at[job, 0]
        to = here.device(z=t // 2, x=t % 2)
        return pltpu.make_async_copy(src, dst, q_s.at[t]), remote(src, dst, q_s.at[t], q_r.at[job], to)

    def launch(copies, t):
        stay, leave = copies(t)
        pl.when(chip == t)(stay.start)
        pl.when(chip != t)(leave.start)

    between = {1: 1, 3: 2, 7: 3}
    for j in range(chips):
        @pl.when(has == 1)
        def _(j=j):
            key_tile(j)
            launch(kv_copies, j)

        if j in between:
            advance(between[j])

    @pl.when(has == 1)
    def _():
        for i in range(chips):
            rows = slice(i * tile, (i + 1) * tile)
            both = jnp.concatenate([gqt_ref[0, :, rows], gqt_ref[1, :, rows]], axis=0) * factor
            gsend[i, 0] = both.T.astype(LOW)
            launch(q_copies, i)

    def mix_y():
        return remote(head_sum.at[:, :, 1 - y], hs_in, ex_s.at[0], ex_r.at[0], here.device(y=1 - y))

    def mix_copies(t):
        src, dst = head_sum.at[t // 2, t % 2, y], mix_in.at[job]
        to = here.device(z=t // 2, x=t % 2)
        return pltpu.make_async_copy(src, dst, mix_s.at[t]), remote(src, dst, mix_s.at[t], mix_r.at[job], to)

    @pl.when(has == 1)
    def _():
        for i in range(chips):
            h_copy(i).wait()
            right = jnp.concatenate([gsend[i, t] for t in range(3)], axis=1)
            part = dot(hbuf[i % 2], right, (0, 0))
            if i == 0:
                head_acc[...] = part
            else:
                head_acc[...] += part
            if i + 2 < chips:
                h_copy(i + 2).start()
        for u in range(parts // 2):
            zz, xx, yy = u // (2 * ny), (u // ny) % 2, u % ny
            head_sum[zz, xx, yy] = head_acc[u * unit : (u + 1) * unit, :].astype(LOW)
        mix_y().start()

    advance(4)

    @pl.when(has == 1)
    def _():
        mix_y().wait_recv()
        mix_y().wait_send()
        add_into(
            lambda i: head_sum.at[lax.div(i, 2), lax.rem(i, 2), y],
            lambda i: hs_in.at[lax.div(i, 2), lax.rem(i, 2)],
            chips,
        )
        for t in range(chips):
            launch(mix_copies, t)

    biases = []
    for t in (0, 2):
        acc = jnp.zeros((1, 2 * head), FULL)
        for i in range(chips):
            acc = acc + jnp.sum(gsend[i, t].astype(FULL), axis=0, keepdims=True)
        biases.append(jnp.where(has == 1, acc, 0.0))
    total = jnp.concatenate([pack[:, c, :] for c in range(pack.shape[1])], axis=1)
    for b in range(2):
        rows = lax.broadcasted_iota(jnp.int32, (parts, 2 * head), 0)
        first_entry = (core * per_core + job) * head + b * width
        across = lax.broadcasted_iota(jnp.int32, (1, 2 * head), 1)
        down_lane = lax.broadcasted_iota(jnp.int32, (2 * head, 1), 0)
        owner, _ = bias_piece(lax.rem(across, head) + first_entry, rows_in, ny)
        _, column = bias_piece(lax.rem(down_lane, head) + first_entry, rows_in, ny)
        column = column + lax.div(down_lane, head) * stride
        spread = jnp.where(rows == owner, biases[b], 0.0)
        turn = lax.broadcasted_iota(jnp.int32, (2 * head, 2 * stride), 1) == column
        high = spread.astype(LOW)
        low = (spread - high.astype(FULL)).astype(LOW)
        total = total + dot(high, turn.astype(LOW), (1, 0)) + dot(low, turn.astype(LOW), (1, 0))
    advance(5)

    for copy in exchanges:
        copy.wait_send()
    loads[3].wait()
    for j, slot in enumerate(slots):
        @pl.when(chip != slot)
        def _(j=j, slot=slot):
            to = here.device(z=slot // 2, x=slot % 2)
            remote(gat.at[j, pl.ds(1, 2)], gat.at[j, pl.ds(1, 2)], kv_s.at[0], kv_r.at[j], to).wait_recv()
            remote(gat.at[j, 0], gat.at[j, 0], q_s.at[0], q_r.at[j], to).wait_recv()

        @pl.when(chip == slot)
        def _(j=j, slot=slot):
            kv_copies(slot)[0].wait()
            q_copies(slot)[0].wait()

    def first_swap(d):
        return remote(gh2.at[d, their_rows], gh2_in.at[d], ex_s.at[1 + d], ex_r.at[1 + d], partner)

    for d in range(2):
        lanes = slice(d * head, (d + 1) * head)
        first = None
        for p in range(per_core // 2):
            left = jnp.concatenate(
                [gat[2 * p + o, t][:, lanes] for t in range(3) for o in range(2)], axis=1
            )
            part = dot(left, mw[:, :, :, p * unit : (p + 1) * unit].reshape(width, half), (1, 1))
            first = part if first is None else first + part
        gh2[d] = first
        first_swap(d).start()
    normed, inv = normalize(x2_ref[my_rows, :].astype(FULL))
    for d in range(2):
        first_swap(d).wait_recv()
        grad = gh2[d, my_rows, :] + gh2_in[d]
        for v, row in ((0, jnp.sum(grad * normed, axis=0, keepdims=True)), (1, jnp.sum(grad, axis=0, keepdims=True))):
            total = total + placed(row, wide_owner, in_piece, v * rows_in + d * stride)
        whole = gmid[d] + norm_back(grad, normed, inv, first_gain)
        ing_ref[d] = whole
    for c in range(pack.shape[1]):
        pack[:, c, :] = total[:, c * 128 : (c + 1) * 128]
    me = flat(z, x, y, core)

    def vec_copy(n):
        device, index, _ = others[n]
        return remote(pack.at[index], vec_in.at[me], vec_s.at[n], vec_r.at[n], device)

    def vec_come(n):
        device, _, index = others[n]
        return remote(pack.at[index], vec_in.at[index], vec_s.at[n], vec_r.at[n], device)

    for n in range(len(others)):
        vec_copy(n).start()

    for n in range(6, steps - 1):
        advance(n)
    mine_in = pl.ds(pl.multiple_of(core * rows_in, 8), rows_in)
    their_in = pl.ds(pl.multiple_of((1 - core) * rows_in, 8), rows_in)
    for j, slot in enumerate(slots):
        @pl.when(chip != slot)
        def _(j=j, slot=slot):
            to = here.device(z=slot // 2, x=slot % 2)
            remote(mix_in.at[j], mix_in.at[j], mix_s.at[0], mix_r.at[j], to).wait_recv()

        @pl.when(chip == slot)
        def _(j=j, slot=slot):
            mix_copies(slot)[0].wait()

        mixf[j] = mix_in[j].astype(FULL)
    mix_pass = remote(mixf.at[:, their_in], mix_swap, ex_s.at[5], ex_r.at[5], partner)
    mix_pass.start()

    for n in range(steps - 1, steps):
        advance(n)

    def last_swap(d):
        return remote(fin.at[d, pl.ds(4, slabs - 4), their_in], swap.at[d], ex_s.at[3 + d], ex_r.at[3 + d], partner)

    for d in range(2):
        last_swap(d).start()
    for d in range(2):
        last_swap(d).wait_recv()
    mix_pass.wait_recv()
    for n in range(len(others)):
        vec_come(n).wait_recv()
    vec_in[me] = pack[me]
    vec_ref[...] = jnp.sum(vec_in[...], axis=0)

    give_cot.wait_send()
    give_ow.wait_send()
    finish_sends()
    for j, slot in enumerate(slots):
        pl.when(chip != slot)(go_copies(j)[1].wait_send)

    @pl.when(has == 1)
    def _():
        for t in range(chips):
            @pl.when(chip != t)
            def _(t=t):
                kv_copies(t)[1].wait_send()
                q_copies(t)[1].wait_send()
                mix_copies(t)[1].wait_send()

    for d in range(2):
        first_swap(d).wait_send()
        last_swap(d).wait_send()
    mix_pass.wait_send()
    for n in range(len(others)):
        vec_copy(n).wait_send()


def finish_kernel(
    nz, act, ing, fin, swap, mixf, mix_swap, vec,
    act_ref, ing_ref, gain1_ref, shift1_ref, mix_ref, mixb_ref, out_ref, outb_ref, gain2_ref, shift2_ref, up_ref, upb_ref,
    dn_ref, dnb_ref,
):
    ny = 2
    core = lax.rem(lax.axis_index("seq"), 2)
    width = ing.shape[2]
    slabs, unit = fin.shape[1], fin.shape[2]
    rows_in = unit // 2
    per_core, head = mixf.shape[0], width // HEADS
    from_row = lax.broadcasted_iota(jnp.int32, (width, width), 0)
    turn = (from_row == natural_of((1, width), 1, rows_in, ny)).astype(LOW)
    mine_in = pl.ds(pl.multiple_of(core * rows_in, 8), rows_in)
    is_first = core == 0

    def by_core(a, b):
        return jnp.where(is_first, a, b), jnp.where(is_first, b, a)

    hidden = (slabs - 5) * fin.shape[3]
    block = hidden // (2 * nz)
    sides = [by_core(mixf[j, mine_in, :], mix_swap[j]) for j in range(per_core)]
    for d in range(2):
        act_ref[d] = dot(act[d], turn, (1, 1)).astype(LOW)
        top_half = jnp.concatenate([fin[d, 0], fin[d, 1]], axis=1)
        low_half = jnp.concatenate([fin[d, 2], fin[d, 3]], axis=1)
        ours = jnp.concatenate([fin[d, s, mine_in, :] for s in range(4, slabs - 1)], axis=1)
        came = jnp.concatenate([swap[d, s] for s in range(slabs - 5)], axis=1)
        one, two = by_core(ours, came)
        blocks = []
        for i in range(hidden // block):
            blocks += [one[:, i * block : (i + 1) * block], two[:, i * block : (i + 1) * block]]
        up_ref[d] = jnp.concatenate(blocks, axis=1)
        one, two = by_core(fin[d, slabs - 1, mine_in, :], swap[d, slabs - 5])
        stacked = [ing[d], top_half, low_half, jnp.concatenate([one, two], axis=1)]
        moved = split_dot(jnp.concatenate(stacked, axis=0), turn, (1, 1))
        span = ing.shape[1]
        ing_ref[d] = moved[:span]
        dn_ref[d] = moved[span : span + 2 * unit]
        out_ref[d] = moved[span + 2 * unit :]
        blocks = []
        for t in range(3):
            for c in range(2):
                for j in range(per_core):
                    start = t * 2 * head + d * head
                    blocks.append(sides[j][c][:, start : start + head])
        mix_ref[d] = jnp.concatenate(blocks, axis=1)
    flat = jnp.concatenate([vec[c : c + 1, :] for c in range(vec.shape[0])], axis=1)
    stride = flat.shape[1] // 2
    smalls = (gain1_ref, shift1_ref, gain2_ref, shift2_ref, outb_ref, dnb_ref, mixb_ref, upb_ref)
    start = 0
    for ref in smalls:
        size = ref.shape[1]
        for d in range(2):
            ref[d : d + 1, :] = flat[:, d * stride + start : d * stride + start + size]
        start += size


def finish(nz, act, ing, fin, swap, mixf, mix_swap, vec):
    width = ing.shape[2]
    slabs, unit, half = fin.shape[1:]
    rows_in = unit // 2
    hidden = (slabs - 5) * half

    def full(*shape):
        return jax.ShapeDtypeStruct((2,) + shape, FULL)

    small = full(rows_in)
    return pl.pallas_call(
        partial(finish_kernel, nz),
        out_shape=(
            jax.ShapeDtypeStruct(act.shape, LOW), jax.ShapeDtypeStruct(ing.shape, FULL), small, small,
            full(rows_in, 3 * width), full(2 * rows_in), full(rows_in, width), small, small, small,
            full(rows_in, 2 * hidden), full(2 * unit), full(2 * unit, width), small,
        ),
        compiler_params=pltpu.CompilerParams(vmem_limit_bytes=60 << 20),
        name="finish",
    )(act, ing, fin, swap, mixf, mix_swap, vec)


def rest(nz, x2, attended, cot, mw_all, up, dn, q, k, v, out_t, top, first_low):
    length, head = q.shape
    _, span, width = cot.shape
    hidden = dn.shape[0]
    half = width // 2
    chips = 2 * nz
    parts = 8 * nz
    rows = 2 * span
    per_core = HEADS // 2
    unit = up.shape[4]
    units = mw_all.shape[:3]
    rows_in = unit // 2
    slabs = 9
    anywhere = pl.BlockSpec(memory_space=pl.ANY)
    vmem = pl.BlockSpec(memory_space=pltpu.VMEM)
    low, full = partial(pltpu.VMEM, dtype=LOW), partial(pltpu.VMEM, dtype=FULL)
    return pl.pallas_call(
        partial(rest_kernel, nz, 512),
        out_shape=(
            jax.ShapeDtypeStruct((2, span, width), LOW),
            jax.ShapeDtypeStruct((2, span, width), FULL),
            jax.ShapeDtypeStruct((2, slabs, unit, half), FULL),
            jax.ShapeDtypeStruct((2, slabs - 4, rows_in, half), FULL),
            jax.ShapeDtypeStruct((per_core, unit, half), FULL),
            jax.ShapeDtypeStruct((per_core, rows_in, half), FULL),
            jax.ShapeDtypeStruct((5, 128), FULL),
        ),
        in_specs=[vmem] * 3 + [anywhere] * 3 + [vmem] * 5 + [anywhere],
        out_specs=[vmem] * 7,
        scratch_shapes=[
            low(units + (unit, hidden)),
            low((hidden, width)),
            low((2,) + units + (unit, half)),
            low((width, width)),
            low((width, width)),
            low(units + (16, half)),
            low((rows, width)),
            low((2, rows, width)),
            low((2, rows, width)),
            low((2, rows, hidden)),
            low((2, rows, hidden)),
            full((rows, width)),
            full((2, rows, width)),
            full((2, span, width)),
            full((2, rows, width)),
            full((2, span, width)),
            full((2, span, width)),
            low((2, rows, width)),
            low((2,) + units + (slabs, unit, half)),
            low((per_core, rows, 2 * head)),
            low((chips, rows, 2 * head)),
            low((head, length)),
            low((2, head, length)),
            full((2, 1, length)),
            full((2, head, length)),
            low((chips, 3, rows, 2 * head)),
            low((per_core, 3, rows, 2 * head)),
            low(units + (per_core // 2 * unit, half)),
            low((2, rows, width)),
            full((width, half)),
            low(units + (unit, half)),
            low((nz, 2, unit, half)),
            low((per_core, unit, half)),
            low((2, nz, 2, slabs, unit, half)),
            low((2, nz, slabs, unit, half)),
            low((2, nz + 1, slabs, unit, half)),
            full((parts, 5, 128)),
            full((parts, 5, 128)),
            DMA((8,)),
            DMA((8,)),
            DMA((8,)),
            DMA((2,)),
            DMA((per_core,)),
            DMA((chips,)),
            DMA((chips,)),
            DMA((per_core,)),
            DMA((chips,)),
            DMA((per_core,)),
            DMA((2, nz, 3)),
            DMA((2, nz, 3)),
            DMA((2, nz, 3)),
            DMA((2, nz, 3)),
            DMA((2, nz, 3)),
            DMA((2, 2, nz, 3)),
            DMA((6,)),
            DMA((6,)),
            DMA((parts - 1,)),
            DMA((parts - 1,)),
            DMA((chips,)),
            DMA((per_core,)),
        ],
        compiler_params=pltpu.CompilerParams(vmem_limit_bytes=62 << 20, collective_id=1, has_side_effects=True),
        cost_estimate=pl.CostEstimate(
            flops=60 * rows * width * hidden, bytes_accessed=60 * width * hidden, transcendentals=length * length
        ),
        name="rest",
    )(x2, attended, cot, mw_all, up, dn, q, k, v, out_t, top, first_low)


def plain_on_device(
    inputs,
    attend_gain,
    attend_shift,
    mixing_weight,
    mixing_bias,
    output_weight,
    output_bias,
    feed_gain,
    feed_shift,
    up_weight,
    up_bias,
    down_weight,
    down_bias,
    cotangent,
):
    place = Place()
    _, span, width = inputs.shape
    nz, ny, core, chip = place.nz, place.ny, place.core, place.chip
    chips = nz * 2
    parts = chips * 2 * ny
    head = width // HEADS
    per_core = HEADS // 2
    slots = [int((j + 0.5) * chips / per_core) for j in range(per_core)]
    half = width // 2
    hidden = up_weight.shape[1]
    rows_in = width // parts
    rows_hid = hidden // parts
    groups = [[2 * i + c for i in range(chips)] for c in range(2)]

    def exchange(values):
        return lax.all_to_all(values, "seq", 0, 0, axis_index_groups=groups, tiled=True)

    def spread(blocks):
        filled = [jnp.zeros_like(blocks[0])] * chips
        for j, slot in enumerate(slots):
            filled[slot] = blocks[j]
        return jnp.stack(filled)

    def collect(blocks):
        return jnp.stack([blocks[slot] for slot in slots])

    owned = [-1] * chips
    for j, slot in enumerate(slots):
        owned[slot] = j
    my_head = jnp.array(owned, jnp.int32)[chip]
    busy = (my_head >= 0).astype(FULL)
    my_head = jnp.maximum(my_head, 0)

    def by_core(values, dim):
        mine = lax.dynamic_index_in_dim(values, core, dim, keepdims=False)
        theirs = lax.dynamic_index_in_dim(values, 1 - core, dim, keepdims=False)
        return mine, theirs

    vectors = jnp.concatenate(
        [attend_gain, attend_shift, feed_gain, feed_shift, output_bias, down_bias, mixing_bias, up_bias]
    )
    vectors = place.both(vectors, vectors)
    vectors = place.gather(vectors, "z", 0)
    vectors = place.gather(vectors, "x", 1)
    vectors = place.gather(vectors, "y", 3)
    vectors = vectors.reshape(parts, -1).astype(FULL)
    cuts = [vectors[:, i * rows_in : (i + 1) * rows_in].reshape(-1) for i in range(6)]
    first_gain, first_shift, second_gain, second_shift, out_bias, down_bias_all = cuts
    mix_bias = vectors[:, 6 * rows_in : 8 * rows_in].reshape(2, HEADS, head)
    up_bias_all = vectors[:, 8 * rows_in :].reshape(chips, 2, ny * rows_hid)
    up_bias_mine = lax.dynamic_index_in_dim(up_bias_all, core, 1, keepdims=False).reshape(-1)

    own = inputs.reshape(span, width)
    column = [own] + [place.send(own, "z", d) for d in range(1, nz)]
    beside = [place.send(piece, "x") for piece in column]
    x_all = jnp.zeros((nz, 2, span, width), LOW)
    for d in range(nz):
        at = lax.rem(place.z + nz - d, nz)
        x_all = lax.dynamic_update_slice(x_all, column[d][None, None], (at, place.x, 0, 0))
        x_all = lax.dynamic_update_slice(x_all, beside[d][None, None], (at, 1 - place.x, 0, 0))
    x_all = place.both(x_all, x_all).transpose(1, 2, 0, 3, 4)
    x_all = x_all.reshape(chips * 2 * span, width)

    def gather_rows(mine, theirs):
        block = place.both(mine, theirs)
        block = place.gather(block, "z", 0)
        block = place.gather(block, "x", 1)
        block = place.gather(block, "y", 3)
        return block.reshape(parts * block.shape[-2], block.shape[-1])

    mixing = mixing_weight.reshape(rows_in, 3, 2, half)
    mine, theirs = by_core(mixing, 2)
    mixing = gather_rows(mine.reshape(rows_in, -1), theirs.reshape(rows_in, -1))
    mine, theirs = by_core(output_weight.reshape(rows_in, 2, half), 1)
    out_half = gather_rows(mine, theirs)
    out_all = place.both(out_half, out_half).transpose(1, 0, 2).reshape(width, width)
    mine, theirs = by_core(up_weight.reshape(rows_in, chips, 2, ny * rows_hid), 2)
    up = gather_rows(mine.reshape(rows_in, -1), theirs.reshape(rows_in, -1))
    down = place.gather(down_weight, "z", 0)
    down = place.gather(down, "x", 1)
    down = place.gather(down, "y", 2).reshape(chips * ny * rows_hid, width)

    mixing = mixing.reshape(width, 3, per_core, head)
    head_weight = lax.dynamic_index_in_dim(mixing, my_head, 2, keepdims=False).reshape(width, 3 * head)
    whole_head = core * per_core + my_head
    head_bias = lax.dynamic_index_in_dim(mix_bias, whole_head, 1, keepdims=False)
    head_bias = jnp.concatenate([head_bias[0], jnp.zeros((head,), FULL), head_bias[1]])
    first_low, q, k, v, out, out_t, top = attend_plain(
        x_all, first_gain[None], first_shift[None], head_weight, head_bias[None]
    )
    attended = collect(exchange(out.reshape(chips, 2 * span, head)))
    attended = attended.transpose(1, 0, 2).reshape(2 * span, half)
    attended = place.both(attended, attended).transpose(1, 0, 2).reshape(2 * span, width)

    residual = lax.dynamic_slice_in_dim(x_all, chip * 2 * span, 2 * span, 0).astype(FULL)
    branch = dot(attended, out_all, (1, 0)) + out_bias
    scale = jnp.array(SCALES, FULL)[:, None, None]
    middle = residual + scale * branch
    second_normed, second_inv = normalize(middle)
    second_low = (second_normed * second_gain + second_shift).astype(LOW)
    rows = second_low.reshape(4 * span, width)
    hidden_pre = dot(rows, up, (1, 0)) + up_bias_mine
    activated, gelu_back = jax.vjp(partial(jax.nn.gelu, approximate=True), hidden_pre)
    activated_low = activated.astype(LOW)
    feed_part = dot(activated_low, down, (1, 0)).reshape(2, 2, span, width)
    mine, theirs = by_core(feed_part, 1)
    feed_own = mine + place.send(theirs, "core") + down_bias_all

    def own_rows(values):
        return lax.dynamic_index_in_dim(
            values.reshape((2, 2, span) + values.shape[2:]), core, 1, keepdims=False
        )

    activations = (own_rows(middle) + scale * feed_own).astype(LOW)
    upstream_own = cotangent.reshape(2, span, width)
    upstream = place.both(upstream_own, upstream_own).transpose(1, 0, 2, 3)
    down_in = (scale[..., None] * upstream.astype(FULL)).astype(LOW).reshape(4 * span, width)
    hidden_low = gelu_back(dot(down_in, down, (1, 1)))[0].astype(LOW)
    second_part = dot(hidden_low, up, (1, 1)).reshape(2, 2, span, width)
    mine, theirs = by_core(second_part, 1)
    second_grad = mine + place.send(theirs, "core")
    normed_own, inv_own = own_rows(second_normed), own_rows(second_inv)
    middle_grad = upstream_own.astype(FULL) + norm_back(second_grad, normed_own, inv_own, second_gain)
    branch_own = (scale * middle_grad).astype(LOW)
    branch_low = place.both(branch_own, branch_own).transpose(1, 0, 2, 3).reshape(2, 2 * span, width)
    out_rows = lax.dynamic_slice_in_dim(out_all, core * half, half, 0)
    go = dot(branch_low.reshape(4 * span, width), out_rows, (1, 1)).astype(LOW)
    go = go.reshape(2, 2 * span, per_core, head).transpose(2, 1, 0, 3).reshape(per_core, 2 * span, 2 * head)
    go = exchange(spread(go)).reshape(chips * 2 * span, 2 * head)

    gq, gk, gv = attend_back(q, k, v, out_t, top, go)
    head_grads = jnp.concatenate([gq, gk, gv], axis=1)

    depth_rows = second_low.reshape(2, 2 * span, width)
    hidden_rows = hidden_low.reshape(2, 2 * span, -1)
    active_rows = activated_low.reshape(2, 2 * span, -1)
    in_rows = down_in.reshape(2, 2 * span, width)
    branch_cols = lax.dynamic_slice_in_dim(branch_low, core * half, half, 2)
    orders = (("y", "x"), ("x", "y"))

    def scatter_chips(values, order):
        dims = {"x": 1, "y": 2}
        values = place.scatter(values, order[0], dims[order[0]]).astype(LOW)
        values = place.scatter(values, order[1], 1).astype(LOW)
        return place.scatter(values, "z", 0)

    def scatter_rows(values, order):
        shaped = values.reshape(nz, 2, 2, ny, rows_in, -1).transpose(0, 1, 3, 2, 4, 5)
        summed = scatter_chips(shaped, order)
        mine, theirs = by_core(summed, 0)
        return place.both(mine, theirs)

    down_grads, up_grads, out_grads = [], [], []
    for depth in range(2):
        grad = dot(active_rows[depth], in_rows[depth], (0, 0)).astype(LOW)
        down_grads.append(scatter_chips(grad.reshape(nz, 2, ny, rows_hid, width), orders[depth]))
    for depth in range(2):
        grad = dot(depth_rows[depth], hidden_rows[depth], (0, 0)).astype(LOW)
        grad = scatter_rows(grad, orders[depth]).reshape(2, rows_in, chips, -1)
        up_grads.append(grad.transpose(1, 2, 0, 3).reshape(rows_in, hidden))
    for depth in range(2):
        grad = dot(attended, branch_cols[depth], (0, 0)).astype(LOW)
        out_grads.append(scatter_rows(grad, orders[depth]).transpose(1, 0, 2).reshape(rows_in, width))

    head_sum = dot(first_low, head_grads, (0, 0)).astype(LOW).reshape(nz, 2, 2, ny, rows_in, 6 * head)
    head_sum = place.scatter(head_sum, "y", 3).astype(LOW).reshape(chips, 2, rows_in, 6 * head)
    head_sum = collect(exchange(head_sum))
    mine, theirs = by_core(head_sum, 1)
    mixing_grad = place.both(mine, theirs).reshape(HEADS, rows_in, 3, 2, head)
    mixing_grad = mixing_grad.transpose(3, 1, 2, 0, 4).reshape(2, rows_in, 3 * width).astype(FULL)

    mixed_grads = collect(exchange(head_grads.reshape(chips, 2 * span, 6 * head)))
    mixed_grads = mixed_grads.reshape(per_core, 2 * span, 3, 2, head).transpose(3, 1, 2, 0, 4)
    mixed_grads = mixed_grads.reshape(4 * span, 3 * half)
    first_part = dot(mixed_grads, mixing.reshape(width, 3 * half), (1, 1)).reshape(2, 2, span, width)
    mine, theirs = by_core(first_part, 1)
    first_grad = mine + place.send(theirs, "core")
    first_normed, first_inv = normalize(own.astype(FULL))
    input_grad = middle_grad + norm_back(first_grad, first_normed, first_inv, first_gain)

    bias_sum = jnp.sum(head_grads.astype(FULL), axis=0).reshape(3, 2, head) * busy
    spot = (jnp.arange(HEADS) == whole_head).astype(FULL)[None, None, :, None]
    bias_sum = (jnp.stack([bias_sum[0], bias_sum[2]], axis=1)[:, :, None, :] * spot).reshape(2, parts, -1)
    hidden_sum = jnp.sum(hidden_rows.astype(FULL), axis=1).reshape(2, chips, 1, ny * rows_hid)
    hidden_spot = (jnp.arange(2) == core).astype(FULL)[None, None, :, None]
    hidden_sum = (hidden_sum * hidden_spot).reshape(2, parts, rows_hid)
    in_own = (scale * upstream_own.astype(FULL)).astype(LOW)
    sums = [
        jnp.sum(first_grad * first_normed, axis=1),
        jnp.sum(first_grad, axis=1),
        jnp.sum(second_grad * normed_own, axis=1),
        jnp.sum(second_grad, axis=1),
        jnp.sum(branch_own.astype(FULL), axis=1),
        jnp.sum(in_own.astype(FULL), axis=1),
    ]
    sums = [item.reshape(2, parts, rows_in) for item in sums] + [bias_sum, hidden_sum]
    sums = jnp.concatenate(sums, axis=2).reshape(2, nz, 2, 2, ny, -1)
    sums = place.scatter(sums, "y", 4)
    sums = place.scatter(sums, "x", 2)
    sums = place.scatter(sums, "core", 2)
    sums = place.scatter(sums, "z", 1)
    small = [sums[:, i * rows_in : (i + 1) * rows_in] for i in range(6)]
    return (
        activations[:, None],
        input_grad[:, None],
        small[0],
        small[1],
        mixing_grad,
        sums[:, 6 * rows_in : 8 * rows_in],
        jnp.stack(out_grads),
        small[4],
        small[2],
        small[3],
        jnp.stack(up_grads),
        sums[:, 8 * rows_in :],
        jnp.stack(down_grads),
        small[5],
    )


def on_device(
    inputs,
    attend_gain,
    attend_shift,
    mixing_weight,
    mixing_bias,
    output_weight,
    output_bias,
    feed_gain,
    feed_shift,
    up_weight,
    up_bias,
    down_weight,
    down_bias,
    cotangent,
):
    place = Place()
    _, span, width = inputs.shape
    nz, ny, core, chip = place.nz, place.ny, place.core, place.chip
    chips = nz * 2
    parts = chips * 2 * ny
    head = width // HEADS
    per_core = HEADS // 2
    half = width // 2
    hidden = up_weight.shape[1]
    rows_in = width // parts
    rows_hid = hidden // parts
    groups = [[2 * i + c for i in range(chips)] for c in range(2)]

    def by_core(values, dim):
        mine = lax.dynamic_index_in_dim(values, core, dim, keepdims=False)
        theirs = lax.dynamic_index_in_dim(values, 1 - core, dim, keepdims=False)
        return mine, theirs

    own = inputs.reshape(span, width)
    pairs = per_core // 2
    mix = mixing_weight.reshape(rows_in, 3, 2, pairs, 2, head).transpose(2, 3, 0, 1, 4, 5)
    mix = mix.reshape(2, pairs, rows_in, half)
    out_cols = output_weight.reshape(rows_in, 2, half).transpose(1, 0, 2)[:, None]
    vectors, start = jnp.zeros((half,), LOW), 0
    for piece in (
        attend_gain, attend_shift, feed_gain, feed_shift, output_bias, down_bias, mixing_bias, up_bias
    ):
        vectors = vectors + jnp.pad(piece, (start, half - start - piece.shape[0]))
        start += piece.shape[0]
    vectors = jnp.broadcast_to(jnp.pad(vectors[None], ((0, 7), (0, 0))), (2, 8, half))
    packed = jnp.concatenate([mix.reshape(2, pairs * rows_in, half), out_cols[:, 0], vectors], axis=1)
    up_cols = up_weight.reshape(rows_in, chips, 2, ny * rows_hid).transpose(2, 0, 1, 3).reshape(2, rows_in, -1)
    mine, theirs = by_core(packed, 0)
    packed = place.both(mine, theirs)
    cut = pairs * rows_in
    pair_rows = packed[:, :cut].reshape(2, pairs, rows_in, half).transpose(1, 0, 2, 3).reshape(2 * cut, half)
    packed_rows = jnp.concatenate([pair_rows, packed[:, cut + rows_in :].reshape(16, half)])
    mine, theirs = by_core(up_cols, 0)
    up_unit = place.both(mine, theirs).reshape(2 * rows_in, -1, half).transpose(1, 0, 2)
    up_unit = jnp.concatenate([up_unit, packed[:, cut : cut + rows_in].reshape(1, 2 * rows_in, half)])

    mw_all, up_all, dn_all, first_low, q, k, v, out_t, top, attended, x2 = attend(
        nz, ny, own, packed_rows, up_unit, down_weight
    )

    raw = rest(
        nz, x2.reshape(2 * span, width), attended, cotangent.reshape(2, span, width), mw_all,
        up_all, dn_all.reshape(-1, width), q, k, v, out_t, top, first_low,
    )
    activations, input_grad, *others = finish(nz, *raw)
    return (activations[:, None], input_grad[:, None], *others)


def tiles_well(mesh):
    ny, seq = mesh.shape["batch"], mesh.shape["seq"]
    rows_in = 768 // (seq * ny)
    return ny == 2 and seq // 2 >= HEADS // 2 and 2 * rows_in % 16 == 0 and 2 * rows_in * seq * ny == 2 * 768


def solution(mesh):
    shard = P(("seq", "batch"))
    grad = P(None, ("seq", "batch"))
    row = P(None, "batch", "seq", None)
    return jax.shard_map(
        on_device if tiles_well(mesh) else plain_on_device,
        mesh=mesh,
        in_specs=(P("batch", "seq", None),) + (shard,) * 12 + (row,),
        out_specs=(row, row) + (grad,) * 12,
        check_vma=False,
    )
```

```python
from functools import partial

import jax
import jax.numpy as jnp
from jax import lax
from jax.experimental import pallas as pl
from jax.experimental.pallas import tpu as pltpu
from jax.sharding import PartitionSpec as P

HEADS = 12
EPS = 1e-05
SCALES = (12.0 ** (-0.5), 48.0 ** (-0.5))
NEGATIVE = -1e30
LOW = jnp.bfloat16
FULL = jnp.float32
TILE = 256


def normalize(values):
    average = jnp.mean(values, axis=-1, keepdims=True)
    centered = values - average
    inv_std = lax.rsqrt(jnp.mean(centered * centered, axis=-1, keepdims=True) + EPS)
    return centered * inv_std, inv_std


def norm_back(gradient, normed, inv_std, gain):
    scaled = gradient * gain
    inner = (
        scaled
        - jnp.mean(scaled, axis=-1, keepdims=True)
        - normed * jnp.mean(scaled * normed, axis=-1, keepdims=True)
    )
    return inv_std * inner


def dot(a, b, dims):
    return lax.dot_general(a, b, ((dims[:1], dims[1:]), ((), ())), preferred_element_type=FULL)


class Place:
    def __init__(self):
        self.s = lax.axis_size("seq")
        self.ny = lax.axis_size("batch")
        self.nz = self.s // 4
        seq = lax.axis_index("seq")
        self.y = lax.axis_index("batch")
        self.core = lax.rem(seq, 2)
        self.chip = seq // 2
        self.x = lax.rem(self.chip, 2)
        self.z = self.chip // 2
        self.sizes = {"z": self.nz, "x": 2, "y": self.ny, "core": 2}
        self.at = {"z": self.z, "x": self.x, "y": self.y, "core": self.core}

    def send(self, values, axis, d=1):
        pairs = []
        for s in range(self.s):
            for y in range(self.ny):
                c, x, z, t = s % 2, (s // 2) % 2, s // 4, y
                if axis == "z":
                    z = (z + d) % self.nz
                elif axis == "x":
                    x = 1 - x
                elif axis == "core":
                    c = 1 - c
                else:
                    t = (y + d) % self.ny
                pairs.append((s * self.ny + y, ((z * 2 + x) * 2 + c) * self.ny + t))
        return lax.ppermute(values, ("seq", "batch"), pairs)

    def gather(self, values, axis, dim):
        size, at = self.sizes[axis], self.at[axis]
        shape = values.shape[:dim] + (size,) + values.shape[dim:]
        whole = lax.dynamic_update_slice_in_dim(
            jnp.zeros(shape, values.dtype), jnp.expand_dims(values, dim), at, dim
        )
        for d in range(1, size):
            piece = jnp.expand_dims(self.send(values, axis, d), dim)
            whole = lax.dynamic_update_slice_in_dim(whole, piece, lax.rem(at + size - d, size), dim)
        return whole

    def scatter(self, values, axis, dim):
        size, at = self.sizes[axis], self.at[axis]

        def pick(i):
            return lax.dynamic_index_in_dim(values, lax.rem(i, size), dim, keepdims=False)

        total = pick(at).astype(FULL)
        for d in range(1, size):
            total = total + self.send(pick(at + d), axis, d).astype(FULL)
        return total

    def both(self, mine, theirs):
        got = self.send(theirs, "core")
        first = self.core == 0
        return jnp.stack([jnp.where(first, mine, got), jnp.where(first, got, mine)])


def attend_plain_kernel(x_ref, gain_ref, shift_ref, w_ref, b_ref, h_ref, q_ref, k_ref, v_ref, o_ref, ot_ref, top_ref, vt_ref):
    length = x_ref.shape[0]
    head = q_ref.shape[1]
    tiles = length // TILE

    def project(i, _):
        rows = pl.ds(pl.multiple_of(i * TILE, TILE), TILE)
        normed, _ = normalize(x_ref[rows, :].astype(FULL))
        low = (normed * gain_ref[...] + shift_ref[...]).astype(LOW)
        h_ref[rows, :] = low
        mixed = dot(low, w_ref[...], (1, 0)) + b_ref[...]
        q_ref[rows, :] = (mixed[:, :head].astype(LOW) * (head ** (-0.5))).astype(LOW)
        k_ref[rows, :] = mixed[:, head : 2 * head].astype(LOW)
        value = mixed[:, 2 * head :].astype(LOW)
        v_ref[rows, :] = value
        vt_ref[:, rows] = value.T
        return 0

    lax.fori_loop(0, tiles, project, 0)

    def query_tile(i, _):
        rows = pl.ds(pl.multiple_of(i * TILE, TILE), TILE)
        query = q_ref[rows, :]

        def absorb(j, carry, masked):
            top, total, acc = carry
            keys = pl.ds(pl.multiple_of(j * TILE, TILE), TILE)
            scores = dot(k_ref[keys, :], query, (1, 1))
            if masked:
                key_pos = lax.broadcasted_iota(jnp.int32, scores.shape, 0)
                query_pos = lax.broadcasted_iota(jnp.int32, scores.shape, 1)
                scores = jnp.where(key_pos <= query_pos, scores, NEGATIVE)
            new_top = jnp.maximum(top, jnp.max(scores, axis=0, keepdims=True))
            weights = jnp.exp(scores - new_top)
            keep = jnp.exp(top - new_top)
            total = total * keep + jnp.sum(weights, axis=0, keepdims=True)
            acc = acc * keep + dot(vt_ref[:, keys], weights.astype(LOW), (1, 0))
            return new_top, total, acc

        start = (
            jnp.full((1, TILE), NEGATIVE, FULL),
            jnp.zeros((1, TILE), FULL),
            jnp.zeros((head, TILE), FULL),
        )
        carry = lax.fori_loop(0, i, lambda j, c: absorb(j, c, False), start)
        top, total, acc = absorb(i, carry, True)
        out = acc / total
        ot_ref[:, rows] = out
        o_ref[rows, :] = out.T.astype(LOW)
        top_ref[:, rows] = top + jnp.log(total)
        return 0

    lax.fori_loop(0, tiles, query_tile, 0)


def attend_plain(x_all, gain, shift, weight, bias):
    length, head = x_all.shape[0], weight.shape[1] // 3
    low = jax.ShapeDtypeStruct((length, head), LOW)
    return pl.pallas_call(
        attend_plain_kernel,
        out_shape=(
            jax.ShapeDtypeStruct(x_all.shape, LOW),
            low,
            low,
            low,
            low,
            jax.ShapeDtypeStruct((head, length), FULL),
            jax.ShapeDtypeStruct((1, length), FULL),
        ),
        scratch_shapes=[pltpu.VMEM((head, length), LOW)],
        compiler_params=pltpu.CompilerParams(vmem_limit_bytes=48 << 20),
        cost_estimate=pl.CostEstimate(
            flops=6 * length * length * head, bytes_accessed=8 * length * 768, transcendentals=length * length
        ),
        name="attend_plain",
    )(x_all, gain, shift, weight, bias)


def attend_back_kernel(
    q_ref, k_ref, v_ref, ot_ref, top_ref, go_ref, gq_ref, gk_ref, gv_ref, kt_ref, got_ref, delta_ref, gqt_ref
):
    length, head = q_ref.shape
    tiles = length // TILE
    factor = head ** (-0.5)

    def prepare(i, _):
        rows = pl.ds(pl.multiple_of(i * TILE, TILE), TILE)
        kt_ref[:, rows] = k_ref[rows, :].T
        up = go_ref[rows, :].T
        for d in range(2):
            mine = up[d * head : (d + 1) * head, :]
            got_ref[d, :, rows] = mine
            delta_ref[d, :, rows] = jnp.sum(mine.astype(FULL) * ot_ref[:, rows], axis=0, keepdims=True)
            gqt_ref[d, :, rows] = jnp.zeros((head, TILE), FULL)
        return 0

    lax.fori_loop(0, tiles, prepare, 0)

    def key_tile(j, _):
        keys = pl.ds(pl.multiple_of(j * TILE, TILE), TILE)
        key = k_ref[keys, :]
        value = v_ref[keys, :]
        key_t = kt_ref[:, keys]

        def step(i, carry, masked):
            gv, gk0, gk1 = carry
            rows = pl.ds(pl.multiple_of(i * TILE, TILE), TILE)
            query = q_ref[rows, :]
            scores = dot(key, query, (1, 1))
            if masked:
                key_pos = lax.broadcasted_iota(jnp.int32, scores.shape, 0)
                query_pos = lax.broadcasted_iota(jnp.int32, scores.shape, 1)
                scores = jnp.where(key_pos <= query_pos, scores, NEGATIVE)
            probs = jnp.exp(scores - top_ref[:, rows])
            gv = gv + dot(probs.astype(LOW), go_ref[rows, :], (1, 0))
            gks = [gk0, gk1]
            for d in range(2):
                prob_grad = dot(value, got_ref[d, :, rows], (1, 0))
                score_low = (probs * (prob_grad - delta_ref[d, :, rows])).astype(LOW)
                gks[d] = gks[d] + dot(score_low, query, (1, 0))
                gqt_ref[d, :, rows] += dot(key_t, score_low, (1, 0))
            return gv, gks[0], gks[1]

        zero = jnp.zeros((TILE, head), FULL)
        carry = step(j, (jnp.zeros((TILE, 2 * head), FULL), zero, zero), True)
        gv, gk0, gk1 = lax.fori_loop(j + 1, tiles, lambda i, c: step(i, c, False), carry)
        gv_ref[keys, :] = gv.astype(LOW)
        gk_ref[keys, :] = jnp.concatenate([gk0, gk1], axis=1).astype(LOW)
        return 0

    lax.fori_loop(0, tiles, key_tile, 0)

    def finish(i, _):
        rows = pl.ds(pl.multiple_of(i * TILE, TILE), TILE)
        both = jnp.concatenate([gqt_ref[0, :, rows], gqt_ref[1, :, rows]], axis=0) * factor
        gq_ref[rows, :] = both.T.astype(LOW)
        return 0

    lax.fori_loop(0, tiles, finish, 0)


def attend_back(q, k, v, out_t, top, go):
    length, head = q.shape
    pair = jax.ShapeDtypeStruct((length, 2 * head), LOW)
    return pl.pallas_call(
        attend_back_kernel,
        out_shape=(pair, pair, pair),
        scratch_shapes=[
            pltpu.VMEM((head, length), LOW),
            pltpu.VMEM((2, head, length), LOW),
            pltpu.VMEM((2, 1, length), FULL),
            pltpu.VMEM((2, head, length), FULL),
        ],
        compiler_params=pltpu.CompilerParams(vmem_limit_bytes=48 << 20),
        cost_estimate=pl.CostEstimate(
            flops=20 * length * length * head, bytes_accessed=16 * length * head, transcendentals=length * length
        ),
        name="attend_back",
    )(q, k, v, out_t, top, go)


MESH = pl.DeviceIdType.MESH
DMA = pltpu.SemaphoreType.DMA


class Here:
    def __init__(self, nz, ny):
        self.nz, self.ny = nz, ny
        seq = lax.axis_index("seq")
        self.y = lax.axis_index("batch")
        self.core = lax.rem(seq, 2)
        self.chip = lax.div(seq, 2)
        self.x = lax.rem(self.chip, 2)
        self.z = lax.div(self.chip, 2)

    def device(self, z=None, x=None, core=None, y=None):
        z = self.z if z is None else z
        x = self.x if x is None else x
        core = self.core if core is None else core
        y = self.y if y is None else y
        return ((z * 2 + x) * 2 + core, y)

    def before(self, d):
        return lax.rem(self.z + self.nz - d, self.nz)

    def after(self, d):
        return lax.rem(self.z + d, self.nz)


def remote(src, dst, send, recv, device):
    return pltpu.make_async_remote_copy(
        src_ref=src, dst_ref=dst, send_sem=send, recv_sem=recv, device_id=device, device_id_type=MESH
    )


class Gather:
    def __init__(self, here, own, whole, x_first, sems):
        self.here, self.own, self.whole, self.x_first = here, own, whole, x_first
        self.zs, self.zr, self.as_, self.ar, self.bs, self.br, self.local = sems
        self.kept = pltpu.make_async_copy(own, whole.at[here.z, here.x, here.y], self.local)

    @staticmethod
    def scratch(nz, ny):
        return [DMA((2, nz)), DMA((nz,)), DMA((nz, ny)), DMA((nz, ny)), DMA((nz, 2, ny)), DMA((nz, 2, ny)), DMA]

    def _along(self, source, up, own=False):
        h = self.here
        spot = self.whole.at[source, h.x, h.y]
        to = h.device(z=lax.min(h.z + 1, h.nz - 1)) if up else h.device(z=lax.max(h.z - 1, 0))
        src = self.own if own else spot
        return remote(src, spot, self.zs.at[0 if up else 1, source], self.zr.at[source], to)

    def _to_x(self, source, y, out, own=False):
        h = self.here
        spot = self.whole.at[source, h.x if out else 1 - h.x, y]
        s, r = (self.as_, self.ar) if self.x_first else (self.bs, self.br)
        i = (source, 0) if self.x_first else (source, 0, y)
        return remote(self.own if own else spot, spot, s.at[i], r.at[i], h.device(x=1 - h.x))

    def _to_y(self, source, x, e, out, own=False):
        h = self.here
        spot = self.whole.at[source, x, h.y if out else lax.rem(h.y + h.ny - e, h.ny)]
        s, r = (self.bs, self.br) if self.x_first else (self.as_, self.ar)
        i = (source, x, e) if self.x_first else (source, e)
        return remote(self.own if own else spot, spot, s.at[i], r.at[i], h.device(y=lax.rem(h.y + e, h.ny)))

    def start_z(self):
        h = self.here
        pl.when(h.z < h.nz - 1)(self._along(h.z, True, True).start)
        pl.when(h.z > 0)(self._along(h.z, False, True).start)

    def take_z(self, source, up):
        h = self.here
        self._along(source, up).wait_recv()
        pl.when(h.z < h.nz - 1 if up else h.z > 0)(self._along(source, up).start)

    def spread(self, source, own):
        h = self.here
        if self.x_first:
            self._to_x(source, h.y, True, own).start()
            for e in range(1, h.ny):
                self._to_y(source, h.x, e, True, own).start()
        else:
            for e in range(1, h.ny):
                self._to_y(source, h.x, e, True, own).start()
            self._to_x(source, h.y, True, own).start()

    def second(self, source):
        h = self.here
        if self.x_first:
            self._to_x(source, h.y, False).wait_recv()
            for e in range(1, h.ny):
                self._to_y(source, 1 - h.x, e, True).start()
        else:
            for e in range(1, h.ny):
                self._to_y(source, h.x, e, False).wait_recv()
                self._to_x(source, lax.rem(h.y + h.ny - e, h.ny), True).start()

    def third(self, source):
        h = self.here
        if self.x_first:
            for e in range(1, h.ny):
                self._to_y(source, h.x, e, False).wait_recv()
                self._to_y(source, 1 - h.x, e, False).wait_recv()
        else:
            for y in range(h.ny):
                self._to_x(source, y, False).wait_recv()

    def finish(self):
        h = self.here
        for source in range(h.nz):
            pl.when(jnp.logical_and(source <= h.z, h.z < h.nz - 1))(self._along(source, True).wait_send)
            pl.when(jnp.logical_and(source >= h.z, h.z > 0))(self._along(source, False).wait_send)
            if self.x_first:
                self._to_x(source, h.y, True).wait_send()
                for e in range(1, h.ny):
                    for x in range(2):
                        self._to_y(source, x, e, True).wait_send()
            else:
                for e in range(1, h.ny):
                    self._to_y(source, h.x, e, True).wait_send()
                for y in range(h.ny):
                    self._to_x(source, y, True).wait_send()


class GatherRows:
    def __init__(self, here, own, whole, sems):
        self.here, self.own, self.whole = here, own, whole
        self.zs, self.zr, self.xs, self.xr, self.cs, self.cr, self.local = sems
        self.kept = pltpu.make_async_copy(own, whole.at[here.z, here.x, here.core], self.local)

    @staticmethod
    def scratch(nz):
        return [DMA((2, nz)), DMA((nz,)), DMA((nz,)), DMA((nz,)), DMA((nz, 2)), DMA((nz, 2)), DMA]

    def _along(self, source, up, own=False):
        h = self.here
        spot = self.whole.at[source, h.x, h.core]
        to = h.device(z=lax.min(h.z + 1, h.nz - 1)) if up else h.device(z=lax.max(h.z - 1, 0))
        src = self.own if own else spot
        return remote(src, spot, self.zs.at[0 if up else 1, source], self.zr.at[source], to)

    def _to_x(self, source, out, own=False):
        h = self.here
        spot = self.whole.at[source, h.x if out else 1 - h.x, h.core]
        return remote(self.own if own else spot, spot, self.xs.at[source], self.xr.at[source], h.device(x=1 - h.x))

    def _to_core(self, source, x, out, own=False):
        h = self.here
        spot = self.whole.at[source, x, h.core if out else 1 - h.core]
        return remote(self.own if own else spot, spot, self.cs.at[source, x], self.cr.at[source, x], h.device(core=1 - h.core))

    start_z = Gather.start_z
    take_z = Gather.take_z

    def spread(self, source, own):
        self._to_x(source, True, own).start()
        self._to_core(source, self.here.x, True, own).start()

    def second(self, source):
        self._to_x(source, False).wait_recv()
        self._to_core(source, 1 - self.here.x, True).start()

    def third(self, source):
        for x in range(2):
            self._to_core(source, x, False).wait_recv()

    def finish(self):
        h = self.here
        for source in range(h.nz):
            pl.when(jnp.logical_and(source <= h.z, h.z < h.nz - 1))(self._along(source, True).wait_send)
            pl.when(jnp.logical_and(source >= h.z, h.z > 0))(self._along(source, False).wait_send)
            self._to_x(source, True).wait_send()
            for x in range(2):
                self._to_core(source, x, True).wait_send()


def at_distance(here, k, act):
    if k == 0:
        act(here.z, None)
    else:
        pl.when(here.z >= k)(lambda: act(here.z - k, True))
        pl.when(here.z + k < here.nz)(lambda: act(here.z + k, False))


def natural_of(shape, axis, rows_in, ny):
    lane = lax.broadcasted_iota(jnp.int32, shape, axis)
    within = lax.rem(lane, 2 * ny * rows_in)
    core = lax.rem(lax.div(within, rows_in), 2)
    y = lax.div(within, 2 * rows_in)
    return lane - within + (core * ny + y) * rows_in + lax.rem(lane, rows_in)


def bias_piece(entry, rows_in, ny):
    device = lax.div(entry, 2 * rows_in)
    chip = lax.div(device, 2 * ny)
    row = chip * 2 * ny + lax.rem(device, ny) * 2 + lax.rem(lax.div(device, ny), 2)
    return row, 6 * rows_in + lax.rem(entry, 2 * rows_in)


def greet(devices):
    barrier = pltpu.get_barrier_semaphore()
    for device in devices:
        pl.semaphore_signal(barrier, inc=1, device_id=device, device_id_type=MESH)
    return lambda: pl.semaphore_wait(barrier, len(devices))


def owner_of(chips):
    per_core = HEADS // 2
    return [int((j + 0.5) * chips / per_core) for j in range(per_core)]


def head_here(chip, slots):
    mine, has = jnp.int32(0), jnp.int32(0)
    for j, slot in enumerate(slots):
        same = (chip == slot).astype(jnp.int32)
        mine = mine + j * same
        has = has + same
    return mine, has


def attend_kernel(
    nz, ny, x_ref, mw_ref, up_ref, dn_ref,
    mw_all, up_all, dn_all, h_ref, q_ref, k_ref, v_ref, ot_ref, top_ref, att_ref, x2_ref,
    xs, wt, vc, vt_ref, o_ref, pm, x_own, up_own, dn_own, xn, flat_ref, load, att_s, att_r, pass_s, pass_r, *sems,
):
    here = Here(nz, ny)
    chips = 2 * nz
    slots = owner_of(chips)
    head = q_ref.shape[1]
    width = x_ref.shape[1]
    tile = 2 * x_ref.shape[0]
    mine, has = head_here(here.chip, slots)
    odd = lax.rem(mine, 2) == 1
    rows_sems, mw_sems, up_sems, dn_sems = sems[:7], sems[7:14], sems[14:21], sems[21:28]

    peers = [here.device(z=here.after(d)) for d in range(1, nz)]
    peers += [here.device(x=1 - here.x), here.device(core=1 - here.core)]
    peers += [here.device(z=here.after(d), x=1 - here.x) for d in range(1, nz)]
    peers += [here.device(y=lax.rem(here.y + e, ny)) for e in range(1, ny)]
    met = greet(peers)
    half = width // 2
    unit = up_ref.shape[1]
    rows_in = unit // 2
    pair_rows = HEADS // 4 * unit
    from_row = lax.broadcasted_iota(jnp.int32, (width, width), 0)
    pm[...] = (from_row == natural_of((1, width), 1, rows_in, ny)).astype(LOW)
    x_own[...] = dot(x_ref[...], pm[...], (1, 0)).astype(LOW)
    dn_own[...] = dot(dn_ref[...], pm[...], (1, 0)).astype(LOW)
    up_own[...] = up_ref[...]
    up_own[4] = dot(up_ref[4], pm[:half, :half], (1, 0)).astype(LOW)
    rows = GatherRows(here, x_own, xs, rows_sems)
    mw = Gather(here, mw_ref, mw_all, True, mw_sems)
    up = Gather(here, up_own, up_all, True, up_sems)
    dn = Gather(here, dn_own, dn_all, False, dn_sems)
    first, later = (rows, mw), (up, dn)
    for item in first + later:
        item.kept.start()
    met()

    def take(items, k):
        def act(source, way):
            for item in items:
                if k:
                    item.take_z(source, way)
            for item in items:
                item.spread(source, k == 0)

        at_distance(here, k, act)

    def then(items, k, stage):
        def act(source, _):
            for item in items:
                getattr(item, stage)(source)

        at_distance(here, k, act)

    for item in first:
        item.start_z()
    take(first, 0)
    for k in range(1, nz):
        take(first, k)
        then(first, k - 1, "second")
    for item in later:
        item.start_z()
    then(first, nz - 1, "second")
    take(later, 0)
    for k in range(nz):
        then((rows,), k, "third")
    rows.kept.wait()
    keep_rows = pltpu.make_async_copy(xs.at[here.z, here.x], x2_ref, load.at[2])
    keep_rows.start()

    @pl.when(has == 1)
    def _():
        for i in range(chips):
            xn[i], _ = normalize(xs[i // 2, i % 2].reshape(tile, width).astype(FULL))

    for k in range(nz):
        then((mw,), k, "third")
    mw.kept.wait()
    my_pair = pl.ds(pl.multiple_of(lax.div(mine, 2) * unit, unit), unit)
    pair = pltpu.make_async_copy(mw_all.at[:, :, :, my_pair], wt, load.at[0])
    pair.start()
    vectors = pltpu.make_async_copy(mw_all.at[:, :, :, pl.ds(pair_rows, 16)], vc, load.at[1])
    vectors.start()
    pair.wait()
    vectors.wait()

    steps = []
    for k in range(1, nz):
        steps += [partial(take, later, k), partial(then, later, k - 1, "second")]
    steps += [partial(then, later, nz - 1, "second")] + [partial(then, later, k, "third") for k in range(nz)]

    @pl.when(has == 1)
    def _():
        pieces = vc[...].reshape(-1, vc.shape[-1])
        count = 2 * chips * ny
        pick_row = lax.broadcasted_iota(jnp.int32, (count, pieces.shape[0]), 0) * 8
        pick = (pick_row == lax.broadcasted_iota(jnp.int32, pick_row.shape, 1)).astype(LOW)
        pieces = dot(pick, pieces, (1, 0)).astype(LOW)
        lane = lax.broadcasted_iota(jnp.int32, (1, width), 1)
        pair_lane = lax.broadcasted_iota(jnp.int32, (1, 2 * head), 1)
        pair_lane = pair_lane + (here.core * (HEADS // 4) + lax.div(mine, 2)) * 2 * head
        q_row, q_col = bias_piece(pair_lane, rows_in, ny)
        v_row, v_col = bias_piece(pair_lane + width, rows_in, ny)
        none = jnp.full((1, 2 * head), -1, jnp.int32)
        in_row, owner = lax.rem(lane, rows_in), lax.div(lane, rows_in)
        cols = jnp.concatenate([in_row, rows_in + in_row, q_col, none, v_col], axis=1)
        owners = jnp.concatenate([owner, owner, q_row, none, v_row], axis=1)
        spot = lax.broadcasted_iota(jnp.int32, (pieces.shape[1], cols.shape[1]), 0)
        moved = dot(pieces, (spot == cols).astype(LOW), (1, 0))
        from_row = lax.broadcasted_iota(jnp.int32, moved.shape, 0)
        flat_ref[...] = jnp.sum(jnp.where(from_row == owners, moved, 0.0), axis=0, keepdims=True)

    def choose(values):
        return jnp.where(odd, values[:, head:], values[:, :head])

    def project(i):
        span = slice(i * tile, (i + 1) * tile)
        low = (xn[i] * flat_ref[:, :width] + flat_ref[:, width : 2 * width]).astype(LOW)
        h_ref[span, :] = low
        mixed = (dot(low, wt[...].reshape(width, -1), (1, 0)) + flat_ref[:, 2 * width :]).astype(LOW)
        q_ref[span, :] = (choose(mixed[:, : 2 * head]) * (head ** (-0.5))).astype(LOW)
        k_ref[span, :] = choose(mixed[:, 2 * head : 4 * head])
        value = choose(mixed[:, 4 * head :])
        v_ref[span, :] = value
        vt_ref[:, span] = value.T

    def query_tile(i):
        span = slice(i * tile, (i + 1) * tile)
        query = q_ref[span, :]

        def absorb(j, carry, masked):
            top, total, acc = carry
            keys = slice(j * tile, (j + 1) * tile)
            scores = dot(k_ref[keys, :], query, (1, 1))
            if masked:
                key_pos = lax.broadcasted_iota(jnp.int32, scores.shape, 0)
                query_pos = lax.broadcasted_iota(jnp.int32, scores.shape, 1)
                scores = jnp.where(key_pos <= query_pos, scores, NEGATIVE)
            new_top = jnp.maximum(top, jnp.max(scores, axis=0, keepdims=True))
            weights = jnp.exp(scores - new_top)
            keep = jnp.exp(top - new_top)
            total = total * keep + jnp.sum(weights, axis=0, keepdims=True)
            acc = acc * keep + dot(vt_ref[:, keys], weights.astype(LOW), (1, 0))
            return new_top, total, acc

        carry = (jnp.full((1, tile), NEGATIVE, FULL), jnp.zeros((1, tile), FULL), jnp.zeros((head, tile), FULL))
        for j in range(i + 1):
            carry = absorb(j, carry, j == i)
        top, total, acc = carry
        out = acc / total
        ot_ref[:, span] = out
        o_ref[i] = out.T.astype(LOW)
        top_ref[:, span] = top + jnp.log(total)

    def hand(i):
        spot = att_ref.at[here.core, mine]
        return (
            pltpu.make_async_copy(o_ref.at[i], spot, att_s.at[i]),
            remote(o_ref.at[i], spot, att_s.at[i], att_r.at[mine], here.device(z=i // 2, x=i % 2)),
        )

    @pl.when(has == 1)
    def _():
        for i in range(chips):
            project(i)

    for i in range(chips):
        @pl.when(has == 1)
        def _(i=i):
            query_tile(i)
            stay, leave = hand(i)
            pl.when(here.chip == i)(stay.start)
            pl.when(here.chip != i)(leave.start)

        if i < len(steps):
            steps[i]()
    for step in steps[chips:]:
        step()

    for i in range(chips):
        @pl.when(has == 1)
        def _(i=i):
            stay, leave = hand(i)
            pl.when(here.chip == i)(stay.wait)
            pl.when(here.chip != i)(leave.wait_send)

    for j, slot in enumerate(slots):
        @pl.when(here.chip != slot)
        def _(j=j, slot=slot):
            spot = att_ref.at[here.core, j]
            remote(spot, spot, att_s.at[0], att_r.at[j], here.device(z=slot // 2, x=slot % 2)).wait_recv()

    spot = att_ref.at[here.core]
    give = remote(spot, spot, pass_s, pass_r, here.device(core=1 - here.core))
    give.start()
    spot = att_ref.at[1 - here.core]
    remote(spot, spot, pass_s, pass_r, here.device(core=1 - here.core)).wait_recv()
    give.wait_send()
    keep_rows.wait()
    for item in later:
        item.kept.wait()
    for item in first + later:
        item.finish()


def attend(nz, ny, own, mw, up, dn):
    span, width = own.shape
    length = 4 * nz * span
    head = width // HEADS
    units = (nz, 2, ny)
    low = jax.ShapeDtypeStruct((length, head), LOW)
    anywhere = pl.BlockSpec(memory_space=pl.ANY)
    vmem = pl.BlockSpec(memory_space=pltpu.VMEM)
    return pl.pallas_call(
        partial(attend_kernel, nz, ny),
        out_shape=(
            jax.ShapeDtypeStruct(units + mw.shape, LOW),
            jax.ShapeDtypeStruct(units + up.shape, LOW),
            jax.ShapeDtypeStruct(units + dn.shape, LOW),
            jax.ShapeDtypeStruct((length, width), LOW),
            low,
            low,
            low,
            jax.ShapeDtypeStruct((head, length), FULL),
            jax.ShapeDtypeStruct((1, length), FULL),
            jax.ShapeDtypeStruct((2, HEADS // 2, 2 * span, head), LOW),
            jax.ShapeDtypeStruct((2, span, width), LOW),
        ),
        in_specs=[vmem] * 4,
        out_specs=[anywhere] * 3 + [vmem] * 6 + [anywhere] * 2,
        scratch_shapes=[
            pltpu.VMEM((nz, 2, 2, span, width), LOW),
            pltpu.VMEM(units + up.shape[1:], LOW),
            pltpu.VMEM(units + (16,) + mw.shape[1:], LOW),
            pltpu.VMEM((head, length), LOW),
            pltpu.VMEM((2 * nz, 2 * span, head), LOW),
            pltpu.VMEM((width, width), LOW),
            pltpu.VMEM(own.shape, LOW),
            pltpu.VMEM(up.shape, LOW),
            pltpu.VMEM(dn.shape, LOW),
            pltpu.VMEM((2 * nz, 2 * span, width), FULL),
            pltpu.VMEM((1, 2 * width + width // 2), FULL),
            DMA((3,)),
            DMA((2 * nz,)),
            DMA((HEADS // 2,)),
            DMA,
            DMA,
        ]
        + GatherRows.scratch(nz)
        + Gather.scratch(nz, ny) * 3,
        compiler_params=pltpu.CompilerParams(vmem_limit_bytes=56 << 20, collective_id=0, has_side_effects=True),
        cost_estimate=pl.CostEstimate(
            flops=6 * length * length * head, bytes_accessed=8 * length * width, transcendentals=length * length
        ),
        name="attend",
    )(own, mw, up, dn)


GELU_K = 0.7978845608028654
GELU_C = 0.044715


def gelu_pair(u):
    square = u * u
    tanh = jnp.tanh(GELU_K * u * (1.0 + GELU_C * square))
    half = 0.5 * (1.0 + tanh)
    slope = half + (0.5 * GELU_K) * u * (1.0 - tanh * tanh) * (1.0 + 3.0 * GELU_C * square)
    return u * half, slope


def split_dot(values, turn, dims):
    high = values.astype(LOW)
    rest = values - high.astype(FULL)
    middle = rest.astype(LOW)
    low = (rest - middle.astype(FULL)).astype(LOW)
    return dot(high, turn, dims) + dot(middle, turn, dims) + dot(low, turn, dims)


def rest_kernel(
    nz, hidden_tile,
    x2_ref, att_ref, cot_ref, mw_all, up_ref, dn_ref,
    q_ref, k_ref, v_ref, ot_ref, top_ref, h_all,
    act_ref, ing_ref, fin, swap, mixf, mix_swap, vec_ref,
    up, dn, ow, own, pm, vc, att, cot, h2, act_low, gu, branch, feed, feed_in, gh2, gh2_in, gmid, eb, grads, go_send,
    go_all, kt_ref, got_ref, delta_ref, gqt_ref, gsend, gat, mw, hbuf, head_acc, head_sum, hs_in, mix_in,
    r1, r2, r3, pack, vec_in,
    load, near_s, near_r, h_s, go_s, go_r, kv_s, kv_r, q_s, q_r, s1, t1, s2, t2, s3, t3, ex_s, ex_r,
    vec_s, vec_r, mix_s, mix_r,
):
    ny = 2
    here = Here(nz, ny)
    core, chip, x, y, z = here.core, here.chip, here.x, here.y, here.z
    chips = 2 * nz
    parts = 4 * nz * ny
    slots = owner_of(chips)
    per_core = len(slots)
    length, head = q_ref.shape
    tile = length // chips
    _, span, width = cot_ref.shape
    half = width // 2
    hidden = dn_ref.shape[0]
    rows_hid = 2 * hidden // parts
    factor = head ** (-0.5)
    job, has = head_here(chip, slots)
    partner = here.device(core=1 - core)
    slabs, unit = grads.shape[4], grads.shape[5]
    pairs = per_core // 2
    rows_in = unit // 2
    my_rows = pl.ds(pl.multiple_of(core * span, span), span)
    their_rows = pl.ds(pl.multiple_of((1 - core) * span, span), span)

    def flat(zz, xx, yy, cc):
        return ((zz * 2 + xx) * ny + yy) * 2 + cc

    others = []
    for dz in range(nz):
        for dx in range(2):
            for dy in range(ny):
                for dc in range(2):
                    if dz or dx or dy or dc:
                        zz = lax.rem(z + dz, nz)
                        xx = 1 - x if dx else x
                        yy = 1 - y if dy else y
                        cc = 1 - core if dc else core
                        behind = (lax.rem(z + nz - dz, nz), xx, yy, cc)
                        others.append((here.device(zz, xx, cc, yy), flat(zz, xx, yy, cc), flat(*behind)))

    loads = [
        pltpu.make_async_copy(up_ref.at[:, :, :, 4], ow.at[core], load.at[0]),
        pltpu.make_async_copy(mw_all.at[:, :, :, pl.ds(pairs * unit, 16)], vc, load.at[1]),
        pltpu.make_async_copy(dn_ref, dn, load.at[2]),
        pltpu.make_async_copy(mw_all.at[:, :, :, pl.ds(0, pairs * unit)], mw, load.at[3]),
    ]
    for t in range(4):
        spot = up.at[:, :, :, :, pl.ds(t * half, half)]
        loads.append(pltpu.make_async_copy(up_ref.at[:, :, :, t], spot, load.at[4 + t]))
    for copy in loads:
        copy.start()
    met = greet([device for device, _, _ in others])

    def pass_on(i, src, dst):
        return remote(src, dst, near_s.at[i], near_r.at[i], partner)

    natural = natural_of((1, width), 1, rows_in, ny)
    from_row = lax.broadcasted_iota(jnp.int32, (width, width), 0)
    pm[...] = (from_row == natural).astype(LOW)
    for d in range(2):
        cot[d, my_rows, :] = dot(cot_ref[d], pm[...], (1, 0)).astype(LOW)
    met()
    give_cot = pass_on(0, cot.at[:, my_rows], cot.at[:, my_rows])
    give_cot.start()
    loads[0].wait()
    give_ow = pass_on(1, ow.at[core], ow.at[core])
    give_ow.start()

    wide = lax.broadcasted_iota(jnp.int32, (1, width), 1)
    wide_owner = lax.div(wide, rows_in)
    hid = lax.broadcasted_iota(jnp.int32, (1, hidden), 1)
    hid_owner = lax.div(hid, rows_hid) * 2 + core
    in_row = lax.rem(wide, rows_in)
    cols = [in_row + i * rows_in for i in (2, 3, 4, 5, 0)] + [lax.rem(hid, rows_hid) + 8 * rows_in]
    cols = jnp.concatenate(cols, axis=1)
    owners = jnp.concatenate([wide_owner] * 5 + [hid_owner], axis=1)
    loads[1].wait()
    pieces = vc[...].reshape(-1, vc.shape[-1])
    pick_row = lax.broadcasted_iota(jnp.int32, (parts, pieces.shape[0]), 0) * 8
    pick = (pick_row == lax.broadcasted_iota(jnp.int32, pick_row.shape, 1)).astype(LOW)
    pieces = dot(pick, pieces, (1, 0)).astype(LOW)
    spot = lax.broadcasted_iota(jnp.int32, (pieces.shape[1], cols.shape[1]), 0)
    moved = dot(pieces, (spot == cols).astype(LOW), (1, 0))
    piece_row = lax.broadcasted_iota(jnp.int32, moved.shape, 0)
    vectors = jnp.sum(jnp.where(piece_row == owners, moved, 0.0), axis=0, keepdims=True)
    gain, shift, out_bias, down_bias, first_gain = (vectors[:, i * width : (i + 1) * width] for i in range(5))
    up_bias = vectors[:, 5 * width :]

    natural_att = jnp.concatenate([att_ref[c, j] for c in range(2) for j in range(per_core)], axis=1)
    att[...] = dot(natural_att, pm[...], (1, 0)).astype(LOW)
    remote(ow.at[1 - core], ow.at[1 - core], near_s.at[1], near_r.at[1], partner).wait_recv()
    for c in range(2):
        own[:, c * half : (c + 1) * half] = dot(pm[...], ow[c].reshape(width, half), (1, 0)).astype(LOW)
    branch[...] = dot(natural_att, own[...], (1, 0)) + out_bias

    def middle_of(d, rows):
        return x2_ref[rows, :].astype(FULL) + SCALES[d] * branch[rows, :]

    for d in range(2):
        n, _ = normalize(middle_of(d, slice(None)))
        h2[d] = (n * gain + shift).astype(LOW)
    theirs_cot = cot.at[:, their_rows]
    remote(theirs_cot, theirs_cot, near_s.at[0], near_r.at[0], partner).wait_recv()
    loads[2].wait()
    for copy in loads[4:]:
        copy.wait()

    def up_cols(cut):
        return up[:, :, :, :, cut].reshape(width, -1)

    def upstream(d):
        return (SCALES[d] * cot[d].astype(FULL)).astype(LOW)

    stride = pack.shape[1] * pack.shape[2] // 2
    lane = lax.broadcasted_iota(jnp.int32, (width, 128), 0)
    in_piece = (lax.rem(lane, rows_in) == lax.broadcasted_iota(jnp.int32, lane.shape, 1)).astype(LOW)

    def placed(vector, owner, turn, start):
        rows = lax.broadcasted_iota(jnp.int32, (parts, vector.shape[1]), 0)
        spread = jnp.where(rows == owner, vector, 0.0)
        high = spread.astype(LOW)
        low = (spread - high.astype(FULL)).astype(LOW)
        values = dot(high, turn, (1, 0)) + dot(low, turn, (1, 0))
        return jnp.pad(values, ((0, 0), (start, 2 * stride)))[:, : 2 * stride]

    sums = {}

    def row_sum(v, d, values):
        sums[v, d] = jnp.sum(values, axis=0, keepdims=True)

    exchanges = []

    def forth(d):
        low_in = upstream(d)
        ups = []
        for t in range(0, hidden, hidden_tile):
            cut = slice(t, t + hidden_tile)
            u = dot(h2[d], up_cols(cut), (1, 0)) + up_bias[:, cut]
            active, slope = gelu_pair(u)
            active = active.astype(LOW)
            act_low[d, :, cut] = active
            grad = (dot(low_in, dn[cut, :], (1, 1)) * slope).astype(LOW)
            gu[d, :, cut] = grad
            ups.append(jnp.sum(grad.astype(FULL), axis=0, keepdims=True))
        sums["up", d] = jnp.concatenate(ups, axis=1)

    def back_to_width(d):
        gh2[d] = dot(gu[d], up_cols(slice(None)), (1, 1))
        feed[d] = dot(act_low[d], dn[...], (1, 0))
        for i, (src, dst) in ((2, (gh2, gh2_in)), (4, (feed, feed_in))):
            copy = pass_on(i + d, src.at[d, their_rows], dst.at[d])
            copy.start()
            exchanges.append(copy)

    def keep(d, values, first_row, first_col, base, rows_of):
        for i in range(0, values.shape[0], unit):
            row = first_row + i
            u, within = row // rows_of, (row % rows_of) // unit
            place = (u // (2 * ny), (u // ny) % 2, u % ny)
            for c in range(0, values.shape[1], half):
                slab = base + within * 2 + (first_col + c) // half
                grads[(d,) + place + (slab,)] = values[i : i + unit, c : c + half]

    def down_grads(d):
        low_in = upstream(d)
        for t in range(0, hidden, half):
            keep(d, dot(act_low[d, :, t : t + half], low_in, (0, 0)).astype(LOW), t, 0, 0, 2 * unit)

    def up_grads(d):
        for t in range(0, hidden, 2 * half):
            for m in range(0, width, half):
                part = dot(h2[d, :, m : m + half], gu[d, :, t : t + 2 * half], (0, 0)).astype(LOW)
                keep(d, part, m, t, 4, unit)

    def norm_feed_back(d):
        remote(gh2_in.at[d], gh2_in.at[d], near_s.at[2 + d], near_r.at[2 + d], partner).wait_recv()
        grad = gh2[d, my_rows, :] + gh2_in[d]
        n, r = normalize(middle_of(d, my_rows))
        row_sum(2, d, grad * n)
        row_sum(3, d, grad)
        own_cot = cot[d, my_rows, :].astype(FULL)
        middle_grad = own_cot + norm_back(grad, n, r, gain)
        gmid[d] = middle_grad
        branch_low = (SCALES[d] * middle_grad).astype(LOW)
        row_sum(4, d, branch_low.astype(FULL))
        row_sum(5, d, (SCALES[d] * own_cot).astype(LOW).astype(FULL))
        eb[d, my_rows, :] = branch_low
        copy = pass_on(6 + d, eb.at[d, my_rows], eb.at[d, my_rows])
        copy.start()
        exchanges.append(copy)

    zis = []
    for i in range((nz + 1) // 2):
        zis += [nz - 1 - i] + ([i] if i != nz - 1 - i else [])
    cuts = [(0, slabs // 2), (slabs // 2, slabs)]
    chunks = [(zi, part) for part in range(len(cuts)) for zi in zis]

    def y_first(d, zi, part):
        return d == 0 or chunks.index((zi, part)) % 2 == 1

    def mine(d, zi, part, i, slab):
        return grads.at[d, zi, i, y, slab] if y_first(d, zi, part) else grads.at[d, zi, x, i, slab]

    def some(part):
        return pl.ds(cuts[part][0], cuts[part][1] - cuts[part][0])

    def stage1(d, zi, part):
        slab = some(part)
        if y_first(d, zi, part):
            src, to = grads.at[d, zi, :, 1 - y, slab], here.device(y=1 - y)
        else:
            src, to = grads.at[d, zi, 1 - x, :, slab], here.device(x=1 - x)
        return remote(src, r1.at[d, zi, :, slab], s1.at[d, zi, part], t1.at[d, zi, part], to)

    def stage2(d, zi, part):
        slab = some(part)
        if y_first(d, zi, part):
            src, to = mine(d, zi, part, 1 - x, slab), here.device(x=1 - x)
        else:
            src, to = mine(d, zi, part, 1 - y, slab), here.device(y=1 - y)
        return remote(src, r2.at[d, zi, slab], s2.at[d, zi, part], t2.at[d, zi, part], to)

    def spare(zi, up):
        return zi if up else jnp.where(z - 1 == zi, nz, zi)

    def stage3(d, zi, part, up):
        to = here.device(z=lax.min(z + 1, nz - 1)) if up else here.device(z=lax.max(z - 1, 0))
        way = 0 if up else 1
        slab = some(part)
        src, dst = r2.at[d, zi, slab], r3.at[d, spare(zi, up), slab]
        return remote(src, dst, s3.at[d, zi, part], t3.at[d, way, zi, part], to)

    def arrive3(d, zi, part, up):
        way = 0 if up else 1
        spot = r3.at[d, zi, some(part)]
        return remote(spot, spot, s3.at[d, zi, part], t3.at[d, way, zi, part], partner)

    def begin(d, n):
        if n < len(chunks):
            stage1(d, *chunks[n]).start()

    def add_into(target, other, lead):
        def one(i, _):
            a, b = target(i), other(i)
            a[...] = (a[...].astype(FULL) + b[...].astype(FULL)).astype(LOW)
            return 0

        lax.fori_loop(0, lead, one, 0)

    def after1(d, zi, part):
        stage1(d, zi, part).wait_recv()
        low, high = cuts[part]
        size = high - low
        add_into(
            lambda i: mine(d, zi, part, lax.div(i, size), low + lax.rem(i, size)),
            lambda i: r1.at[d, zi, lax.div(i, size), low + lax.rem(i, size)],
            2 * size,
        )
        stage2(d, zi, part).start()

    def after2(d, zi, part):
        low, high = cuts[part]
        stage2(d, zi, part).wait_recv()
        own_place = x if y_first(d, zi, part) else y
        add_into(lambda i: r2.at[d, zi, low + i], lambda i: mine(d, zi, part, own_place, low + i), high - low)
        if zi > 0:
            pl.when(z == 0)(stage3(d, zi, part, True).start)
        if zi < nz - 1:
            pl.when(z == nz - 1)(stage3(d, zi, part, False).start)

    def after3(d, zi, part, far):
        low, high = cuts[part]
        if far < zi:
            @pl.when(z == far)
            def _():
                arrive3(d, zi, part, True).wait_recv()
                add_into(lambda i: r2.at[d, zi, low + i], lambda i: r3.at[d, zi, low + i], high - low)
                stage3(d, zi, part, True).start()

        if nz - 1 - far > zi:
            @pl.when(z == nz - 1 - far)
            def _():
                arrive3(d, zi, part, False).wait_recv()
                add_into(lambda i: r2.at[d, zi, low + i], lambda i: r3.at[d, zi, low + i], high - low)
                stage3(d, zi, part, False).start()

    def last3(d, zi, part):
        low, high = cuts[part]

        @pl.when(z == zi)
        def _():
            if zi > 0:
                arrive3(d, zi, part, True).wait_recv()
            if zi < nz - 1:
                arrive3(d, zi, part, False).wait_recv()

            def one(i, _):
                total = r2[d, zi, i].astype(FULL)
                if zi > 0:
                    total = total + r3[d, zi, i].astype(FULL)
                if zi < nz - 1:
                    total = total + r3[d, nz, i].astype(FULL)
                fin[d, i] = total
                return 0

            lax.fori_loop(low, high, one, 0)

    def advance(n):
        stages = [after1, after2] + [partial(after3, far=far) for far in range(1, nz - 1)] + [last3]
        for behind, stage in enumerate(stages):
            for d in range(2):
                if 0 <= n - behind < len(chunks):
                    stage(d, *chunks[n - behind])
                if not behind:
                    begin(d, n + 2)

    steps = len(chunks) + nz

    def finish_sends():
        for zi, part in chunks:
            for d in range(2):
                stage1(d, zi, part).wait_send()
                stage2(d, zi, part).wait_send()
                pl.when(z != zi)(stage3(d, zi, part, True).wait_send)

    for d in range(2):
        forth(d)
        down_grads(d)
        begin(d, 0)
        begin(d, 1)
    for d in range(2):
        back_to_width(d)
    up_grads(0)
    norm_feed_back(0)
    up_grads(1)
    norm_feed_back(1)

    def go_copies(j):
        slot = slots[j]
        return (
            pltpu.make_async_copy(go_send.at[j], go_all.at[chip], go_s.at[j]),
            remote(go_send.at[j], go_all.at[chip], go_s.at[j], go_r.at[chip], here.device(z=slot // 2, x=slot % 2)),
        )

    own_half = own.at[pl.ds(pl.multiple_of(core * half, half), half), :]
    for d in range(2):
        spot = eb.at[d, their_rows]
        remote(spot, spot, near_s.at[6 + d], near_r.at[6 + d], partner).wait_recv()
        go = dot(eb[d], own_half[...], (1, 1)).astype(LOW)
        for j in range(per_core):
            go_send[j, :, d * head : (d + 1) * head] = go[:, j * head : (j + 1) * head]
    for j, slot in enumerate(slots):
        stay, leave = go_copies(j)
        pl.when(chip == slot)(stay.start)
        pl.when(chip != slot)(leave.start)
    for d in range(2):
        ours = eb[d, :, pl.ds(pl.multiple_of(core * half, half), half)]
        for m in range(0, width, half):
            keep(d, dot(att[:, m : m + half], ours, (0, 0)).astype(LOW), m, 0, 8, unit)

    for d in range(2):
        remote(feed_in.at[d], feed_in.at[d], near_s.at[4 + d], near_r.at[4 + d], partner).wait_recv()
        out = middle_of(d, my_rows) + SCALES[d] * (feed[d, my_rows, :] + feed_in[d] + down_bias)
        act_ref[d] = out.astype(LOW)
    total = jnp.zeros((parts, 2 * stride), FULL)
    for v in range(2, 6):
        for d in range(2):
            total = total + placed(sums[v, d], wide_owner, in_piece, v * rows_in + d * stride)
    hid_lane = lax.broadcasted_iota(jnp.int32, (hidden, 128), 0)
    in_hidden = (lax.rem(hid_lane, rows_hid) == lax.broadcasted_iota(jnp.int32, hid_lane.shape, 1)).astype(LOW)
    for d in range(2):
        total = total + placed(sums["up", d], hid_owner, in_hidden, 8 * rows_in + d * stride)
    for c in range(pack.shape[1]):
        pack[:, c, :] = total[:, c * 128 : (c + 1) * 128]
    advance(0)

    def h_copy(i):
        rows = slice(i * tile, (i + 1) * tile)
        return pltpu.make_async_copy(h_all.at[rows], hbuf.at[i % 2], h_s.at[i % 2])

    @pl.when(has == 1)
    def _():
        h_copy(0).start()
        h_copy(1).start()
        for t in range(chips):
            stay = pltpu.make_async_copy(go_send.at[0], go_all.at[t], go_s.at[job])
            come = remote(go_send.at[0], go_all.at[t], go_s.at[0], go_r.at[t], here.device(z=t // 2, x=t % 2))
            pl.when(chip == t)(stay.wait)
            pl.when(chip != t)(come.wait_recv)
        for i in range(chips):
            rows = slice(i * tile, (i + 1) * tile)
            kt_ref[:, rows] = k_ref[rows, :].T
            up_t = go_all[i].T
            for d in range(2):
                part = up_t[d * head : (d + 1) * head, :]
                got_ref[d, :, rows] = part
                delta_ref[d, :, rows] = jnp.sum(part.astype(FULL) * ot_ref[:, rows], axis=0, keepdims=True)
                gqt_ref[d, :, rows] = jnp.zeros((head, tile), FULL)

    def key_tile(j):
        keys = slice(j * tile, (j + 1) * tile)
        key = k_ref[keys, :]
        value = v_ref[keys, :]
        key_t = kt_ref[:, keys]

        def step(i, carry, masked):
            gv, gk0, gk1 = carry
            rows = pl.ds(i * tile if masked else pl.multiple_of(i * tile, tile), tile)
            query = q_ref[rows, :]
            scores = dot(key, query, (1, 1))
            if masked:
                key_pos = lax.broadcasted_iota(jnp.int32, scores.shape, 0)
                query_pos = lax.broadcasted_iota(jnp.int32, scores.shape, 1)
                scores = jnp.where(key_pos <= query_pos, scores, NEGATIVE)
            probs = jnp.exp(scores - top_ref[:, rows])
            gv = gv + dot(probs.astype(LOW), go_all[i], (1, 0))
            gks = [gk0, gk1]
            for d in range(2):
                prob_grad = dot(value, got_ref[d, :, rows], (1, 0))
                score_low = (probs * (prob_grad - delta_ref[d, :, rows])).astype(LOW)
                gks[d] = gks[d] + dot(score_low, query, (1, 0))
                gqt_ref[d, :, rows] += dot(key_t, score_low, (1, 0))
            return gv, gks[0], gks[1]

        zero = jnp.zeros((tile, head), FULL)
        carry = step(j, (jnp.zeros((tile, 2 * head), FULL), zero, zero), True)
        gv, gk0, gk1 = lax.fori_loop(j + 1, chips, lambda i, c: step(i, c, False), carry)
        gsend[j, 1] = jnp.concatenate([gk0, gk1], axis=1).astype(LOW)
        gsend[j, 2] = gv.astype(LOW)

    def kv_copies(t):
        src, dst = gsend.at[t, pl.ds(1, 2)], gat.at[job, pl.ds(1, 2)]
        to = here.device(z=t // 2, x=t % 2)
        return pltpu.make_async_copy(src, dst, kv_s.at[t]), remote(src, dst, kv_s.at[t], kv_r.at[job], to)

    def q_copies(t):
        src, dst = gsend.at[t, 0], gat.at[job, 0]
        to = here.device(z=t // 2, x=t % 2)
        return pltpu.make_async_copy(src, dst, q_s.at[t]), remote(src, dst, q_s.at[t], q_r.at[job], to)

    def launch(copies, t):
        stay, leave = copies(t)
        pl.when(chip == t)(stay.start)
        pl.when(chip != t)(leave.start)

    between = {1: 1, 3: 2, 7: 3}
    for j in range(chips):
        @pl.when(has == 1)
        def _(j=j):
            key_tile(j)
            launch(kv_copies, j)

        if j in between:
            advance(between[j])

    @pl.when(has == 1)
    def _():
        for i in range(chips):
            rows = slice(i * tile, (i + 1) * tile)
            both = jnp.concatenate([gqt_ref[0, :, rows], gqt_ref[1, :, rows]], axis=0) * factor
            gsend[i, 0] = both.T.astype(LOW)
            launch(q_copies, i)

    def mix_y():
        return remote(head_sum.at[:, :, 1 - y], hs_in, ex_s.at[0], ex_r.at[0], here.device(y=1 - y))

    def mix_copies(t):
        src, dst = head_sum.at[t // 2, t % 2, y], mix_in.at[job]
        to = here.device(z=t // 2, x=t % 2)
        return pltpu.make_async_copy(src, dst, mix_s.at[t]), remote(src, dst, mix_s.at[t], mix_r.at[job], to)

    @pl.when(has == 1)
    def _():
        for i in range(chips):
            h_copy(i).wait()
            right = jnp.concatenate([gsend[i, t] for t in range(3)], axis=1)
            part = dot(hbuf[i % 2], right, (0, 0))
            if i == 0:
                head_acc[...] = part
            else:
                head_acc[...] += part
            if i + 2 < chips:
                h_copy(i + 2).start()
        for u in range(parts // 2):
            zz, xx, yy = u // (2 * ny), (u // ny) % 2, u % ny
            head_sum[zz, xx, yy] = head_acc[u * unit : (u + 1) * unit, :].astype(LOW)
        mix_y().start()

    advance(4)

    @pl.when(has == 1)
    def _():
        mix_y().wait_recv()
        mix_y().wait_send()
        add_into(
            lambda i: head_sum.at[lax.div(i, 2), lax.rem(i, 2), y],
            lambda i: hs_in.at[lax.div(i, 2), lax.rem(i, 2)],
            chips,
        )
        for t in range(chips):
            launch(mix_copies, t)

    biases = []
    for t in (0, 2):
        acc = jnp.zeros((1, 2 * head), FULL)
        for i in range(chips):
            acc = acc + jnp.sum(gsend[i, t].astype(FULL), axis=0, keepdims=True)
        biases.append(jnp.where(has == 1, acc, 0.0))
    total = jnp.concatenate([pack[:, c, :] for c in range(pack.shape[1])], axis=1)
    for b in range(2):
        rows = lax.broadcasted_iota(jnp.int32, (parts, 2 * head), 0)
        first_entry = (core * per_core + job) * head + b * width
        across = lax.broadcasted_iota(jnp.int32, (1, 2 * head), 1)
        down_lane = lax.broadcasted_iota(jnp.int32, (2 * head, 1), 0)
        owner, _ = bias_piece(lax.rem(across, head) + first_entry, rows_in, ny)
        _, column = bias_piece(lax.rem(down_lane, head) + first_entry, rows_in, ny)
        column = column + lax.div(down_lane, head) * stride
        spread = jnp.where(rows == owner, biases[b], 0.0)
        turn = lax.broadcasted_iota(jnp.int32, (2 * head, 2 * stride), 1) == column
        high = spread.astype(LOW)
        low = (spread - high.astype(FULL)).astype(LOW)
        total = total + dot(high, turn.astype(LOW), (1, 0)) + dot(low, turn.astype(LOW), (1, 0))
    advance(5)

    for copy in exchanges:
        copy.wait_send()
    loads[3].wait()
    for j, slot in enumerate(slots):
        @pl.when(chip != slot)
        def _(j=j, slot=slot):
            to = here.device(z=slot // 2, x=slot % 2)
            remote(gat.at[j, pl.ds(1, 2)], gat.at[j, pl.ds(1, 2)], kv_s.at[0], kv_r.at[j], to).wait_recv()
            remote(gat.at[j, 0], gat.at[j, 0], q_s.at[0], q_r.at[j], to).wait_recv()

        @pl.when(chip == slot)
        def _(j=j, slot=slot):
            kv_copies(slot)[0].wait()
            q_copies(slot)[0].wait()

    def first_swap(d):
        return remote(gh2.at[d, their_rows], gh2_in.at[d], ex_s.at[1 + d], ex_r.at[1 + d], partner)

    for d in range(2):
        lanes = slice(d * head, (d + 1) * head)
        first = None
        for p in range(per_core // 2):
            left = jnp.concatenate(
                [gat[2 * p + o, t][:, lanes] for t in range(3) for o in range(2)], axis=1
            )
            part = dot(left, mw[:, :, :, p * unit : (p + 1) * unit].reshape(width, half), (1, 1))
            first = part if first is None else first + part
        gh2[d] = first
        first_swap(d).start()
    normed, inv = normalize(x2_ref[my_rows, :].astype(FULL))
    for d in range(2):
        first_swap(d).wait_recv()
        grad = gh2[d, my_rows, :] + gh2_in[d]
        for v, row in ((0, jnp.sum(grad * normed, axis=0, keepdims=True)), (1, jnp.sum(grad, axis=0, keepdims=True))):
            total = total + placed(row, wide_owner, in_piece, v * rows_in + d * stride)
        whole = gmid[d] + norm_back(grad, normed, inv, first_gain)
        ing_ref[d] = whole
    for c in range(pack.shape[1]):
        pack[:, c, :] = total[:, c * 128 : (c + 1) * 128]
    me = flat(z, x, y, core)

    def vec_copy(n):
        device, index, _ = others[n]
        return remote(pack.at[index], vec_in.at[me], vec_s.at[n], vec_r.at[n], device)

    def vec_come(n):
        device, _, index = others[n]
        return remote(pack.at[index], vec_in.at[index], vec_s.at[n], vec_r.at[n], device)

    for n in range(len(others)):
        vec_copy(n).start()

    for n in range(6, steps - 1):
        advance(n)
    mine_in = pl.ds(pl.multiple_of(core * rows_in, 8), rows_in)
    their_in = pl.ds(pl.multiple_of((1 - core) * rows_in, 8), rows_in)
    for j, slot in enumerate(slots):
        @pl.when(chip != slot)
        def _(j=j, slot=slot):
            to = here.device(z=slot // 2, x=slot % 2)
            remote(mix_in.at[j], mix_in.at[j], mix_s.at[0], mix_r.at[j], to).wait_recv()

        @pl.when(chip == slot)
        def _(j=j, slot=slot):
            mix_copies(slot)[0].wait()

        mixf[j] = mix_in[j].astype(FULL)
    mix_pass = remote(mixf.at[:, their_in], mix_swap, ex_s.at[5], ex_r.at[5], partner)
    mix_pass.start()

    for n in range(steps - 1, steps):
        advance(n)

    def last_swap(d):
        return remote(fin.at[d, pl.ds(4, slabs - 4), their_in], swap.at[d], ex_s.at[3 + d], ex_r.at[3 + d], partner)

    for d in range(2):
        last_swap(d).start()
    for d in range(2):
        last_swap(d).wait_recv()
    mix_pass.wait_recv()
    for n in range(len(others)):
        vec_come(n).wait_recv()
    vec_in[me] = pack[me]
    vec_ref[...] = jnp.sum(vec_in[...], axis=0)

    give_cot.wait_send()
    give_ow.wait_send()
    finish_sends()
    for j, slot in enumerate(slots):
        pl.when(chip != slot)(go_copies(j)[1].wait_send)

    @pl.when(has == 1)
    def _():
        for t in range(chips):
            @pl.when(chip != t)
            def _(t=t):
                kv_copies(t)[1].wait_send()
                q_copies(t)[1].wait_send()
                mix_copies(t)[1].wait_send()

    for d in range(2):
        first_swap(d).wait_send()
        last_swap(d).wait_send()
    mix_pass.wait_send()
    for n in range(len(others)):
        vec_copy(n).wait_send()


def finish_kernel(
    nz, act, ing, fin, swap, mixf, mix_swap, vec,
    act_ref, ing_ref, gain1_ref, shift1_ref, mix_ref, mixb_ref, out_ref, outb_ref, gain2_ref, shift2_ref, up_ref, upb_ref,
    dn_ref, dnb_ref,
):
    ny = 2
    core = lax.rem(lax.axis_index("seq"), 2)
    width = ing.shape[2]
    slabs, unit = fin.shape[1], fin.shape[2]
    rows_in = unit // 2
    per_core, head = mixf.shape[0], width // HEADS
    from_row = lax.broadcasted_iota(jnp.int32, (width, width), 0)
    turn = (from_row == natural_of((1, width), 1, rows_in, ny)).astype(LOW)
    mine_in = pl.ds(pl.multiple_of(core * rows_in, 8), rows_in)
    is_first = core == 0

    def by_core(a, b):
        return jnp.where(is_first, a, b), jnp.where(is_first, b, a)

    hidden = (slabs - 5) * fin.shape[3]
    block = hidden // (2 * nz)
    sides = [by_core(mixf[j, mine_in, :], mix_swap[j]) for j in range(per_core)]
    for d in range(2):
        act_ref[d] = dot(act[d], turn, (1, 1)).astype(LOW)
        top_half = jnp.concatenate([fin[d, 0], fin[d, 1]], axis=1)
        low_half = jnp.concatenate([fin[d, 2], fin[d, 3]], axis=1)
        ours = jnp.concatenate([fin[d, s, mine_in, :] for s in range(4, slabs - 1)], axis=1)
        came = jnp.concatenate([swap[d, s] for s in range(slabs - 5)], axis=1)
        one, two = by_core(ours, came)
        blocks = []
        for i in range(hidden // block):
            blocks += [one[:, i * block : (i + 1) * block], two[:, i * block : (i + 1) * block]]
        up_ref[d] = jnp.concatenate(blocks, axis=1)
        one, two = by_core(fin[d, slabs - 1, mine_in, :], swap[d, slabs - 5])
        stacked = [ing[d], top_half, low_half, jnp.concatenate([one, two], axis=1)]
        moved = split_dot(jnp.concatenate(stacked, axis=0), turn, (1, 1))
        span = ing.shape[1]
        ing_ref[d] = moved[:span]
        dn_ref[d] = moved[span : span + 2 * unit]
        out_ref[d] = moved[span + 2 * unit :]
        blocks = []
        for t in range(3):
            for c in range(2):
                for j in range(per_core):
                    start = t * 2 * head + d * head
                    blocks.append(sides[j][c][:, start : start + head])
        mix_ref[d] = jnp.concatenate(blocks, axis=1)
    flat = jnp.concatenate([vec[c : c + 1, :] for c in range(vec.shape[0])], axis=1)
    stride = flat.shape[1] // 2
    smalls = (gain1_ref, shift1_ref, gain2_ref, shift2_ref, outb_ref, dnb_ref, mixb_ref, upb_ref)
    start = 0
    for ref in smalls:
        size = ref.shape[1]
        for d in range(2):
            ref[d : d + 1, :] = flat[:, d * stride + start : d * stride + start + size]
        start += size


def finish(nz, act, ing, fin, swap, mixf, mix_swap, vec):
    width = ing.shape[2]
    slabs, unit, half = fin.shape[1:]
    rows_in = unit // 2
    hidden = (slabs - 5) * half

    def full(*shape):
        return jax.ShapeDtypeStruct((2,) + shape, FULL)

    small = full(rows_in)
    return pl.pallas_call(
        partial(finish_kernel, nz),
        out_shape=(
            jax.ShapeDtypeStruct(act.shape, LOW), jax.ShapeDtypeStruct(ing.shape, FULL), small, small,
            full(rows_in, 3 * width), full(2 * rows_in), full(rows_in, width), small, small, small,
            full(rows_in, 2 * hidden), full(2 * unit), full(2 * unit, width), small,
        ),
        compiler_params=pltpu.CompilerParams(vmem_limit_bytes=60 << 20),
        name="finish",
    )(act, ing, fin, swap, mixf, mix_swap, vec)


def rest(nz, x2, attended, cot, mw_all, up, dn, q, k, v, out_t, top, first_low):
    length, head = q.shape
    _, span, width = cot.shape
    hidden = dn.shape[0]
    half = width // 2
    chips = 2 * nz
    parts = 8 * nz
    rows = 2 * span
    per_core = HEADS // 2
    unit = up.shape[4]
    units = mw_all.shape[:3]
    rows_in = unit // 2
    slabs = 9
    anywhere = pl.BlockSpec(memory_space=pl.ANY)
    vmem = pl.BlockSpec(memory_space=pltpu.VMEM)
    low, full = partial(pltpu.VMEM, dtype=LOW), partial(pltpu.VMEM, dtype=FULL)
    return pl.pallas_call(
        partial(rest_kernel, nz, 512),
        out_shape=(
            jax.ShapeDtypeStruct((2, span, width), LOW),
            jax.ShapeDtypeStruct((2, span, width), FULL),
            jax.ShapeDtypeStruct((2, slabs, unit, half), FULL),
            jax.ShapeDtypeStruct((2, slabs - 4, rows_in, half), FULL),
            jax.ShapeDtypeStruct((per_core, unit, half), FULL),
            jax.ShapeDtypeStruct((per_core, rows_in, half), FULL),
            jax.ShapeDtypeStruct((5, 128), FULL),
        ),
        in_specs=[vmem] * 3 + [anywhere] * 3 + [vmem] * 5 + [anywhere],
        out_specs=[vmem] * 7,
        scratch_shapes=[
            low(units + (unit, hidden)),
            low((hidden, width)),
            low((2,) + units + (unit, half)),
            low((width, width)),
            low((width, width)),
            low(units + (16, half)),
            low((rows, width)),
            low((2, rows, width)),
            low((2, rows, width)),
            low((2, rows, hidden)),
            low((2, rows, hidden)),
            full((rows, width)),
            full((2, rows, width)),
            full((2, span, width)),
            full((2, rows, width)),
            full((2, span, width)),
            full((2, span, width)),
            low((2, rows, width)),
            low((2,) + units + (slabs, unit, half)),
            low((per_core, rows, 2 * head)),
            low((chips, rows, 2 * head)),
            low((head, length)),
            low((2, head, length)),
            full((2, 1, length)),
            full((2, head, length)),
            low((chips, 3, rows, 2 * head)),
            low((per_core, 3, rows, 2 * head)),
            low(units + (per_core // 2 * unit, half)),
            low((2, rows, width)),
            full((width, half)),
            low(units + (unit, half)),
            low((nz, 2, unit, half)),
            low((per_core, unit, half)),
            low((2, nz, 2, slabs, unit, half)),
            low((2, nz, slabs, unit, half)),
            low((2, nz + 1, slabs, unit, half)),
            full((parts, 5, 128)),
            full((parts, 5, 128)),
            DMA((8,)),
            DMA((8,)),
            DMA((8,)),
            DMA((2,)),
            DMA((per_core,)),
            DMA((chips,)),
            DMA((chips,)),
            DMA((per_core,)),
            DMA((chips,)),
            DMA((per_core,)),
            DMA((2, nz, 3)),
            DMA((2, nz, 3)),
            DMA((2, nz, 3)),
            DMA((2, nz, 3)),
            DMA((2, nz, 3)),
            DMA((2, 2, nz, 3)),
            DMA((6,)),
            DMA((6,)),
            DMA((parts - 1,)),
            DMA((parts - 1,)),
            DMA((chips,)),
            DMA((per_core,)),
        ],
        compiler_params=pltpu.CompilerParams(vmem_limit_bytes=62 << 20, collective_id=1, has_side_effects=True),
        cost_estimate=pl.CostEstimate(
            flops=60 * rows * width * hidden, bytes_accessed=60 * width * hidden, transcendentals=length * length
        ),
        name="rest",
    )(x2, attended, cot, mw_all, up, dn, q, k, v, out_t, top, first_low)


def plain_on_device(
    inputs,
    attend_gain,
    attend_shift,
    mixing_weight,
    mixing_bias,
    output_weight,
    output_bias,
    feed_gain,
    feed_shift,
    up_weight,
    up_bias,
    down_weight,
    down_bias,
    cotangent,
):
    place = Place()
    _, span, width = inputs.shape
    nz, ny, core, chip = place.nz, place.ny, place.core, place.chip
    chips = nz * 2
    parts = chips * 2 * ny
    head = width // HEADS
    per_core = HEADS // 2
    slots = [int((j + 0.5) * chips / per_core) for j in range(per_core)]
    half = width // 2
    hidden = up_weight.shape[1]
    rows_in = width // parts
    rows_hid = hidden // parts
    groups = [[2 * i + c for i in range(chips)] for c in range(2)]

    def exchange(values):
        return lax.all_to_all(values, "seq", 0, 0, axis_index_groups=groups, tiled=True)

    def spread(blocks):
        filled = [jnp.zeros_like(blocks[0])] * chips
        for j, slot in enumerate(slots):
            filled[slot] = blocks[j]
        return jnp.stack(filled)

    def collect(blocks):
        return jnp.stack([blocks[slot] for slot in slots])

    owned = [-1] * chips
    for j, slot in enumerate(slots):
        owned[slot] = j
    my_head = jnp.array(owned, jnp.int32)[chip]
    busy = (my_head >= 0).astype(FULL)
    my_head = jnp.maximum(my_head, 0)

    def by_core(values, dim):
        mine = lax.dynamic_index_in_dim(values, core, dim, keepdims=False)
        theirs = lax.dynamic_index_in_dim(values, 1 - core, dim, keepdims=False)
        return mine, theirs

    vectors = jnp.concatenate(
        [attend_gain, attend_shift, feed_gain, feed_shift, output_bias, down_bias, mixing_bias, up_bias]
    )
    vectors = place.both(vectors, vectors)
    vectors = place.gather(vectors, "z", 0)
    vectors = place.gather(vectors, "x", 1)
    vectors = place.gather(vectors, "y", 3)
    vectors = vectors.reshape(parts, -1).astype(FULL)
    cuts = [vectors[:, i * rows_in : (i + 1) * rows_in].reshape(-1) for i in range(6)]
    first_gain, first_shift, second_gain, second_shift, out_bias, down_bias_all = cuts
    mix_bias = vectors[:, 6 * rows_in : 8 * rows_in].reshape(2, HEADS, head)
    up_bias_all = vectors[:, 8 * rows_in :].reshape(chips, 2, ny * rows_hid)
    up_bias_mine = lax.dynamic_index_in_dim(up_bias_all, core, 1, keepdims=False).reshape(-1)

    own = inputs.reshape(span, width)
    column = [own] + [place.send(own, "z", d) for d in range(1, nz)]
    beside = [place.send(piece, "x") for piece in column]
    x_all = jnp.zeros((nz, 2, span, width), LOW)
    for d in range(nz):
        at = lax.rem(place.z + nz - d, nz)
        x_all = lax.dynamic_update_slice(x_all, column[d][None, None], (at, place.x, 0, 0))
        x_all = lax.dynamic_update_slice(x_all, beside[d][None, None], (at, 1 - place.x, 0, 0))
    x_all = place.both(x_all, x_all).transpose(1, 2, 0, 3, 4)
    x_all = x_all.reshape(chips * 2 * span, width)

    def gather_rows(mine, theirs):
        block = place.both(mine, theirs)
        block = place.gather(block, "z", 0)
        block = place.gather(block, "x", 1)
        block = place.gather(block, "y", 3)
        return block.reshape(parts * block.shape[-2], block.shape[-1])

    mixing = mixing_weight.reshape(rows_in, 3, 2, half)
    mine, theirs = by_core(mixing, 2)
    mixing = gather_rows(mine.reshape(rows_in, -1), theirs.reshape(rows_in, -1))
    mine, theirs = by_core(output_weight.reshape(rows_in, 2, half), 1)
    out_half = gather_rows(mine, theirs)
    out_all = place.both(out_half, out_half).transpose(1, 0, 2).reshape(width, width)
    mine, theirs = by_core(up_weight.reshape(rows_in, chips, 2, ny * rows_hid), 2)
    up = gather_rows(mine.reshape(rows_in, -1), theirs.reshape(rows_in, -1))
    down = place.gather(down_weight, "z", 0)
    down = place.gather(down, "x", 1)
    down = place.gather(down, "y", 2).reshape(chips * ny * rows_hid, width)

    mixing = mixing.reshape(width, 3, per_core, head)
    head_weight = lax.dynamic_index_in_dim(mixing, my_head, 2, keepdims=False).reshape(width, 3 * head)
    whole_head = core * per_core + my_head
    head_bias = lax.dynamic_index_in_dim(mix_bias, whole_head, 1, keepdims=False)
    head_bias = jnp.concatenate([head_bias[0], jnp.zeros((head,), FULL), head_bias[1]])
    first_low, q, k, v, out, out_t, top = attend_plain(
        x_all, first_gain[None], first_shift[None], head_weight, head_bias[None]
    )
    attended = collect(exchange(out.reshape(chips, 2 * span, head)))
    attended = attended.transpose(1, 0, 2).reshape(2 * span, half)
    attended = place.both(attended, attended).transpose(1, 0, 2).reshape(2 * span, width)

    residual = lax.dynamic_slice_in_dim(x_all, chip * 2 * span, 2 * span, 0).astype(FULL)
    branch = dot(attended, out_all, (1, 0)) + out_bias
    scale = jnp.array(SCALES, FULL)[:, None, None]
    middle = residual + scale * branch
    second_normed, second_inv = normalize(middle)
    second_low = (second_normed * second_gain + second_shift).astype(LOW)
    rows = second_low.reshape(4 * span, width)
    hidden_pre = dot(rows, up, (1, 0)) + up_bias_mine
    activated, gelu_back = jax.vjp(partial(jax.nn.gelu, approximate=True), hidden_pre)
    activated_low = activated.astype(LOW)
    feed_part = dot(activated_low, down, (1, 0)).reshape(2, 2, span, width)
    mine, theirs = by_core(feed_part, 1)
    feed_own = mine + place.send(theirs, "core") + down_bias_all

    def own_rows(values):
        return lax.dynamic_index_in_dim(
            values.reshape((2, 2, span) + values.shape[2:]), core, 1, keepdims=False
        )

    activations = (own_rows(middle) + scale * feed_own).astype(LOW)
    upstream_own = cotangent.reshape(2, span, width)
    upstream = place.both(upstream_own, upstream_own).transpose(1, 0, 2, 3)
    down_in = (scale[..., None] * upstream.astype(FULL)).astype(LOW).reshape(4 * span, width)
    hidden_low = gelu_back(dot(down_in, down, (1, 1)))[0].astype(LOW)
    second_part = dot(hidden_low, up, (1, 1)).reshape(2, 2, span, width)
    mine, theirs = by_core(second_part, 1)
    second_grad = mine + place.send(theirs, "core")
    normed_own, inv_own = own_rows(second_normed), own_rows(second_inv)
    middle_grad = upstream_own.astype(FULL) + norm_back(second_grad, normed_own, inv_own, second_gain)
    branch_own = (scale * middle_grad).astype(LOW)
    branch_low = place.both(branch_own, branch_own).transpose(1, 0, 2, 3).reshape(2, 2 * span, width)
    out_rows = lax.dynamic_slice_in_dim(out_all, core * half, half, 0)
    go = dot(branch_low.reshape(4 * span, width), out_rows, (1, 1)).astype(LOW)
    go = go.reshape(2, 2 * span, per_core, head).transpose(2, 1, 0, 3).reshape(per_core, 2 * span, 2 * head)
    go = exchange(spread(go)).reshape(chips * 2 * span, 2 * head)

    gq, gk, gv = attend_back(q, k, v, out_t, top, go)
    head_grads = jnp.concatenate([gq, gk, gv], axis=1)

    depth_rows = second_low.reshape(2, 2 * span, width)
    hidden_rows = hidden_low.reshape(2, 2 * span, -1)
    active_rows = activated_low.reshape(2, 2 * span, -1)
    in_rows = down_in.reshape(2, 2 * span, width)
    branch_cols = lax.dynamic_slice_in_dim(branch_low, core * half, half, 2)
    orders = (("y", "x"), ("x", "y"))

    def scatter_chips(values, order):
        dims = {"x": 1, "y": 2}
        values = place.scatter(values, order[0], dims[order[0]]).astype(LOW)
        values = place.scatter(values, order[1], 1).astype(LOW)
        return place.scatter(values, "z", 0)

    def scatter_rows(values, order):
        shaped = values.reshape(nz, 2, 2, ny, rows_in, -1).transpose(0, 1, 3, 2, 4, 5)
        summed = scatter_chips(shaped, order)
        mine, theirs = by_core(summed, 0)
        return place.both(mine, theirs)

    down_grads, up_grads, out_grads = [], [], []
    for depth in range(2):
        grad = dot(active_rows[depth], in_rows[depth], (0, 0)).astype(LOW)
        down_grads.append(scatter_chips(grad.reshape(nz, 2, ny, rows_hid, width), orders[depth]))
    for depth in range(2):
        grad = dot(depth_rows[depth], hidden_rows[depth], (0, 0)).astype(LOW)
        grad = scatter_rows(grad, orders[depth]).reshape(2, rows_in, chips, -1)
        up_grads.append(grad.transpose(1, 2, 0, 3).reshape(rows_in, hidden))
    for depth in range(2):
        grad = dot(attended, branch_cols[depth], (0, 0)).astype(LOW)
        out_grads.append(scatter_rows(grad, orders[depth]).transpose(1, 0, 2).reshape(rows_in, width))

    head_sum = dot(first_low, head_grads, (0, 0)).astype(LOW).reshape(nz, 2, 2, ny, rows_in, 6 * head)
    head_sum = place.scatter(head_sum, "y", 3).astype(LOW).reshape(chips, 2, rows_in, 6 * head)
    head_sum = collect(exchange(head_sum))
    mine, theirs = by_core(head_sum, 1)
    mixing_grad = place.both(mine, theirs).reshape(HEADS, rows_in, 3, 2, head)
    mixing_grad = mixing_grad.transpose(3, 1, 2, 0, 4).reshape(2, rows_in, 3 * width).astype(FULL)

    mixed_grads = collect(exchange(head_grads.reshape(chips, 2 * span, 6 * head)))
    mixed_grads = mixed_grads.reshape(per_core, 2 * span, 3, 2, head).transpose(3, 1, 2, 0, 4)
    mixed_grads = mixed_grads.reshape(4 * span, 3 * half)
    first_part = dot(mixed_grads, mixing.reshape(width, 3 * half), (1, 1)).reshape(2, 2, span, width)
    mine, theirs = by_core(first_part, 1)
    first_grad = mine + place.send(theirs, "core")
    first_normed, first_inv = normalize(own.astype(FULL))
    input_grad = middle_grad + norm_back(first_grad, first_normed, first_inv, first_gain)

    bias_sum = jnp.sum(head_grads.astype(FULL), axis=0).reshape(3, 2, head) * busy
    spot = (jnp.arange(HEADS) == whole_head).astype(FULL)[None, None, :, None]
    bias_sum = (jnp.stack([bias_sum[0], bias_sum[2]], axis=1)[:, :, None, :] * spot).reshape(2, parts, -1)
    hidden_sum = jnp.sum(hidden_rows.astype(FULL), axis=1).reshape(2, chips, 1, ny * rows_hid)
    hidden_spot = (jnp.arange(2) == core).astype(FULL)[None, None, :, None]
    hidden_sum = (hidden_sum * hidden_spot).reshape(2, parts, rows_hid)
    in_own = (scale * upstream_own.astype(FULL)).astype(LOW)
    sums = [
        jnp.sum(first_grad * first_normed, axis=1),
        jnp.sum(first_grad, axis=1),
        jnp.sum(second_grad * normed_own, axis=1),
        jnp.sum(second_grad, axis=1),
        jnp.sum(branch_own.astype(FULL), axis=1),
        jnp.sum(in_own.astype(FULL), axis=1),
    ]
    sums = [item.reshape(2, parts, rows_in) for item in sums] + [bias_sum, hidden_sum]
    sums = jnp.concatenate(sums, axis=2).reshape(2, nz, 2, 2, ny, -1)
    sums = place.scatter(sums, "y", 4)
    sums = place.scatter(sums, "x", 2)
    sums = place.scatter(sums, "core", 2)
    sums = place.scatter(sums, "z", 1)
    small = [sums[:, i * rows_in : (i + 1) * rows_in] for i in range(6)]
    return (
        activations[:, None],
        input_grad[:, None],
        small[0],
        small[1],
        mixing_grad,
        sums[:, 6 * rows_in : 8 * rows_in],
        jnp.stack(out_grads),
        small[4],
        small[2],
        small[3],
        jnp.stack(up_grads),
        sums[:, 8 * rows_in :],
        jnp.stack(down_grads),
        small[5],
    )


def on_device(
    inputs,
    attend_gain,
    attend_shift,
    mixing_weight,
    mixing_bias,
    output_weight,
    output_bias,
    feed_gain,
    feed_shift,
    up_weight,
    up_bias,
    down_weight,
    down_bias,
    cotangent,
):
    place = Place()
    _, span, width = inputs.shape
    nz, ny, core, chip = place.nz, place.ny, place.core, place.chip
    chips = nz * 2
    parts = chips * 2 * ny
    head = width // HEADS
    per_core = HEADS // 2
    half = width // 2
    hidden = up_weight.shape[1]
    rows_in = width // parts
    rows_hid = hidden // parts
    groups = [[2 * i + c for i in range(chips)] for c in range(2)]

    def by_core(values, dim):
        mine = lax.dynamic_index_in_dim(values, core, dim, keepdims=False)
        theirs = lax.dynamic_index_in_dim(values, 1 - core, dim, keepdims=False)
        return mine, theirs

    own = inputs.reshape(span, width)
    pairs = per_core // 2
    mix = mixing_weight.reshape(rows_in, 3, 2, pairs, 2, head).transpose(2, 3, 0, 1, 4, 5)
    mix = mix.reshape(2, pairs, rows_in, half)
    out_cols = output_weight.reshape(rows_in, 2, half).transpose(1, 0, 2)[:, None]
    vectors, start = jnp.zeros((half,), LOW), 0
    for piece in (
        attend_gain, attend_shift, feed_gain, feed_shift, output_bias, down_bias, mixing_bias, up_bias
    ):
        vectors = vectors + jnp.pad(piece, (start, half - start - piece.shape[0]))
        start += piece.shape[0]
    vectors = jnp.broadcast_to(jnp.pad(vectors[None], ((0, 7), (0, 0))), (2, 8, half))
    packed = jnp.concatenate([mix.reshape(2, pairs * rows_in, half), out_cols[:, 0], vectors], axis=1)
    up_cols = up_weight.reshape(rows_in, chips, 2, ny * rows_hid).transpose(2, 0, 1, 3).reshape(2, rows_in, -1)
    mine, theirs = by_core(packed, 0)
    packed = place.both(mine, theirs)
    cut = pairs * rows_in
    pair_rows = packed[:, :cut].reshape(2, pairs, rows_in, half).transpose(1, 0, 2, 3).reshape(2 * cut, half)
    packed_rows = jnp.concatenate([pair_rows, packed[:, cut + rows_in :].reshape(16, half)])
    mine, theirs = by_core(up_cols, 0)
    up_unit = place.both(mine, theirs).reshape(2 * rows_in, -1, half).transpose(1, 0, 2)
    up_unit = jnp.concatenate([up_unit, packed[:, cut : cut + rows_in].reshape(1, 2 * rows_in, half)])

    mw_all, up_all, dn_all, first_low, q, k, v, out_t, top, attended, x2 = attend(
        nz, ny, own, packed_rows, up_unit, down_weight
    )

    raw = rest(
        nz, x2.reshape(2 * span, width), attended, cotangent.reshape(2, span, width), mw_all,
        up_all, dn_all.reshape(-1, width), q, k, v, out_t, top, first_low,
    )
    activations, input_grad, *others = finish(nz, *raw)
    return (activations[:, None], input_grad[:, None], *others)


def tiles_well(mesh):
    ny, seq = mesh.shape["batch"], mesh.shape["seq"]
    rows_in = 768 // (seq * ny)
    return ny == 2 and seq // 2 >= HEADS // 2 and 2 * rows_in % 16 == 0 and 2 * rows_in * seq * ny == 2 * 768


def solution(mesh):
    shard = P(("seq", "batch"))
    grad = P(None, ("seq", "batch"))
    row = P(None, "batch", "seq", None)
    return jax.shard_map(
        on_device if tiles_well(mesh) else plain_on_device,
        mesh=mesh,
        in_specs=(P("batch", "seq", None),) + (shard,) * 12 + (row,),
        out_specs=(row, row) + (grad,) * 12,
        check_vma=False,
    )
```

```python
from functools import partial

import jax
import jax.numpy as jnp
from jax import lax
from jax.experimental import pallas as pl
from jax.experimental.pallas import tpu as pltpu
from jax.sharding import PartitionSpec as P

HEADS = 12
EPS = 1e-05
SCALES = (12.0 ** (-0.5), 48.0 ** (-0.5))
NEGATIVE = -1e30
LOW = jnp.bfloat16
FULL = jnp.float32
TILE = 256


def normalize(values):
    average = jnp.mean(values, axis=-1, keepdims=True)
    centered = values - average
    inv_std = lax.rsqrt(jnp.mean(centered * centered, axis=-1, keepdims=True) + EPS)
    return centered * inv_std, inv_std


def norm_back(gradient, normed, inv_std, gain):
    scaled = gradient * gain
    inner = (
        scaled
        - jnp.mean(scaled, axis=-1, keepdims=True)
        - normed * jnp.mean(scaled * normed, axis=-1, keepdims=True)
    )
    return inv_std * inner


def dot(a, b, dims):
    return lax.dot_general(a, b, ((dims[:1], dims[1:]), ((), ())), preferred_element_type=FULL)


class Place:
    def __init__(self):
        self.s = lax.axis_size("seq")
        self.ny = lax.axis_size("batch")
        self.nz = self.s // 4
        seq = lax.axis_index("seq")
        self.y = lax.axis_index("batch")
        self.core = lax.rem(seq, 2)
        self.chip = seq // 2
        self.x = lax.rem(self.chip, 2)
        self.z = self.chip // 2
        self.sizes = {"z": self.nz, "x": 2, "y": self.ny, "core": 2}
        self.at = {"z": self.z, "x": self.x, "y": self.y, "core": self.core}

    def send(self, values, axis, d=1):
        pairs = []
        for s in range(self.s):
            for y in range(self.ny):
                c, x, z, t = s % 2, (s // 2) % 2, s // 4, y
                if axis == "z":
                    z = (z + d) % self.nz
                elif axis == "x":
                    x = 1 - x
                elif axis == "core":
                    c = 1 - c
                else:
                    t = (y + d) % self.ny
                pairs.append((s * self.ny + y, ((z * 2 + x) * 2 + c) * self.ny + t))
        return lax.ppermute(values, ("seq", "batch"), pairs)

    def gather(self, values, axis, dim):
        size, at = self.sizes[axis], self.at[axis]
        shape = values.shape[:dim] + (size,) + values.shape[dim:]
        whole = lax.dynamic_update_slice_in_dim(
            jnp.zeros(shape, values.dtype), jnp.expand_dims(values, dim), at, dim
        )
        for d in range(1, size):
            piece = jnp.expand_dims(self.send(values, axis, d), dim)
            whole = lax.dynamic_update_slice_in_dim(whole, piece, lax.rem(at + size - d, size), dim)
        return whole

    def scatter(self, values, axis, dim):
        size, at = self.sizes[axis], self.at[axis]

        def pick(i):
            return lax.dynamic_index_in_dim(values, lax.rem(i, size), dim, keepdims=False)

        total = pick(at).astype(FULL)
        for d in range(1, size):
            total = total + self.send(pick(at + d), axis, d).astype(FULL)
        return total

    def both(self, mine, theirs):
        got = self.send(theirs, "core")
        first = self.core == 0
        return jnp.stack([jnp.where(first, mine, got), jnp.where(first, got, mine)])


def attend_plain_kernel(x_ref, gain_ref, shift_ref, w_ref, b_ref, h_ref, q_ref, k_ref, v_ref, o_ref, ot_ref, top_ref, vt_ref):
    length = x_ref.shape[0]
    head = q_ref.shape[1]
    tiles = length // TILE

    def project(i, _):
        rows = pl.ds(pl.multiple_of(i * TILE, TILE), TILE)
        normed, _ = normalize(x_ref[rows, :].astype(FULL))
        low = (normed * gain_ref[...] + shift_ref[...]).astype(LOW)
        h_ref[rows, :] = low
        mixed = dot(low, w_ref[...], (1, 0)) + b_ref[...]
        q_ref[rows, :] = (mixed[:, :head].astype(LOW) * (head ** (-0.5))).astype(LOW)
        k_ref[rows, :] = mixed[:, head : 2 * head].astype(LOW)
        value = mixed[:, 2 * head :].astype(LOW)
        v_ref[rows, :] = value
        vt_ref[:, rows] = value.T
        return 0

    lax.fori_loop(0, tiles, project, 0)

    def query_tile(i, _):
        rows = pl.ds(pl.multiple_of(i * TILE, TILE), TILE)
        query = q_ref[rows, :]

        def absorb(j, carry, masked):
            top, total, acc = carry
            keys = pl.ds(pl.multiple_of(j * TILE, TILE), TILE)
            scores = dot(k_ref[keys, :], query, (1, 1))
            if masked:
                key_pos = lax.broadcasted_iota(jnp.int32, scores.shape, 0)
                query_pos = lax.broadcasted_iota(jnp.int32, scores.shape, 1)
                scores = jnp.where(key_pos <= query_pos, scores, NEGATIVE)
            new_top = jnp.maximum(top, jnp.max(scores, axis=0, keepdims=True))
            weights = jnp.exp(scores - new_top)
            keep = jnp.exp(top - new_top)
            total = total * keep + jnp.sum(weights, axis=0, keepdims=True)
            acc = acc * keep + dot(vt_ref[:, keys], weights.astype(LOW), (1, 0))
            return new_top, total, acc

        start = (
            jnp.full((1, TILE), NEGATIVE, FULL),
            jnp.zeros((1, TILE), FULL),
            jnp.zeros((head, TILE), FULL),
        )
        carry = lax.fori_loop(0, i, lambda j, c: absorb(j, c, False), start)
        top, total, acc = absorb(i, carry, True)
        out = acc / total
        ot_ref[:, rows] = out
        o_ref[rows, :] = out.T.astype(LOW)
        top_ref[:, rows] = top + jnp.log(total)
        return 0

    lax.fori_loop(0, tiles, query_tile, 0)


def attend_plain(x_all, gain, shift, weight, bias):
    length, head = x_all.shape[0], weight.shape[1] // 3
    low = jax.ShapeDtypeStruct((length, head), LOW)
    return pl.pallas_call(
        attend_plain_kernel,
        out_shape=(
            jax.ShapeDtypeStruct(x_all.shape, LOW),
            low,
            low,
            low,
            low,
            jax.ShapeDtypeStruct((head, length), FULL),
            jax.ShapeDtypeStruct((1, length), FULL),
        ),
        scratch_shapes=[pltpu.VMEM((head, length), LOW)],
        compiler_params=pltpu.CompilerParams(vmem_limit_bytes=48 << 20),
        cost_estimate=pl.CostEstimate(
            flops=6 * length * length * head, bytes_accessed=8 * length * 768, transcendentals=length * length
        ),
        name="attend_plain",
    )(x_all, gain, shift, weight, bias)


def attend_back_kernel(
    q_ref, k_ref, v_ref, ot_ref, top_ref, go_ref, gq_ref, gk_ref, gv_ref, kt_ref, got_ref, delta_ref, gqt_ref
):
    length, head = q_ref.shape
    tiles = length // TILE
    factor = head ** (-0.5)

    def prepare(i, _):
        rows = pl.ds(pl.multiple_of(i * TILE, TILE), TILE)
        kt_ref[:, rows] = k_ref[rows, :].T
        up = go_ref[rows, :].T
        for d in range(2):
            mine = up[d * head : (d + 1) * head, :]
            got_ref[d, :, rows] = mine
            delta_ref[d, :, rows] = jnp.sum(mine.astype(FULL) * ot_ref[:, rows], axis=0, keepdims=True)
            gqt_ref[d, :, rows] = jnp.zeros((head, TILE), FULL)
        return 0

    lax.fori_loop(0, tiles, prepare, 0)

    def key_tile(j, _):
        keys = pl.ds(pl.multiple_of(j * TILE, TILE), TILE)
        key = k_ref[keys, :]
        value = v_ref[keys, :]
        key_t = kt_ref[:, keys]

        def step(i, carry, masked):
            gv, gk0, gk1 = carry
            rows = pl.ds(pl.multiple_of(i * TILE, TILE), TILE)
            query = q_ref[rows, :]
            scores = dot(key, query, (1, 1))
            if masked:
                key_pos = lax.broadcasted_iota(jnp.int32, scores.shape, 0)
                query_pos = lax.broadcasted_iota(jnp.int32, scores.shape, 1)
                scores = jnp.where(key_pos <= query_pos, scores, NEGATIVE)
            probs = jnp.exp(scores - top_ref[:, rows])
            gv = gv + dot(probs.astype(LOW), go_ref[rows, :], (1, 0))
            gks = [gk0, gk1]
            for d in range(2):
                prob_grad = dot(value, got_ref[d, :, rows], (1, 0))
                score_low = (probs * (prob_grad - delta_ref[d, :, rows])).astype(LOW)
                gks[d] = gks[d] + dot(score_low, query, (1, 0))
                gqt_ref[d, :, rows] += dot(key_t, score_low, (1, 0))
            return gv, gks[0], gks[1]

        zero = jnp.zeros((TILE, head), FULL)
        carry = step(j, (jnp.zeros((TILE, 2 * head), FULL), zero, zero), True)
        gv, gk0, gk1 = lax.fori_loop(j + 1, tiles, lambda i, c: step(i, c, False), carry)
        gv_ref[keys, :] = gv.astype(LOW)
        gk_ref[keys, :] = jnp.concatenate([gk0, gk1], axis=1).astype(LOW)
        return 0

    lax.fori_loop(0, tiles, key_tile, 0)

    def finish(i, _):
        rows = pl.ds(pl.multiple_of(i * TILE, TILE), TILE)
        both = jnp.concatenate([gqt_ref[0, :, rows], gqt_ref[1, :, rows]], axis=0) * factor
        gq_ref[rows, :] = both.T.astype(LOW)
        return 0

    lax.fori_loop(0, tiles, finish, 0)


def attend_back(q, k, v, out_t, top, go):
    length, head = q.shape
    pair = jax.ShapeDtypeStruct((length, 2 * head), LOW)
    return pl.pallas_call(
        attend_back_kernel,
        out_shape=(pair, pair, pair),
        scratch_shapes=[
            pltpu.VMEM((head, length), LOW),
            pltpu.VMEM((2, head, length), LOW),
            pltpu.VMEM((2, 1, length), FULL),
            pltpu.VMEM((2, head, length), FULL),
        ],
        compiler_params=pltpu.CompilerParams(vmem_limit_bytes=48 << 20),
        cost_estimate=pl.CostEstimate(
            flops=20 * length * length * head, bytes_accessed=16 * length * head, transcendentals=length * length
        ),
        name="attend_back",
    )(q, k, v, out_t, top, go)


MESH = pl.DeviceIdType.MESH
DMA = pltpu.SemaphoreType.DMA


class Here:
    def __init__(self, nz, ny):
        self.nz, self.ny = nz, ny
        seq = lax.axis_index("seq")
        self.y = lax.axis_index("batch")
        self.core = lax.rem(seq, 2)
        self.chip = lax.div(seq, 2)
        self.x = lax.rem(self.chip, 2)
        self.z = lax.div(self.chip, 2)

    def device(self, z=None, x=None, core=None, y=None):
        z = self.z if z is None else z
        x = self.x if x is None else x
        core = self.core if core is None else core
        y = self.y if y is None else y
        return ((z * 2 + x) * 2 + core, y)

    def before(self, d):
        return lax.rem(self.z + self.nz - d, self.nz)

    def after(self, d):
        return lax.rem(self.z + d, self.nz)


def remote(src, dst, send, recv, device):
    return pltpu.make_async_remote_copy(
        src_ref=src, dst_ref=dst, send_sem=send, recv_sem=recv, device_id=device, device_id_type=MESH
    )


class Gather:
    def __init__(self, here, own, whole, x_first, sems):
        self.here, self.own, self.whole, self.x_first = here, own, whole, x_first
        self.zs, self.zr, self.as_, self.ar, self.bs, self.br, self.local = sems
        self.kept = pltpu.make_async_copy(own, whole.at[here.z, here.x, here.y], self.local)

    @staticmethod
    def scratch(nz, ny):
        return [DMA((2, nz)), DMA((nz,)), DMA((nz, ny)), DMA((nz, ny)), DMA((nz, 2, ny)), DMA((nz, 2, ny)), DMA]

    def _along(self, source, up, own=False):
        h = self.here
        spot = self.whole.at[source, h.x, h.y]
        to = h.device(z=lax.min(h.z + 1, h.nz - 1)) if up else h.device(z=lax.max(h.z - 1, 0))
        src = self.own if own else spot
        return remote(src, spot, self.zs.at[0 if up else 1, source], self.zr.at[source], to)

    def _to_x(self, source, y, out, own=False):
        h = self.here
        spot = self.whole.at[source, h.x if out else 1 - h.x, y]
        s, r = (self.as_, self.ar) if self.x_first else (self.bs, self.br)
        i = (source, 0) if self.x_first else (source, 0, y)
        return remote(self.own if own else spot, spot, s.at[i], r.at[i], h.device(x=1 - h.x))

    def _to_y(self, source, x, e, out, own=False):
        h = self.here
        spot = self.whole.at[source, x, h.y if out else lax.rem(h.y + h.ny - e, h.ny)]
        s, r = (self.bs, self.br) if self.x_first else (self.as_, self.ar)
        i = (source, x, e) if self.x_first else (source, e)
        return remote(self.own if own else spot, spot, s.at[i], r.at[i], h.device(y=lax.rem(h.y + e, h.ny)))

    def start_z(self):
        h = self.here
        pl.when(h.z < h.nz - 1)(self._along(h.z, True, True).start)
        pl.when(h.z > 0)(self._along(h.z, False, True).start)

    def take_z(self, source, up):
        h = self.here
        self._along(source, up).wait_recv()
        pl.when(h.z < h.nz - 1 if up else h.z > 0)(self._along(source, up).start)

    def spread(self, source, own):
        h = self.here
        if self.x_first:
            self._to_x(source, h.y, True, own).start()
            for e in range(1, h.ny):
                self._to_y(source, h.x, e, True, own).start()
        else:
            for e in range(1, h.ny):
                self._to_y(source, h.x, e, True, own).start()
            self._to_x(source, h.y, True, own).start()

    def second(self, source):
        h = self.here
        if self.x_first:
            self._to_x(source, h.y, False).wait_recv()
            for e in range(1, h.ny):
                self._to_y(source, 1 - h.x, e, True).start()
        else:
            for e in range(1, h.ny):
                self._to_y(source, h.x, e, False).wait_recv()
                self._to_x(source, lax.rem(h.y + h.ny - e, h.ny), True).start()

    def third(self, source):
        h = self.here
        if self.x_first:
            for e in range(1, h.ny):
                self._to_y(source, h.x, e, False).wait_recv()
                self._to_y(source, 1 - h.x, e, False).wait_recv()
        else:
            for y in range(h.ny):
                self._to_x(source, y, False).wait_recv()

    def finish(self):
        h = self.here
        for source in range(h.nz):
            pl.when(jnp.logical_and(source <= h.z, h.z < h.nz - 1))(self._along(source, True).wait_send)
            pl.when(jnp.logical_and(source >= h.z, h.z > 0))(self._along(source, False).wait_send)
            if self.x_first:
                self._to_x(source, h.y, True).wait_send()
                for e in range(1, h.ny):
                    for x in range(2):
                        self._to_y(source, x, e, True).wait_send()
            else:
                for e in range(1, h.ny):
                    self._to_y(source, h.x, e, True).wait_send()
                for y in range(h.ny):
                    self._to_x(source, y, True).wait_send()


class GatherRows:
    def __init__(self, here, own, whole, sems):
        self.here, self.own, self.whole = here, own, whole
        self.zs, self.zr, self.xs, self.xr, self.cs, self.cr, self.local = sems
        self.kept = pltpu.make_async_copy(own, whole.at[here.z, here.x, here.core], self.local)

    @staticmethod
    def scratch(nz):
        return [DMA((2, nz)), DMA((nz,)), DMA((nz,)), DMA((nz,)), DMA((nz, 2)), DMA((nz, 2)), DMA]

    def _along(self, source, up, own=False):
        h = self.here
        spot = self.whole.at[source, h.x, h.core]
        to = h.device(z=lax.min(h.z + 1, h.nz - 1)) if up else h.device(z=lax.max(h.z - 1, 0))
        src = self.own if own else spot
        return remote(src, spot, self.zs.at[0 if up else 1, source], self.zr.at[source], to)

    def _to_x(self, source, out, own=False):
        h = self.here
        spot = self.whole.at[source, h.x if out else 1 - h.x, h.core]
        return remote(self.own if own else spot, spot, self.xs.at[source], self.xr.at[source], h.device(x=1 - h.x))

    def _to_core(self, source, x, out, own=False):
        h = self.here
        spot = self.whole.at[source, x, h.core if out else 1 - h.core]
        return remote(self.own if own else spot, spot, self.cs.at[source, x], self.cr.at[source, x], h.device(core=1 - h.core))

    start_z = Gather.start_z
    take_z = Gather.take_z

    def spread(self, source, own):
        self._to_x(source, True, own).start()
        self._to_core(source, self.here.x, True, own).start()

    def second(self, source):
        self._to_x(source, False).wait_recv()
        self._to_core(source, 1 - self.here.x, True).start()

    def third(self, source):
        for x in range(2):
            self._to_core(source, x, False).wait_recv()

    def finish(self):
        h = self.here
        for source in range(h.nz):
            pl.when(jnp.logical_and(source <= h.z, h.z < h.nz - 1))(self._along(source, True).wait_send)
            pl.when(jnp.logical_and(source >= h.z, h.z > 0))(self._along(source, False).wait_send)
            self._to_x(source, True).wait_send()
            for x in range(2):
                self._to_core(source, x, True).wait_send()


def at_distance(here, k, act):
    if k == 0:
        act(here.z, None)
    else:
        pl.when(here.z >= k)(lambda: act(here.z - k, True))
        pl.when(here.z + k < here.nz)(lambda: act(here.z + k, False))


def natural_of(shape, axis, rows_in, ny):
    lane = lax.broadcasted_iota(jnp.int32, shape, axis)
    within = lax.rem(lane, 2 * ny * rows_in)
    core = lax.rem(lax.div(within, rows_in), 2)
    y = lax.div(within, 2 * rows_in)
    return lane - within + (core * ny + y) * rows_in + lax.rem(lane, rows_in)


def bias_piece(entry, rows_in, ny):
    device = lax.div(entry, 2 * rows_in)
    chip = lax.div(device, 2 * ny)
    row = chip * 2 * ny + lax.rem(device, ny) * 2 + lax.rem(lax.div(device, ny), 2)
    return row, 6 * rows_in + lax.rem(entry, 2 * rows_in)


def greet(devices):
    barrier = pltpu.get_barrier_semaphore()
    for device in devices:
        pl.semaphore_signal(barrier, inc=1, device_id=device, device_id_type=MESH)
    return lambda: pl.semaphore_wait(barrier, len(devices))


def owner_of(chips):
    per_core = HEADS // 2
    return [int((j + 0.5) * chips / per_core) for j in range(per_core)]


def head_here(chip, slots):
    mine, has = jnp.int32(0), jnp.int32(0)
    for j, slot in enumerate(slots):
        same = (chip == slot).astype(jnp.int32)
        mine = mine + j * same
        has = has + same
    return mine, has


def attend_kernel(
    nz, ny, x_ref, mw_ref, up_ref, dn_ref,
    mw_all, up_all, dn_all, h_all, q_all, k_all, v_all, ot_all, top_all, att_ref, x2_ref,
    h_ref, q_ref, k_ref, v_ref, ot_ref, top_ref, out_s,
    xs, wt, vc, vt_ref, o_ref, pm, x_own, up_own, dn_own, xn, flat_ref, load, att_s, att_r, pass_s, pass_r, *sems,
):
    here = Here(nz, ny)
    chips = 2 * nz
    slots = owner_of(chips)
    head = q_ref.shape[1]
    width = x_ref.shape[1]
    tile = 2 * x_ref.shape[0]
    mine, has = head_here(here.chip, slots)
    odd = lax.rem(mine, 2) == 1
    rows_sems, mw_sems, up_sems, dn_sems = sems[:7], sems[7:14], sems[14:21], sems[21:28]

    peers = [here.device(z=here.after(d)) for d in range(1, nz)]
    peers += [here.device(x=1 - here.x), here.device(core=1 - here.core)]
    peers += [here.device(z=here.after(d), x=1 - here.x) for d in range(1, nz)]
    peers += [here.device(y=lax.rem(here.y + e, ny)) for e in range(1, ny)]
    met = greet(peers)
    half = width // 2
    unit = up_ref.shape[1]
    rows_in = unit // 2
    pair_rows = HEADS // 4 * unit
    from_row = lax.broadcasted_iota(jnp.int32, (width, width), 0)
    pm[...] = (from_row == natural_of((1, width), 1, rows_in, ny)).astype(LOW)
    x_own[...] = dot(x_ref[...], pm[...], (1, 0)).astype(LOW)
    dn_own[...] = dot(dn_ref[...], pm[...], (1, 0)).astype(LOW)
    up_own[...] = up_ref[...]
    up_own[4] = dot(up_ref[4], pm[:half, :half], (1, 0)).astype(LOW)
    rows = GatherRows(here, x_own, xs, rows_sems)
    mw = Gather(here, mw_ref, mw_all, True, mw_sems)
    up = Gather(here, up_own, up_all, True, up_sems)
    dn = Gather(here, dn_own, dn_all, False, dn_sems)
    first, later = (rows, mw), (up, dn)
    for item in first + later:
        item.kept.start()
    met()

    def take(items, k):
        def act(source, way):
            for item in items:
                if k:
                    item.take_z(source, way)
            for item in items:
                item.spread(source, k == 0)

        at_distance(here, k, act)

    def then(items, k, stage):
        def act(source, _):
            for item in items:
                getattr(item, stage)(source)

        at_distance(here, k, act)

    for item in first:
        item.start_z()
    take(first, 0)
    for k in range(1, nz):
        take(first, k)
        then(first, k - 1, "second")
    for item in later:
        item.start_z()
    then(first, nz - 1, "second")
    take(later, 0)
    for k in range(nz):
        then((rows,), k, "third")
    rows.kept.wait()
    keep_rows = pltpu.make_async_copy(xs.at[here.z, here.x], x2_ref, load.at[2])
    keep_rows.start()

    @pl.when(has == 1)
    def _():
        for i in range(chips):
            xn[i], _ = normalize(xs[i // 2, i % 2].reshape(tile, width).astype(FULL))

    for k in range(nz):
        then((mw,), k, "third")
    mw.kept.wait()
    my_pair = pl.ds(pl.multiple_of(lax.div(mine, 2) * unit, unit), unit)
    pair = pltpu.make_async_copy(mw_all.at[:, :, :, my_pair], wt, load.at[0])
    pair.start()
    vectors = pltpu.make_async_copy(mw_all.at[:, :, :, pl.ds(pair_rows, 16)], vc, load.at[1])
    vectors.start()
    pair.wait()
    vectors.wait()

    steps = []
    for k in range(1, nz):
        steps += [partial(take, later, k), partial(then, later, k - 1, "second")]
    steps += [partial(then, later, nz - 1, "second")] + [partial(then, later, k, "third") for k in range(nz)]

    @pl.when(has == 1)
    def _():
        pieces = vc[...].reshape(-1, vc.shape[-1])
        count = 2 * chips * ny
        pick_row = lax.broadcasted_iota(jnp.int32, (count, pieces.shape[0]), 0) * 8
        pick = (pick_row == lax.broadcasted_iota(jnp.int32, pick_row.shape, 1)).astype(LOW)
        pieces = dot(pick, pieces, (1, 0)).astype(LOW)
        lane = lax.broadcasted_iota(jnp.int32, (1, width), 1)
        pair_lane = lax.broadcasted_iota(jnp.int32, (1, 2 * head), 1)
        pair_lane = pair_lane + (here.core * (HEADS // 4) + lax.div(mine, 2)) * 2 * head
        q_row, q_col = bias_piece(pair_lane, rows_in, ny)
        v_row, v_col = bias_piece(pair_lane + width, rows_in, ny)
        none = jnp.full((1, 2 * head), -1, jnp.int32)
        in_row, owner = lax.rem(lane, rows_in), lax.div(lane, rows_in)
        cols = jnp.concatenate([in_row, rows_in + in_row, q_col, none, v_col], axis=1)
        owners = jnp.concatenate([owner, owner, q_row, none, v_row], axis=1)
        spot = lax.broadcasted_iota(jnp.int32, (pieces.shape[1], cols.shape[1]), 0)
        moved = dot(pieces, (spot == cols).astype(LOW), (1, 0))
        from_row = lax.broadcasted_iota(jnp.int32, moved.shape, 0)
        flat_ref[...] = jnp.sum(jnp.where(from_row == owners, moved, 0.0), axis=0, keepdims=True)

    def choose(values):
        return jnp.where(odd, values[:, head:], values[:, :head])

    def project(i):
        span = slice(i * tile, (i + 1) * tile)
        low = (xn[i] * flat_ref[:, :width] + flat_ref[:, width : 2 * width]).astype(LOW)
        h_ref[span, :] = low
        mixed = (dot(low, wt[...].reshape(width, -1), (1, 0)) + flat_ref[:, 2 * width :]).astype(LOW)
        q_ref[span, :] = (choose(mixed[:, : 2 * head]) * (head ** (-0.5))).astype(LOW)
        k_ref[span, :] = choose(mixed[:, 2 * head : 4 * head])
        value = choose(mixed[:, 4 * head :])
        v_ref[span, :] = value
        vt_ref[:, span] = value.T

    def query_tile(i):
        span = slice(i * tile, (i + 1) * tile)
        query = q_ref[span, :]

        def absorb(j, carry, masked):
            top, total, acc = carry
            keys = slice(j * tile, (j + 1) * tile)
            scores = dot(k_ref[keys, :], query, (1, 1))
            if masked:
                key_pos = lax.broadcasted_iota(jnp.int32, scores.shape, 0)
                query_pos = lax.broadcasted_iota(jnp.int32, scores.shape, 1)
                scores = jnp.where(key_pos <= query_pos, scores, NEGATIVE)
            new_top = jnp.maximum(top, jnp.max(scores, axis=0, keepdims=True))
            weights = jnp.exp(scores - new_top)
            keep = jnp.exp(top - new_top)
            total = total * keep + jnp.sum(weights, axis=0, keepdims=True)
            acc = acc * keep + dot(vt_ref[:, keys], weights.astype(LOW), (1, 0))
            return new_top, total, acc

        carry = (jnp.full((1, tile), NEGATIVE, FULL), jnp.zeros((1, tile), FULL), jnp.zeros((head, tile), FULL))
        for j in range(i + 1):
            carry = absorb(j, carry, j == i)
        top, total, acc = carry
        out = acc / total
        ot_ref[:, span] = out
        o_ref[i] = out.T.astype(LOW)
        top_ref[:, span] = top + jnp.log(total)

    def hand(i):
        spot = att_ref.at[here.core, mine]
        return (
            pltpu.make_async_copy(o_ref.at[i], spot, att_s.at[i]),
            remote(o_ref.at[i], spot, att_s.at[i], att_r.at[mine], here.device(z=i // 2, x=i % 2)),
        )

    pairs_out = (h_ref, h_all), (q_ref, q_all), (k_ref, k_all), (v_ref, v_all), (ot_ref, ot_all), (top_ref, top_all)
    leaving = [pltpu.make_async_copy(src, dst, out_s.at[i]) for i, (src, dst) in enumerate(pairs_out)]

    @pl.when(has == 1)
    def _():
        for i in range(chips):
            project(i)
        for copy in leaving[:4]:
            copy.start()

    for i in range(chips):
        @pl.when(has == 1)
        def _(i=i):
            query_tile(i)
            stay, leave = hand(i)
            pl.when(here.chip == i)(stay.start)
            pl.when(here.chip != i)(leave.start)

        if i < len(steps):
            steps[i]()
    for step in steps[chips:]:
        step()

    for i in range(chips):
        @pl.when(has == 1)
        def _(i=i):
            stay, leave = hand(i)
            pl.when(here.chip == i)(stay.wait)
            pl.when(here.chip != i)(leave.wait_send)

    @pl.when(has == 1)
    def _():
        for copy in leaving[4:]:
            copy.start()
        for copy in leaving:
            copy.wait()

    for j, slot in enumerate(slots):
        @pl.when(here.chip != slot)
        def _(j=j, slot=slot):
            spot = att_ref.at[here.core, j]
            remote(spot, spot, att_s.at[0], att_r.at[j], here.device(z=slot // 2, x=slot % 2)).wait_recv()

    spot = att_ref.at[here.core]
    give = remote(spot, spot, pass_s, pass_r, here.device(core=1 - here.core))
    give.start()
    spot = att_ref.at[1 - here.core]
    remote(spot, spot, pass_s, pass_r, here.device(core=1 - here.core)).wait_recv()
    give.wait_send()
    keep_rows.wait()
    for item in later:
        item.kept.wait()
    for item in first + later:
        item.finish()


def attend(nz, ny, own, mw, up, dn):
    span, width = own.shape
    length = 4 * nz * span
    head = width // HEADS
    units = (nz, 2, ny)
    low = jax.ShapeDtypeStruct((length, head), LOW)
    anywhere = pl.BlockSpec(memory_space=pl.ANY)
    vmem = pl.BlockSpec(memory_space=pltpu.VMEM)
    return pl.pallas_call(
        partial(attend_kernel, nz, ny),
        out_shape=(
            jax.ShapeDtypeStruct(units + mw.shape, LOW),
            jax.ShapeDtypeStruct(units + up.shape, LOW),
            jax.ShapeDtypeStruct(units + dn.shape, LOW),
            jax.ShapeDtypeStruct((length, width), LOW),
            low,
            low,
            low,
            jax.ShapeDtypeStruct((head, length), FULL),
            jax.ShapeDtypeStruct((1, length), FULL),
            jax.ShapeDtypeStruct((2, HEADS // 2, 2 * span, head), LOW),
            jax.ShapeDtypeStruct((2, span, width), LOW),
        ),
        in_specs=[vmem] * 4,
        out_specs=[anywhere] * 11,
        scratch_shapes=[
            pltpu.VMEM((length, width), LOW),
            pltpu.VMEM((length, head), LOW),
            pltpu.VMEM((length, head), LOW),
            pltpu.VMEM((length, head), LOW),
            pltpu.VMEM((head, length), FULL),
            pltpu.VMEM((1, length), FULL),
            DMA((6,)),
            pltpu.VMEM((nz, 2, 2, span, width), LOW),
            pltpu.VMEM(units + up.shape[1:], LOW),
            pltpu.VMEM(units + (16,) + mw.shape[1:], LOW),
            pltpu.VMEM((head, length), LOW),
            pltpu.VMEM((2 * nz, 2 * span, head), LOW),
            pltpu.VMEM((width, width), LOW),
            pltpu.VMEM(own.shape, LOW),
            pltpu.VMEM(up.shape, LOW),
            pltpu.VMEM(dn.shape, LOW),
            pltpu.VMEM((2 * nz, 2 * span, width), FULL),
            pltpu.VMEM((1, 2 * width + width // 2), FULL),
            DMA((3,)),
            DMA((2 * nz,)),
            DMA((HEADS // 2,)),
            DMA,
            DMA,
        ]
        + GatherRows.scratch(nz)
        + Gather.scratch(nz, ny) * 3,
        compiler_params=pltpu.CompilerParams(vmem_limit_bytes=56 << 20, collective_id=0, has_side_effects=True),
        cost_estimate=pl.CostEstimate(
            flops=6 * length * length * head, bytes_accessed=8 * length * width, transcendentals=length * length
        ),
        name="attend",
    )(own, mw, up, dn)


GELU_K = 0.7978845608028654
GELU_C = 0.044715


def gelu_pair(u):
    square = u * u
    tanh = jnp.tanh(GELU_K * u * (1.0 + GELU_C * square))
    half = 0.5 * (1.0 + tanh)
    slope = half + (0.5 * GELU_K) * u * (1.0 - tanh * tanh) * (1.0 + 3.0 * GELU_C * square)
    return u * half, slope


def split_dot(values, turn, dims):
    high = values.astype(LOW)
    rest = values - high.astype(FULL)
    middle = rest.astype(LOW)
    low = (rest - middle.astype(FULL)).astype(LOW)
    return dot(high, turn, dims) + dot(middle, turn, dims) + dot(low, turn, dims)


def rest_kernel(
    nz, hidden_tile,
    x2_ref, att_ref, cot_ref, mw_all, up_ref, dn_ref,
    q_all, k_all, v_all, ot_all, top_all, h_all,
    act_ref, ing_ref, fin, swap, mixf, mix_swap, vec_ref,
    up, dn, ow, own, pm, vc, att, cot, h2, act_low, gu, branch, feed, feed_in, gh2, gh2_in, gmid, eb, grads, go_send,
    go_all, kt_ref, got_ref, delta_ref, gqt_ref, gsend, gat, mw, hbuf, head_acc, head_sum, hs_in, mix_in,
    r1, r2, r3, pack, vec_in, q_ref, k_ref, v_ref, ot_ref, top_ref, in_s,
    load, near_s, near_r, h_s, go_s, go_r, kv_s, kv_r, q_s, q_r, s1, t1, s2, t2, s3, t3, ex_s, ex_r,
    vec_s, vec_r, mix_s, mix_r,
):
    ny = 2
    here = Here(nz, ny)
    core, chip, x, y, z = here.core, here.chip, here.x, here.y, here.z
    chips = 2 * nz
    parts = 4 * nz * ny
    slots = owner_of(chips)
    per_core = len(slots)
    length, head = q_ref.shape
    tile = length // chips
    _, span, width = cot_ref.shape
    half = width // 2
    hidden = dn_ref.shape[0]
    rows_hid = 2 * hidden // parts
    factor = head ** (-0.5)
    job, has = head_here(chip, slots)
    partner = here.device(core=1 - core)
    slabs, unit = grads.shape[4], grads.shape[5]
    pairs = per_core // 2
    rows_in = unit // 2
    my_rows = pl.ds(pl.multiple_of(core * span, span), span)
    their_rows = pl.ds(pl.multiple_of((1 - core) * span, span), span)

    def flat(zz, xx, yy, cc):
        return ((zz * 2 + xx) * ny + yy) * 2 + cc

    others = []
    for dz in range(nz):
        for dx in range(2):
            for dy in range(ny):
                for dc in range(2):
                    if dz or dx or dy or dc:
                        zz = lax.rem(z + dz, nz)
                        xx = 1 - x if dx else x
                        yy = 1 - y if dy else y
                        cc = 1 - core if dc else core
                        behind = (lax.rem(z + nz - dz, nz), xx, yy, cc)
                        others.append((here.device(zz, xx, cc, yy), flat(zz, xx, yy, cc), flat(*behind)))

    loads = [
        pltpu.make_async_copy(up_ref.at[:, :, :, 4], ow.at[core], load.at[0]),
        pltpu.make_async_copy(mw_all.at[:, :, :, pl.ds(pairs * unit, 16)], vc, load.at[1]),
        pltpu.make_async_copy(dn_ref, dn, load.at[2]),
        pltpu.make_async_copy(mw_all.at[:, :, :, pl.ds(0, pairs * unit)], mw, load.at[3]),
    ]
    for t in range(4):
        spot = up.at[:, :, :, :, pl.ds(t * half, half)]
        loads.append(pltpu.make_async_copy(up_ref.at[:, :, :, t], spot, load.at[4 + t]))
    for copy in loads:
        copy.start()
    met = greet([device for device, _, _ in others])
    pairs_in = (q_all, q_ref), (k_all, k_ref), (v_all, v_ref), (ot_all, ot_ref), (top_all, top_ref)
    entering = [pltpu.make_async_copy(src, dst, in_s.at[i]) for i, (src, dst) in enumerate(pairs_in)]
    for copy in entering:
        copy.start()

    def pass_on(i, src, dst):
        return remote(src, dst, near_s.at[i], near_r.at[i], partner)

    natural = natural_of((1, width), 1, rows_in, ny)
    from_row = lax.broadcasted_iota(jnp.int32, (width, width), 0)
    pm[...] = (from_row == natural).astype(LOW)
    for d in range(2):
        cot[d, my_rows, :] = dot(cot_ref[d], pm[...], (1, 0)).astype(LOW)
    met()
    give_cot = pass_on(0, cot.at[:, my_rows], cot.at[:, my_rows])
    give_cot.start()
    loads[0].wait()
    give_ow = pass_on(1, ow.at[core], ow.at[core])
    give_ow.start()

    wide = lax.broadcasted_iota(jnp.int32, (1, width), 1)
    wide_owner = lax.div(wide, rows_in)
    hid = lax.broadcasted_iota(jnp.int32, (1, hidden), 1)
    hid_owner = lax.div(hid, rows_hid) * 2 + core
    in_row = lax.rem(wide, rows_in)
    cols = [in_row + i * rows_in for i in (2, 3, 4, 5, 0)] + [lax.rem(hid, rows_hid) + 8 * rows_in]
    cols = jnp.concatenate(cols, axis=1)
    owners = jnp.concatenate([wide_owner] * 5 + [hid_owner], axis=1)
    loads[1].wait()
    pieces = vc[...].reshape(-1, vc.shape[-1])
    pick_row = lax.broadcasted_iota(jnp.int32, (parts, pieces.shape[0]), 0) * 8
    pick = (pick_row == lax.broadcasted_iota(jnp.int32, pick_row.shape, 1)).astype(LOW)
    pieces = dot(pick, pieces, (1, 0)).astype(LOW)
    spot = lax.broadcasted_iota(jnp.int32, (pieces.shape[1], cols.shape[1]), 0)
    moved = dot(pieces, (spot == cols).astype(LOW), (1, 0))
    piece_row = lax.broadcasted_iota(jnp.int32, moved.shape, 0)
    vectors = jnp.sum(jnp.where(piece_row == owners, moved, 0.0), axis=0, keepdims=True)
    gain, shift, out_bias, down_bias, first_gain = (vectors[:, i * width : (i + 1) * width] for i in range(5))
    up_bias = vectors[:, 5 * width :]

    natural_att = jnp.concatenate([att_ref[c, j] for c in range(2) for j in range(per_core)], axis=1)
    att[...] = dot(natural_att, pm[...], (1, 0)).astype(LOW)
    remote(ow.at[1 - core], ow.at[1 - core], near_s.at[1], near_r.at[1], partner).wait_recv()
    for c in range(2):
        own[:, c * half : (c + 1) * half] = dot(pm[...], ow[c].reshape(width, half), (1, 0)).astype(LOW)
    branch[...] = dot(natural_att, own[...], (1, 0)) + out_bias

    def middle_of(d, rows):
        return x2_ref[rows, :].astype(FULL) + SCALES[d] * branch[rows, :]

    for d in range(2):
        n, _ = normalize(middle_of(d, slice(None)))
        h2[d] = (n * gain + shift).astype(LOW)
    theirs_cot = cot.at[:, their_rows]
    remote(theirs_cot, theirs_cot, near_s.at[0], near_r.at[0], partner).wait_recv()
    loads[2].wait()
    for copy in loads[4:]:
        copy.wait()

    def up_cols(cut):
        return up[:, :, :, :, cut].reshape(width, -1)

    def upstream(d):
        return (SCALES[d] * cot[d].astype(FULL)).astype(LOW)

    stride = pack.shape[1] * pack.shape[2] // 2
    lane = lax.broadcasted_iota(jnp.int32, (width, 128), 0)
    in_piece = (lax.rem(lane, rows_in) == lax.broadcasted_iota(jnp.int32, lane.shape, 1)).astype(LOW)

    def placed(vector, owner, turn, start):
        rows = lax.broadcasted_iota(jnp.int32, (parts, vector.shape[1]), 0)
        spread = jnp.where(rows == owner, vector, 0.0)
        high = spread.astype(LOW)
        low = (spread - high.astype(FULL)).astype(LOW)
        values = dot(high, turn, (1, 0)) + dot(low, turn, (1, 0))
        return jnp.pad(values, ((0, 0), (start, 2 * stride)))[:, : 2 * stride]

    sums = {}

    def row_sum(v, d, values):
        sums[v, d] = jnp.sum(values, axis=0, keepdims=True)

    exchanges = []

    def forth(d):
        low_in = upstream(d)
        ups = []
        for t in range(0, hidden, hidden_tile):
            cut = slice(t, t + hidden_tile)
            u = dot(h2[d], up_cols(cut), (1, 0)) + up_bias[:, cut]
            active, slope = gelu_pair(u)
            active = active.astype(LOW)
            act_low[d, :, cut] = active
            grad = (dot(low_in, dn[cut, :], (1, 1)) * slope).astype(LOW)
            gu[d, :, cut] = grad
            ups.append(jnp.sum(grad.astype(FULL), axis=0, keepdims=True))
        sums["up", d] = jnp.concatenate(ups, axis=1)

    def back_to_width(d):
        gh2[d] = dot(gu[d], up_cols(slice(None)), (1, 1))
        feed[d] = dot(act_low[d], dn[...], (1, 0))
        for i, (src, dst) in ((2, (gh2, gh2_in)), (4, (feed, feed_in))):
            copy = pass_on(i + d, src.at[d, their_rows], dst.at[d])
            copy.start()
            exchanges.append(copy)

    def keep(d, values, first_row, first_col, base, rows_of):
        for i in range(0, values.shape[0], unit):
            row = first_row + i
            u, within = row // rows_of, (row % rows_of) // unit
            place = (u // (2 * ny), (u // ny) % 2, u % ny)
            for c in range(0, values.shape[1], half):
                slab = base + within * 2 + (first_col + c) // half
                grads[(d,) + place + (slab,)] = values[i : i + unit, c : c + half]

    def down_grads(d):
        low_in = upstream(d)
        for t in range(0, hidden, half):
            keep(d, dot(act_low[d, :, t : t + half], low_in, (0, 0)).astype(LOW), t, 0, 0, 2 * unit)

    def up_grads(d):
        for t in range(0, hidden, 2 * half):
            for m in range(0, width, half):
                part = dot(h2[d, :, m : m + half], gu[d, :, t : t + 2 * half], (0, 0)).astype(LOW)
                keep(d, part, m, t, 4, unit)

    def norm_feed_back(d):
        remote(gh2_in.at[d], gh2_in.at[d], near_s.at[2 + d], near_r.at[2 + d], partner).wait_recv()
        grad = gh2[d, my_rows, :] + gh2_in[d]
        n, r = normalize(middle_of(d, my_rows))
        row_sum(2, d, grad * n)
        row_sum(3, d, grad)
        own_cot = cot[d, my_rows, :].astype(FULL)
        middle_grad = own_cot + norm_back(grad, n, r, gain)
        gmid[d] = middle_grad
        branch_low = (SCALES[d] * middle_grad).astype(LOW)
        row_sum(4, d, branch_low.astype(FULL))
        row_sum(5, d, (SCALES[d] * own_cot).astype(LOW).astype(FULL))
        eb[d, my_rows, :] = branch_low
        copy = pass_on(6 + d, eb.at[d, my_rows], eb.at[d, my_rows])
        copy.start()
        exchanges.append(copy)

    zis = []
    for i in range((nz + 1) // 2):
        zis += [nz - 1 - i] + ([i] if i != nz - 1 - i else [])
    cuts = [(0, slabs // 2), (slabs // 2, slabs)]
    chunks = [(zi, part) for part in range(len(cuts)) for zi in zis]

    def y_first(d, zi, part):
        return d == 0 or chunks.index((zi, part)) % 2 == 1

    def mine(d, zi, part, i, slab):
        return grads.at[d, zi, i, y, slab] if y_first(d, zi, part) else grads.at[d, zi, x, i, slab]

    def some(part):
        return pl.ds(cuts[part][0], cuts[part][1] - cuts[part][0])

    def stage1(d, zi, part):
        slab = some(part)
        if y_first(d, zi, part):
            src, to = grads.at[d, zi, :, 1 - y, slab], here.device(y=1 - y)
        else:
            src, to = grads.at[d, zi, 1 - x, :, slab], here.device(x=1 - x)
        return remote(src, r1.at[d, zi, :, slab], s1.at[d, zi, part], t1.at[d, zi, part], to)

    def stage2(d, zi, part):
        slab = some(part)
        if y_first(d, zi, part):
            src, to = mine(d, zi, part, 1 - x, slab), here.device(x=1 - x)
        else:
            src, to = mine(d, zi, part, 1 - y, slab), here.device(y=1 - y)
        return remote(src, r2.at[d, zi, slab], s2.at[d, zi, part], t2.at[d, zi, part], to)

    def spare(zi, up):
        return zi if up else jnp.where(z - 1 == zi, nz, zi)

    def stage3(d, zi, part, up):
        to = here.device(z=lax.min(z + 1, nz - 1)) if up else here.device(z=lax.max(z - 1, 0))
        way = 0 if up else 1
        slab = some(part)
        src, dst = r2.at[d, zi, slab], r3.at[d, spare(zi, up), slab]
        return remote(src, dst, s3.at[d, zi, part], t3.at[d, way, zi, part], to)

    def arrive3(d, zi, part, up):
        way = 0 if up else 1
        spot = r3.at[d, zi, some(part)]
        return remote(spot, spot, s3.at[d, zi, part], t3.at[d, way, zi, part], partner)

    def begin(d, n):
        if n < len(chunks):
            stage1(d, *chunks[n]).start()

    def add_into(target, other, lead):
        def one(i, _):
            a, b = target(i), other(i)
            a[...] = (a[...].astype(FULL) + b[...].astype(FULL)).astype(LOW)
            return 0

        lax.fori_loop(0, lead, one, 0)

    def after1(d, zi, part):
        stage1(d, zi, part).wait_recv()
        low, high = cuts[part]
        size = high - low
        add_into(
            lambda i: mine(d, zi, part, lax.div(i, size), low + lax.rem(i, size)),
            lambda i: r1.at[d, zi, lax.div(i, size), low + lax.rem(i, size)],
            2 * size,
        )
        stage2(d, zi, part).start()

    def after2(d, zi, part):
        low, high = cuts[part]
        stage2(d, zi, part).wait_recv()
        own_place = x if y_first(d, zi, part) else y
        add_into(lambda i: r2.at[d, zi, low + i], lambda i: mine(d, zi, part, own_place, low + i), high - low)
        if zi > 0:
            pl.when(z == 0)(stage3(d, zi, part, True).start)
        if zi < nz - 1:
            pl.when(z == nz - 1)(stage3(d, zi, part, False).start)

    def after3(d, zi, part, far):
        low, high = cuts[part]
        if far < zi:
            @pl.when(z == far)
            def _():
                arrive3(d, zi, part, True).wait_recv()
                add_into(lambda i: r2.at[d, zi, low + i], lambda i: r3.at[d, zi, low + i], high - low)
                stage3(d, zi, part, True).start()

        if nz - 1 - far > zi:
            @pl.when(z == nz - 1 - far)
            def _():
                arrive3(d, zi, part, False).wait_recv()
                add_into(lambda i: r2.at[d, zi, low + i], lambda i: r3.at[d, zi, low + i], high - low)
                stage3(d, zi, part, False).start()

    def last3(d, zi, part):
        low, high = cuts[part]

        @pl.when(z == zi)
        def _():
            if zi > 0:
                arrive3(d, zi, part, True).wait_recv()
            if zi < nz - 1:
                arrive3(d, zi, part, False).wait_recv()

            def one(i, _):
                total = r2[d, zi, i].astype(FULL)
                if zi > 0:
                    total = total + r3[d, zi, i].astype(FULL)
                if zi < nz - 1:
                    total = total + r3[d, nz, i].astype(FULL)
                fin[d, i] = total
                return 0

            lax.fori_loop(low, high, one, 0)

    def advance(n):
        stages = [after1, after2] + [partial(after3, far=far) for far in range(1, nz - 1)] + [last3]
        for behind, stage in enumerate(stages):
            for d in range(2):
                if 0 <= n - behind < len(chunks):
                    stage(d, *chunks[n - behind])
                if not behind:
                    begin(d, n + 2)

    steps = len(chunks) + nz

    def finish_sends():
        for zi, part in chunks:
            for d in range(2):
                stage1(d, zi, part).wait_send()
                stage2(d, zi, part).wait_send()
                pl.when(z != zi)(stage3(d, zi, part, True).wait_send)

    for d in range(2):
        forth(d)
        down_grads(d)
        begin(d, 0)
        begin(d, 1)
    for d in range(2):
        back_to_width(d)
    up_grads(0)
    norm_feed_back(0)
    up_grads(1)
    norm_feed_back(1)

    def go_copies(j):
        slot = slots[j]
        return (
            pltpu.make_async_copy(go_send.at[j], go_all.at[chip], go_s.at[j]),
            remote(go_send.at[j], go_all.at[chip], go_s.at[j], go_r.at[chip], here.device(z=slot // 2, x=slot % 2)),
        )

    own_half = own.at[pl.ds(pl.multiple_of(core * half, half), half), :]
    for d in range(2):
        spot = eb.at[d, their_rows]
        remote(spot, spot, near_s.at[6 + d], near_r.at[6 + d], partner).wait_recv()
        go = dot(eb[d], own_half[...], (1, 1)).astype(LOW)
        for j in range(per_core):
            go_send[j, :, d * head : (d + 1) * head] = go[:, j * head : (j + 1) * head]
    for j, slot in enumerate(slots):
        stay, leave = go_copies(j)
        pl.when(chip == slot)(stay.start)
        pl.when(chip != slot)(leave.start)
    for d in range(2):
        ours = eb[d, :, pl.ds(pl.multiple_of(core * half, half), half)]
        for m in range(0, width, half):
            keep(d, dot(att[:, m : m + half], ours, (0, 0)).astype(LOW), m, 0, 8, unit)

    for d in range(2):
        remote(feed_in.at[d], feed_in.at[d], near_s.at[4 + d], near_r.at[4 + d], partner).wait_recv()
        out = middle_of(d, my_rows) + SCALES[d] * (feed[d, my_rows, :] + feed_in[d] + down_bias)
        act_ref[d] = out.astype(LOW)
    total = jnp.zeros((parts, 2 * stride), FULL)
    for v in range(2, 6):
        for d in range(2):
            total = total + placed(sums[v, d], wide_owner, in_piece, v * rows_in + d * stride)
    hid_lane = lax.broadcasted_iota(jnp.int32, (hidden, 128), 0)
    in_hidden = (lax.rem(hid_lane, rows_hid) == lax.broadcasted_iota(jnp.int32, hid_lane.shape, 1)).astype(LOW)
    for d in range(2):
        total = total + placed(sums["up", d], hid_owner, in_hidden, 8 * rows_in + d * stride)
    for c in range(pack.shape[1]):
        pack[:, c, :] = total[:, c * 128 : (c + 1) * 128]
    advance(0)

    for copy in entering:
        copy.wait()

    def h_copy(i):
        rows = slice(i * tile, (i + 1) * tile)
        return pltpu.make_async_copy(h_all.at[rows], hbuf.at[i % 2], h_s.at[i % 2])

    @pl.when(has == 1)
    def _():
        h_copy(0).start()
        h_copy(1).start()
        for t in range(chips):
            stay = pltpu.make_async_copy(go_send.at[0], go_all.at[t], go_s.at[job])
            come = remote(go_send.at[0], go_all.at[t], go_s.at[0], go_r.at[t], here.device(z=t // 2, x=t % 2))
            pl.when(chip == t)(stay.wait)
            pl.when(chip != t)(come.wait_recv)
        for i in range(chips):
            rows = slice(i * tile, (i + 1) * tile)
            kt_ref[:, rows] = k_ref[rows, :].T
            up_t = go_all[i].T
            for d in range(2):
                part = up_t[d * head : (d + 1) * head, :]
                got_ref[d, :, rows] = part
                delta_ref[d, :, rows] = jnp.sum(part.astype(FULL) * ot_ref[:, rows], axis=0, keepdims=True)
                gqt_ref[d, :, rows] = jnp.zeros((head, tile), FULL)

    def key_tile(j):
        keys = slice(j * tile, (j + 1) * tile)
        key = k_ref[keys, :]
        value = v_ref[keys, :]
        key_t = kt_ref[:, keys]

        def step(i, carry, masked):
            gv, gk0, gk1 = carry
            rows = pl.ds(i * tile if masked else pl.multiple_of(i * tile, tile), tile)
            query = q_ref[rows, :]
            scores = dot(key, query, (1, 1))
            if masked:
                key_pos = lax.broadcasted_iota(jnp.int32, scores.shape, 0)
                query_pos = lax.broadcasted_iota(jnp.int32, scores.shape, 1)
                scores = jnp.where(key_pos <= query_pos, scores, NEGATIVE)
            probs = jnp.exp(scores - top_ref[:, rows])
            gv = gv + dot(probs.astype(LOW), go_all[i], (1, 0))
            gks = [gk0, gk1]
            for d in range(2):
                prob_grad = dot(value, got_ref[d, :, rows], (1, 0))
                score_low = (probs * (prob_grad - delta_ref[d, :, rows])).astype(LOW)
                gks[d] = gks[d] + dot(score_low, query, (1, 0))
                gqt_ref[d, :, rows] += dot(key_t, score_low, (1, 0))
            return gv, gks[0], gks[1]

        zero = jnp.zeros((tile, head), FULL)
        carry = step(j, (jnp.zeros((tile, 2 * head), FULL), zero, zero), True)
        gv, gk0, gk1 = lax.fori_loop(j + 1, chips, lambda i, c: step(i, c, False), carry)
        gsend[j, 1] = jnp.concatenate([gk0, gk1], axis=1).astype(LOW)
        gsend[j, 2] = gv.astype(LOW)

    def kv_copies(t):
        src, dst = gsend.at[t, pl.ds(1, 2)], gat.at[job, pl.ds(1, 2)]
        to = here.device(z=t // 2, x=t % 2)
        return pltpu.make_async_copy(src, dst, kv_s.at[t]), remote(src, dst, kv_s.at[t], kv_r.at[job], to)

    def q_copies(t):
        src, dst = gsend.at[t, 0], gat.at[job, 0]
        to = here.device(z=t // 2, x=t % 2)
        return pltpu.make_async_copy(src, dst, q_s.at[t]), remote(src, dst, q_s.at[t], q_r.at[job], to)

    def launch(copies, t):
        stay, leave = copies(t)
        pl.when(chip == t)(stay.start)
        pl.when(chip != t)(leave.start)

    between = {1: 1, 3: 2, 7: 3}
    for j in range(chips):
        @pl.when(has == 1)
        def _(j=j):
            key_tile(j)
            launch(kv_copies, j)

        if j in between:
            advance(between[j])

    @pl.when(has == 1)
    def _():
        for i in range(chips):
            rows = slice(i * tile, (i + 1) * tile)
            both = jnp.concatenate([gqt_ref[0, :, rows], gqt_ref[1, :, rows]], axis=0) * factor
            gsend[i, 0] = both.T.astype(LOW)
            launch(q_copies, i)

    def mix_y():
        return remote(head_sum.at[:, :, 1 - y], hs_in, ex_s.at[0], ex_r.at[0], here.device(y=1 - y))

    def mix_copies(t):
        src, dst = head_sum.at[t // 2, t % 2, y], mix_in.at[job]
        to = here.device(z=t // 2, x=t % 2)
        return pltpu.make_async_copy(src, dst, mix_s.at[t]), remote(src, dst, mix_s.at[t], mix_r.at[job], to)

    @pl.when(has == 1)
    def _():
        for i in range(chips):
            h_copy(i).wait()
            right = jnp.concatenate([gsend[i, t] for t in range(3)], axis=1)
            part = dot(hbuf[i % 2], right, (0, 0))
            if i == 0:
                head_acc[...] = part
            else:
                head_acc[...] += part
            if i + 2 < chips:
                h_copy(i + 2).start()
        for u in range(parts // 2):
            zz, xx, yy = u // (2 * ny), (u // ny) % 2, u % ny
            head_sum[zz, xx, yy] = head_acc[u * unit : (u + 1) * unit, :].astype(LOW)
        mix_y().start()

    advance(4)

    @pl.when(has == 1)
    def _():
        mix_y().wait_recv()
        mix_y().wait_send()
        add_into(
            lambda i: head_sum.at[lax.div(i, 2), lax.rem(i, 2), y],
            lambda i: hs_in.at[lax.div(i, 2), lax.rem(i, 2)],
            chips,
        )
        for t in range(chips):
            launch(mix_copies, t)

    biases = []
    for t in (0, 2):
        acc = jnp.zeros((1, 2 * head), FULL)
        for i in range(chips):
            acc = acc + jnp.sum(gsend[i, t].astype(FULL), axis=0, keepdims=True)
        biases.append(jnp.where(has == 1, acc, 0.0))
    total = jnp.concatenate([pack[:, c, :] for c in range(pack.shape[1])], axis=1)
    for b in range(2):
        rows = lax.broadcasted_iota(jnp.int32, (parts, 2 * head), 0)
        first_entry = (core * per_core + job) * head + b * width
        across = lax.broadcasted_iota(jnp.int32, (1, 2 * head), 1)
        down_lane = lax.broadcasted_iota(jnp.int32, (2 * head, 1), 0)
        owner, _ = bias_piece(lax.rem(across, head) + first_entry, rows_in, ny)
        _, column = bias_piece(lax.rem(down_lane, head) + first_entry, rows_in, ny)
        column = column + lax.div(down_lane, head) * stride
        spread = jnp.where(rows == owner, biases[b], 0.0)
        turn = lax.broadcasted_iota(jnp.int32, (2 * head, 2 * stride), 1) == column
        high = spread.astype(LOW)
        low = (spread - high.astype(FULL)).astype(LOW)
        total = total + dot(high, turn.astype(LOW), (1, 0)) + dot(low, turn.astype(LOW), (1, 0))
    advance(5)

    for copy in exchanges:
        copy.wait_send()
    loads[3].wait()
    for j, slot in enumerate(slots):
        @pl.when(chip != slot)
        def _(j=j, slot=slot):
            to = here.device(z=slot // 2, x=slot % 2)
            remote(gat.at[j, pl.ds(1, 2)], gat.at[j, pl.ds(1, 2)], kv_s.at[0], kv_r.at[j], to).wait_recv()
            remote(gat.at[j, 0], gat.at[j, 0], q_s.at[0], q_r.at[j], to).wait_recv()

        @pl.when(chip == slot)
        def _(j=j, slot=slot):
            kv_copies(slot)[0].wait()
            q_copies(slot)[0].wait()

    def first_swap(d):
        return remote(gh2.at[d, their_rows], gh2_in.at[d], ex_s.at[1 + d], ex_r.at[1 + d], partner)

    for d in range(2):
        lanes = slice(d * head, (d + 1) * head)
        first = None
        for p in range(per_core // 2):
            left = jnp.concatenate(
                [gat[2 * p + o, t][:, lanes] for t in range(3) for o in range(2)], axis=1
            )
            part = dot(left, mw[:, :, :, p * unit : (p + 1) * unit].reshape(width, half), (1, 1))
            first = part if first is None else first + part
        gh2[d] = first
        first_swap(d).start()
    normed, inv = normalize(x2_ref[my_rows, :].astype(FULL))
    for d in range(2):
        first_swap(d).wait_recv()
        grad = gh2[d, my_rows, :] + gh2_in[d]
        for v, row in ((0, jnp.sum(grad * normed, axis=0, keepdims=True)), (1, jnp.sum(grad, axis=0, keepdims=True))):
            total = total + placed(row, wide_owner, in_piece, v * rows_in + d * stride)
        whole = gmid[d] + norm_back(grad, normed, inv, first_gain)
        ing_ref[d] = whole
    for c in range(pack.shape[1]):
        pack[:, c, :] = total[:, c * 128 : (c + 1) * 128]
    me = flat(z, x, y, core)

    def vec_copy(n):
        device, index, _ = others[n]
        return remote(pack.at[index], vec_in.at[me], vec_s.at[n], vec_r.at[n], device)

    def vec_come(n):
        device, _, index = others[n]
        return remote(pack.at[index], vec_in.at[index], vec_s.at[n], vec_r.at[n], device)

    for n in range(len(others)):
        vec_copy(n).start()

    for n in range(6, steps - 1):
        advance(n)
    mine_in = pl.ds(pl.multiple_of(core * rows_in, 8), rows_in)
    their_in = pl.ds(pl.multiple_of((1 - core) * rows_in, 8), rows_in)
    for j, slot in enumerate(slots):
        @pl.when(chip != slot)
        def _(j=j, slot=slot):
            to = here.device(z=slot // 2, x=slot % 2)
            remote(mix_in.at[j], mix_in.at[j], mix_s.at[0], mix_r.at[j], to).wait_recv()

        @pl.when(chip == slot)
        def _(j=j, slot=slot):
            mix_copies(slot)[0].wait()

        mixf[j] = mix_in[j].astype(FULL)
    mix_pass = remote(mixf.at[:, their_in], mix_swap, ex_s.at[5], ex_r.at[5], partner)
    mix_pass.start()

    for n in range(steps - 1, steps):
        advance(n)

    def last_swap(d):
        return remote(fin.at[d, pl.ds(4, slabs - 4), their_in], swap.at[d], ex_s.at[3 + d], ex_r.at[3 + d], partner)

    for d in range(2):
        last_swap(d).start()
    for d in range(2):
        last_swap(d).wait_recv()
    mix_pass.wait_recv()
    for n in range(len(others)):
        vec_come(n).wait_recv()
    vec_in[me] = pack[me]
    vec_ref[...] = jnp.sum(vec_in[...], axis=0)

    give_cot.wait_send()
    give_ow.wait_send()
    finish_sends()
    for j, slot in enumerate(slots):
        pl.when(chip != slot)(go_copies(j)[1].wait_send)

    @pl.when(has == 1)
    def _():
        for t in range(chips):
            @pl.when(chip != t)
            def _(t=t):
                kv_copies(t)[1].wait_send()
                q_copies(t)[1].wait_send()
                mix_copies(t)[1].wait_send()

    for d in range(2):
        first_swap(d).wait_send()
        last_swap(d).wait_send()
    mix_pass.wait_send()
    for n in range(len(others)):
        vec_copy(n).wait_send()


def finish_kernel(
    nz, act, ing, fin, swap, mixf, mix_swap, vec,
    act_ref, ing_ref, gain1_ref, shift1_ref, mix_ref, mixb_ref, out_ref, outb_ref, gain2_ref, shift2_ref, up_ref, upb_ref,
    dn_ref, dnb_ref,
):
    ny = 2
    core = lax.rem(lax.axis_index("seq"), 2)
    width = ing.shape[2]
    slabs, unit = fin.shape[1], fin.shape[2]
    rows_in = unit // 2
    per_core, head = mixf.shape[0], width // HEADS
    from_row = lax.broadcasted_iota(jnp.int32, (width, width), 0)
    turn = (from_row == natural_of((1, width), 1, rows_in, ny)).astype(LOW)
    mine_in = pl.ds(pl.multiple_of(core * rows_in, 8), rows_in)
    is_first = core == 0

    def by_core(a, b):
        return jnp.where(is_first, a, b), jnp.where(is_first, b, a)

    hidden = (slabs - 5) * fin.shape[3]
    block = hidden // (2 * nz)
    sides = [by_core(mixf[j, mine_in, :], mix_swap[j]) for j in range(per_core)]
    for d in range(2):
        act_ref[d] = dot(act[d], turn, (1, 1)).astype(LOW)
        top_half = jnp.concatenate([fin[d, 0], fin[d, 1]], axis=1)
        low_half = jnp.concatenate([fin[d, 2], fin[d, 3]], axis=1)
        ours = jnp.concatenate([fin[d, s, mine_in, :] for s in range(4, slabs - 1)], axis=1)
        came = jnp.concatenate([swap[d, s] for s in range(slabs - 5)], axis=1)
        one, two = by_core(ours, came)
        blocks = []
        for i in range(hidden // block):
            blocks += [one[:, i * block : (i + 1) * block], two[:, i * block : (i + 1) * block]]
        up_ref[d] = jnp.concatenate(blocks, axis=1)
        one, two = by_core(fin[d, slabs - 1, mine_in, :], swap[d, slabs - 5])
        stacked = [ing[d], top_half, low_half, jnp.concatenate([one, two], axis=1)]
        moved = split_dot(jnp.concatenate(stacked, axis=0), turn, (1, 1))
        span = ing.shape[1]
        ing_ref[d] = moved[:span]
        dn_ref[d] = moved[span : span + 2 * unit]
        out_ref[d] = moved[span + 2 * unit :]
        blocks = []
        for t in range(3):
            for c in range(2):
                for j in range(per_core):
                    start = t * 2 * head + d * head
                    blocks.append(sides[j][c][:, start : start + head])
        mix_ref[d] = jnp.concatenate(blocks, axis=1)
    flat = jnp.concatenate([vec[c : c + 1, :] for c in range(vec.shape[0])], axis=1)
    stride = flat.shape[1] // 2
    smalls = (gain1_ref, shift1_ref, gain2_ref, shift2_ref, outb_ref, dnb_ref, mixb_ref, upb_ref)
    start = 0
    for ref in smalls:
        size = ref.shape[1]
        for d in range(2):
            ref[d : d + 1, :] = flat[:, d * stride + start : d * stride + start + size]
        start += size


def finish(nz, act, ing, fin, swap, mixf, mix_swap, vec):
    width = ing.shape[2]
    slabs, unit, half = fin.shape[1:]
    rows_in = unit // 2
    hidden = (slabs - 5) * half

    def full(*shape):
        return jax.ShapeDtypeStruct((2,) + shape, FULL)

    small = full(rows_in)
    return pl.pallas_call(
        partial(finish_kernel, nz),
        out_shape=(
            jax.ShapeDtypeStruct(act.shape, LOW), jax.ShapeDtypeStruct(ing.shape, FULL), small, small,
            full(rows_in, 3 * width), full(2 * rows_in), full(rows_in, width), small, small, small,
            full(rows_in, 2 * hidden), full(2 * unit), full(2 * unit, width), small,
        ),
        compiler_params=pltpu.CompilerParams(vmem_limit_bytes=60 << 20),
        name="finish",
    )(act, ing, fin, swap, mixf, mix_swap, vec)


def rest(nz, x2, attended, cot, mw_all, up, dn, q, k, v, out_t, top, first_low):
    length, head = q.shape
    _, span, width = cot.shape
    hidden = dn.shape[0]
    half = width // 2
    chips = 2 * nz
    parts = 8 * nz
    rows = 2 * span
    per_core = HEADS // 2
    unit = up.shape[4]
    units = mw_all.shape[:3]
    rows_in = unit // 2
    slabs = 9
    anywhere = pl.BlockSpec(memory_space=pl.ANY)
    vmem = pl.BlockSpec(memory_space=pltpu.VMEM)
    low, full = partial(pltpu.VMEM, dtype=LOW), partial(pltpu.VMEM, dtype=FULL)
    return pl.pallas_call(
        partial(rest_kernel, nz, 512),
        out_shape=(
            jax.ShapeDtypeStruct((2, span, width), LOW),
            jax.ShapeDtypeStruct((2, span, width), FULL),
            jax.ShapeDtypeStruct((2, slabs, unit, half), FULL),
            jax.ShapeDtypeStruct((2, slabs - 4, rows_in, half), FULL),
            jax.ShapeDtypeStruct((per_core, unit, half), FULL),
            jax.ShapeDtypeStruct((per_core, rows_in, half), FULL),
            jax.ShapeDtypeStruct((5, 128), FULL),
        ),
        in_specs=[vmem] * 3 + [anywhere] * 9,
        out_specs=[vmem] * 7,
        scratch_shapes=[
            low(units + (unit, hidden)),
            low((hidden, width)),
            low((2,) + units + (unit, half)),
            low((width, width)),
            low((width, width)),
            low(units + (16, half)),
            low((rows, width)),
            low((2, rows, width)),
            low((2, rows, width)),
            low((2, rows, hidden)),
            low((2, rows, hidden)),
            full((rows, width)),
            full((2, rows, width)),
            full((2, span, width)),
            full((2, rows, width)),
            full((2, span, width)),
            full((2, span, width)),
            low((2, rows, width)),
            low((2,) + units + (slabs, unit, half)),
            low((per_core, rows, 2 * head)),
            low((chips, rows, 2 * head)),
            low((head, length)),
            low((2, head, length)),
            full((2, 1, length)),
            full((2, head, length)),
            low((chips, 3, rows, 2 * head)),
            low((per_core, 3, rows, 2 * head)),
            low(units + (per_core // 2 * unit, half)),
            low((2, rows, width)),
            full((width, half)),
            low(units + (unit, half)),
            low((nz, 2, unit, half)),
            low((per_core, unit, half)),
            low((2, nz, 2, slabs, unit, half)),
            low((2, nz, slabs, unit, half)),
            low((2, nz + 1, slabs, unit, half)),
            full((parts, 5, 128)),
            full((parts, 5, 128)),
            low((length, head)),
            low((length, head)),
            low((length, head)),
            full((head, length)),
            full((1, length)),
            DMA((5,)),
            DMA((8,)),
            DMA((8,)),
            DMA((8,)),
            DMA((2,)),
            DMA((per_core,)),
            DMA((chips,)),
            DMA((chips,)),
            DMA((per_core,)),
            DMA((chips,)),
            DMA((per_core,)),
            DMA((2, nz, 3)),
            DMA((2, nz, 3)),
            DMA((2, nz, 3)),
            DMA((2, nz, 3)),
            DMA((2, nz, 3)),
            DMA((2, 2, nz, 3)),
            DMA((6,)),
            DMA((6,)),
            DMA((parts - 1,)),
            DMA((parts - 1,)),
            DMA((chips,)),
            DMA((per_core,)),
        ],
        compiler_params=pltpu.CompilerParams(vmem_limit_bytes=62 << 20, collective_id=1, has_side_effects=True),
        cost_estimate=pl.CostEstimate(
            flops=60 * rows * width * hidden, bytes_accessed=60 * width * hidden, transcendentals=length * length
        ),
        name="rest",
    )(x2, attended, cot, mw_all, up, dn, q, k, v, out_t, top, first_low)


def plain_on_device(
    inputs,
    attend_gain,
    attend_shift,
    mixing_weight,
    mixing_bias,
    output_weight,
    output_bias,
    feed_gain,
    feed_shift,
    up_weight,
    up_bias,
    down_weight,
    down_bias,
    cotangent,
):
    place = Place()
    _, span, width = inputs.shape
    nz, ny, core, chip = place.nz, place.ny, place.core, place.chip
    chips = nz * 2
    parts = chips * 2 * ny
    head = width // HEADS
    per_core = HEADS // 2
    slots = [int((j + 0.5) * chips / per_core) for j in range(per_core)]
    half = width // 2
    hidden = up_weight.shape[1]
    rows_in = width // parts
    rows_hid = hidden // parts
    groups = [[2 * i + c for i in range(chips)] for c in range(2)]

    def exchange(values):
        return lax.all_to_all(values, "seq", 0, 0, axis_index_groups=groups, tiled=True)

    def spread(blocks):
        filled = [jnp.zeros_like(blocks[0])] * chips
        for j, slot in enumerate(slots):
            filled[slot] = blocks[j]
        return jnp.stack(filled)

    def collect(blocks):
        return jnp.stack([blocks[slot] for slot in slots])

    owned = [-1] * chips
    for j, slot in enumerate(slots):
        owned[slot] = j
    my_head = jnp.array(owned, jnp.int32)[chip]
    busy = (my_head >= 0).astype(FULL)
    my_head = jnp.maximum(my_head, 0)

    def by_core(values, dim):
        mine = lax.dynamic_index_in_dim(values, core, dim, keepdims=False)
        theirs = lax.dynamic_index_in_dim(values, 1 - core, dim, keepdims=False)
        return mine, theirs

    vectors = jnp.concatenate(
        [attend_gain, attend_shift, feed_gain, feed_shift, output_bias, down_bias, mixing_bias, up_bias]
    )
    vectors = place.both(vectors, vectors)
    vectors = place.gather(vectors, "z", 0)
    vectors = place.gather(vectors, "x", 1)
    vectors = place.gather(vectors, "y", 3)
    vectors = vectors.reshape(parts, -1).astype(FULL)
    cuts = [vectors[:, i * rows_in : (i + 1) * rows_in].reshape(-1) for i in range(6)]
    first_gain, first_shift, second_gain, second_shift, out_bias, down_bias_all = cuts
    mix_bias = vectors[:, 6 * rows_in : 8 * rows_in].reshape(2, HEADS, head)
    up_bias_all = vectors[:, 8 * rows_in :].reshape(chips, 2, ny * rows_hid)
    up_bias_mine = lax.dynamic_index_in_dim(up_bias_all, core, 1, keepdims=False).reshape(-1)

    own = inputs.reshape(span, width)
    column = [own] + [place.send(own, "z", d) for d in range(1, nz)]
    beside = [place.send(piece, "x") for piece in column]
    x_all = jnp.zeros((nz, 2, span, width), LOW)
    for d in range(nz):
        at = lax.rem(place.z + nz - d, nz)
        x_all = lax.dynamic_update_slice(x_all, column[d][None, None], (at, place.x, 0, 0))
        x_all = lax.dynamic_update_slice(x_all, beside[d][None, None], (at, 1 - place.x, 0, 0))
    x_all = place.both(x_all, x_all).transpose(1, 2, 0, 3, 4)
    x_all = x_all.reshape(chips * 2 * span, width)

    def gather_rows(mine, theirs):
        block = place.both(mine, theirs)
        block = place.gather(block, "z", 0)
        block = place.gather(block, "x", 1)
        block = place.gather(block, "y", 3)
        return block.reshape(parts * block.shape[-2], block.shape[-1])

    mixing = mixing_weight.reshape(rows_in, 3, 2, half)
    mine, theirs = by_core(mixing, 2)
    mixing = gather_rows(mine.reshape(rows_in, -1), theirs.reshape(rows_in, -1))
    mine, theirs = by_core(output_weight.reshape(rows_in, 2, half), 1)
    out_half = gather_rows(mine, theirs)
    out_all = place.both(out_half, out_half).transpose(1, 0, 2).reshape(width, width)
    mine, theirs = by_core(up_weight.reshape(rows_in, chips, 2, ny * rows_hid), 2)
    up = gather_rows(mine.reshape(rows_in, -1), theirs.reshape(rows_in, -1))
    down = place.gather(down_weight, "z", 0)
    down = place.gather(down, "x", 1)
    down = place.gather(down, "y", 2).reshape(chips * ny * rows_hid, width)

    mixing = mixing.reshape(width, 3, per_core, head)
    head_weight = lax.dynamic_index_in_dim(mixing, my_head, 2, keepdims=False).reshape(width, 3 * head)
    whole_head = core * per_core + my_head
    head_bias = lax.dynamic_index_in_dim(mix_bias, whole_head, 1, keepdims=False)
    head_bias = jnp.concatenate([head_bias[0], jnp.zeros((head,), FULL), head_bias[1]])
    first_low, q, k, v, out, out_t, top = attend_plain(
        x_all, first_gain[None], first_shift[None], head_weight, head_bias[None]
    )
    attended = collect(exchange(out.reshape(chips, 2 * span, head)))
    attended = attended.transpose(1, 0, 2).reshape(2 * span, half)
    attended = place.both(attended, attended).transpose(1, 0, 2).reshape(2 * span, width)

    residual = lax.dynamic_slice_in_dim(x_all, chip * 2 * span, 2 * span, 0).astype(FULL)
    branch = dot(attended, out_all, (1, 0)) + out_bias
    scale = jnp.array(SCALES, FULL)[:, None, None]
    middle = residual + scale * branch
    second_normed, second_inv = normalize(middle)
    second_low = (second_normed * second_gain + second_shift).astype(LOW)
    rows = second_low.reshape(4 * span, width)
    hidden_pre = dot(rows, up, (1, 0)) + up_bias_mine
    activated, gelu_back = jax.vjp(partial(jax.nn.gelu, approximate=True), hidden_pre)
    activated_low = activated.astype(LOW)
    feed_part = dot(activated_low, down, (1, 0)).reshape(2, 2, span, width)
    mine, theirs = by_core(feed_part, 1)
    feed_own = mine + place.send(theirs, "core") + down_bias_all

    def own_rows(values):
        return lax.dynamic_index_in_dim(
            values.reshape((2, 2, span) + values.shape[2:]), core, 1, keepdims=False
        )

    activations = (own_rows(middle) + scale * feed_own).astype(LOW)
    upstream_own = cotangent.reshape(2, span, width)
    upstream = place.both(upstream_own, upstream_own).transpose(1, 0, 2, 3)
    down_in = (scale[..., None] * upstream.astype(FULL)).astype(LOW).reshape(4 * span, width)
    hidden_low = gelu_back(dot(down_in, down, (1, 1)))[0].astype(LOW)
    second_part = dot(hidden_low, up, (1, 1)).reshape(2, 2, span, width)
    mine, theirs = by_core(second_part, 1)
    second_grad = mine + place.send(theirs, "core")
    normed_own, inv_own = own_rows(second_normed), own_rows(second_inv)
    middle_grad = upstream_own.astype(FULL) + norm_back(second_grad, normed_own, inv_own, second_gain)
    branch_own = (scale * middle_grad).astype(LOW)
    branch_low = place.both(branch_own, branch_own).transpose(1, 0, 2, 3).reshape(2, 2 * span, width)
    out_rows = lax.dynamic_slice_in_dim(out_all, core * half, half, 0)
    go = dot(branch_low.reshape(4 * span, width), out_rows, (1, 1)).astype(LOW)
    go = go.reshape(2, 2 * span, per_core, head).transpose(2, 1, 0, 3).reshape(per_core, 2 * span, 2 * head)
    go = exchange(spread(go)).reshape(chips * 2 * span, 2 * head)

    gq, gk, gv = attend_back(q, k, v, out_t, top, go)
    head_grads = jnp.concatenate([gq, gk, gv], axis=1)

    depth_rows = second_low.reshape(2, 2 * span, width)
    hidden_rows = hidden_low.reshape(2, 2 * span, -1)
    active_rows = activated_low.reshape(2, 2 * span, -1)
    in_rows = down_in.reshape(2, 2 * span, width)
    branch_cols = lax.dynamic_slice_in_dim(branch_low, core * half, half, 2)
    orders = (("y", "x"), ("x", "y"))

    def scatter_chips(values, order):
        dims = {"x": 1, "y": 2}
        values = place.scatter(values, order[0], dims[order[0]]).astype(LOW)
        values = place.scatter(values, order[1], 1).astype(LOW)
        return place.scatter(values, "z", 0)

    def scatter_rows(values, order):
        shaped = values.reshape(nz, 2, 2, ny, rows_in, -1).transpose(0, 1, 3, 2, 4, 5)
        summed = scatter_chips(shaped, order)
        mine, theirs = by_core(summed, 0)
        return place.both(mine, theirs)

    down_grads, up_grads, out_grads = [], [], []
    for depth in range(2):
        grad = dot(active_rows[depth], in_rows[depth], (0, 0)).astype(LOW)
        down_grads.append(scatter_chips(grad.reshape(nz, 2, ny, rows_hid, width), orders[depth]))
    for depth in range(2):
        grad = dot(depth_rows[depth], hidden_rows[depth], (0, 0)).astype(LOW)
        grad = scatter_rows(grad, orders[depth]).reshape(2, rows_in, chips, -1)
        up_grads.append(grad.transpose(1, 2, 0, 3).reshape(rows_in, hidden))
    for depth in range(2):
        grad = dot(attended, branch_cols[depth], (0, 0)).astype(LOW)
        out_grads.append(scatter_rows(grad, orders[depth]).transpose(1, 0, 2).reshape(rows_in, width))

    head_sum = dot(first_low, head_grads, (0, 0)).astype(LOW).reshape(nz, 2, 2, ny, rows_in, 6 * head)
    head_sum = place.scatter(head_sum, "y", 3).astype(LOW).reshape(chips, 2, rows_in, 6 * head)
    head_sum = collect(exchange(head_sum))
    mine, theirs = by_core(head_sum, 1)
    mixing_grad = place.both(mine, theirs).reshape(HEADS, rows_in, 3, 2, head)
    mixing_grad = mixing_grad.transpose(3, 1, 2, 0, 4).reshape(2, rows_in, 3 * width).astype(FULL)

    mixed_grads = collect(exchange(head_grads.reshape(chips, 2 * span, 6 * head)))
    mixed_grads = mixed_grads.reshape(per_core, 2 * span, 3, 2, head).transpose(3, 1, 2, 0, 4)
    mixed_grads = mixed_grads.reshape(4 * span, 3 * half)
    first_part = dot(mixed_grads, mixing.reshape(width, 3 * half), (1, 1)).reshape(2, 2, span, width)
    mine, theirs = by_core(first_part, 1)
    first_grad = mine + place.send(theirs, "core")
    first_normed, first_inv = normalize(own.astype(FULL))
    input_grad = middle_grad + norm_back(first_grad, first_normed, first_inv, first_gain)

    bias_sum = jnp.sum(head_grads.astype(FULL), axis=0).reshape(3, 2, head) * busy
    spot = (jnp.arange(HEADS) == whole_head).astype(FULL)[None, None, :, None]
    bias_sum = (jnp.stack([bias_sum[0], bias_sum[2]], axis=1)[:, :, None, :] * spot).reshape(2, parts, -1)
    hidden_sum = jnp.sum(hidden_rows.astype(FULL), axis=1).reshape(2, chips, 1, ny * rows_hid)
    hidden_spot = (jnp.arange(2) == core).astype(FULL)[None, None, :, None]
    hidden_sum = (hidden_sum * hidden_spot).reshape(2, parts, rows_hid)
    in_own = (scale * upstream_own.astype(FULL)).astype(LOW)
    sums = [
        jnp.sum(first_grad * first_normed, axis=1),
        jnp.sum(first_grad, axis=1),
        jnp.sum(second_grad * normed_own, axis=1),
        jnp.sum(second_grad, axis=1),
        jnp.sum(branch_own.astype(FULL), axis=1),
        jnp.sum(in_own.astype(FULL), axis=1),
    ]
    sums = [item.reshape(2, parts, rows_in) for item in sums] + [bias_sum, hidden_sum]
    sums = jnp.concatenate(sums, axis=2).reshape(2, nz, 2, 2, ny, -1)
    sums = place.scatter(sums, "y", 4)
    sums = place.scatter(sums, "x", 2)
    sums = place.scatter(sums, "core", 2)
    sums = place.scatter(sums, "z", 1)
    small = [sums[:, i * rows_in : (i + 1) * rows_in] for i in range(6)]
    return (
        activations[:, None],
        input_grad[:, None],
        small[0],
        small[1],
        mixing_grad,
        sums[:, 6 * rows_in : 8 * rows_in],
        jnp.stack(out_grads),
        small[4],
        small[2],
        small[3],
        jnp.stack(up_grads),
        sums[:, 8 * rows_in :],
        jnp.stack(down_grads),
        small[5],
    )


def on_device(
    inputs,
    attend_gain,
    attend_shift,
    mixing_weight,
    mixing_bias,
    output_weight,
    output_bias,
    feed_gain,
    feed_shift,
    up_weight,
    up_bias,
    down_weight,
    down_bias,
    cotangent,
):
    place = Place()
    _, span, width = inputs.shape
    nz, ny, core, chip = place.nz, place.ny, place.core, place.chip
    chips = nz * 2
    parts = chips * 2 * ny
    head = width // HEADS
    per_core = HEADS // 2
    half = width // 2
    hidden = up_weight.shape[1]
    rows_in = width // parts
    rows_hid = hidden // parts
    groups = [[2 * i + c for i in range(chips)] for c in range(2)]

    def by_core(values, dim):
        mine = lax.dynamic_index_in_dim(values, core, dim, keepdims=False)
        theirs = lax.dynamic_index_in_dim(values, 1 - core, dim, keepdims=False)
        return mine, theirs

    own = inputs.reshape(span, width)
    pairs = per_core // 2
    mix = mixing_weight.reshape(rows_in, 3, 2, pairs, 2, head).transpose(2, 3, 0, 1, 4, 5)
    mix = mix.reshape(2, pairs, rows_in, half)
    out_cols = output_weight.reshape(rows_in, 2, half).transpose(1, 0, 2)[:, None]
    vectors, start = jnp.zeros((half,), LOW), 0
    for piece in (
        attend_gain, attend_shift, feed_gain, feed_shift, output_bias, down_bias, mixing_bias, up_bias
    ):
        vectors = vectors + jnp.pad(piece, (start, half - start - piece.shape[0]))
        start += piece.shape[0]
    vectors = jnp.broadcast_to(jnp.pad(vectors[None], ((0, 7), (0, 0))), (2, 8, half))
    packed = jnp.concatenate([mix.reshape(2, pairs * rows_in, half), out_cols[:, 0], vectors], axis=1)
    up_cols = up_weight.reshape(rows_in, chips, 2, ny * rows_hid).transpose(2, 0, 1, 3).reshape(2, rows_in, -1)
    mine, theirs = by_core(packed, 0)
    packed = place.both(mine, theirs)
    cut = pairs * rows_in
    pair_rows = packed[:, :cut].reshape(2, pairs, rows_in, half).transpose(1, 0, 2, 3).reshape(2 * cut, half)
    packed_rows = jnp.concatenate([pair_rows, packed[:, cut + rows_in :].reshape(16, half)])
    mine, theirs = by_core(up_cols, 0)
    up_unit = place.both(mine, theirs).reshape(2 * rows_in, -1, half).transpose(1, 0, 2)
    up_unit = jnp.concatenate([up_unit, packed[:, cut : cut + rows_in].reshape(1, 2 * rows_in, half)])

    mw_all, up_all, dn_all, first_low, q, k, v, out_t, top, attended, x2 = attend(
        nz, ny, own, packed_rows, up_unit, down_weight
    )

    raw = rest(
        nz, x2.reshape(2 * span, width), attended, cotangent.reshape(2, span, width), mw_all,
        up_all, dn_all.reshape(-1, width), q, k, v, out_t, top, first_low,
    )
    activations, input_grad, *others = finish(nz, *raw)
    return (activations[:, None], input_grad[:, None], *others)


def tiles_well(mesh):
    ny, seq = mesh.shape["batch"], mesh.shape["seq"]
    rows_in = 768 // (seq * ny)
    return ny == 2 and seq // 2 >= HEADS // 2 and 2 * rows_in % 16 == 0 and 2 * rows_in * seq * ny == 2 * 768


def solution(mesh):
    shard = P(("seq", "batch"))
    grad = P(None, ("seq", "batch"))
    row = P(None, "batch", "seq", None)
    return jax.shard_map(
        on_device if tiles_well(mesh) else plain_on_device,
        mesh=mesh,
        in_specs=(P("batch", "seq", None),) + (shard,) * 12 + (row,),
        out_specs=(row, row) + (grad,) * 12,
        check_vma=False,
    )
```
